32 devices in a mesh: plane: 4 (over y, x), wire: 4 (over z), tick: 2 (over core).
Axes of the slice: x: 2, y: 2, z: 4, core: 2. Of those that a mesh axis runs over, the one named last changes fastest.
Arguments:
- raw: bfloat16 [4096, 4096], P(('plane', 'wire'), 'tick'), may hold values from -6 to 6
- chan_mask: int32 [4096], P(('plane', 'wire')), may hold values 0 or 1
- kernel: bfloat16 [4, 21, 256], P('plane'), may hold values from -0.078125 to 0.078125
- geometry: bfloat16 [128, 32, 128], replicated, may hold values from -1 to 1
- roi_block: int32 [3264], P(('plane', 'wire', 'tick')), may hold values from 0 to 127, as said below
- roi_owner: int32 [3264], P(('plane', 'wire', 'tick')), may hold values from 0 to 15, as said below
Outputs:
- signal: bfloat16 [4096, 4096], P(('plane', 'wire'), 'tick')
- image: float32 [2048, 4096], P(('plane', 'wire'), 'tick')
The draws below stay inside these ranges and needn't reach their ends.
Inputs may be any that keep to these rules, and one draw needn't show every extreme that they name: `roi_block`: the 102 ids of one device are distinct. `roi_owner`: owner o is the device of the same tick shard whose index over plane and wire together is o. A device names one owner in at most 25 slots; in every tick shard one owner is named in exactly 25 slots by every device of that shard.
All inputs are finite; a program needn't handle non-finite values. No bound on the sum of `chan_mask` on one device may be relied on, other than what follows from the above.
Results may differ from the reference program's by a relative error of at most 0.0029.
Values may be sent and summed in bfloat16 or wider, within the bound.
No kernel may reach another device: no remote copies, remote signals or barrier semaphores. Data moves between devices by JAX's collectives and lax.ppermute only.
A program may use at most 64 MiB of HBM per device.

```python
import jax
import jax.numpy as jnp
from jax import lax

WD = 256
TK = 2048
KW = 21
KT = 256
WB = 32
TB = 128
CELLS = 128
WBLK = 8
TBLK = 16
NBLK = 128
SLOTS = 102
CAP = 25
OWNERS = 16
TSHARDS = 2
WIRES = 4096
TICKS = 4096
GEOS = 128
N_PLANE = 4
N_WIRE = 4
N_TICK = 2


def roi_tables(key):
    base = jax.random.fold_in(key, 7)
    hot_key, dev_key = jax.random.split(base, 2)
    hot_owner = jax.random.randint(hot_key, (TSHARDS,), 0, OWNERS)

    def one_device(dev_rng, device):
        perm_key, shift_key, order_key = jax.random.split(dev_rng, 3)
        block_list = jax.random.permutation(perm_key, NBLK)[:SLOTS]
        target = hot_owner[device % TSHARDS]
        positions = jnp.arange(SLOTS, dtype=jnp.int32)
        shift = jax.random.randint(shift_key, (), 0, OWNERS - 1)
        others = (target + 1 + (positions - CAP + shift) % (OWNERS - 1)) % OWNERS
        dest_list = jnp.where(positions < CAP, target, others)
        order = jax.random.permutation(order_key, SLOTS)
        return (block_list, dest_list[order])
    dev_keys = jax.random.split(dev_key, OWNERS * TSHARDS)
    block_all, dest_all = jax.vmap(one_device)(dev_keys, jnp.arange(OWNERS * TSHARDS, dtype=jnp.int32))
    return (block_all.reshape(-1).astype(jnp.int32), dest_all.reshape(-1).astype(jnp.int32))


def draw_roi_block(key, part):
    return roi_tables(key)[0]


def draw_roi_owner(key, part):
    return roi_tables(key)[1]


def plant(array, rng, low, top_value):
    dims = array.shape
    place = [jax.random.randint(jax.random.fold_in(rng, axis), (), 0, dims[axis]) for axis in range(len(dims))]
    array = array.at[tuple(place)].set(low)
    longest = dims.index(max(dims))
    place[longest] = (place[longest] + 1) % dims[longest]
    return array.at[tuple(place)].set(top_value)


def block_levels(rng, extent, cuts, smallest, top_value):
    def one(position, parts):
        steps = jax.random.uniform(jax.random.fold_in(jax.random.fold_in(rng, 6), position), (parts,), jnp.float32, smallest / len(cuts), top_value / len(cuts))
        return jnp.repeat(jnp.exp(steps), extent[position] // parts).reshape((-1,) + (1,) * (len(extent) - position - 1))

    loudness = one(*cuts[0])
    for cut in cuts[1:]:
        loudness = loudness * one(*cut)
    return loudness


def scatter_about(key, extent, width, bound, cuts=(), kind=jnp.bfloat16):
    drawn = width * jax.random.normal(key, extent, jnp.float32)
    if cuts:
        drawn = drawn * block_levels(key, extent, cuts, -0.22, 0.18)
    return jnp.clip(drawn, -bound, bound).astype(kind)


def setup_inputs(seed: int = 0) -> dict:
    key_list = jax.random.split(jax.random.key(seed), 7)
    return {
        "raw": scatter_about(key_list[0], (WIRES, TICKS), 1.0, 6.0, ((0, 16), (1, 2))),
        "chan_mask": plant((jax.random.randint(key_list[1], (WIRES,), 0, 16) < 15).astype(jnp.int32), jax.random.fold_in(key_list[1], 1), 0, 1),
        "kernel": scatter_about(key_list[2], (N_PLANE, KW, KT), (KW * KT) ** -0.5, 0.078125, ((0, 4),)),
        "geometry": scatter_about(key_list[3], (GEOS, WB, CELLS), WB ** -0.5, 1.0),
        "roi_block": draw_roi_block(jax.random.fold_in(key_list[6], 71), 0),
        "roi_owner": draw_roi_owner(jax.random.fold_in(key_list[6], 71), 0),
    }


def reference(raw, chan_mask, kernel, geometry, roi_block, roi_owner):
    group_wires = N_WIRE * WD
    half_w = KW // 2
    half_t = KT // 2
    fft_length = TICKS + KT
    masked = raw * chan_mask[:, None].astype(jnp.bfloat16)
    planes_in = masked.astype(jnp.float32).reshape(N_PLANE, group_wires, TICKS)

    def deconvolve(pieces):
        plane_data, plane_kernel = pieces
        spectrum = jnp.fft.rfft(plane_data, n=fft_length, axis=-1)
        spectrum = jnp.pad(spectrum, ((half_w, half_w), (0, 0)))
        kernel_spec = jnp.fft.rfft(plane_kernel.astype(jnp.float32), n=fft_length, axis=-1)
        accum = jnp.zeros((group_wires, spectrum.shape[1]), spectrum.dtype)
        for tap_index in range(KW):
            accum = accum + kernel_spec[tap_index][None, :] * spectrum[tap_index:tap_index + group_wires]
        return jnp.fft.irfft(accum, n=fft_length, axis=-1)[:, half_t:half_t + TICKS]

    filtered = lax.map(deconvolve, (planes_in, kernel))
    signal = filtered.reshape(WIRES, TICKS).astype(jnp.bfloat16)

    grid = signal.reshape(N_PLANE, N_WIRE, WBLK, WB, N_TICK, TBLK, TB)
    block_tiles = grid.transpose(4, 0, 1, 2, 5, 3, 6).reshape(N_TICK, OWNERS, NBLK, WB, TB)
    block_ids = roi_block.reshape(OWNERS, N_TICK, SLOTS).transpose(1, 0, 2)
    owner_ids = roi_owner.reshape(OWNERS, N_TICK, SLOTS).transpose(1, 0, 2)

    def per_tick(pieces):
        tiles_now, ids_now, owners_now = pieces
        chosen = jnp.take_along_axis(tiles_now, ids_now[:, :, None, None], axis=1)
        chosen = chosen.reshape(OWNERS * SLOTS, WB, TB).astype(jnp.float32)
        geo_index = (jnp.arange(OWNERS, dtype=jnp.int32)[:, None] * WBLK + ids_now // TBLK).reshape(-1)
        geo_rows = geometry[geo_index].astype(jnp.float32)
        products = jnp.einsum('swc,swt->sct', geo_rows, chosen, precision=lax.Precision.HIGHEST)
        seg_keys = (owners_now * TBLK + ids_now % TBLK).reshape(-1).astype(jnp.int32)
        summed = jax.ops.segment_sum(products, seg_keys, num_segments=OWNERS * TBLK)
        return summed.reshape(OWNERS, TBLK, CELLS, TB).transpose(0, 2, 1, 3).reshape(OWNERS, CELLS, TK)

    images = lax.map(per_tick, (block_tiles, block_ids, owner_ids))
    image = images.transpose(1, 2, 0, 3).reshape(OWNERS * CELLS, TICKS)
    return signal, image
```

```python
import functools

import jax
import jax.numpy as jnp
from jax import lax
from jax.experimental import pallas as pl
from jax.experimental.pallas import tpu as pltpu
from jax.sharding import PartitionSpec as P

TB = 128
CAP = 25
PAD = 16
MIB = 1024 * 1024


def vmem():
    return pl.BlockSpec(memory_space=pltpu.VMEM)


def smem():
    return pl.BlockSpec(memory_space=pltpu.SMEM)


def plan_kernel(owner_total, share, tick_count, where_ref, rows_ref, own_ref, out_ref):
    me = where_ref[0]
    tick = where_ref[1]
    lanes = lax.broadcasted_iota(jnp.int32, (1, 128), 1)
    best = jnp.zeros((1, 1), jnp.float32)
    hot_mine = jnp.zeros((1, 1), jnp.float32)
    for shard in range(tick_count):
        owners = rows_ref[pl.ds(shard * owner_total, owner_total), :] >> 7
        least = jnp.full((1, 128), -1.0, jnp.float32)
        most = jnp.zeros((1, 128), jnp.float32)
        for owner in range(owner_total):
            named = jnp.sum((owners == owner).astype(jnp.float32), axis=1, keepdims=True)
            least = jnp.where(lanes == owner, jnp.min(named, axis=0, keepdims=True), least)
            most = jnp.where(lanes == owner, jnp.max(named, axis=0, keepdims=True), most)
        top = jnp.max(least, axis=1, keepdims=True)
        lane_f = lanes.astype(jnp.float32)
        hot = jnp.min(jnp.where(least == top, lane_f, 127.0), axis=1, keepdims=True)
        others = jnp.max(jnp.where(lane_f == hot, 0.0, most), axis=1, keepdims=True)
        best = jnp.maximum(best, others)
        hot_mine = jnp.where(tick == shard, hot, hot_mine)
    rounds = jnp.zeros((1, 1), jnp.float32)
    for step in range(-(-CAP // share)):
        rounds = rounds + (best > step * share).astype(jnp.float32)

    before = (
        lax.broadcasted_iota(jnp.int32, (128, 128), 0)
        < lax.broadcasted_iota(jnp.int32, (128, 128), 1)
    ).astype(jnp.bfloat16)

    mine = own_ref[...]
    rows = lax.broadcasted_iota(jnp.int32, (owner_total, 128), 0)
    member = (mine >> 7) == rows
    rank = jnp.dot(member.astype(jnp.bfloat16), before, preferred_element_type=jnp.float32)
    rows_f = rows.astype(jnp.float32)
    block = (mine & 127).astype(jnp.float32)
    slots = float(owner_total * share)
    place = jnp.where(rank < share, rows_f * share + rank, slots + 128.0)
    place = jnp.where(rows_f == hot_mine, slots + block, place)
    place = jnp.sum(jnp.where(member, place, 0.0), axis=0, keepdims=True)

    shard_rows = rows_ref[pl.ds(pl.multiple_of(tick * owner_total, 8), owner_total), :]
    to_me = (shard_rows >> 7) == me
    rank = jnp.dot(to_me.astype(jnp.bfloat16), before, preferred_element_type=jnp.float32)
    blocks = (shard_rows & 127).astype(jnp.float32)
    table = jnp.zeros((owner_total, 128), jnp.float32)
    for slot in range(share):
        got = jnp.sum(jnp.where(to_me & (rank == slot), blocks, 0.0), axis=1, keepdims=True)
        table = jnp.where(lanes == slot, got, table)

    facts = jnp.where(lanes == 0, hot_mine, jnp.where(lanes == 1, rounds, 0.0))
    out_ref[0:1, :] = place.astype(jnp.int32)
    out_ref[1:2, :] = facts.astype(jnp.int32)
    out_ref[2:3, :] = mine & 127
    out_ref[3:8, :] = jnp.zeros((5, 128), jnp.int32)
    out_ref[8 : 8 + owner_total, :] = table.astype(jnp.int32)


def make_plan(packed, me, tick, owner_total, share, tick_count):
    rows = lax.all_gather(packed, ("tick", "plane", "wire"), axis=0, tiled=True)
    return pl.pallas_call(
        functools.partial(plan_kernel, owner_total, share, tick_count),
        out_shape=jax.ShapeDtypeStruct((8 + owner_total, 128), jnp.int32),
        in_specs=[smem(), vmem(), vmem()],
        out_specs=vmem(),
        name="plan",
    )(jnp.stack([me, tick]), rows, packed), rows


def band_kernel(taps_w, taps_ref, band_ref):
    row = lax.broadcasted_iota(jnp.int32, (TB, TB), 0)
    col = lax.broadcasted_iota(jnp.int32, (TB, TB), 1)
    zero = jnp.zeros((TB, TB), jnp.bfloat16)
    pairs = (taps_w + 1) // 2
    for piece in range(3):
        band_ref[piece, 0:TB, TB : 2 * TB] = zero
        band_ref[piece, (2 * pairs - 1) * TB : 2 * pairs * TB, 0:TB] = zero
    taps = taps_ref[...].astype(jnp.float32)
    for tap in range(taps_w):
        spread = jnp.broadcast_to(taps[tap : tap + 1], (TB, 2 * TB))
        rolled = pltpu.roll(spread, TB, 1, stride=1, stride_axis=0)
        middle = rolled[:, :TB]
        outer = rolled[:, TB:]
        bands = (
            jnp.where(col < row, outer, 0.0).astype(jnp.bfloat16),
            middle.astype(jnp.bfloat16),
            jnp.where(col >= row, outer, 0.0).astype(jnp.bfloat16),
        )
        for first, second in ((0, 0), (1, 1), (1, 0), (0, 1)):
            if (tap - first + second) % 2:
                continue
            start = (tap - first + second) * TB + first * TB
            for piece in range(3):
                band_ref[piece, start : start + TB, second * TB : (second + 1) * TB] = bands[piece]


def make_bands(taps):
    taps_w = taps.shape[0]
    return pl.pallas_call(
        functools.partial(band_kernel, taps_w),
        out_shape=jax.ShapeDtypeStruct((3, (taps_w + 1) * TB, 2 * TB), jnp.bfloat16),
        in_specs=[vmem()],
        out_specs=vmem(),
        cost_estimate=pl.CostEstimate(flops=10**9, bytes_accessed=6 * MIB, transcendentals=0),
        compiler_params=pltpu.CompilerParams(vmem_limit_bytes=16 * MIB),
        name="bands",
    )(taps)


def conv_kernel(
    taps_w,
    slots,
    slot_count,
    plan_ref,
    where_ref,
    raw_ref,
    mask_ref,
    left_ref,
    right_ref,
    top_ref,
    bottom_ref,
    band_ref,
    geo_ref,
    signal_ref,
    payload_ref,
    partial_ref,
    wide_ref,
    lhs_ref,
    weave_ref,
    tiles_ref,
):
    wires, ticks = raw_ref.shape
    blocks = ticks // TB
    half = wires // 2
    block_wires = geo_ref.shape[1]
    wire_blocks = wires // block_wires

    first = PAD - taps_w // 2
    mask = mask_ref[...].astype(jnp.float32)
    for block in range(blocks + 2):
        columns = slice(block * TB, (block + 1) * TB)
        if block == 0:
            inner = left_ref[...].astype(jnp.float32)
        elif block == blocks + 1:
            inner = right_ref[...].astype(jnp.float32)
        else:
            inner = raw_ref[:, (block - 1) * TB : block * TB].astype(jnp.float32) * mask
        wide_ref[block, 0:PAD] = top_ref[:, columns].astype(jnp.float32)
        wide_ref[block, PAD : PAD + wires] = inner
        wide_ref[block, PAD + wires :] = bottom_ref[:, columns].astype(jnp.float32)

    def spread(block, carry):
        for wire in range(taps_w + 1):
            lhs_ref[block, :, wire * TB : (wire + 1) * TB] = wide_ref[
                block, pl.ds(first + wire, half, stride=2), :
            ].astype(jnp.bfloat16)
        return carry

    lax.fori_loop(0, blocks + 2, spread, 0)

    chunk = 4

    def convolve(step, carry):
        total = jnp.zeros((chunk * half, 2 * TB), jnp.float32)
        for piece in range(3):
            rows = lhs_ref[pl.ds(step * chunk + piece, chunk)].reshape(chunk * half, -1)
            total = total + jnp.dot(rows, band_ref[piece], preferred_element_type=jnp.float32)
        for index in range(chunk):
            part = total[index * half : (index + 1) * half]
            weave_ref[pl.ds(0, half, stride=2), :] = part[:, :TB]
            weave_ref[pl.ds(1, half, stride=2), :] = part[:, TB:]
            at = pl.multiple_of((step * chunk + index) * TB, TB)
            signal_ref[:, pl.ds(at, TB)] = weave_ref[...].astype(jnp.bfloat16)
        return carry

    lax.fori_loop(0, blocks // chunk, convolve, 0)

    tiles_ref[...] = jnp.zeros_like(tiles_ref)

    def pack(slot, carry):
        block = plan_ref[2, slot]
        place = plan_ref[0, slot]
        wire = pl.multiple_of((block // blocks) * block_wires, block_wires)
        tick = pl.multiple_of((block % blocks) * TB, TB)
        tiles_ref[place] = signal_ref[pl.ds(wire, block_wires), pl.ds(tick, TB)]
        return carry

    lax.fori_loop(0, slot_count, pack, 0, unroll=6)
    payload_ref[...] = tiles_ref[0:slots]

    source = where_ref[0]
    rows = geo_ref[pl.ds(source * wire_blocks, wire_blocks)].reshape(wires, -1)
    for block in range(0, blocks, 2):
        chosen = jnp.concatenate(
            [
                jnp.concatenate(
                    [tiles_ref[slots + line * blocks + block + side] for line in range(wire_blocks)],
                    axis=0,
                )
                for side in range(2)
            ],
            axis=1,
        )
        sums = lax.dot_general(
            rows, chosen, (((0,), (0,)), ((), ())), preferred_element_type=jnp.float32
        ).astype(jnp.bfloat16)
        partial_ref[block] = sums[:, :TB]
        partial_ref[block + 1] = sums[:, TB:]


def convolve_and_pack(plan, place, raw, mask, left, right, top, bottom, bands, geometry, slots, slot_count):
    wires, ticks = raw.shape
    taps_w = bands.shape[1] // TB - 1
    block_wires = geometry.shape[1]
    cells = geometry.shape[2]
    tick_blocks = ticks // TB
    tile_total = slots + (wires // block_wires) * tick_blocks + 1
    flops = 2 * tick_blocks * (wires // 2) * 3 * (taps_w + 1) * TB * 2 * TB
    return pl.pallas_call(
        functools.partial(conv_kernel, taps_w, slots, slot_count),
        out_shape=(
            jax.ShapeDtypeStruct((wires, ticks), jnp.bfloat16),
            jax.ShapeDtypeStruct((slots, block_wires, TB), jnp.bfloat16),
            jax.ShapeDtypeStruct((tick_blocks, cells, TB), jnp.bfloat16),
        ),
        in_specs=[smem(), smem()] + [vmem()] * 8,
        out_specs=(vmem(), vmem(), vmem()),
        scratch_shapes=[
            pltpu.VMEM((tick_blocks + 2, wires + 2 * PAD, TB), jnp.float32),
            pltpu.VMEM((tick_blocks + 2, wires // 2, (taps_w + 1) * TB), jnp.bfloat16),
            pltpu.VMEM((wires, TB), jnp.float32),
            pltpu.VMEM((tile_total, block_wires, TB), jnp.bfloat16),
        ],
        cost_estimate=pl.CostEstimate(flops=flops, bytes_accessed=8 * MIB, transcendentals=0),
        compiler_params=pltpu.CompilerParams(vmem_limit_bytes=44 * MIB),
        name="deconvolve",
    )(plan, place, raw, mask, left, right, top, bottom, bands, geometry)


def image_kernel(owner_total, share, plan_ref, where_ref, arrived_ref, geo_ref, image_ref):
    cells, ticks = image_ref.shape
    blocks = ticks // TB
    block_wires = geo_ref.shape[1]
    wire_blocks = geo_ref.shape[0] // owner_total
    image_ref[...] = jnp.zeros_like(image_ref)
    is_hot = plan_ref[1, 0] == where_ref[0]

    @pl.when(is_hot)
    def _():
        for source in range(owner_total):
            sums = arrived_ref[source * share : source * share + cells // block_wires]
            image_ref[:, source * TB : (source + 1) * TB] = sums.reshape(cells, TB).astype(
                jnp.float32
            )

    @pl.when(jnp.logical_not(is_hot))
    def _():
        def add(source, carry):
            products = []
            for slot in range(share):
                block = plan_ref[8 + source, slot]
                row = source * wire_blocks + block // blocks
                products.append(
                    (
                        pl.multiple_of((block % blocks) * TB, TB),
                        lax.dot_general(
                            geo_ref[row],
                            arrived_ref[source * share + slot],
                            (((0,), (0,)), ((), ())),
                            preferred_element_type=jnp.float32,
                        ),
                    )
                )
            for at, product in products:
                image_ref[:, pl.ds(at, TB)] += product
            return carry

        lax.fori_loop(0, owner_total, add, 0)


def make_image(plan, place, arrived, geometry, owner_total, share, ticks):
    return pl.pallas_call(
        functools.partial(image_kernel, owner_total, share),
        out_shape=jax.ShapeDtypeStruct((geometry.shape[2], ticks), jnp.float32),
        in_specs=[smem(), smem(), vmem(), vmem()],
        out_specs=vmem(),
        cost_estimate=pl.CostEstimate(flops=10**8, bytes_accessed=3 * MIB, transcendentals=0),
        compiler_params=pltpu.CompilerParams(vmem_limit_bytes=16 * MIB),
        name="image",
    )(plan, place, arrived, geometry)


def further_round(step, image, signal, geometry, rows, packed, hot, me, tick, owner_total, share):
    block_wires = geometry.shape[1]
    wire_count, tick_count = signal.shape
    blocks = tick_count // TB
    wire_blocks = wire_count // block_wires
    ids = jnp.arange(owner_total, dtype=jnp.int32)

    def ranks(owners):
        member = (owners[..., None] == ids).astype(jnp.int32)
        before = jnp.cumsum(member, axis=-2) - member
        return jnp.sum(before * member, axis=-1) - step * share

    def live(owners, rank):
        return (owners < owner_total) & (owners != hot) & (rank >= 0) & (rank < share)

    owners = packed[0] >> 7
    block = packed[0] & 127
    rank = ranks(owners)
    place = jnp.where(live(owners, rank), owners * share + rank, owner_total * share)
    tiles = signal.reshape(wire_blocks, block_wires, blocks, TB).transpose(0, 2, 1, 3)
    tiles = tiles.reshape(wire_blocks * blocks, block_wires, TB)[block]
    payload = jnp.zeros((owner_total * share, block_wires, TB), jnp.bfloat16)
    payload = payload.at[place].set(tiles, mode="drop")
    arrived = lax.all_to_all(
        payload.reshape(owner_total, share, block_wires, TB),
        ("plane", "wire"),
        split_axis=0,
        concat_axis=0,
        tiled=True,
    ).reshape(owner_total * share, block_wires, TB)

    shard = lax.dynamic_slice_in_dim(rows, tick * owner_total, owner_total, 0)
    owners = shard >> 7
    rank = ranks(owners)
    source = jnp.arange(owner_total, dtype=jnp.int32)[:, None]
    place = jnp.where(
        live(owners, rank) & (owners == me), source * share + rank, owner_total * share
    ).reshape(-1)
    table = jnp.zeros((owner_total * share,), jnp.int32)
    block = table.at[place].set((shard & 127).reshape(-1), mode="drop")
    geo_id = table.at[place].set(
        (source * wire_blocks + (shard & 127) // blocks).reshape(-1), mode="drop"
    )
    products = jnp.einsum(
        "swc,swt->sct", geometry[geo_id], arrived, preferred_element_type=jnp.float32
    )
    summed = jax.ops.segment_sum(products, block % blocks, num_segments=blocks)
    return image + summed.transpose(1, 0, 2).reshape(image.shape)


def tick_halo(raw, mask, width):
    devices = lax.axis_size("tick")
    tick = lax.axis_index("tick")
    last = raw[:, -width:] * mask
    leading = raw[:, :width] * mask
    if devices == 2:
        got = lax.ppermute(jnp.where(tick == 0, last, leading), "tick", [(0, 1), (1, 0)])
        nothing = jnp.zeros_like(got)
        return jnp.where(tick == 0, nothing, got), jnp.where(tick == 0, got, nothing)
    up = [(i, i + 1) for i in range(devices - 1)]
    down = [(i + 1, i) for i in range(devices - 1)]
    return lax.ppermute(last, "tick", up), lax.ppermute(leading, "tick", down)


def wire_halo(raw, mask, left, right):
    devices = lax.axis_size("wire")
    up = [(i, i + 1) for i in range(devices - 1)]
    down = [(i + 1, i) for i in range(devices - 1)]

    def edge(where):
        return jnp.concatenate([left[where], raw[where] * mask[where], right[where]], axis=1)

    top = lax.ppermute(edge(slice(-PAD, None)), "wire", up)
    bottom = lax.ppermute(edge(slice(0, PAD)), "wire", down)
    return top, bottom


def exchange(array):
    return lax.all_to_all(array, ("plane", "wire"), split_axis=0, concat_axis=0, tiled=True)


def shards(raw, chan_mask, kernel, geometry, roi_block, roi_owner):
    wires, ticks = raw.shape
    slot_count = roi_block.shape[0]
    block_wires = geometry.shape[1]
    cells = geometry.shape[2]
    tick_blocks = ticks // TB
    owner_total = lax.axis_size("plane") * lax.axis_size("wire")
    tick_total = lax.axis_size("tick")
    share = -(-(slot_count - CAP) // (owner_total - 1))
    me = lax.axis_index("plane") * lax.axis_size("wire") + lax.axis_index("wire")
    tick = lax.axis_index("tick")
    place = jnp.stack([me, tick])

    packed = jnp.pad(
        roi_owner * 128 + roi_block, (0, 128 - slot_count), constant_values=owner_total * 128
    )[None]
    plan, rows = make_plan(packed, me, tick, owner_total, share, tick_total)

    mask = chan_mask[:, None].astype(jnp.bfloat16)
    left, right = tick_halo(raw, mask, TB)
    top, bottom = wire_halo(raw, mask, left, right)
    bands = make_bands(kernel[0])
    signal, payload, partial = convolve_and_pack(
        plan, place, raw, mask, left, right, top, bottom, bands, geometry, owner_total * share, slot_count
    )

    pieces = exchange(partial)
    sums = jnp.sum(pieces.astype(jnp.float32), axis=0).astype(jnp.bfloat16)
    hot = plan[1, 0]
    payload = payload.reshape(owner_total, share, block_wires, TB)
    payload = lax.dynamic_update_slice(
        payload, sums.reshape(1, cells // block_wires, block_wires, TB), (hot, 0, 0, 0)
    )
    arrived = exchange(payload).reshape(owner_total * share, block_wires, TB)
    image = make_image(plan, place, arrived, geometry, owner_total, share, ticks)

    image = lax.fori_loop(
        1,
        plan[1, 1],
        lambda step, now: further_round(
            step, now, signal, geometry, rows, packed, hot, me, tick, owner_total, share
        ),
        image,
    )
    return signal, image


def solution(mesh):
    in_specs = (
        P(("plane", "wire"), "tick"),
        P(("plane", "wire")),
        P("plane", None, None),
        P(),
        P(("plane", "wire", "tick")),
        P(("plane", "wire", "tick")),
    )
    out_specs = (P(("plane", "wire"), "tick"), P(("plane", "wire"), "tick"))
    return jax.shard_map(shards, mesh=mesh, in_specs=in_specs, out_specs=out_specs, check_vma=False)
```

```python
import functools

import jax
import jax.numpy as jnp
from jax import lax
from jax.experimental import pallas as pl
from jax.experimental.pallas import tpu as pltpu
from jax.sharding import PartitionSpec as P

TB = 128
CAP = 25
PAD = 16
MIB = 1024 * 1024


def vmem():
    return pl.BlockSpec(memory_space=pltpu.VMEM)


def smem():
    return pl.BlockSpec(memory_space=pltpu.SMEM)


def plan_kernel(owner_total, share, rows_ref, own_ref, out_ref):
    lanes = lax.broadcasted_iota(jnp.int32, (1, 128), 1)
    lane_f = lanes.astype(jnp.float32)
    every = rows_ref[...]
    owners = every >> 7
    mine = own_ref[...]
    me = jnp.sum(jnp.where(lanes == 127, mine & 127, 0).astype(jnp.float32), axis=1, keepdims=True)

    least = jnp.full((1, 128), -1.0, jnp.float32)
    most = jnp.zeros((1, 128), jnp.float32)
    for owner in range(owner_total):
        named = jnp.sum((owners == owner).astype(jnp.float32), axis=1, keepdims=True)
        least = jnp.where(lanes == owner, jnp.min(named, axis=0, keepdims=True), least)
        most = jnp.where(lanes == owner, jnp.max(named, axis=0, keepdims=True), most)
    top = jnp.max(least, axis=1, keepdims=True)
    hot = jnp.min(jnp.where(least == top, lane_f, 127.0), axis=1, keepdims=True)
    fullest = jnp.max(jnp.where(lane_f == hot, 0.0, most), axis=1, keepdims=True)
    rounds = jnp.zeros((1, 1), jnp.float32)
    for step in range(-(-CAP // share)):
        rounds = rounds + (fullest > step * share).astype(jnp.float32)

    before = (
        lax.broadcasted_iota(jnp.int32, (128, 128), 0)
        < lax.broadcasted_iota(jnp.int32, (128, 128), 1)
    ).astype(jnp.bfloat16)

    rows = lax.broadcasted_iota(jnp.int32, (owner_total, 128), 0)
    member = (mine >> 7) == rows
    rank = jnp.dot(member.astype(jnp.bfloat16), before, preferred_element_type=jnp.float32)
    rows_f = rows.astype(jnp.float32)
    slots = float(owner_total * share)
    place = jnp.where(rank < share, rows_f * share + rank, slots + 128.0)
    place = jnp.where(rows_f == hot, slots + (mine & 127).astype(jnp.float32), place)
    place = jnp.sum(jnp.where(member, place, 0.0), axis=0, keepdims=True)

    to_me = owners.astype(jnp.float32) == me
    rank = jnp.dot(to_me.astype(jnp.bfloat16), before, preferred_element_type=jnp.float32)
    blocks = (every & 127).astype(jnp.float32)
    table = jnp.zeros((owner_total, 128), jnp.float32)
    for slot in range(share):
        got = jnp.sum(jnp.where(to_me & (rank == slot), blocks, 0.0), axis=1, keepdims=True)
        table = jnp.where(lanes == slot, got, table)

    facts = jnp.where(lanes == 0, hot, jnp.where(lanes == 1, rounds, jnp.where(lanes == 2, me, 0.0)))
    out_ref[0:1, :] = place.astype(jnp.int32)
    out_ref[1:2, :] = facts.astype(jnp.int32)
    out_ref[2:3, :] = mine & 127
    out_ref[3:8, :] = jnp.zeros((5, 128), jnp.int32)
    out_ref[8 : 8 + owner_total, :] = table.astype(jnp.int32)


def make_plan(packed, owner_total, share):
    rows = exchange(jnp.broadcast_to(packed[None], (owner_total, 1, 128)))[:, 0]
    plan = pl.pallas_call(
        functools.partial(plan_kernel, owner_total, share),
        out_shape=jax.ShapeDtypeStruct((8 + owner_total, 128), jnp.int32),
        in_specs=[vmem(), vmem()],
        out_specs=vmem(),
        name="plan",
    )(rows, packed)
    return plan, rows


def agree(rounds):
    devices = lax.axis_size("tick")
    reach = 1
    while reach < devices:
        ring = [(i, (i + reach) % devices) for i in range(devices)]
        rounds = jnp.maximum(rounds, lax.ppermute(rounds, "tick", ring))
        reach *= 2
    return rounds


def band_kernel(taps_w, taps_ref, band_ref):
    row = lax.broadcasted_iota(jnp.int32, (TB, TB), 0)
    col = lax.broadcasted_iota(jnp.int32, (TB, TB), 1)
    pairs = (taps_w + 1) // 2
    band_ref[0, 0 : 3 * TB, TB : 2 * TB] = jnp.zeros((3 * TB, TB), jnp.bfloat16)
    band_ref[pairs - 1, 3 * TB : 6 * TB, 0:TB] = jnp.zeros((3 * TB, TB), jnp.bfloat16)
    taps = taps_ref[...].astype(jnp.float32)
    for tap in range(taps_w):
        spread = jnp.broadcast_to(taps[tap : tap + 1], (TB, 2 * TB))
        rolled = pltpu.roll(spread, TB, 1, stride=1, stride_axis=0)
        middle = rolled[:, :TB]
        outer = rolled[:, TB:]
        bands = (
            jnp.where(col < row, outer, 0.0).astype(jnp.bfloat16),
            middle.astype(jnp.bfloat16),
            jnp.where(col >= row, outer, 0.0).astype(jnp.bfloat16),
        )
        for first, second in ((0, 0), (1, 1), (1, 0), (0, 1)):
            if (tap - first + second) % 2:
                continue
            pair = (tap - first + second) // 2
            for piece in range(3):
                start = (first * 3 + piece) * TB
                band_ref[pair, start : start + TB, second * TB : (second + 1) * TB] = bands[piece]


def make_bands(taps):
    taps_w = taps.shape[0]
    return pl.pallas_call(
        functools.partial(band_kernel, taps_w),
        out_shape=jax.ShapeDtypeStruct(((taps_w + 1) // 2, 6 * TB, 2 * TB), jnp.bfloat16),
        in_specs=[vmem()],
        out_specs=vmem(),
        cost_estimate=pl.CostEstimate(flops=10**9, bytes_accessed=6 * MIB, transcendentals=0),
        compiler_params=pltpu.CompilerParams(vmem_limit_bytes=16 * MIB),
        name="bands",
    )(taps)


def conv_kernel(
    taps_w,
    slots,
    slot_count,
    plan_ref,
    raw_hbm,
    mask_ref,
    left_ref,
    right_ref,
    top_ref,
    bottom_ref,
    band_ref,
    geo_ref,
    signal_ref,
    payload_ref,
    partial_ref,
    raw_ref,
    wide_ref,
    lhs_ref,
    out_ref,
    tiles_ref,
    raw_sem,
):
    wires, ticks = raw_ref.shape
    blocks = ticks // TB
    half = wires // 2
    block_wires = geo_ref.shape[1]
    wire_blocks = wires // block_wires
    pitch = wide_ref.shape[0] // (wires + 2 * PAD)
    reach = (taps_w + 1) // 2
    groups = raw_sem.shape[0]
    span = wires // groups
    first = PAD - taps_w // 2

    copies = [
        pltpu.make_async_copy(
            raw_hbm.at[pl.ds(group * span, span)],
            raw_ref.at[pl.ds(group * span, span)],
            raw_sem.at[group],
        )
        for group in range(groups)
    ]
    for copy in copies:
        copy.start()

    for block in range(blocks + 2):
        columns = slice(block * TB, (block + 1) * TB)
        wide_ref[pl.ds(block, PAD, stride=pitch), :] = top_ref[:, columns].astype(jnp.float32)
        wide_ref[pl.ds((PAD + wires) * pitch + block, PAD, stride=pitch), :] = bottom_ref[
            :, columns
        ].astype(jnp.float32)
    wide_ref[pl.ds(PAD * pitch, wires, stride=pitch), :] = left_ref[...].astype(jnp.float32)
    wide_ref[pl.ds(PAD * pitch + blocks + 1, wires, stride=pitch), :] = right_ref[...].astype(
        jnp.float32
    )

    def fill(group):
        copies[group].wait()
        lines = slice(group * span, (group + 1) * span)
        mask = mask_ref[lines].astype(jnp.float32)
        for block in range(blocks):
            inner = raw_ref[lines, block * TB : (block + 1) * TB].astype(jnp.float32) * mask
            wide_ref[pl.ds((PAD + group * span) * pitch + block + 1, span, stride=pitch), :] = inner

    def spread(pair):
        for side in range(2):
            line = (first + 2 * pair + side) * pitch
            for piece in range(3):
                at = (side * 3 + piece) * TB
                lhs_ref[pair, :, at : at + TB] = wide_ref[
                    pl.ds(line + piece, blocks), :
                ].astype(jnp.bfloat16)

    chunk = half // groups
    lead = reach - 1

    def last_pair(group):
        return min((group + 1) * chunk, half) + lead

    for group in range(groups):
        fill(group)
        if group == 0:
            continue
        if group == 1:
            for pair in range(0, last_pair(0)):
                spread(pair)

    for group in range(groups):
        pending = list(range(last_pair(group), last_pair(group + 1))) if group + 1 < groups else []
        each = -(-len(pending) // reach)
        total = jnp.zeros((chunk * blocks, 2 * TB), jnp.float32)
        for step in range(reach):
            rows = lhs_ref[group * chunk + step : (group + 1) * chunk + step]
            total = total + jnp.dot(
                rows.reshape(chunk * blocks, 6 * TB), band_ref[step], preferred_element_type=jnp.float32
            )
            for pair in pending[step * each : (step + 1) * each]:
                spread(pair)
        for pair in range(chunk):
            for side in range(2):
                out_ref[group % 2, pl.ds((2 * pair + side) * blocks, blocks), :] = total[
                    pair * blocks : (pair + 1) * blocks, side * TB : (side + 1) * TB
                ]
        for block in range(blocks):
            signal_ref[group * span : (group + 1) * span, block * TB : (block + 1) * TB] = out_ref[
                group % 2, pl.ds(block, span, stride=blocks), :
            ].astype(jnp.bfloat16)

    tiles_ref[...] = jnp.zeros_like(tiles_ref)

    def pack(slot, carry):
        block = plan_ref[2, slot]
        place = plan_ref[0, slot]
        wire = pl.multiple_of((block // blocks) * block_wires, block_wires)
        tick = pl.multiple_of((block % blocks) * TB, TB)
        tiles_ref[place] = signal_ref[pl.ds(wire, block_wires), pl.ds(tick, TB)]
        return carry

    lax.fori_loop(0, slot_count, pack, 0, unroll=6)
    payload_ref[...] = tiles_ref[0:slots]

    source = plan_ref[1, 2]
    rows = geo_ref[pl.ds(source * wire_blocks, wire_blocks)].reshape(wires, -1)
    for block in range(0, blocks, 2):
        chosen = jnp.concatenate(
            [
                jnp.concatenate(
                    [tiles_ref[slots + line * blocks + block + side] for line in range(wire_blocks)],
                    axis=0,
                )
                for side in range(2)
            ],
            axis=1,
        )
        sums = lax.dot_general(
            rows, chosen, (((0,), (0,)), ((), ())), preferred_element_type=jnp.float32
        ).astype(jnp.bfloat16)
        partial_ref[block] = sums[:, :TB]
        partial_ref[block + 1] = sums[:, TB:]


def convolve_and_pack(plan, raw, mask, left, right, top, bottom, bands, geometry, slots, slot_count):
    wires, ticks = raw.shape
    reach = bands.shape[0]
    taps_w = 2 * reach - 1
    block_wires = geometry.shape[1]
    cells = geometry.shape[2]
    tick_blocks = ticks // TB
    tile_total = slots + 128 + 1
    pitch = -(-(tick_blocks + 2) // 8) * 8
    groups = 4
    flops = 2 * tick_blocks * (wires // 2) * 3 * (taps_w + 1) * TB * 2 * TB
    return pl.pallas_call(
        functools.partial(conv_kernel, taps_w, slots, slot_count),
        out_shape=(
            jax.ShapeDtypeStruct((wires, ticks), jnp.bfloat16),
            jax.ShapeDtypeStruct((slots, block_wires, TB), jnp.bfloat16),
            jax.ShapeDtypeStruct((tick_blocks, cells, TB), jnp.bfloat16),
        ),
        in_specs=[smem(), pl.BlockSpec(memory_space=pl.ANY)] + [vmem()] * 7,
        out_specs=(vmem(), vmem(), vmem()),
        scratch_shapes=[
            pltpu.VMEM((wires, ticks), jnp.bfloat16),
            pltpu.VMEM(((wires + 2 * PAD) * pitch, TB), jnp.float32),
            pltpu.VMEM((wires // 2 + reach - 1, tick_blocks, 6 * TB), jnp.bfloat16),
            pltpu.VMEM((2, wires // groups * tick_blocks, TB), jnp.float32),
            pltpu.VMEM((tile_total, block_wires, TB), jnp.bfloat16),
            pltpu.SemaphoreType.DMA((groups,)),
        ],
        cost_estimate=pl.CostEstimate(flops=flops, bytes_accessed=8 * MIB, transcendentals=0),
        compiler_params=pltpu.CompilerParams(vmem_limit_bytes=40 * MIB),
        name="deconvolve",
    )(plan, raw, mask, left, right, top, bottom, bands, geometry)


def image_kernel(owner_total, share, start, plan_ref, arrived_ref, geo_ref, *refs):
    image_ref = refs[-1]
    cells, ticks = image_ref.shape
    blocks = ticks // TB
    block_wires = geo_ref.shape[1]
    wire_blocks = geo_ref.shape[0] // owner_total
    image_ref[...] = jnp.zeros_like(image_ref) if start else refs[0][...]
    is_hot = plan_ref[1, 0] == plan_ref[1, 2]

    if start:

        @pl.when(is_hot)
        def _():
            for source in range(owner_total):
                sums = arrived_ref[source * share : source * share + cells // block_wires]
                image_ref[:, source * TB : (source + 1) * TB] = sums.reshape(cells, TB).astype(
                    jnp.float32
                )

    @pl.when(jnp.logical_not(is_hot))
    def _():
        def add(source, carry):
            products = []
            for slot in range(share):
                block = plan_ref[8 + source, slot]
                row = source * wire_blocks + block // blocks
                products.append(
                    (
                        pl.multiple_of((block % blocks) * TB, TB),
                        lax.dot_general(
                            geo_ref[row],
                            arrived_ref[source * share + slot],
                            (((0,), (0,)), ((), ())),
                            preferred_element_type=jnp.float32,
                        ),
                    )
                )
            for at, product in products:
                image_ref[:, pl.ds(at, TB)] += product
            return carry

        lax.fori_loop(0, owner_total, add, 0)


def make_image(plan, arrived, geometry, owner_total, share, ticks, image=None):
    before = () if image is None else (image,)
    return pl.pallas_call(
        functools.partial(image_kernel, owner_total, share, image is None),
        out_shape=jax.ShapeDtypeStruct((geometry.shape[2], ticks), jnp.float32),
        in_specs=[smem()] + [vmem()] * (2 + len(before)),
        out_specs=vmem(),
        cost_estimate=pl.CostEstimate(flops=10**8, bytes_accessed=3 * MIB, transcendentals=0),
        compiler_params=pltpu.CompilerParams(vmem_limit_bytes=16 * MIB),
        name="image" if image is None else "image_more",
    )(plan, arrived, geometry, *before)


def further_round(step, image, signal, geometry, rows, packed, plan, owner_total, share):
    step, signal, rows, packed, plan = lax.optimization_barrier((step, signal, rows, packed, plan))
    hot = plan[1, 0]
    me = plan[1, 2]
    block_wires = geometry.shape[1]
    wire_count, tick_count = signal.shape
    blocks = tick_count // TB
    wire_blocks = wire_count // block_wires
    ids = jnp.arange(owner_total, dtype=jnp.int32)

    def ranks(owners):
        member = (owners[..., None] == ids).astype(jnp.int32)
        before = jnp.cumsum(member, axis=-2) - member
        return jnp.sum(before * member, axis=-1) - step * share

    def live(owners, rank):
        return (owners < owner_total) & (owners != hot) & (rank >= 0) & (rank < share)

    owners = packed[0] >> 7
    block = packed[0] & 127
    rank = ranks(owners)
    place = jnp.where(live(owners, rank), owners * share + rank, owner_total * share)
    tiles = signal.reshape(wire_blocks, block_wires, blocks, TB).transpose(0, 2, 1, 3)
    tiles = tiles.reshape(wire_blocks * blocks, block_wires, TB)[block]
    payload = jnp.zeros((owner_total * share, block_wires, TB), jnp.bfloat16)
    payload = payload.at[place].set(tiles, mode="drop")
    arrived = exchange(payload.reshape(owner_total, share, block_wires, TB))

    owners = rows >> 7
    rank = ranks(owners)
    source = jnp.arange(owner_total, dtype=jnp.int32)[:, None]
    line = jnp.where(live(owners, rank) & (owners == me), source, owner_total)
    table = jnp.zeros((owner_total, 128), jnp.int32)
    table = table.at[line, jnp.maximum(rank, 0)].set(rows & 127, mode="drop")
    plan = jnp.concatenate([plan[:8], table], axis=0)
    return make_image(
        plan,
        arrived.reshape(owner_total * share, block_wires, TB),
        geometry,
        owner_total,
        share,
        tick_count,
        image,
    )


def tick_halo(raw, mask, width):
    devices = lax.axis_size("tick")
    tick = lax.axis_index("tick")
    last = raw[:, -width:] * mask
    leading = raw[:, :width] * mask
    if devices == 2:
        got = lax.ppermute(jnp.where(tick == 0, last, leading), "tick", [(0, 1), (1, 0)])
        nothing = jnp.zeros_like(got)
        return jnp.where(tick == 0, nothing, got), jnp.where(tick == 0, got, nothing)
    up = [(i, i + 1) for i in range(devices - 1)]
    down = [(i + 1, i) for i in range(devices - 1)]
    return lax.ppermute(last, "tick", up), lax.ppermute(leading, "tick", down)


def wire_halo(raw, mask, left, right):
    devices = lax.axis_size("wire")
    up = [(i, i + 1) for i in range(devices - 1)]
    down = [(i + 1, i) for i in range(devices - 1)]

    def edge(where):
        return jnp.concatenate([left[where], raw[where] * mask[where], right[where]], axis=1)

    top = lax.ppermute(edge(slice(-PAD, None)), "wire", up)
    bottom = lax.ppermute(edge(slice(0, PAD)), "wire", down)
    return top, bottom


def exchange(array):
    return lax.all_to_all(array, ("plane", "wire"), split_axis=0, concat_axis=0, tiled=True)


def shards(raw, chan_mask, kernel, geometry, roi_block, roi_owner):
    wires, ticks = raw.shape
    slot_count = roi_block.shape[0]
    block_wires = geometry.shape[1]
    cells = geometry.shape[2]
    owner_total = lax.axis_size("plane") * lax.axis_size("wire")
    share = -(-(slot_count - CAP) // (owner_total - 1))
    me = lax.axis_index("plane") * lax.axis_size("wire") + lax.axis_index("wire")

    packed = jnp.pad(
        roi_owner * 128 + roi_block, (0, 128 - slot_count), constant_values=owner_total * 128
    )
    packed = jnp.where(jnp.arange(128) == 127, owner_total * 128 + me, packed)[None]
    plan, rows = make_plan(packed, owner_total, share)

    mask = chan_mask[:, None].astype(jnp.bfloat16)
    left, right = tick_halo(raw, mask, TB)
    top, bottom = wire_halo(raw, mask, left, right)
    bands = make_bands(kernel[0])
    signal, payload, partial = convolve_and_pack(
        plan, raw, mask, left, right, top, bottom, bands, geometry, owner_total * share, slot_count
    )

    pieces = exchange(partial)
    sums = jnp.sum(pieces.astype(jnp.float32), axis=0).astype(jnp.bfloat16)
    payload = payload.reshape(owner_total, share, block_wires, TB)
    payload = lax.dynamic_update_slice(
        payload, sums.reshape(1, cells // block_wires, block_wires, TB), (plan[1, 0], 0, 0, 0)
    )
    arrived = exchange(payload).reshape(owner_total * share, block_wires, TB)
    image = make_image(plan, arrived, geometry, owner_total, share, ticks)

    rounds = agree(plan[1:2, 1:2])[0, 0]
    image = lax.fori_loop(
        1,
        rounds,
        lambda step, now: further_round(
            step, now, signal, geometry, rows, packed, plan, owner_total, share
        ),
        image,
    )
    return signal, image


def solution(mesh):
    in_specs = (
        P(("plane", "wire"), "tick"),
        P(("plane", "wire")),
        P("plane", None, None),
        P(),
        P(("plane", "wire", "tick")),
        P(("plane", "wire", "tick")),
    )
    out_specs = (P(("plane", "wire"), "tick"), P(("plane", "wire"), "tick"))
    return jax.shard_map(shards, mesh=mesh, in_specs=in_specs, out_specs=out_specs, check_vma=False)
```

```python
import functools

import jax
import jax.numpy as jnp
from jax import lax
from jax.experimental import pallas as pl
from jax.experimental.pallas import tpu as pltpu
from jax.sharding import PartitionSpec as P

TB = 128
CAP = 25
PAD = 16
MIB = 1024 * 1024


def vmem():
    return pl.BlockSpec(memory_space=pltpu.VMEM)


def smem():
    return pl.BlockSpec(memory_space=pltpu.SMEM)


def plan_kernel(owner_total, share, rows_ref, own_ref, out_ref):
    lanes = lax.broadcasted_iota(jnp.int32, (1, 128), 1)
    lane_f = lanes.astype(jnp.float32)
    every = rows_ref[...]
    owners = every >> 7
    mine = own_ref[...]
    me = jnp.sum(jnp.where(lanes == 127, mine & 127, 0).astype(jnp.float32), axis=1, keepdims=True)

    least = jnp.full((1, 128), -1.0, jnp.float32)
    most = jnp.zeros((1, 128), jnp.float32)
    for owner in range(owner_total):
        named = jnp.sum((owners == owner).astype(jnp.float32), axis=1, keepdims=True)
        least = jnp.where(lanes == owner, jnp.min(named, axis=0, keepdims=True), least)
        most = jnp.where(lanes == owner, jnp.max(named, axis=0, keepdims=True), most)
    top = jnp.max(least, axis=1, keepdims=True)
    hot = jnp.min(jnp.where(least == top, lane_f, 127.0), axis=1, keepdims=True)
    fullest = jnp.max(jnp.where(lane_f == hot, 0.0, most), axis=1, keepdims=True)
    rounds = jnp.zeros((1, 1), jnp.float32)
    for step in range(-(-CAP // share)):
        rounds = rounds + (fullest > step * share).astype(jnp.float32)

    before = (
        lax.broadcasted_iota(jnp.int32, (128, 128), 0)
        < lax.broadcasted_iota(jnp.int32, (128, 128), 1)
    ).astype(jnp.bfloat16)

    rows = lax.broadcasted_iota(jnp.int32, (owner_total, 128), 0)
    member = (mine >> 7) == rows
    rank = jnp.dot(member.astype(jnp.bfloat16), before, preferred_element_type=jnp.float32)
    rows_f = rows.astype(jnp.float32)
    slots = float(owner_total * share)
    place = jnp.where(rank < share, rows_f * share + rank, slots + 128.0)
    place = jnp.where(rows_f == hot, slots + (mine & 127).astype(jnp.float32), place)
    place = jnp.sum(jnp.where(member, place, 0.0), axis=0, keepdims=True)

    to_me = owners.astype(jnp.float32) == me
    rank = jnp.dot(to_me.astype(jnp.bfloat16), before, preferred_element_type=jnp.float32)
    blocks = (every & 127).astype(jnp.float32)
    table = jnp.zeros((owner_total, 128), jnp.float32)
    for slot in range(share):
        got = jnp.sum(jnp.where(to_me & (rank == slot), blocks, 0.0), axis=1, keepdims=True)
        table = jnp.where(lanes == slot, got, table)

    facts = jnp.where(lanes == 0, hot, jnp.where(lanes == 1, rounds, jnp.where(lanes == 2, me, 0.0)))
    out_ref[0:1, :] = place.astype(jnp.int32)
    out_ref[1:2, :] = facts.astype(jnp.int32)
    out_ref[2:3, :] = mine & 127
    out_ref[3:8, :] = jnp.zeros((5, 128), jnp.int32)
    out_ref[8 : 8 + owner_total, :] = table.astype(jnp.int32)


def make_plan(packed, rows, owner_total, share):
    plan = pl.pallas_call(
        functools.partial(plan_kernel, owner_total, share),
        out_shape=jax.ShapeDtypeStruct((8 + owner_total, 128), jnp.int32),
        in_specs=[vmem(), vmem()],
        out_specs=vmem(),
        compiler_params=pltpu.CompilerParams(vmem_limit_bytes=2 * MIB),
        name="plan",
    )(rows, packed)
    return plan


def agree(rounds):
    devices = lax.axis_size("tick")
    reach = 1
    while reach < devices:
        ring = [(i, (i + reach) % devices) for i in range(devices)]
        rounds = jnp.maximum(rounds, lax.ppermute(rounds, "tick", ring))
        reach *= 2
    return rounds


def band_kernel(taps_w, taps_ref, band_ref):
    row = lax.broadcasted_iota(jnp.int32, (TB, TB), 0)
    col = lax.broadcasted_iota(jnp.int32, (TB, TB), 1)
    pairs = (taps_w + 1) // 2
    band_ref[0, 0 : 3 * TB, TB : 2 * TB] = jnp.zeros((3 * TB, TB), jnp.bfloat16)
    band_ref[pairs - 1, 3 * TB : 6 * TB, 0:TB] = jnp.zeros((3 * TB, TB), jnp.bfloat16)
    taps = taps_ref[...].astype(jnp.float32)
    for tap in range(taps_w):
        spread = jnp.broadcast_to(taps[tap : tap + 1], (TB, 2 * TB))
        rolled = pltpu.roll(spread, TB, 1, stride=1, stride_axis=0)
        middle = rolled[:, :TB]
        outer = rolled[:, TB:]
        bands = (
            jnp.where(col < row, outer, 0.0).astype(jnp.bfloat16),
            middle.astype(jnp.bfloat16),
            jnp.where(col >= row, outer, 0.0).astype(jnp.bfloat16),
        )
        for first, second in ((0, 0), (1, 1), (1, 0), (0, 1)):
            if (tap - first + second) % 2:
                continue
            pair = (tap - first + second) // 2
            for piece in range(3):
                start = (first * 3 + piece) * TB
                band_ref[pair, start : start + TB, second * TB : (second + 1) * TB] = bands[piece]


def make_bands(taps):
    taps_w = taps.shape[0]
    return pl.pallas_call(
        functools.partial(band_kernel, taps_w),
        out_shape=jax.ShapeDtypeStruct(((taps_w + 1) // 2, 6 * TB, 2 * TB), jnp.bfloat16),
        in_specs=[vmem()],
        out_specs=vmem(),
        cost_estimate=pl.CostEstimate(flops=10**9, bytes_accessed=6 * MIB, transcendentals=0),
        compiler_params=pltpu.CompilerParams(vmem_limit_bytes=16 * MIB),
        name="bands",
    )(taps)


def spread_pair(wide_ref, lhs_view, line, pitch, blocks):
    for side in range(2):
        for piece in range(3):
            at = (side * 3 + piece) * TB
            lhs_view[:, at : at + TB] = wide_ref[
                pl.ds((line + side) * pitch + piece, blocks), :
            ].astype(jnp.bfloat16)


def write_lines(total, out_view, signal_ref, line, pairs, blocks):
    for pair in range(pairs):
        for side in range(2):
            out_view[pl.ds((2 * pair + side) * blocks, blocks), :] = total[
                pair * blocks : (pair + 1) * blocks, side * TB : (side + 1) * TB
            ]
    for block in range(blocks):
        signal_ref[line : line + 2 * pairs, block * TB : (block + 1) * TB] = out_view[
            pl.ds(block, 2 * pairs, stride=blocks), :
        ].astype(jnp.bfloat16)


def inner_kernel(
    chunks,
    raw_hbm,
    mask_ref,
    left_ref,
    right_ref,
    band_ref,
    inner_ref,
    raw_ref,
    wide_ref,
    lhs_ref,
    out_ref,
    raw_sem,
):
    wires, ticks = raw_ref.shape
    blocks = ticks // TB
    pitch = wide_ref.shape[0] // wires
    reach = band_ref.shape[0]
    groups = raw_sem.shape[0]
    span = wires // groups

    copies = [
        pltpu.make_async_copy(
            raw_hbm.at[pl.ds(group * span, span)],
            raw_ref.at[pl.ds(group * span, span)],
            raw_sem.at[group],
        )
        for group in range(groups)
    ]
    for copy in copies:
        copy.start()
    wide_ref[pl.ds(0, wires, stride=pitch), :] = left_ref[...].astype(jnp.float32)
    wide_ref[pl.ds(blocks + 1, wires, stride=pitch), :] = right_ref[...].astype(jnp.float32)

    def fill(group, block):
        lines = slice(group * span, (group + 1) * span)
        inner = raw_ref[lines, block * TB : (block + 1) * TB].astype(jnp.float32) * mask_ref[
            lines
        ].astype(jnp.float32)
        wide_ref[pl.ds(group * span * pitch + block + 1, span, stride=pitch), :] = inner

    margin = reach - 1
    begin = PAD // 2
    state = {"group": 0, "pair": begin}

    def prepare(upto):
        todo = []
        while state["pair"] < upto:
            line = 2 * state["pair"] - margin
            while state["group"] < groups and line + 1 >= state["group"] * span:
                group = state["group"]
                todo.append(lambda group=group: copies[group].wait())
                for block in range(blocks):
                    todo.append(lambda group=group, block=block: fill(group, block))
                state["group"] += 1
            todo.append(
                lambda line=line, pair=state["pair"]: spread_pair(
                    wide_ref, lhs_ref.at[pair - begin], line, pitch, blocks
                )
            )
            state["pair"] += 1
        return todo

    pair = begin
    for job in prepare(pair + chunks[0] + margin):
        job()
    for index, size in enumerate(chunks):
        todo = prepare(pair + size + chunks[index + 1] + margin) if index + 1 < len(chunks) else []
        each = -(-len(todo) // reach)
        total = jnp.zeros((size * blocks, 2 * TB), jnp.float32)
        for step in range(reach):
            rows = lhs_ref[pair - begin + step : pair - begin + step + size]
            total = total + jnp.dot(
                rows.reshape(size * blocks, 6 * TB), band_ref[step], preferred_element_type=jnp.float32
            )
            for job in todo[step * each : (step + 1) * each]:
                job()
        write_lines(total, out_ref.at[index % 2], inner_ref, 2 * (pair - begin), size, blocks)
        pair += size


def convolve_inner(raw, mask, left, right, bands):
    wires, ticks = raw.shape
    reach = bands.shape[0]
    blocks = ticks // TB
    pitch = -(-(blocks + 2) // 8) * 8
    pairs = (wires - 2 * PAD) // 2
    chunks = []
    while sum(chunks) < pairs:
        chunks.append(min(32 if chunks else 24, pairs - sum(chunks)))
    groups = 4
    flops = 2 * blocks * pairs * reach * 6 * TB * 2 * TB
    return pl.pallas_call(
        functools.partial(inner_kernel, tuple(chunks)),
        out_shape=jax.ShapeDtypeStruct((wires - 2 * PAD, ticks), jnp.bfloat16),
        in_specs=[pl.BlockSpec(memory_space=pl.ANY)] + [vmem()] * 4,
        out_specs=vmem(),
        scratch_shapes=[
            pltpu.VMEM((wires, ticks), jnp.bfloat16),
            pltpu.VMEM((wires * pitch, TB), jnp.float32),
            pltpu.VMEM((pairs + reach - 1, blocks, 6 * TB), jnp.bfloat16),
            pltpu.VMEM((2, 2 * max(chunks) * blocks, TB), jnp.float32),
            pltpu.SemaphoreType.DMA((groups,)),
        ],
        cost_estimate=pl.CostEstimate(flops=flops, bytes_accessed=6 * MIB, transcendentals=0),
        compiler_params=pltpu.CompilerParams(vmem_limit_bytes=28 * MIB),
        name="inner",
    )(raw, mask, left, right, bands)


def edge_kernel(
    slots,
    slot_count,
    plan_ref,
    inner_ref,
    raw_ref,
    mask_ref,
    left_ref,
    right_ref,
    top_ref,
    bottom_ref,
    band_ref,
    geo_ref,
    signal_ref,
    payload_ref,
    partial_ref,
    wide_ref,
    lhs_ref,
    out_ref,
    tiles_ref,
):
    wires, ticks = signal_ref.shape
    blocks = ticks // TB
    reach = band_ref.shape[0]
    block_wires = geo_ref.shape[1]
    wire_blocks = wires // block_wires
    near = 2 * PAD
    lines = PAD + near
    pitch = wide_ref.shape[1] // lines
    pairs = PAD // 2
    margin = reach - 1

    signal_ref[PAD : wires - PAD] = inner_ref[...]
    tiles_ref[...] = jnp.zeros_like(tiles_ref)

    for end in range(2):
        halo_ref = (top_ref, bottom_ref)[end]
        mine = (slice(0, near), slice(wires - near, wires))[end]
        halo_at = (0, near)[end]
        mine_at = (PAD, 0)[end]
        mask = mask_ref[mine].astype(jnp.float32)
        for block in range(blocks + 2):
            columns = slice(block * TB, (block + 1) * TB)
            if block == 0:
                inner = left_ref[mine].astype(jnp.float32)
            elif block == blocks + 1:
                inner = right_ref[mine].astype(jnp.float32)
            else:
                inner = raw_ref[mine, (block - 1) * TB : block * TB].astype(jnp.float32) * mask
            wide_ref[end, pl.ds(halo_at * pitch + block, PAD, stride=pitch), :] = halo_ref[
                :, columns
            ].astype(jnp.float32)
            wide_ref[end, pl.ds(mine_at * pitch + block, near, stride=pitch), :] = inner
        first = (PAD, near - PAD)[end] - margin
        for pair in range(pairs + margin):
            spread_pair(
                wide_ref.at[end], lhs_ref.at[end, pair], first + 2 * pair, pitch, blocks
            )

    total = jnp.zeros((2 * pairs * blocks, 2 * TB), jnp.float32)
    for step in range(reach):
        rows = jnp.concatenate(
            [
                lhs_ref[end, step : step + pairs].reshape(pairs * blocks, 6 * TB)
                for end in range(2)
            ],
            axis=0,
        )
        total = total + jnp.dot(rows, band_ref[step], preferred_element_type=jnp.float32)
    for end in range(2):
        write_lines(
            total[end * pairs * blocks : (end + 1) * pairs * blocks],
            out_ref.at[end],
            signal_ref,
            (0, wires - PAD)[end],
            pairs,
            blocks,
        )

    def pack(slot, carry):
        block = plan_ref[2, slot]
        place = plan_ref[0, slot]
        wire = pl.multiple_of((block // blocks) * block_wires, block_wires)
        tick = pl.multiple_of((block % blocks) * TB, TB)
        tiles_ref[place] = signal_ref[pl.ds(wire, block_wires), pl.ds(tick, TB)]
        return carry

    lax.fori_loop(0, slot_count, pack, 0, unroll=6)
    payload_ref[...] = tiles_ref[0:slots]

    source = plan_ref[1, 2]
    rows = geo_ref[pl.ds(source * wire_blocks, wire_blocks)].reshape(wires, -1)
    for block in range(0, blocks, 2):
        chosen = jnp.concatenate(
            [
                jnp.concatenate(
                    [tiles_ref[slots + line * blocks + block + side] for line in range(wire_blocks)],
                    axis=0,
                )
                for side in range(2)
            ],
            axis=1,
        )
        sums = lax.dot_general(
            rows, chosen, (((0,), (0,)), ((), ())), preferred_element_type=jnp.float32
        ).astype(jnp.bfloat16)
        partial_ref[block] = sums[:, :TB]
        partial_ref[block + 1] = sums[:, TB:]


def convolve_edges(
    plan, inner, raw, mask, left, right, top, bottom, bands, geometry, slots, slot_count
):
    wires, ticks = raw.shape
    reach = bands.shape[0]
    block_wires = geometry.shape[1]
    cells = geometry.shape[2]
    blocks = ticks // TB
    pitch = -(-(blocks + 2) // 8) * 8
    flops = 2 * blocks * PAD * reach * 6 * TB * 2 * TB
    return pl.pallas_call(
        functools.partial(edge_kernel, slots, slot_count),
        out_shape=(
            jax.ShapeDtypeStruct((wires, ticks), jnp.bfloat16),
            jax.ShapeDtypeStruct((slots, block_wires, TB), jnp.bfloat16),
            jax.ShapeDtypeStruct((blocks, cells, TB), jnp.bfloat16),
        ),
        in_specs=[smem()] + [vmem()] * 9,
        out_specs=(vmem(), vmem(), vmem()),
        scratch_shapes=[
            pltpu.VMEM((2, 3 * PAD * pitch, TB), jnp.float32),
            pltpu.VMEM((2, PAD // 2 + reach - 1, blocks, 6 * TB), jnp.bfloat16),
            pltpu.VMEM((2, PAD * blocks, TB), jnp.float32),
            pltpu.VMEM((slots + 128 + 1, block_wires, TB), jnp.bfloat16),
        ],
        cost_estimate=pl.CostEstimate(flops=flops, bytes_accessed=6 * MIB, transcendentals=0),
        compiler_params=pltpu.CompilerParams(vmem_limit_bytes=24 * MIB),
        name="edges",
    )(plan, inner, raw, mask, left, right, top, bottom, bands, geometry)


def image_kernel(owner_total, share, start, plan_ref, arrived_ref, geo_ref, *refs):
    image_ref = refs[-1]
    cells, ticks = image_ref.shape
    blocks = ticks // TB
    block_wires = geo_ref.shape[1]
    wire_blocks = geo_ref.shape[0] // owner_total
    image_ref[...] = jnp.zeros_like(image_ref) if start else refs[0][...]
    is_hot = plan_ref[1, 0] == plan_ref[1, 2]

    if start:

        @pl.when(is_hot)
        def _():
            for source in range(owner_total):
                sums = arrived_ref[source * share : source * share + cells // block_wires]
                image_ref[:, source * TB : (source + 1) * TB] = sums.reshape(cells, TB).astype(
                    jnp.float32
                )

    @pl.when(jnp.logical_not(is_hot))
    def _():
        def add(source, carry):
            products = []
            for slot in range(share):
                block = plan_ref[8 + source, slot]
                row = source * wire_blocks + block // blocks
                products.append(
                    (
                        pl.multiple_of((block % blocks) * TB, TB),
                        lax.dot_general(
                            geo_ref[row],
                            arrived_ref[source * share + slot],
                            (((0,), (0,)), ((), ())),
                            preferred_element_type=jnp.float32,
                        ),
                    )
                )
            for at, product in products:
                image_ref[:, pl.ds(at, TB)] += product
            return carry

        lax.fori_loop(0, owner_total, add, 0)


def make_image(plan, arrived, geometry, owner_total, share, ticks, image=None):
    before = () if image is None else (image,)
    return pl.pallas_call(
        functools.partial(image_kernel, owner_total, share, image is None),
        out_shape=jax.ShapeDtypeStruct((geometry.shape[2], ticks), jnp.float32),
        in_specs=[smem()] + [vmem()] * (2 + len(before)),
        out_specs=vmem(),
        cost_estimate=pl.CostEstimate(flops=10**8, bytes_accessed=3 * MIB, transcendentals=0),
        compiler_params=pltpu.CompilerParams(vmem_limit_bytes=16 * MIB),
        name="image" if image is None else "image_more",
    )(plan, arrived, geometry, *before)


def further_round(step, image, signal, geometry, rows, packed, plan, owner_total, share):
    step, signal, rows, packed, plan = lax.optimization_barrier((step, signal, rows, packed, plan))
    hot = plan[1, 0]
    me = plan[1, 2]
    block_wires = geometry.shape[1]
    wire_count, tick_count = signal.shape
    blocks = tick_count // TB
    wire_blocks = wire_count // block_wires
    ids = jnp.arange(owner_total, dtype=jnp.int32)

    def ranks(owners):
        member = (owners[..., None] == ids).astype(jnp.int32)
        before = jnp.cumsum(member, axis=-2) - member
        return jnp.sum(before * member, axis=-1) - step * share

    def live(owners, rank):
        return (owners < owner_total) & (owners != hot) & (rank >= 0) & (rank < share)

    owners = packed[0] >> 7
    block = packed[0] & 127
    rank = ranks(owners)
    place = jnp.where(live(owners, rank), owners * share + rank, owner_total * share)
    tiles = signal.reshape(wire_blocks, block_wires, blocks, TB).transpose(0, 2, 1, 3)
    tiles = tiles.reshape(wire_blocks * blocks, block_wires, TB)[block]
    payload = jnp.zeros((owner_total * share, block_wires, TB), jnp.bfloat16)
    payload = payload.at[place].set(tiles, mode="drop")
    arrived = exchange(payload.reshape(owner_total, share, block_wires, TB))

    owners = rows >> 7
    rank = ranks(owners)
    source = jnp.arange(owner_total, dtype=jnp.int32)[:, None]
    line = jnp.where(live(owners, rank) & (owners == me), source, owner_total)
    table = jnp.zeros((owner_total, 128), jnp.int32)
    table = table.at[line, jnp.maximum(rank, 0)].set(rows & 127, mode="drop")
    plan = jnp.concatenate([plan[:8], table], axis=0)
    return make_image(
        plan,
        arrived.reshape(owner_total * share, block_wires, TB),
        geometry,
        owner_total,
        share,
        tick_count,
        image,
    )


def tick_halo(raw, mask, width):
    devices = lax.axis_size("tick")
    tick = lax.axis_index("tick")
    last = raw[:, -width:] * mask
    leading = raw[:, :width] * mask
    if devices == 2:
        got = lax.ppermute(jnp.where(tick == 0, last, leading), "tick", [(0, 1), (1, 0)])
        nothing = jnp.zeros_like(got)
        return jnp.where(tick == 0, nothing, got), jnp.where(tick == 0, got, nothing)
    up = [(i, i + 1) for i in range(devices - 1)]
    down = [(i + 1, i) for i in range(devices - 1)]
    return lax.ppermute(last, "tick", up), lax.ppermute(leading, "tick", down)


def wire_halo(raw, mask, left, right):
    devices = lax.axis_size("wire")
    up = [(i, i + 1) for i in range(devices - 1)]
    down = [(i + 1, i) for i in range(devices - 1)]

    def edge(where):
        return jnp.concatenate([left[where], raw[where] * mask[where], right[where]], axis=1)

    top = lax.ppermute(edge(slice(-PAD, None)), "wire", up)
    bottom = lax.ppermute(edge(slice(0, PAD)), "wire", down)
    return top, bottom


def exchange(array):
    return lax.all_to_all(array, ("plane", "wire"), split_axis=0, concat_axis=0, tiled=True)


def shards(raw, chan_mask, kernel, geometry, roi_block, roi_owner):
    wires, ticks = raw.shape
    slot_count = roi_block.shape[0]
    block_wires = geometry.shape[1]
    cells = geometry.shape[2]
    owner_total = lax.axis_size("plane") * lax.axis_size("wire")
    share = -(-(slot_count - CAP) // (owner_total - 1))
    me = lax.axis_index("plane") * lax.axis_size("wire") + lax.axis_index("wire")

    packed = jnp.pad(
        roi_owner * 128 + roi_block, (0, 128 - slot_count), constant_values=owner_total * 128
    )
    packed = jnp.where(jnp.arange(128) == 127, owner_total * 128 + me, packed)[None]
    rows = lax.all_gather(packed, ("plane", "wire"), axis=0, tiled=True)

    mask = chan_mask[:, None].astype(jnp.bfloat16)
    left, right = tick_halo(raw, mask, TB)
    top, bottom = wire_halo(raw, mask, left, right)
    bands = make_bands(kernel[0])
    inner = convolve_inner(raw, mask, left, right, bands)
    rows, inner = lax.optimization_barrier((rows, inner))
    plan = make_plan(packed, rows, owner_total, share)
    signal, payload, partial = convolve_edges(
        plan,
        inner,
        raw,
        mask,
        left,
        right,
        top,
        bottom,
        bands,
        geometry,
        owner_total * share,
        slot_count,
    )

    late_plan, partial = lax.optimization_barrier((plan, partial))
    pieces = exchange(partial)
    sums = jnp.sum(pieces.astype(jnp.float32), axis=0).astype(jnp.bfloat16)
    payload = payload.reshape(owner_total, share, block_wires, TB)
    payload = lax.dynamic_update_slice(
        payload, sums.reshape(1, cells // block_wires, block_wires, TB), (late_plan[1, 0], 0, 0, 0)
    )
    arrived = exchange(payload).reshape(owner_total * share, block_wires, TB)
    image = make_image(plan, arrived, geometry, owner_total, share, ticks)

    rounds = agree(late_plan[1:2, 1:2])[0, 0]
    image = lax.fori_loop(
        1,
        rounds,
        lambda step, now: further_round(
            step, now, signal, geometry, rows, packed, plan, owner_total, share
        ),
        image,
    )
    return signal, image


def solution(mesh):
    in_specs = (
        P(("plane", "wire"), "tick"),
        P(("plane", "wire")),
        P("plane", None, None),
        P(),
        P(("plane", "wire", "tick")),
        P(("plane", "wire", "tick")),
    )
    out_specs = (P(("plane", "wire"), "tick"), P(("plane", "wire"), "tick"))
    return jax.shard_map(shards, mesh=mesh, in_specs=in_specs, out_specs=out_specs, check_vma=False)
```

```python
import functools

import jax
import jax.numpy as jnp
from jax import lax
from jax.experimental import pallas as pl
from jax.experimental.pallas import tpu as pltpu
from jax.sharding import PartitionSpec as P

TB = 128
CAP = 25
PAD = 16
MIB = 1024 * 1024


def vmem():
    return pl.BlockSpec(memory_space=pltpu.VMEM)


def smem():
    return pl.BlockSpec(memory_space=pltpu.SMEM)


GROUP = 8


def lane_numbers():
    return lax.broadcasted_iota(jnp.int32, (1, 128), 1)


def earlier_lanes():
    return (
        lax.broadcasted_iota(jnp.int32, (128, 128), 0)
        < lax.broadcasted_iota(jnp.int32, (128, 128), 1)
    ).astype(jnp.bfloat16)


def count_before(member, before):
    return jnp.dot(
        member.astype(jnp.float32).astype(jnp.bfloat16), before, preferred_element_type=jnp.float32
    )


def most_named(owners, owner_total):
    lanes = lane_numbers()
    counts = jnp.full(owners.shape, -1.0, jnp.float32)
    for owner in range(owner_total):
        named = jnp.sum((owners == owner).astype(jnp.float32), axis=1, keepdims=True)
        counts = jnp.where(lanes == owner, named, counts)
    top = jnp.max(counts, axis=1, keepdims=True)
    chosen = jnp.min(
        jnp.where(counts == top, lanes.astype(jnp.float32), 127.0), axis=1, keepdims=True
    )
    return counts, chosen


def send_kernel(owner_total, share, own_ref, column_ref, out_ref):
    lanes = lane_numbers()
    own = own_ref[...]
    _, hot = most_named(own >> 7, owner_total)
    me = jnp.sum(jnp.where(lanes == 127, own & 127, 0).astype(jnp.float32), axis=1, keepdims=True)
    rows = lax.broadcasted_iota(jnp.int32, (owner_total, 128), 0)
    member = (own >> 7) == rows
    rank = count_before(member, earlier_lanes())
    place = jnp.where(rank < share, rows.astype(jnp.float32) * share + rank, -1.0)
    place = jnp.where(rows.astype(jnp.float32) == hot, -2.0, place)
    place = jnp.sum(jnp.where(member, place + 3.0, 0.0), axis=0, keepdims=True)

    column = column_ref[...]
    here = ((column & 127) == lanes) & ((column >> 7) < owner_total)
    spread = jnp.transpose(jnp.broadcast_to(place, (128, 128)))
    placed = jnp.sum(jnp.where(here, spread, 0.0), axis=0, keepdims=True)
    trash = float(owner_total * share)
    out_ref[...] = jnp.zeros_like(out_ref)
    out_ref[0:1, :] = jnp.where(placed >= 3.0, placed - 3.0, trash).astype(jnp.int32)
    out_ref[1:2, :] = jnp.where(lanes == 0, hot, jnp.where(lanes == 2, me, 0.0)).astype(jnp.int32)
    out_ref[2:3, :] = (placed == 1.0).astype(jnp.int32)


def make_send_plan(packed, owner_total, share):
    return pl.pallas_call(
        functools.partial(send_kernel, owner_total, share),
        out_shape=jax.ShapeDtypeStruct((8, 128), jnp.int32),
        in_specs=[vmem(), vmem()],
        out_specs=vmem(),
        compiler_params=pltpu.CompilerParams(vmem_limit_bytes=2 * MIB),
        name="send_plan",
    )(packed, packed.reshape(128, 1))


def receive_kernel(owner_total, share, wire_blocks, tick_blocks, rows_ref, own_ref, out_ref):
    lanes = lane_numbers()
    lane_f = lanes.astype(jnp.float32)
    every = rows_ref[...]
    owners = every >> 7
    own = own_ref[...]
    me = jnp.sum(jnp.where(lanes == 127, own & 127, 0).astype(jnp.float32), axis=1, keepdims=True)

    counts, chosen = most_named(owners, owner_total)
    hot = jnp.max(chosen, axis=0, keepdims=True)
    agreed = hot == jnp.min(chosen, axis=0, keepdims=True)
    left = jnp.where(agreed & (lane_f == hot), 0.0, counts)
    fullest = jnp.max(jnp.max(left, axis=1, keepdims=True), axis=0, keepdims=True)
    start = agreed.astype(jnp.float32)
    trips = -start
    for step in range(-(-CAP // share)):
        trips = trips + (fullest > step * share).astype(jnp.float32)
    trips = jnp.maximum(trips, 0.0)
    hot = jnp.where(agreed, hot, -1.0)

    to_me = owners.astype(jnp.float32) == me
    before = earlier_lanes()
    rank = count_before(to_me, before)
    blocks = every & 127
    source = lax.broadcasted_iota(jnp.int32, (owner_total, 128), 0)
    line = (source * wire_blocks + blocks // tick_blocks).astype(jnp.float32)
    tick = (blocks % tick_blocks).astype(jnp.float32)
    lines = jnp.zeros((1, 128), jnp.float32)
    ticks = jnp.full((1, 128), -1.0, jnp.float32)
    for slot in range(share):
        got = to_me & (rank == slot)
        here = lanes == source * share + slot
        for value, where in ((line, 0), (tick + 1.0, 1)):
            one = jnp.sum(jnp.where(got, value, 0.0), axis=1, keepdims=True)
            one = jnp.sum(jnp.where(here, one, 0.0), axis=0, keepdims=True)
            if where == 0:
                lines = lines + one
            else:
                ticks = ticks + one

    block_rows = lax.broadcasted_iota(jnp.int32, (tick_blocks, 128), 0).astype(jnp.float32)
    member = block_rows == ticks
    rank = count_before(member, before)
    total = jnp.sum(member.astype(jnp.float32), axis=1, keepdims=True)
    groups = jnp.zeros_like(total)
    for step in range(0, owner_total * share, GROUP):
        groups = groups + (total > step).astype(jnp.float32)
    lower = (
        lax.broadcasted_iota(jnp.int32, (tick_blocks, tick_blocks), 0)
        > lax.broadcasted_iota(jnp.int32, (tick_blocks, tick_blocks), 1)
    ).astype(jnp.bfloat16)
    base = jnp.dot(
        lower,
        jnp.broadcast_to(groups, (tick_blocks, 128)).astype(jnp.bfloat16),
        preferred_element_type=jnp.float32,
    )
    place = jnp.sum(jnp.where(member, base * GROUP + rank, 0.0), axis=0, keepdims=True)
    trash = float(group_total(owner_total, share, tick_blocks) * GROUP)
    place = jnp.where(ticks < 0.0, trash, place)
    inside = (base <= lane_f) & (lane_f < base + groups)
    group_tick = jnp.sum(jnp.where(inside, block_rows, 0.0), axis=0, keepdims=True)

    facts = jnp.where(lanes == 0, hot, 0.0)
    facts = jnp.where(lanes == 1, trips, facts)
    facts = jnp.where(lanes == 2, me, facts)
    facts = jnp.where(lanes == 3, start, facts)
    out_ref[...] = jnp.zeros_like(out_ref)
    out_ref[0:1, :] = place.astype(jnp.int32)
    out_ref[1:2, :] = facts.astype(jnp.int32)
    out_ref[2:3, :] = lines.astype(jnp.int32)
    out_ref[3:4, :] = group_tick.astype(jnp.int32)


def group_total(owner_total, share, tick_blocks):
    return (owner_total * share - tick_blocks) // GROUP + tick_blocks


def make_receive_plan(rows, packed, owner_total, share, wire_blocks, tick_blocks):
    return pl.pallas_call(
        functools.partial(receive_kernel, owner_total, share, wire_blocks, tick_blocks),
        out_shape=jax.ShapeDtypeStruct((8, 128), jnp.int32),
        in_specs=[vmem(), vmem()],
        out_specs=vmem(),
        compiler_params=pltpu.CompilerParams(vmem_limit_bytes=2 * MIB),
        name="receive_plan",
    )(rows, packed)


def agree(rounds):
    devices = lax.axis_size("tick")
    reach = 1
    while reach < devices:
        ring = [(i, (i + reach) % devices) for i in range(devices)]
        rounds = jnp.maximum(rounds, lax.ppermute(rounds, "tick", ring))
        reach *= 2
    return rounds


def band_kernel(taps_w, taps_ref, band_ref):
    row = lax.broadcasted_iota(jnp.int32, (TB, TB), 0)
    col = lax.broadcasted_iota(jnp.int32, (TB, TB), 1)
    pairs = (taps_w + 1) // 2
    band_ref[0, 0 : 3 * TB, TB : 2 * TB] = jnp.zeros((3 * TB, TB), jnp.bfloat16)
    band_ref[pairs - 1, 3 * TB : 6 * TB, 0:TB] = jnp.zeros((3 * TB, TB), jnp.bfloat16)
    taps = taps_ref[...].astype(jnp.float32)
    for tap in range(taps_w):
        spread = jnp.broadcast_to(taps[tap : tap + 1], (TB, 2 * TB))
        rolled = pltpu.roll(spread, TB, 1, stride=1, stride_axis=0)
        middle = rolled[:, :TB]
        outer = rolled[:, TB:]
        bands = (
            jnp.where(col < row, outer, 0.0).astype(jnp.bfloat16),
            middle.astype(jnp.bfloat16),
            jnp.where(col >= row, outer, 0.0).astype(jnp.bfloat16),
        )
        for first, second in ((0, 0), (1, 1), (1, 0), (0, 1)):
            if (tap - first + second) % 2:
                continue
            pair = (tap - first + second) // 2
            for piece in range(3):
                start = (first * 3 + piece) * TB
                band_ref[pair, start : start + TB, second * TB : (second + 1) * TB] = bands[piece]


def make_bands(taps):
    taps_w = taps.shape[0]
    return pl.pallas_call(
        functools.partial(band_kernel, taps_w),
        out_shape=jax.ShapeDtypeStruct(((taps_w + 1) // 2, 6 * TB, 2 * TB), jnp.bfloat16),
        in_specs=[vmem()],
        out_specs=vmem(),
        cost_estimate=pl.CostEstimate(flops=10**9, bytes_accessed=6 * MIB, transcendentals=0),
        compiler_params=pltpu.CompilerParams(vmem_limit_bytes=16 * MIB),
        name="bands",
    )(taps)


def spread_pair(wide_ref, lhs_view, line, pitch, blocks):
    for side in range(2):
        for piece in range(3):
            at = (side * 3 + piece) * TB
            lhs_view[:, at : at + TB] = wide_ref[
                pl.ds((line + side) * pitch + piece, blocks), :
            ].astype(jnp.bfloat16)


def write_lines(total, out_view, signal_ref, line, pairs, blocks):
    for pair in range(pairs):
        for side in range(2):
            out_view[pl.ds((2 * pair + side) * blocks, blocks), :] = total[
                pair * blocks : (pair + 1) * blocks, side * TB : (side + 1) * TB
            ]
    for block in range(blocks):
        signal_ref[line : line + 2 * pairs, block * TB : (block + 1) * TB] = out_view[
            pl.ds(block, 2 * pairs, stride=blocks), :
        ].astype(jnp.bfloat16)


def inner_kernel(
    chunks,
    raw_hbm,
    mask_ref,
    left_ref,
    right_ref,
    band_ref,
    inner_ref,
    raw_ref,
    wide_ref,
    lhs_ref,
    out_ref,
    raw_sem,
):
    wires, ticks = raw_ref.shape
    blocks = ticks // TB
    pitch = wide_ref.shape[0] // wires
    reach = band_ref.shape[0]
    groups = raw_sem.shape[0]
    span = wires // groups

    copies = [
        pltpu.make_async_copy(
            raw_hbm.at[pl.ds(group * span, span)],
            raw_ref.at[pl.ds(group * span, span)],
            raw_sem.at[group],
        )
        for group in range(groups)
    ]
    for copy in copies:
        copy.start()
    wide_ref[pl.ds(0, wires, stride=pitch), :] = left_ref[...].astype(jnp.float32)
    wide_ref[pl.ds(blocks + 1, wires, stride=pitch), :] = right_ref[...].astype(jnp.float32)

    def fill(group, block):
        lines = slice(group * span, (group + 1) * span)
        inner = raw_ref[lines, block * TB : (block + 1) * TB].astype(jnp.float32) * mask_ref[
            lines
        ].astype(jnp.float32)
        wide_ref[pl.ds(group * span * pitch + block + 1, span, stride=pitch), :] = inner

    margin = reach - 1
    begin = PAD // 2
    state = {"group": 0, "pair": begin}

    def prepare(upto):
        todo = []
        while state["pair"] < upto:
            line = 2 * state["pair"] - margin
            while state["group"] < groups and line + 1 >= state["group"] * span:
                group = state["group"]
                todo.append(lambda group=group: copies[group].wait())
                for block in range(blocks):
                    todo.append(lambda group=group, block=block: fill(group, block))
                state["group"] += 1
            todo.append(
                lambda line=line, pair=state["pair"]: spread_pair(
                    wide_ref, lhs_ref.at[pair - begin], line, pitch, blocks
                )
            )
            state["pair"] += 1
        return todo

    pair = begin
    for job in prepare(pair + chunks[0] + margin):
        job()
    for index, size in enumerate(chunks):
        todo = prepare(pair + size + chunks[index + 1] + margin) if index + 1 < len(chunks) else []
        each = -(-len(todo) // reach)
        total = jnp.zeros((size * blocks, 2 * TB), jnp.float32)
        for step in range(reach):
            rows = lhs_ref[pair - begin + step : pair - begin + step + size]
            total = total + jnp.dot(
                rows.reshape(size * blocks, 6 * TB), band_ref[step], preferred_element_type=jnp.float32
            )
            for job in todo[step * each : (step + 1) * each]:
                job()
        write_lines(total, out_ref.at[index % 2], inner_ref, 2 * (pair - begin), size, blocks)
        pair += size


def convolve_inner(raw, mask, left, right, bands):
    wires, ticks = raw.shape
    reach = bands.shape[0]
    blocks = ticks // TB
    pitch = -(-(blocks + 2) // 8) * 8
    pairs = (wires - 2 * PAD) // 2
    chunks = []
    while sum(chunks) < pairs:
        chunks.append(min(32 if chunks else 24, pairs - sum(chunks)))
    groups = 4
    flops = 2 * blocks * pairs * reach * 6 * TB * 2 * TB
    return pl.pallas_call(
        functools.partial(inner_kernel, tuple(chunks)),
        out_shape=jax.ShapeDtypeStruct((wires - 2 * PAD, ticks), jnp.bfloat16),
        in_specs=[pl.BlockSpec(memory_space=pl.ANY)] + [vmem()] * 4,
        out_specs=vmem(),
        scratch_shapes=[
            pltpu.VMEM((wires, ticks), jnp.bfloat16),
            pltpu.VMEM((wires * pitch, TB), jnp.float32),
            pltpu.VMEM((pairs + reach - 1, blocks, 6 * TB), jnp.bfloat16),
            pltpu.VMEM((2, 2 * max(chunks) * blocks, TB), jnp.float32),
            pltpu.SemaphoreType.DMA((groups,)),
        ],
        cost_estimate=pl.CostEstimate(flops=flops, bytes_accessed=6 * MIB, transcendentals=0),
        compiler_params=pltpu.CompilerParams(vmem_limit_bytes=28 * MIB),
        name="inner",
    )(raw, mask, left, right, bands)


def edge_kernel(
    plan_ref,
    inner_ref,
    raw_ref,
    mask_ref,
    left_ref,
    right_ref,
    top_ref,
    bottom_ref,
    band_ref,
    geo_ref,
    signal_ref,
    partial_ref,
    wide_ref,
    lhs_ref,
    out_ref,
):
    wires, ticks = signal_ref.shape
    blocks = ticks // TB
    reach = band_ref.shape[0]
    block_wires = geo_ref.shape[1]
    wire_blocks = wires // block_wires
    near = 2 * PAD
    lines = PAD + near
    pitch = wide_ref.shape[1] // lines
    pairs = PAD // 2
    margin = reach - 1

    signal_ref[PAD : wires - PAD] = inner_ref[...]

    for end in range(2):
        halo_ref = (top_ref, bottom_ref)[end]
        mine = (slice(0, near), slice(wires - near, wires))[end]
        halo_at = (0, near)[end]
        mine_at = (PAD, 0)[end]
        mask = mask_ref[mine].astype(jnp.float32)
        for block in range(blocks + 2):
            columns = slice(block * TB, (block + 1) * TB)
            if block == 0:
                inner = left_ref[mine].astype(jnp.float32)
            elif block == blocks + 1:
                inner = right_ref[mine].astype(jnp.float32)
            else:
                inner = raw_ref[mine, (block - 1) * TB : block * TB].astype(jnp.float32) * mask
            wide_ref[end, pl.ds(halo_at * pitch + block, PAD, stride=pitch), :] = halo_ref[
                :, columns
            ].astype(jnp.float32)
            wide_ref[end, pl.ds(mine_at * pitch + block, near, stride=pitch), :] = inner
        first = (PAD, near - PAD)[end] - margin
        for pair in range(pairs + margin):
            spread_pair(
                wide_ref.at[end], lhs_ref.at[end, pair], first + 2 * pair, pitch, blocks
            )

    total = jnp.zeros((2 * pairs * blocks, 2 * TB), jnp.float32)
    for step in range(reach):
        rows = jnp.concatenate(
            [
                lhs_ref[end, step : step + pairs].reshape(pairs * blocks, 6 * TB)
                for end in range(2)
            ],
            axis=0,
        )
        total = total + jnp.dot(rows, band_ref[step], preferred_element_type=jnp.float32)
    for end in range(2):
        write_lines(
            total[end * pairs * blocks : (end + 1) * pairs * blocks],
            out_ref.at[end],
            signal_ref,
            (0, wires - PAD)[end],
            pairs,
            blocks,
        )

    source = plan_ref[1, 2]
    rows = geo_ref[pl.ds(source * wire_blocks, wire_blocks)].reshape(wires, -1)
    for block in range(0, blocks, 2):
        chosen = []
        for side in range(2):
            at = slice((block + side) * TB, (block + side + 1) * TB)
            column = []
            for line in range(wire_blocks):
                tile = signal_ref[line * block_wires : (line + 1) * block_wires, at]
                asked = plan_ref[2, line * blocks + block + side] == 1
                column.append(jnp.where(asked, tile, jnp.zeros_like(tile)))
            chosen.append(jnp.concatenate(column, axis=0))
        sums = lax.dot_general(
            rows,
            jnp.concatenate(chosen, axis=1),
            (((0,), (0,)), ((), ())),
            preferred_element_type=jnp.float32,
        ).astype(jnp.bfloat16)
        partial_ref[block] = sums[:, :TB]
        partial_ref[block + 1] = sums[:, TB:]


def convolve_edges(plan, inner, raw, mask, left, right, top, bottom, bands, geometry):
    wires, ticks = raw.shape
    reach = bands.shape[0]
    cells = geometry.shape[2]
    blocks = ticks // TB
    pitch = -(-(blocks + 2) // 8) * 8
    flops = 2 * blocks * PAD * reach * 6 * TB * 2 * TB
    return pl.pallas_call(
        edge_kernel,
        out_shape=(
            jax.ShapeDtypeStruct((wires, ticks), jnp.bfloat16),
            jax.ShapeDtypeStruct((blocks, cells, TB), jnp.bfloat16),
        ),
        in_specs=[smem()] + [vmem()] * 9,
        out_specs=(vmem(), vmem()),
        scratch_shapes=[
            pltpu.VMEM((2, 3 * PAD * pitch, TB), jnp.float32),
            pltpu.VMEM((2, PAD // 2 + reach - 1, blocks, 6 * TB), jnp.bfloat16),
            pltpu.VMEM((2, PAD * blocks, TB), jnp.float32),
        ],
        cost_estimate=pl.CostEstimate(flops=flops, bytes_accessed=6 * MIB, transcendentals=0),
        compiler_params=pltpu.CompilerParams(vmem_limit_bytes=24 * MIB),
        name="edges",
    )(plan, inner, raw, mask, left, right, top, bottom, bands, geometry)


def pack_kernel(slots, plan_ref, signal_ref, payload_ref, tiles_ref):
    block_wires = payload_ref.shape[1]
    wires, ticks = signal_ref.shape
    blocks = ticks // TB
    tiles_ref[...] = jnp.zeros_like(tiles_ref)
    for line in range(wires // block_wires):
        for block in range(blocks):
            place = plan_ref[0, line * blocks + block]
            tiles_ref[place] = signal_ref[
                line * block_wires : (line + 1) * block_wires, block * TB : (block + 1) * TB
            ]
    payload_ref[...] = tiles_ref[0:slots]


def pack_tiles(plan, signal, slots, block_wires):
    return pl.pallas_call(
        functools.partial(pack_kernel, slots),
        out_shape=jax.ShapeDtypeStruct((slots, block_wires, TB), jnp.bfloat16),
        in_specs=[smem(), vmem()],
        out_specs=vmem(),
        scratch_shapes=[pltpu.VMEM((slots + 1, block_wires, TB), jnp.bfloat16)],
        cost_estimate=pl.CostEstimate(flops=10**8, bytes_accessed=3 * MIB, transcendentals=0),
        compiler_params=pltpu.CompilerParams(vmem_limit_bytes=8 * MIB),
        name="pack",
    )(plan, signal)


def stage_kernel(slots, plan_ref, geo_ref, out_ref, rows_ref):
    groups = out_ref.shape[0]
    rows_ref[...] = jnp.zeros_like(rows_ref)
    for slot in range(slots):
        rows_ref[plan_ref[0, slot]] = geo_ref[plan_ref[2, slot]]
    for group in range(groups):
        rows = rows_ref[group * GROUP : (group + 1) * GROUP]
        out_ref[group] = jnp.transpose(rows.reshape(-1, rows.shape[-1]))


def stage_geometry(plan, geometry, groups, slots):
    _, block_wires, cells = geometry.shape
    return pl.pallas_call(
        functools.partial(stage_kernel, slots),
        out_shape=jax.ShapeDtypeStruct((groups, cells, GROUP * block_wires), jnp.bfloat16),
        in_specs=[smem(), vmem()],
        out_specs=vmem(),
        scratch_shapes=[pltpu.VMEM((groups * GROUP + 1, block_wires, cells), jnp.bfloat16)],
        cost_estimate=pl.CostEstimate(flops=10**8, bytes_accessed=3 * MIB, transcendentals=0),
        compiler_params=pltpu.CompilerParams(vmem_limit_bytes=12 * MIB),
        name="stage",
    )(plan, geometry)


def image_kernel(owner_total, share, plan_ref, arrived_ref, staged_ref, image_ref, tiles_ref, sum_ref):
    cells, ticks = image_ref.shape
    blocks = ticks // TB
    block_wires = arrived_ref.shape[1]
    groups = staged_ref.shape[0]
    is_hot = plan_ref[1, 0] == plan_ref[1, 2]
    counts = plan_ref[1, 3] == 1

    @pl.when(is_hot)
    def _():
        for source in range(owner_total):
            sums = arrived_ref[source * share : source * share + cells // block_wires]
            image_ref[:, source * TB : (source + 1) * TB] = sums.reshape(cells, TB).astype(
                jnp.float32
            )

    @pl.when(jnp.logical_not(is_hot))
    def _():
        sum_ref[...] = jnp.zeros_like(sum_ref)
        tiles_ref[...] = jnp.zeros_like(tiles_ref)

        @pl.when(counts)
        def _():
            for slot in range(owner_total * share):
                tiles_ref[plan_ref[0, slot]] = arrived_ref[slot]
            for group in range(groups):
                tiles = tiles_ref[group * GROUP : (group + 1) * GROUP]
                sum_ref[plan_ref[3, group]] += jnp.dot(
                    staged_ref[group],
                    tiles.reshape(GROUP * block_wires, TB),
                    preferred_element_type=jnp.float32,
                )

        for block in range(blocks):
            image_ref[:, block * TB : (block + 1) * TB] = sum_ref[block]


def make_image(plan, arrived, staged, owner_total, share, ticks):
    groups, cells, _ = staged.shape
    block_wires = arrived.shape[1]
    return pl.pallas_call(
        functools.partial(image_kernel, owner_total, share),
        out_shape=jax.ShapeDtypeStruct((cells, ticks), jnp.float32),
        in_specs=[smem(), vmem(), vmem()],
        out_specs=vmem(),
        scratch_shapes=[
            pltpu.VMEM((groups * GROUP + 1, block_wires, TB), jnp.bfloat16),
            pltpu.VMEM((ticks // TB, cells, TB), jnp.float32),
        ],
        cost_estimate=pl.CostEstimate(flops=10**8, bytes_accessed=3 * MIB, transcendentals=0),
        compiler_params=pltpu.CompilerParams(vmem_limit_bytes=16 * MIB),
        name="image",
    )(plan, arrived, staged)


def more_kernel(owner_total, share, plan_ref, table_ref, arrived_ref, geo_ref, before_ref, image_ref):
    cells, ticks = image_ref.shape
    blocks = ticks // TB
    wire_blocks = geo_ref.shape[0] // owner_total
    image_ref[...] = before_ref[...]

    @pl.when(plan_ref[1, 0] != plan_ref[1, 2])
    def _():
        def add(source, carry):
            for slot in range(share):
                block = table_ref[source, slot]
                at = pl.multiple_of((block % blocks) * TB, TB)
                image_ref[:, pl.ds(at, TB)] += lax.dot_general(
                    geo_ref[source * wire_blocks + block // blocks],
                    arrived_ref[source * share + slot],
                    (((0,), (0,)), ((), ())),
                    preferred_element_type=jnp.float32,
                )
            return carry

        lax.fori_loop(0, owner_total, add, 0)


def add_to_image(plan, table, arrived, geometry, owner_total, share, image):
    return pl.pallas_call(
        functools.partial(more_kernel, owner_total, share),
        out_shape=jax.ShapeDtypeStruct(image.shape, jnp.float32),
        in_specs=[smem(), smem()] + [vmem()] * 3,
        out_specs=vmem(),
        compiler_params=pltpu.CompilerParams(vmem_limit_bytes=16 * MIB),
        name="image_more",
    )(plan, table, arrived, geometry, image)


def further_round(trip, image, signal, geometry, rows, packed, plan, owner_total, share):
    trip, signal, rows, packed, plan = lax.optimization_barrier((trip, signal, rows, packed, plan))
    step = trip + plan[1, 3]
    hot = plan[1, 0]
    me = plan[1, 2]
    block_wires = geometry.shape[1]
    wire_count, tick_count = signal.shape
    blocks = tick_count // TB
    wire_blocks = wire_count // block_wires
    ids = jnp.arange(owner_total, dtype=jnp.int32)

    def ranks(owners):
        member = (owners[..., None] == ids).astype(jnp.int32)
        before = jnp.cumsum(member, axis=-2) - member
        return jnp.sum(before * member, axis=-1) - step * share

    def live(owners, rank):
        return (owners < owner_total) & (owners != hot) & (rank >= 0) & (rank < share)

    owners = packed[0] >> 7
    block = packed[0] & 127
    rank = ranks(owners)
    place = jnp.where(live(owners, rank), owners * share + rank, owner_total * share)
    tiles = signal.reshape(wire_blocks, block_wires, blocks, TB).transpose(0, 2, 1, 3)
    tiles = tiles.reshape(wire_blocks * blocks, block_wires, TB)[block]
    payload = jnp.zeros((owner_total * share, block_wires, TB), jnp.bfloat16)
    payload = payload.at[place].set(tiles, mode="drop")
    arrived = exchange(payload.reshape(owner_total, share, block_wires, TB))

    owners = rows >> 7
    rank = ranks(owners)
    source = jnp.arange(owner_total, dtype=jnp.int32)[:, None]
    line = jnp.where(live(owners, rank) & (owners == me), source, owner_total)
    table = jnp.zeros((owner_total, 128), jnp.int32)
    table = table.at[line, jnp.maximum(rank, 0)].set(rows & 127, mode="drop")
    return add_to_image(
        plan,
        table,
        arrived.reshape(owner_total * share, block_wires, TB),
        geometry,
        owner_total,
        share,
        image,
    )


def tick_halo(raw, mask, width):
    devices = lax.axis_size("tick")
    tick = lax.axis_index("tick")
    last = raw[:, -width:] * mask
    leading = raw[:, :width] * mask
    if devices == 2:
        got = lax.ppermute(jnp.where(tick == 0, last, leading), "tick", [(0, 1), (1, 0)])
        nothing = jnp.zeros_like(got)
        return jnp.where(tick == 0, nothing, got), jnp.where(tick == 0, got, nothing)
    up = [(i, i + 1) for i in range(devices - 1)]
    down = [(i + 1, i) for i in range(devices - 1)]
    return lax.ppermute(last, "tick", up), lax.ppermute(leading, "tick", down)


def wire_halo(raw, mask, left, right):
    devices = lax.axis_size("wire")
    up = [(i, i + 1) for i in range(devices - 1)]
    down = [(i + 1, i) for i in range(devices - 1)]

    def edge(where):
        return jnp.concatenate([left[where], raw[where] * mask[where], right[where]], axis=1)

    top = lax.ppermute(edge(slice(-PAD, None)), "wire", up)
    bottom = lax.ppermute(edge(slice(0, PAD)), "wire", down)
    return top, bottom


def exchange(array):
    return lax.all_to_all(array, ("plane", "wire"), split_axis=0, concat_axis=0, tiled=True)


def shards(raw, chan_mask, kernel, geometry, roi_block, roi_owner):
    wires, ticks = raw.shape
    slot_count = roi_block.shape[0]
    block_wires = geometry.shape[1]
    cells = geometry.shape[2]
    tick_blocks = ticks // TB
    owner_total = lax.axis_size("plane") * lax.axis_size("wire")
    share = -(-(slot_count - CAP) // (owner_total - 1))
    me = lax.axis_index("plane") * lax.axis_size("wire") + lax.axis_index("wire")

    packed = jnp.pad(
        roi_owner * 128 + roi_block, (0, 128 - slot_count), constant_values=owner_total * 128
    )
    packed = jnp.where(jnp.arange(128) == 127, owner_total * 128 + me, packed)[None]

    mask = chan_mask[:, None].astype(jnp.bfloat16)
    left, right = tick_halo(raw, mask, TB)
    top, bottom = wire_halo(raw, mask, left, right)
    bands = make_bands(kernel[0])
    inner = convolve_inner(raw, mask, left, right, bands)
    send_plan = make_send_plan(packed, owner_total, share)
    signal, partial = convolve_edges(
        send_plan, inner, raw, mask, left, right, top, bottom, bands, geometry
    )

    pieces = exchange(partial)
    payload = pack_tiles(send_plan, signal, owner_total * share, block_wires)

    payload, packed = lax.optimization_barrier((payload, packed))
    rows = exchange(jnp.broadcast_to(packed[None], (owner_total, 1, 128)))[:, 0]
    plan = make_receive_plan(
        rows, packed, owner_total, share, wires // block_wires, tick_blocks
    )
    staged = stage_geometry(
        plan, geometry, group_total(owner_total, share, tick_blocks), owner_total * share
    )

    sums = jnp.sum(pieces.astype(jnp.float32), axis=0).astype(jnp.bfloat16)
    payload = lax.dynamic_update_slice(
        payload.reshape(owner_total, share, block_wires, TB),
        sums.reshape(1, cells // block_wires, block_wires, TB),
        (send_plan[1, 0], 0, 0, 0),
    )
    payload, facts = lax.optimization_barrier((payload, plan[1:2, 1:2]))
    arrived = exchange(payload).reshape(owner_total * share, block_wires, TB)
    image = make_image(plan, arrived, staged, owner_total, share, ticks)

    trips = agree(facts)[0, 0]
    image = lax.fori_loop(
        0,
        trips,
        lambda trip, now: further_round(
            trip, now, signal, geometry, rows, packed, plan, owner_total, share
        ),
        image,
    )
    return signal, image


def solution(mesh):
    in_specs = (
        P(("plane", "wire"), "tick"),
        P(("plane", "wire")),
        P("plane", None, None),
        P(),
        P(("plane", "wire", "tick")),
        P(("plane", "wire", "tick")),
    )
    out_specs = (P(("plane", "wire"), "tick"), P(("plane", "wire"), "tick"))
    return jax.shard_map(shards, mesh=mesh, in_specs=in_specs, out_specs=out_specs, check_vma=False)
```

```python
import functools

import jax
import jax.numpy as jnp
from jax import lax
from jax.experimental import pallas as pl
from jax.experimental.pallas import tpu as pltpu
from jax.sharding import PartitionSpec as P

TB = 128
CAP = 25
PAD = 16
TABLE = 8
MIB = 1024 * 1024


def vmem():
    return pl.BlockSpec(memory_space=pltpu.VMEM)


def smem():
    return pl.BlockSpec(memory_space=pltpu.SMEM)


GROUP = 8


def lane_numbers():
    return lax.broadcasted_iota(jnp.int32, (1, 128), 1)


def earlier_lanes():
    return (
        lax.broadcasted_iota(jnp.int32, (128, 128), 0)
        < lax.broadcasted_iota(jnp.int32, (128, 128), 1)
    ).astype(jnp.bfloat16)


def count_before(member, before):
    return jnp.dot(
        member.astype(jnp.float32).astype(jnp.bfloat16), before, preferred_element_type=jnp.float32
    )


def most_named(owners, owner_total):
    lanes = lane_numbers()
    counts = jnp.full(owners.shape, -1.0, jnp.float32)
    for owner in range(owner_total):
        named = jnp.sum((owners == owner).astype(jnp.float32), axis=1, keepdims=True)
        counts = jnp.where(lanes == owner, named, counts)
    top = jnp.max(counts, axis=1, keepdims=True)
    chosen = jnp.min(
        jnp.where(counts == top, lanes.astype(jnp.float32), 127.0), axis=1, keepdims=True
    )
    return counts, chosen


def send_kernel(owner_total, share, own_ref, column_ref, out_ref):
    lanes = lane_numbers()
    own = own_ref[...]
    _, hot = most_named(own >> 7, owner_total)
    me = jnp.sum(jnp.where(lanes == 127, own & 127, 0).astype(jnp.float32), axis=1, keepdims=True)
    rows = lax.broadcasted_iota(jnp.int32, (owner_total, 128), 0)
    member = (own >> 7) == rows
    rank = count_before(member, earlier_lanes())
    place = jnp.where(rank < share, rows.astype(jnp.float32) * share + rank, -1.0)
    place = jnp.where(rows.astype(jnp.float32) == hot, -2.0, place)
    place = jnp.sum(jnp.where(member, place + 3.0, 0.0), axis=0, keepdims=True)

    column = column_ref[...]
    here = ((column & 127) == lanes) & ((column >> 7) < owner_total)
    spread = jnp.transpose(jnp.broadcast_to(place, (128, 128)))
    placed = jnp.sum(jnp.where(here, spread, 0.0), axis=0, keepdims=True)
    trash = float(owner_total * share)
    out_ref[...] = jnp.zeros_like(out_ref)
    out_ref[0:1, :] = jnp.where(placed >= 3.0, placed - 3.0, trash).astype(jnp.int32)
    out_ref[1:2, :] = jnp.where(lanes == 0, hot, jnp.where(lanes == 2, me, 0.0)).astype(jnp.int32)
    out_ref[2:3, :] = (placed == 1.0).astype(jnp.int32)


def make_send_plan(packed, owner_total, share):
    return pl.pallas_call(
        functools.partial(send_kernel, owner_total, share),
        out_shape=jax.ShapeDtypeStruct((8, 128), jnp.int32),
        in_specs=[vmem(), vmem()],
        out_specs=vmem(),
        compiler_params=pltpu.CompilerParams(vmem_limit_bytes=2 * MIB),
        name="send_plan",
    )(packed, packed.reshape(128, 1))


def receive_kernel(owner_total, share, wire_blocks, tick_blocks, rows_ref, own_ref, out_ref):
    lanes = lane_numbers()
    lane_f = lanes.astype(jnp.float32)
    every = rows_ref[...]
    owners = every >> 7
    own = own_ref[...]
    me = jnp.sum(jnp.where(lanes == 127, own & 127, 0).astype(jnp.float32), axis=1, keepdims=True)

    counts, chosen = most_named(owners, owner_total)
    hot = jnp.max(chosen, axis=0, keepdims=True)
    agreed = hot == jnp.min(chosen, axis=0, keepdims=True)
    left = jnp.where(agreed & (lane_f == hot), 0.0, counts)
    fullest = jnp.max(jnp.max(left, axis=1, keepdims=True), axis=0, keepdims=True)
    start = agreed.astype(jnp.float32)
    trips = -start
    for step in range(-(-CAP // share)):
        trips = trips + (fullest > step * share).astype(jnp.float32)
    trips = jnp.maximum(trips, 0.0)
    hot = jnp.where(agreed, hot, -1.0)

    to_me = owners.astype(jnp.float32) == me
    before = earlier_lanes()
    rank = count_before(to_me, before)
    blocks = every & 127
    source = lax.broadcasted_iota(jnp.int32, (owner_total, 128), 0)
    line = (source * wire_blocks + blocks // tick_blocks).astype(jnp.float32)
    tick = (blocks % tick_blocks).astype(jnp.float32)
    lines = jnp.zeros((1, 128), jnp.float32)
    ticks = jnp.full((1, 128), -1.0, jnp.float32)
    for slot in range(share):
        got = to_me & (rank == slot)
        here = lanes == source * share + slot
        for value, where in ((line, 0), (tick + 1.0, 1)):
            one = jnp.sum(jnp.where(got, value, 0.0), axis=1, keepdims=True)
            one = jnp.sum(jnp.where(here, one, 0.0), axis=0, keepdims=True)
            if where == 0:
                lines = lines + one
            else:
                ticks = ticks + one

    block_rows = lax.broadcasted_iota(jnp.int32, (tick_blocks, 128), 0).astype(jnp.float32)
    member = block_rows == ticks
    rank = count_before(member, before)
    total = jnp.sum(member.astype(jnp.float32), axis=1, keepdims=True)
    groups = jnp.zeros_like(total)
    for step in range(0, owner_total * share, GROUP):
        groups = groups + (total > step).astype(jnp.float32)
    lower = (
        lax.broadcasted_iota(jnp.int32, (tick_blocks, tick_blocks), 0)
        > lax.broadcasted_iota(jnp.int32, (tick_blocks, tick_blocks), 1)
    ).astype(jnp.bfloat16)
    base = jnp.dot(
        lower,
        jnp.broadcast_to(groups, (tick_blocks, 128)).astype(jnp.bfloat16),
        preferred_element_type=jnp.float32,
    )
    place = jnp.sum(jnp.where(member, base * GROUP + rank, 0.0), axis=0, keepdims=True)
    trash = float(group_total(owner_total, share, tick_blocks) * GROUP)
    place = jnp.where(ticks < 0.0, trash, place)
    inside = (base <= lane_f) & (lane_f < base + groups)
    group_tick = jnp.sum(jnp.where(inside, block_rows, 0.0), axis=0, keepdims=True)

    facts = jnp.where(lanes == 0, hot, 0.0)
    facts = jnp.where(lanes == 1, trips, facts)
    facts = jnp.where(lanes == 2, me, facts)
    facts = jnp.where(lanes == 3, start, facts)
    out_ref[...] = jnp.zeros_like(out_ref)
    out_ref[0:1, :] = place.astype(jnp.int32)
    out_ref[1:2, :] = facts.astype(jnp.int32)
    out_ref[2:3, :] = lines.astype(jnp.int32)
    out_ref[3:4, :] = group_tick.astype(jnp.int32)


def group_total(owner_total, share, tick_blocks):
    return (owner_total * share - tick_blocks) // GROUP + tick_blocks


def make_receive_plan(rows, packed, owner_total, share, wire_blocks, tick_blocks):
    return pl.pallas_call(
        functools.partial(receive_kernel, owner_total, share, wire_blocks, tick_blocks),
        out_shape=jax.ShapeDtypeStruct((8, 128), jnp.int32),
        in_specs=[vmem(), vmem()],
        out_specs=vmem(),
        compiler_params=pltpu.CompilerParams(vmem_limit_bytes=2 * MIB),
        name="receive_plan",
    )(rows, packed)


def agree(rounds):
    devices = lax.axis_size("tick")
    reach = 1
    while reach < devices:
        ring = [(i, (i + reach) % devices) for i in range(devices)]
        rounds = jnp.maximum(rounds, lax.ppermute(rounds, "tick", ring))
        reach *= 2
    return rounds


def band_kernel(taps_w, taps_ref, band_ref):
    row = lax.broadcasted_iota(jnp.int32, (TB, TB), 0)
    col = lax.broadcasted_iota(jnp.int32, (TB, TB), 1)
    pairs = (taps_w + 1) // 2
    band_ref[0, 0 : 3 * TB, TB : 2 * TB] = jnp.zeros((3 * TB, TB), jnp.bfloat16)
    band_ref[pairs - 1, 3 * TB : 6 * TB, 0:TB] = jnp.zeros((3 * TB, TB), jnp.bfloat16)
    taps = taps_ref[...].astype(jnp.float32)
    for tap in range(taps_w):
        spread = jnp.broadcast_to(taps[tap : tap + 1], (TB, 2 * TB))
        rolled = pltpu.roll(spread, TB, 1, stride=1, stride_axis=0)
        middle = rolled[:, :TB]
        outer = rolled[:, TB:]
        bands = (
            jnp.where(col < row, outer, 0.0).astype(jnp.bfloat16),
            middle.astype(jnp.bfloat16),
            jnp.where(col >= row, outer, 0.0).astype(jnp.bfloat16),
        )
        for first, second in ((0, 0), (1, 1), (1, 0), (0, 1)):
            if (tap - first + second) % 2:
                continue
            pair = (tap - first + second) // 2
            for piece in range(3):
                start = (first * 3 + piece) * TB
                band_ref[pair, start : start + TB, second * TB : (second + 1) * TB] = bands[piece]


def make_bands(taps):
    taps_w = taps.shape[0]
    return pl.pallas_call(
        functools.partial(band_kernel, taps_w),
        out_shape=jax.ShapeDtypeStruct(((taps_w + 1) // 2, 6 * TB, 2 * TB), jnp.bfloat16),
        in_specs=[vmem()],
        out_specs=vmem(),
        cost_estimate=pl.CostEstimate(flops=10**9, bytes_accessed=6 * MIB, transcendentals=0),
        compiler_params=pltpu.CompilerParams(vmem_limit_bytes=16 * MIB),
        name="bands",
    )(taps)


def spread_pair(wide_ref, lhs_view, line, pitch, blocks):
    for side in range(2):
        for piece in range(3):
            at = (side * 3 + piece) * TB
            lhs_view[:, at : at + TB] = wide_ref[
                pl.ds((line + side) * pitch + piece, blocks), :
            ].astype(jnp.bfloat16)


def write_lines(total, out_view, signal_ref, line, pairs, blocks):
    for pair in range(pairs):
        for side in range(2):
            out_view[pl.ds((2 * pair + side) * blocks, blocks), :] = total[
                pair * blocks : (pair + 1) * blocks, side * TB : (side + 1) * TB
            ]
    for block in range(blocks):
        signal_ref[line : line + 2 * pairs, block * TB : (block + 1) * TB] = out_view[
            pl.ds(block, 2 * pairs, stride=blocks), :
        ].astype(jnp.bfloat16)


def inner_kernel(
    chunks,
    raw_hbm,
    mask_ref,
    left_ref,
    right_ref,
    band_ref,
    inner_ref,
    raw_ref,
    wide_ref,
    lhs_ref,
    out_ref,
    raw_sem,
):
    wires, ticks = raw_ref.shape
    blocks = ticks // TB
    pitch = wide_ref.shape[0] // wires
    reach = band_ref.shape[0]
    groups = raw_sem.shape[0]
    span = wires // groups

    copies = [
        pltpu.make_async_copy(
            raw_hbm.at[pl.ds(group * span, span)],
            raw_ref.at[pl.ds(group * span, span)],
            raw_sem.at[group],
        )
        for group in range(groups)
    ]
    for copy in copies:
        copy.start()
    wide_ref[pl.ds(0, wires, stride=pitch), :] = left_ref[...].astype(jnp.float32)
    wide_ref[pl.ds(blocks + 1, wires, stride=pitch), :] = right_ref[...].astype(jnp.float32)

    def fill(group, block):
        lines = slice(group * span, (group + 1) * span)
        inner = raw_ref[lines, block * TB : (block + 1) * TB].astype(jnp.float32) * mask_ref[
            lines
        ].astype(jnp.float32)
        wide_ref[pl.ds(group * span * pitch + block + 1, span, stride=pitch), :] = inner

    margin = reach - 1
    begin = PAD // 2
    state = {"group": 0, "pair": begin}

    def prepare(upto):
        todo = []
        while state["pair"] < upto:
            line = 2 * state["pair"] - margin
            while state["group"] < groups and line + 1 >= state["group"] * span:
                group = state["group"]
                todo.append(lambda group=group: copies[group].wait())
                for block in range(blocks):
                    todo.append(lambda group=group, block=block: fill(group, block))
                state["group"] += 1
            todo.append(
                lambda line=line, pair=state["pair"]: spread_pair(
                    wide_ref, lhs_ref.at[pair - begin], line, pitch, blocks
                )
            )
            state["pair"] += 1
        return todo

    pair = begin
    for job in prepare(pair + chunks[0] + margin):
        job()
    for index, size in enumerate(chunks):
        todo = prepare(pair + size + chunks[index + 1] + margin) if index + 1 < len(chunks) else []
        each = -(-len(todo) // reach)
        total = jnp.zeros((size * blocks, 2 * TB), jnp.float32)
        for step in range(reach):
            rows = lhs_ref[pair - begin + step : pair - begin + step + size]
            total = total + jnp.dot(
                rows.reshape(size * blocks, 6 * TB), band_ref[step], preferred_element_type=jnp.float32
            )
            for job in todo[step * each : (step + 1) * each]:
                job()
        write_lines(total, out_ref.at[index % 2], inner_ref, 2 * (pair - begin), size, blocks)
        pair += size


def convolve_inner(raw, mask, left, right, bands):
    wires, ticks = raw.shape
    reach = bands.shape[0]
    blocks = ticks // TB
    pitch = -(-(blocks + 2) // 8) * 8
    pairs = (wires - 2 * PAD) // 2
    chunks = []
    while sum(chunks) < pairs:
        chunks.append(min(32 if chunks else 24, pairs - sum(chunks)))
    groups = 4
    flops = 2 * blocks * pairs * reach * 6 * TB * 2 * TB
    return pl.pallas_call(
        functools.partial(inner_kernel, tuple(chunks)),
        out_shape=jax.ShapeDtypeStruct((wires - 2 * PAD, ticks), jnp.bfloat16),
        in_specs=[pl.BlockSpec(memory_space=pl.ANY)] + [vmem()] * 4,
        out_specs=vmem(),
        scratch_shapes=[
            pltpu.VMEM((wires, ticks), jnp.bfloat16),
            pltpu.VMEM((wires * pitch, TB), jnp.float32),
            pltpu.VMEM((pairs + reach - 1, blocks, 6 * TB), jnp.bfloat16),
            pltpu.VMEM((2, 2 * max(chunks) * blocks, TB), jnp.float32),
            pltpu.SemaphoreType.DMA((groups,)),
        ],
        cost_estimate=pl.CostEstimate(flops=flops, bytes_accessed=6 * MIB, transcendentals=0),
        compiler_params=pltpu.CompilerParams(vmem_limit_bytes=28 * MIB),
        name="inner",
    )(raw, mask, left, right, bands)


def edge_kernel(
    plan_ref,
    own_ref,
    inner_ref,
    raw_ref,
    mask_ref,
    left_ref,
    right_ref,
    top_ref,
    bottom_ref,
    band_ref,
    geo_ref,
    signal_ref,
    partial_ref,
    wide_ref,
    lhs_ref,
    out_ref,
):
    wires, ticks = signal_ref.shape
    blocks = ticks // TB
    reach = band_ref.shape[0]
    block_wires = geo_ref.shape[1]
    wire_blocks = wires // block_wires
    near = 2 * PAD
    lines = PAD + near
    pitch = wide_ref.shape[1] // lines
    pairs = PAD // 2
    margin = reach - 1

    signal_ref[PAD : wires - PAD] = inner_ref[...]

    for end in range(2):
        halo_ref = (top_ref, bottom_ref)[end]
        mine = (slice(0, near), slice(wires - near, wires))[end]
        halo_at = (0, near)[end]
        mine_at = (PAD, 0)[end]
        mask = mask_ref[mine].astype(jnp.float32)
        for block in range(blocks + 2):
            columns = slice(block * TB, (block + 1) * TB)
            if block == 0:
                inner = left_ref[mine].astype(jnp.float32)
            elif block == blocks + 1:
                inner = right_ref[mine].astype(jnp.float32)
            else:
                inner = raw_ref[mine, (block - 1) * TB : block * TB].astype(jnp.float32) * mask
            wide_ref[end, pl.ds(halo_at * pitch + block, PAD, stride=pitch), :] = halo_ref[
                :, columns
            ].astype(jnp.float32)
            wide_ref[end, pl.ds(mine_at * pitch + block, near, stride=pitch), :] = inner
        first = (PAD, near - PAD)[end] - margin
        for pair in range(pairs + margin):
            spread_pair(
                wide_ref.at[end], lhs_ref.at[end, pair], first + 2 * pair, pitch, blocks
            )

    total = jnp.zeros((2 * pairs * blocks, 2 * TB), jnp.float32)
    for step in range(reach):
        rows = jnp.concatenate(
            [
                lhs_ref[end, step : step + pairs].reshape(pairs * blocks, 6 * TB)
                for end in range(2)
            ],
            axis=0,
        )
        total = total + jnp.dot(rows, band_ref[step], preferred_element_type=jnp.float32)
    for end in range(2):
        write_lines(
            total[end * pairs * blocks : (end + 1) * pairs * blocks],
            out_ref.at[end],
            signal_ref,
            (0, wires - PAD)[end],
            pairs,
            blocks,
        )

    cells = geo_ref.shape[2]
    own = own_ref[...]
    line = lax.broadcasted_iota(jnp.int32, (TABLE, 128), 0)
    table = jnp.where(line == 0, own >> 7, jnp.where(line == 1, own & 127, 0))
    table = table.astype(jnp.float32).astype(jnp.bfloat16)
    for block in range(blocks):
        partial_ref[block, cells : cells + TABLE] = table

    source = plan_ref[1, 2]
    rows = geo_ref[pl.ds(source * wire_blocks, wire_blocks)].reshape(wires, -1)
    for block in range(0, blocks, 2):
        chosen = []
        for side in range(2):
            at = slice((block + side) * TB, (block + side + 1) * TB)
            column = []
            for line in range(wire_blocks):
                tile = signal_ref[line * block_wires : (line + 1) * block_wires, at]
                asked = plan_ref[2, line * blocks + block + side] == 1
                column.append(jnp.where(asked, tile, jnp.zeros_like(tile)))
            chosen.append(jnp.concatenate(column, axis=0))
        sums = lax.dot_general(
            rows,
            jnp.concatenate(chosen, axis=1),
            (((0,), (0,)), ((), ())),
            preferred_element_type=jnp.float32,
        ).astype(jnp.bfloat16)
        partial_ref[block, 0:cells] = sums[:, :TB]
        partial_ref[block + 1, 0:cells] = sums[:, TB:]


def convolve_edges(plan, own, inner, raw, mask, left, right, top, bottom, bands, geometry):
    wires, ticks = raw.shape
    reach = bands.shape[0]
    cells = geometry.shape[2]
    blocks = ticks // TB
    pitch = -(-(blocks + 2) // 8) * 8
    flops = 2 * blocks * PAD * reach * 6 * TB * 2 * TB
    return pl.pallas_call(
        edge_kernel,
        out_shape=(
            jax.ShapeDtypeStruct((wires, ticks), jnp.bfloat16),
            jax.ShapeDtypeStruct((blocks, cells + TABLE, TB), jnp.bfloat16),
        ),
        in_specs=[smem()] + [vmem()] * 10,
        out_specs=(vmem(), vmem()),
        scratch_shapes=[
            pltpu.VMEM((2, 3 * PAD * pitch, TB), jnp.float32),
            pltpu.VMEM((2, PAD // 2 + reach - 1, blocks, 6 * TB), jnp.bfloat16),
            pltpu.VMEM((2, PAD * blocks, TB), jnp.float32),
        ],
        cost_estimate=pl.CostEstimate(flops=flops, bytes_accessed=6 * MIB, transcendentals=0),
        compiler_params=pltpu.CompilerParams(vmem_limit_bytes=24 * MIB),
        name="edges",
    )(plan, own, inner, raw, mask, left, right, top, bottom, bands, geometry)


def pack_kernel(slots, plan_ref, signal_ref, payload_ref, tiles_ref):
    block_wires = payload_ref.shape[1]
    wires, ticks = signal_ref.shape
    blocks = ticks // TB
    tiles_ref[...] = jnp.zeros_like(tiles_ref)
    for line in range(wires // block_wires):
        for block in range(blocks):
            place = plan_ref[0, line * blocks + block]
            tiles_ref[place] = signal_ref[
                line * block_wires : (line + 1) * block_wires, block * TB : (block + 1) * TB
            ]
    payload_ref[...] = tiles_ref[0:slots]


def pack_tiles(plan, signal, slots, block_wires):
    return pl.pallas_call(
        functools.partial(pack_kernel, slots),
        out_shape=jax.ShapeDtypeStruct((slots, block_wires, TB), jnp.bfloat16),
        in_specs=[smem(), vmem()],
        out_specs=vmem(),
        scratch_shapes=[pltpu.VMEM((slots + 1, block_wires, TB), jnp.bfloat16)],
        cost_estimate=pl.CostEstimate(flops=10**8, bytes_accessed=3 * MIB, transcendentals=0),
        compiler_params=pltpu.CompilerParams(vmem_limit_bytes=8 * MIB),
        name="pack",
    )(plan, signal)


def stage_kernel(slots, plan_ref, geo_ref, out_ref, rows_ref):
    groups = out_ref.shape[0]
    rows_ref[...] = jnp.zeros_like(rows_ref)
    for slot in range(slots):
        rows_ref[plan_ref[0, slot]] = geo_ref[plan_ref[2, slot]]
    for group in range(groups):
        rows = rows_ref[group * GROUP : (group + 1) * GROUP]
        out_ref[group] = jnp.transpose(rows.reshape(-1, rows.shape[-1]))


def stage_geometry(plan, geometry, groups, slots):
    _, block_wires, cells = geometry.shape
    return pl.pallas_call(
        functools.partial(stage_kernel, slots),
        out_shape=jax.ShapeDtypeStruct((groups, cells, GROUP * block_wires), jnp.bfloat16),
        in_specs=[smem(), vmem()],
        out_specs=vmem(),
        scratch_shapes=[pltpu.VMEM((groups * GROUP + 1, block_wires, cells), jnp.bfloat16)],
        cost_estimate=pl.CostEstimate(flops=10**8, bytes_accessed=3 * MIB, transcendentals=0),
        compiler_params=pltpu.CompilerParams(vmem_limit_bytes=12 * MIB),
        name="stage",
    )(plan, geometry)


def image_kernel(owner_total, share, plan_ref, arrived_ref, staged_ref, image_ref, tiles_ref, sum_ref):
    cells, ticks = image_ref.shape
    blocks = ticks // TB
    block_wires = arrived_ref.shape[1]
    groups = staged_ref.shape[0]
    is_hot = plan_ref[1, 0] == plan_ref[1, 2]
    counts = plan_ref[1, 3] == 1

    @pl.when(is_hot)
    def _():
        for source in range(owner_total):
            sums = arrived_ref[source * share : source * share + cells // block_wires]
            image_ref[:, source * TB : (source + 1) * TB] = sums.reshape(cells, TB).astype(
                jnp.float32
            )

    @pl.when(jnp.logical_not(is_hot))
    def _():
        sum_ref[...] = jnp.zeros_like(sum_ref)
        tiles_ref[...] = jnp.zeros_like(tiles_ref)

        @pl.when(counts)
        def _():
            for slot in range(owner_total * share):
                tiles_ref[plan_ref[0, slot]] = arrived_ref[slot]
            for group in range(groups):
                tiles = tiles_ref[group * GROUP : (group + 1) * GROUP]
                sum_ref[plan_ref[3, group]] += jnp.dot(
                    staged_ref[group],
                    tiles.reshape(GROUP * block_wires, TB),
                    preferred_element_type=jnp.float32,
                )

        for block in range(blocks):
            image_ref[:, block * TB : (block + 1) * TB] = sum_ref[block]


def make_image(plan, arrived, staged, owner_total, share, ticks):
    groups, cells, _ = staged.shape
    block_wires = arrived.shape[1]
    return pl.pallas_call(
        functools.partial(image_kernel, owner_total, share),
        out_shape=jax.ShapeDtypeStruct((cells, ticks), jnp.float32),
        in_specs=[smem(), vmem(), vmem()],
        out_specs=vmem(),
        scratch_shapes=[
            pltpu.VMEM((groups * GROUP + 1, block_wires, TB), jnp.bfloat16),
            pltpu.VMEM((ticks // TB, cells, TB), jnp.float32),
        ],
        cost_estimate=pl.CostEstimate(flops=10**8, bytes_accessed=3 * MIB, transcendentals=0),
        compiler_params=pltpu.CompilerParams(vmem_limit_bytes=16 * MIB),
        name="image",
    )(plan, arrived, staged)


def more_kernel(owner_total, share, plan_ref, table_ref, arrived_ref, geo_ref, before_ref, image_ref):
    cells, ticks = image_ref.shape
    blocks = ticks // TB
    wire_blocks = geo_ref.shape[0] // owner_total
    image_ref[...] = before_ref[...]

    @pl.when(plan_ref[1, 0] != plan_ref[1, 2])
    def _():
        def add(source, carry):
            for slot in range(share):
                block = table_ref[source, slot]
                at = pl.multiple_of((block % blocks) * TB, TB)
                image_ref[:, pl.ds(at, TB)] += lax.dot_general(
                    geo_ref[source * wire_blocks + block // blocks],
                    arrived_ref[source * share + slot],
                    (((0,), (0,)), ((), ())),
                    preferred_element_type=jnp.float32,
                )
            return carry

        lax.fori_loop(0, owner_total, add, 0)


def add_to_image(plan, table, arrived, geometry, owner_total, share, image):
    return pl.pallas_call(
        functools.partial(more_kernel, owner_total, share),
        out_shape=jax.ShapeDtypeStruct(image.shape, jnp.float32),
        in_specs=[smem(), smem()] + [vmem()] * 3,
        out_specs=vmem(),
        compiler_params=pltpu.CompilerParams(vmem_limit_bytes=16 * MIB),
        name="image_more",
    )(plan, table, arrived, geometry, image)


def further_round(trip, image, signal, geometry, rows, packed, plan, owner_total, share):
    trip, signal, rows, packed, plan = lax.optimization_barrier((trip, signal, rows, packed, plan))
    step = trip + plan[1, 3]
    hot = plan[1, 0]
    me = plan[1, 2]
    block_wires = geometry.shape[1]
    wire_count, tick_count = signal.shape
    blocks = tick_count // TB
    wire_blocks = wire_count // block_wires
    ids = jnp.arange(owner_total, dtype=jnp.int32)

    def ranks(owners):
        member = (owners[..., None] == ids).astype(jnp.int32)
        before = jnp.cumsum(member, axis=-2) - member
        return jnp.sum(before * member, axis=-1) - step * share

    def live(owners, rank):
        return (owners < owner_total) & (owners != hot) & (rank >= 0) & (rank < share)

    owners = packed[0] >> 7
    block = packed[0] & 127
    rank = ranks(owners)
    place = jnp.where(live(owners, rank), owners * share + rank, owner_total * share)
    tiles = signal.reshape(wire_blocks, block_wires, blocks, TB).transpose(0, 2, 1, 3)
    tiles = tiles.reshape(wire_blocks * blocks, block_wires, TB)[block]
    payload = jnp.zeros((owner_total * share, block_wires, TB), jnp.bfloat16)
    payload = payload.at[place].set(tiles, mode="drop")
    arrived = exchange(payload.reshape(owner_total, share, block_wires, TB))

    owners = rows >> 7
    rank = ranks(owners)
    source = jnp.arange(owner_total, dtype=jnp.int32)[:, None]
    line = jnp.where(live(owners, rank) & (owners == me), source, owner_total)
    table = jnp.zeros((owner_total, 128), jnp.int32)
    table = table.at[line, jnp.maximum(rank, 0)].set(rows & 127, mode="drop")
    return add_to_image(
        plan,
        table,
        arrived.reshape(owner_total * share, block_wires, TB),
        geometry,
        owner_total,
        share,
        image,
    )


def tick_halo(raw, mask, width):
    devices = lax.axis_size("tick")
    tick = lax.axis_index("tick")
    last = raw[:, -width:] * mask
    leading = raw[:, :width] * mask
    if devices == 2:
        got = lax.ppermute(jnp.where(tick == 0, last, leading), "tick", [(0, 1), (1, 0)])
        nothing = jnp.zeros_like(got)
        return jnp.where(tick == 0, nothing, got), jnp.where(tick == 0, got, nothing)
    up = [(i, i + 1) for i in range(devices - 1)]
    down = [(i + 1, i) for i in range(devices - 1)]
    return lax.ppermute(last, "tick", up), lax.ppermute(leading, "tick", down)


def wire_halo(raw, mask, left, right):
    devices = lax.axis_size("wire")
    up = [(i, i + 1) for i in range(devices - 1)]
    down = [(i + 1, i) for i in range(devices - 1)]

    def edge(where):
        return jnp.concatenate([left[where], raw[where] * mask[where], right[where]], axis=1)

    top = lax.ppermute(edge(slice(-PAD, None)), "wire", up)
    bottom = lax.ppermute(edge(slice(0, PAD)), "wire", down)
    return top, bottom


def exchange(array):
    return lax.all_to_all(array, ("plane", "wire"), split_axis=0, concat_axis=0, tiled=True)


def shards(raw, chan_mask, kernel, geometry, roi_block, roi_owner):
    wires, ticks = raw.shape
    slot_count = roi_block.shape[0]
    block_wires = geometry.shape[1]
    cells = geometry.shape[2]
    tick_blocks = ticks // TB
    owner_total = lax.axis_size("plane") * lax.axis_size("wire")
    share = -(-(slot_count - CAP) // (owner_total - 1))
    me = lax.axis_index("plane") * lax.axis_size("wire") + lax.axis_index("wire")

    packed = jnp.pad(
        roi_owner * 128 + roi_block, (0, 128 - slot_count), constant_values=owner_total * 128
    )
    packed = jnp.where(jnp.arange(128) == 127, owner_total * 128 + me, packed)[None]

    mask = chan_mask[:, None].astype(jnp.bfloat16)
    left, right = tick_halo(raw, mask, TB)
    top, bottom = wire_halo(raw, mask, left, right)
    bands = make_bands(kernel[0])
    inner = convolve_inner(raw, mask, left, right, bands)
    send_plan = make_send_plan(packed, owner_total, share)
    signal, partial = convolve_edges(
        send_plan, packed, inner, raw, mask, left, right, top, bottom, bands, geometry
    )

    pieces = exchange(partial)
    payload = pack_tiles(send_plan, signal, owner_total * share, block_wires)

    rows = pieces[:, cells].astype(jnp.int32) * 128 + pieces[:, cells + 1].astype(jnp.int32)
    plan = make_receive_plan(
        rows, packed, owner_total, share, wires // block_wires, tick_blocks
    )
    staged = stage_geometry(
        plan, geometry, group_total(owner_total, share, tick_blocks), owner_total * share
    )

    sums = jnp.sum(pieces[:, :cells].astype(jnp.float32), axis=0).astype(jnp.bfloat16)
    payload = lax.dynamic_update_slice(
        payload.reshape(owner_total, share, block_wires, TB),
        sums.reshape(1, cells // block_wires, block_wires, TB),
        (send_plan[1, 0], 0, 0, 0),
    )
    arrived = exchange(payload).reshape(owner_total * share, block_wires, TB)
    image = make_image(plan, arrived, staged, owner_total, share, ticks)

    trips = agree(plan[1:2, 1:2])[0, 0]
    image = lax.fori_loop(
        0,
        trips,
        lambda trip, now: further_round(
            trip, now, signal, geometry, rows, packed, plan, owner_total, share
        ),
        image,
    )
    return signal, image


def solution(mesh):
    in_specs = (
        P(("plane", "wire"), "tick"),
        P(("plane", "wire")),
        P("plane", None, None),
        P(),
        P(("plane", "wire", "tick")),
        P(("plane", "wire", "tick")),
    )
    out_specs = (P(("plane", "wire"), "tick"), P(("plane", "wire"), "tick"))
    return jax.shard_map(shards, mesh=mesh, in_specs=in_specs, out_specs=out_specs, check_vma=False)
```

```python
import functools

import jax
import jax.numpy as jnp
from jax import lax
from jax.experimental import pallas as pl
from jax.experimental.pallas import tpu as pltpu
from jax.sharding import PartitionSpec as P

TB = 128
CAP = 25
PAD = 16
TABLE = 8
MIB = 1024 * 1024


def vmem():
    return pl.BlockSpec(memory_space=pltpu.VMEM)


def smem():
    return pl.BlockSpec(memory_space=pltpu.SMEM)


GROUP = 8


def lane_numbers():
    return lax.broadcasted_iota(jnp.int32, (1, 128), 1)


def earlier_lanes():
    return (
        lax.broadcasted_iota(jnp.int32, (128, 128), 0)
        < lax.broadcasted_iota(jnp.int32, (128, 128), 1)
    ).astype(jnp.bfloat16)


def count_before(member, before):
    return jnp.dot(
        member.astype(jnp.float32).astype(jnp.bfloat16), before, preferred_element_type=jnp.float32
    )


def most_named(owners, owner_total):
    lanes = lane_numbers()
    counts = jnp.full(owners.shape, -1.0, jnp.float32)
    for owner in range(owner_total):
        named = jnp.sum((owners == owner).astype(jnp.float32), axis=1, keepdims=True)
        counts = jnp.where(lanes == owner, named, counts)
    top = jnp.max(counts, axis=1, keepdims=True)
    chosen = jnp.min(
        jnp.where(counts == top, lanes.astype(jnp.float32), 127.0), axis=1, keepdims=True
    )
    return counts, chosen


def send_kernel(owner_total, share, own_ref, column_ref, out_ref):
    lanes = lane_numbers()
    own = own_ref[...]
    _, hot = most_named(own >> 7, owner_total)
    me = jnp.sum(jnp.where(lanes == 127, own & 127, 0).astype(jnp.float32), axis=1, keepdims=True)
    rows = lax.broadcasted_iota(jnp.int32, (owner_total, 128), 0)
    member = (own >> 7) == rows
    rank = count_before(member, earlier_lanes())
    place = jnp.where(rank < share, rows.astype(jnp.float32) * share + rank, -1.0)
    place = jnp.where(rows.astype(jnp.float32) == hot, -2.0, place)
    place = jnp.sum(jnp.where(member, place + 3.0, 0.0), axis=0, keepdims=True)

    column = column_ref[...]
    here = ((column & 127) == lanes) & ((column >> 7) < owner_total)
    spread = jnp.transpose(jnp.broadcast_to(place, (128, 128)))
    placed = jnp.sum(jnp.where(here, spread, 0.0), axis=0, keepdims=True)
    trash = float(owner_total * share)
    out_ref[...] = jnp.zeros_like(out_ref)
    out_ref[0:1, :] = jnp.where(placed >= 3.0, placed - 3.0, trash).astype(jnp.int32)
    out_ref[1:2, :] = jnp.where(lanes == 0, hot, jnp.where(lanes == 2, me, 0.0)).astype(jnp.int32)
    out_ref[2:3, :] = (placed == 1.0).astype(jnp.int32)


def make_send_plan(packed, owner_total, share):
    return pl.pallas_call(
        functools.partial(send_kernel, owner_total, share),
        out_shape=jax.ShapeDtypeStruct((8, 128), jnp.int32),
        in_specs=[vmem(), vmem()],
        out_specs=vmem(),
        compiler_params=pltpu.CompilerParams(vmem_limit_bytes=2 * MIB),
        name="send_plan",
    )(packed, packed.reshape(128, 1))


def receive_kernel(owner_total, share, wire_blocks, tick_blocks, rows_ref, own_ref, out_ref):
    lanes = lane_numbers()
    lane_f = lanes.astype(jnp.float32)
    every = rows_ref[...]
    owners = every >> 7
    own = own_ref[...]
    me = jnp.sum(jnp.where(lanes == 127, own & 127, 0).astype(jnp.float32), axis=1, keepdims=True)

    counts, chosen = most_named(owners, owner_total)
    hot = jnp.max(chosen, axis=0, keepdims=True)
    agreed = hot == jnp.min(chosen, axis=0, keepdims=True)
    left = jnp.where(agreed & (lane_f == hot), 0.0, counts)
    fullest = jnp.max(jnp.max(left, axis=1, keepdims=True), axis=0, keepdims=True)
    start = agreed.astype(jnp.float32)
    trips = -start
    for step in range(-(-CAP // share)):
        trips = trips + (fullest > step * share).astype(jnp.float32)
    trips = jnp.maximum(trips, 0.0)
    hot = jnp.where(agreed, hot, -1.0)

    to_me = owners.astype(jnp.float32) == me
    before = earlier_lanes()
    rank = count_before(to_me, before)
    blocks = every & 127
    source = lax.broadcasted_iota(jnp.int32, (owner_total, 128), 0)
    line = (source * wire_blocks + blocks // tick_blocks).astype(jnp.float32)
    tick = (blocks % tick_blocks).astype(jnp.float32)
    lines = jnp.zeros((1, 128), jnp.float32)
    ticks = jnp.full((1, 128), -1.0, jnp.float32)
    for slot in range(share):
        got = to_me & (rank == slot)
        here = lanes == source * share + slot
        for value, where in ((line, 0), (tick + 1.0, 1)):
            one = jnp.sum(jnp.where(got, value, 0.0), axis=1, keepdims=True)
            one = jnp.sum(jnp.where(here, one, 0.0), axis=0, keepdims=True)
            if where == 0:
                lines = lines + one
            else:
                ticks = ticks + one

    block_rows = lax.broadcasted_iota(jnp.int32, (tick_blocks, 128), 0).astype(jnp.float32)
    member = block_rows == ticks
    rank = count_before(member, before)
    total = jnp.sum(member.astype(jnp.float32), axis=1, keepdims=True)
    groups = jnp.zeros_like(total)
    for step in range(0, owner_total * share, GROUP):
        groups = groups + (total > step).astype(jnp.float32)
    lower = (
        lax.broadcasted_iota(jnp.int32, (tick_blocks, tick_blocks), 0)
        > lax.broadcasted_iota(jnp.int32, (tick_blocks, tick_blocks), 1)
    ).astype(jnp.bfloat16)
    base = jnp.dot(
        lower,
        jnp.broadcast_to(groups, (tick_blocks, 128)).astype(jnp.bfloat16),
        preferred_element_type=jnp.float32,
    )
    place = jnp.sum(jnp.where(member, base * GROUP + rank, 0.0), axis=0, keepdims=True)
    trash = float(group_total(owner_total, share, tick_blocks) * GROUP)
    place = jnp.where(ticks < 0.0, trash, place)
    inside = (base <= lane_f) & (lane_f < base + groups)
    group_tick = jnp.sum(jnp.where(inside, block_rows, 0.0), axis=0, keepdims=True)

    facts = jnp.where(lanes == 0, hot, 0.0)
    facts = jnp.where(lanes == 1, trips, facts)
    facts = jnp.where(lanes == 2, me, facts)
    facts = jnp.where(lanes == 3, start, facts)
    out_ref[...] = jnp.zeros_like(out_ref)
    out_ref[0:1, :] = place.astype(jnp.int32)
    out_ref[1:2, :] = facts.astype(jnp.int32)
    out_ref[2:3, :] = lines.astype(jnp.int32)
    out_ref[3:4, :] = group_tick.astype(jnp.int32)


def group_total(owner_total, share, tick_blocks):
    return (owner_total * share - tick_blocks) // GROUP + tick_blocks


def make_receive_plan(rows, packed, owner_total, share, wire_blocks, tick_blocks):
    return pl.pallas_call(
        functools.partial(receive_kernel, owner_total, share, wire_blocks, tick_blocks),
        out_shape=jax.ShapeDtypeStruct((8, 128), jnp.int32),
        in_specs=[vmem(), vmem()],
        out_specs=vmem(),
        compiler_params=pltpu.CompilerParams(vmem_limit_bytes=2 * MIB),
        name="receive_plan",
    )(rows, packed)


def agree(rounds):
    devices = lax.axis_size("tick")
    reach = 1
    while reach < devices:
        ring = [(i, (i + reach) % devices) for i in range(devices)]
        rounds = jnp.maximum(rounds, lax.ppermute(rounds, "tick", ring))
        reach *= 2
    return rounds


def band_kernel(taps_w, taps_ref, band_ref):
    row = lax.broadcasted_iota(jnp.int32, (TB, TB), 0)
    col = lax.broadcasted_iota(jnp.int32, (TB, TB), 1)
    pairs = (taps_w + 1) // 2
    band_ref[0, 0 : 3 * TB, TB : 2 * TB] = jnp.zeros((3 * TB, TB), jnp.bfloat16)
    band_ref[pairs - 1, 3 * TB : 6 * TB, 0:TB] = jnp.zeros((3 * TB, TB), jnp.bfloat16)
    taps = taps_ref[...].astype(jnp.float32)
    for tap in range(taps_w):
        spread = jnp.broadcast_to(taps[tap : tap + 1], (TB, 2 * TB))
        rolled = pltpu.roll(spread, TB, 1, stride=1, stride_axis=0)
        middle = rolled[:, :TB]
        outer = rolled[:, TB:]
        bands = (
            jnp.where(col < row, outer, 0.0).astype(jnp.bfloat16),
            middle.astype(jnp.bfloat16),
            jnp.where(col >= row, outer, 0.0).astype(jnp.bfloat16),
        )
        for first, second in ((0, 0), (1, 1), (1, 0), (0, 1)):
            if (tap - first + second) % 2:
                continue
            pair = (tap - first + second) // 2
            for piece in range(3):
                start = (first * 3 + piece) * TB
                band_ref[pair, start : start + TB, second * TB : (second + 1) * TB] = bands[piece]


def make_bands(taps):
    taps_w = taps.shape[0]
    return pl.pallas_call(
        functools.partial(band_kernel, taps_w),
        out_shape=jax.ShapeDtypeStruct(((taps_w + 1) // 2, 6 * TB, 2 * TB), jnp.bfloat16),
        in_specs=[vmem()],
        out_specs=vmem(),
        cost_estimate=pl.CostEstimate(flops=10**9, bytes_accessed=6 * MIB, transcendentals=0),
        compiler_params=pltpu.CompilerParams(vmem_limit_bytes=16 * MIB),
        name="bands",
    )(taps)


def spread_pair(wide_ref, lhs_view, line, pitch, blocks):
    for side in range(2):
        for piece in range(3):
            at = (side * 3 + piece) * TB
            lhs_view[:, at : at + TB] = wide_ref[
                pl.ds((line + side) * pitch + piece, blocks), :
            ].astype(jnp.bfloat16)


def write_lines(total, out_view, signal_ref, line, pairs, blocks):
    for pair in range(pairs):
        for side in range(2):
            out_view[pl.ds((2 * pair + side) * blocks, blocks), :] = total[
                pair * blocks : (pair + 1) * blocks, side * TB : (side + 1) * TB
            ]
    for block in range(blocks):
        signal_ref[line : line + 2 * pairs, block * TB : (block + 1) * TB] = out_view[
            pl.ds(block, 2 * pairs, stride=blocks), :
        ].astype(jnp.bfloat16)


def inner_kernel(
    chunks,
    raw_hbm,
    mask_ref,
    left_ref,
    right_ref,
    band_ref,
    inner_ref,
    raw_ref,
    wide_ref,
    lhs_ref,
    out_ref,
    raw_sem,
):
    wires, ticks = raw_ref.shape
    blocks = ticks // TB
    pitch = wide_ref.shape[0] // wires
    reach = band_ref.shape[0]
    groups = raw_sem.shape[0]
    span = wires // groups

    copies = [
        pltpu.make_async_copy(
            raw_hbm.at[pl.ds(group * span, span)],
            raw_ref.at[pl.ds(group * span, span)],
            raw_sem.at[group],
        )
        for group in range(groups)
    ]
    for copy in copies:
        copy.start()
    wide_ref[pl.ds(0, wires, stride=pitch), :] = left_ref[...].astype(jnp.float32)
    wide_ref[pl.ds(blocks + 1, wires, stride=pitch), :] = right_ref[...].astype(jnp.float32)

    def fill(group, block):
        lines = slice(group * span, (group + 1) * span)
        inner = raw_ref[lines, block * TB : (block + 1) * TB].astype(jnp.float32) * mask_ref[
            lines
        ].astype(jnp.float32)
        wide_ref[pl.ds(group * span * pitch + block + 1, span, stride=pitch), :] = inner

    margin = reach - 1
    begin = PAD // 2
    state = {"group": 0, "pair": begin}

    def prepare(upto):
        todo = []
        while state["pair"] < upto:
            line = 2 * state["pair"] - margin
            while state["group"] < groups and line + 1 >= state["group"] * span:
                group = state["group"]
                todo.append(lambda group=group: copies[group].wait())
                for block in range(blocks):
                    todo.append(lambda group=group, block=block: fill(group, block))
                state["group"] += 1
            todo.append(
                lambda line=line, pair=state["pair"]: spread_pair(
                    wide_ref, lhs_ref.at[pair - begin], line, pitch, blocks
                )
            )
            state["pair"] += 1
        return todo

    pair = begin
    for job in prepare(pair + chunks[0] + margin):
        job()
    for index, size in enumerate(chunks):
        todo = prepare(pair + size + chunks[index + 1] + margin) if index + 1 < len(chunks) else []
        each = -(-len(todo) // reach)
        total = jnp.zeros((size * blocks, 2 * TB), jnp.float32)
        for step in range(reach):
            rows = lhs_ref[pair - begin + step : pair - begin + step + size]
            total = total + jnp.dot(
                rows.reshape(size * blocks, 6 * TB), band_ref[step], preferred_element_type=jnp.float32
            )
            for job in todo[step * each : (step + 1) * each]:
                job()
        write_lines(total, out_ref.at[index % 2], inner_ref, 2 * (pair - begin), size, blocks)
        pair += size


def convolve_inner(raw, mask, left, right, bands):
    wires, ticks = raw.shape
    reach = bands.shape[0]
    blocks = ticks // TB
    pitch = -(-(blocks + 2) // 8) * 8
    pairs = (wires - 2 * PAD) // 2
    chunks = []
    while sum(chunks) < pairs:
        chunks.append(min(32 if chunks else 24, pairs - sum(chunks)))
    groups = 4
    flops = 2 * blocks * pairs * reach * 6 * TB * 2 * TB
    return pl.pallas_call(
        functools.partial(inner_kernel, tuple(chunks)),
        out_shape=jax.ShapeDtypeStruct((wires - 2 * PAD, ticks), jnp.bfloat16),
        in_specs=[pl.BlockSpec(memory_space=pl.ANY)] + [vmem()] * 4,
        out_specs=vmem(),
        scratch_shapes=[
            pltpu.VMEM((wires, ticks), jnp.bfloat16),
            pltpu.VMEM((wires * pitch, TB), jnp.float32),
            pltpu.VMEM((pairs + reach - 1, blocks, 6 * TB), jnp.bfloat16),
            pltpu.VMEM((2, 2 * max(chunks) * blocks, TB), jnp.float32),
            pltpu.SemaphoreType.DMA((groups,)),
        ],
        cost_estimate=pl.CostEstimate(flops=flops, bytes_accessed=6 * MIB, transcendentals=0),
        compiler_params=pltpu.CompilerParams(vmem_limit_bytes=28 * MIB),
        name="inner",
    )(raw, mask, left, right, bands)


def edge_kernel(
    plan_ref,
    inner_ref,
    raw_ref,
    mask_ref,
    left_ref,
    right_ref,
    top_ref,
    bottom_ref,
    band_ref,
    geo_ref,
    signal_ref,
    partial_ref,
    wide_ref,
    lhs_ref,
    out_ref,
):
    wires, ticks = signal_ref.shape
    blocks = ticks // TB
    reach = band_ref.shape[0]
    block_wires = geo_ref.shape[1]
    wire_blocks = wires // block_wires
    near = 2 * PAD
    lines = PAD + near
    pitch = wide_ref.shape[1] // lines
    pairs = PAD // 2
    margin = reach - 1

    signal_ref[PAD : wires - PAD] = inner_ref[...]

    for end in range(2):
        halo_ref = (top_ref, bottom_ref)[end]
        mine = (slice(0, near), slice(wires - near, wires))[end]
        halo_at = (0, near)[end]
        mine_at = (PAD, 0)[end]
        mask = mask_ref[mine].astype(jnp.float32)
        for block in range(blocks + 2):
            columns = slice(block * TB, (block + 1) * TB)
            if block == 0:
                inner = left_ref[mine].astype(jnp.float32)
            elif block == blocks + 1:
                inner = right_ref[mine].astype(jnp.float32)
            else:
                inner = raw_ref[mine, (block - 1) * TB : block * TB].astype(jnp.float32) * mask
            wide_ref[end, pl.ds(halo_at * pitch + block, PAD, stride=pitch), :] = halo_ref[
                :, columns
            ].astype(jnp.float32)
            wide_ref[end, pl.ds(mine_at * pitch + block, near, stride=pitch), :] = inner
        first = (PAD, near - PAD)[end] - margin
        for pair in range(pairs + margin):
            spread_pair(
                wide_ref.at[end], lhs_ref.at[end, pair], first + 2 * pair, pitch, blocks
            )

    total = jnp.zeros((2 * pairs * blocks, 2 * TB), jnp.float32)
    for step in range(reach):
        rows = jnp.concatenate(
            [
                lhs_ref[end, step : step + pairs].reshape(pairs * blocks, 6 * TB)
                for end in range(2)
            ],
            axis=0,
        )
        total = total + jnp.dot(rows, band_ref[step], preferred_element_type=jnp.float32)
    for end in range(2):
        write_lines(
            total[end * pairs * blocks : (end + 1) * pairs * blocks],
            out_ref.at[end],
            signal_ref,
            (0, wires - PAD)[end],
            pairs,
            blocks,
        )

    source = plan_ref[1, 2]
    rows = geo_ref[pl.ds(source * wire_blocks, wire_blocks)].reshape(wires, -1)
    for block in range(0, blocks, 2):
        chosen = []
        for side in range(2):
            at = slice((block + side) * TB, (block + side + 1) * TB)
            column = []
            for line in range(wire_blocks):
                tile = signal_ref[line * block_wires : (line + 1) * block_wires, at]
                asked = plan_ref[2, line * blocks + block + side] == 1
                column.append(jnp.where(asked, tile, jnp.zeros_like(tile)))
            chosen.append(jnp.concatenate(column, axis=0))
        sums = lax.dot_general(
            rows,
            jnp.concatenate(chosen, axis=1),
            (((0,), (0,)), ((), ())),
            preferred_element_type=jnp.float32,
        )
        partial_ref[:, block * TB : (block + 2) * TB] = sums


def convolve_edges(plan, inner, raw, mask, left, right, top, bottom, bands, geometry):
    wires, ticks = raw.shape
    reach = bands.shape[0]
    cells = geometry.shape[2]
    blocks = ticks // TB
    pitch = -(-(blocks + 2) // 8) * 8
    flops = 2 * blocks * PAD * reach * 6 * TB * 2 * TB
    return pl.pallas_call(
        edge_kernel,
        out_shape=(
            jax.ShapeDtypeStruct((wires, ticks), jnp.bfloat16),
            jax.ShapeDtypeStruct((cells, ticks), jnp.float32),
        ),
        in_specs=[smem()] + [vmem()] * 9,
        out_specs=(vmem(), vmem()),
        scratch_shapes=[
            pltpu.VMEM((2, 3 * PAD * pitch, TB), jnp.float32),
            pltpu.VMEM((2, PAD // 2 + reach - 1, blocks, 6 * TB), jnp.bfloat16),
            pltpu.VMEM((2, PAD * blocks, TB), jnp.float32),
        ],
        cost_estimate=pl.CostEstimate(flops=flops, bytes_accessed=6 * MIB, transcendentals=0),
        compiler_params=pltpu.CompilerParams(vmem_limit_bytes=24 * MIB),
        name="edges",
    )(plan, inner, raw, mask, left, right, top, bottom, bands, geometry)


def pack_kernel(share, plan_ref, own_ref, signal_ref, payload_ref, tiles_ref):
    owners, height, _ = payload_ref.shape
    block_wires = (height - TABLE) // share
    wires, ticks = signal_ref.shape
    blocks = ticks // TB
    tiles_ref[...] = jnp.zeros_like(tiles_ref)
    for line in range(wires // block_wires):
        for block in range(blocks):
            place = plan_ref[0, line * blocks + block]
            tiles_ref[place] = signal_ref[
                line * block_wires : (line + 1) * block_wires, block * TB : (block + 1) * TB
            ]
    own = own_ref[...]
    line = lax.broadcasted_iota(jnp.int32, (TABLE, 128), 0)
    table = jnp.where(line == 0, own >> 7, jnp.where(line == 1, own & 127, 0))
    table = table.astype(jnp.float32).astype(jnp.bfloat16)
    for owner in range(owners):
        payload_ref[owner, 0 : share * block_wires] = tiles_ref[
            owner * share : (owner + 1) * share
        ].reshape(share * block_wires, TB)
        payload_ref[owner, share * block_wires : height] = table


def pack_tiles(plan, own, signal, owner_total, share, block_wires):
    height = share * block_wires + TABLE
    return pl.pallas_call(
        functools.partial(pack_kernel, share),
        out_shape=jax.ShapeDtypeStruct((owner_total, height, TB), jnp.bfloat16),
        in_specs=[smem(), vmem(), vmem()],
        out_specs=vmem(),
        scratch_shapes=[pltpu.VMEM((owner_total * share + 1, block_wires, TB), jnp.bfloat16)],
        cost_estimate=pl.CostEstimate(flops=10**8, bytes_accessed=3 * MIB, transcendentals=0),
        compiler_params=pltpu.CompilerParams(vmem_limit_bytes=8 * MIB),
        name="pack",
    )(plan, own, signal)


def stage_kernel(slots, plan_ref, geo_ref, out_ref, rows_ref):
    groups = out_ref.shape[0]
    rows_ref[...] = jnp.zeros_like(rows_ref)
    for slot in range(slots):
        rows_ref[plan_ref[0, slot]] = geo_ref[plan_ref[2, slot]]
    for group in range(groups):
        rows = rows_ref[group * GROUP : (group + 1) * GROUP]
        out_ref[group] = jnp.transpose(rows.reshape(-1, rows.shape[-1]))


def stage_geometry(plan, geometry, groups, slots):
    _, block_wires, cells = geometry.shape
    return pl.pallas_call(
        functools.partial(stage_kernel, slots),
        out_shape=jax.ShapeDtypeStruct((groups, cells, GROUP * block_wires), jnp.bfloat16),
        in_specs=[smem(), vmem()],
        out_specs=vmem(),
        scratch_shapes=[pltpu.VMEM((groups * GROUP + 1, block_wires, cells), jnp.bfloat16)],
        cost_estimate=pl.CostEstimate(flops=10**8, bytes_accessed=3 * MIB, transcendentals=0),
        compiler_params=pltpu.CompilerParams(vmem_limit_bytes=12 * MIB),
        name="stage",
    )(plan, geometry)


def image_kernel(share, plan_ref, arrived_ref, staged_ref, busiest_ref, image_ref, tiles_ref, sum_ref):
    cells, ticks = image_ref.shape
    blocks = ticks // TB
    owner_total, height, _ = arrived_ref.shape
    block_wires = (height - TABLE) // share
    groups = staged_ref.shape[0]
    is_hot = plan_ref[1, 0] == plan_ref[1, 2]
    counts = plan_ref[1, 3] == 1

    @pl.when(is_hot)
    def _():
        image_ref[...] = busiest_ref[...]

    @pl.when(jnp.logical_not(is_hot))
    def _():
        sum_ref[...] = jnp.zeros_like(sum_ref)
        tiles_ref[...] = jnp.zeros_like(tiles_ref)

        @pl.when(counts)
        def _():
            for source in range(owner_total):
                for slot in range(share):
                    tiles_ref[plan_ref[0, source * share + slot]] = arrived_ref[
                        source, slot * block_wires : (slot + 1) * block_wires
                    ]
            for group in range(groups):
                tiles = tiles_ref[group * GROUP : (group + 1) * GROUP]
                sum_ref[plan_ref[3, group]] += jnp.dot(
                    staged_ref[group],
                    tiles.reshape(GROUP * block_wires, TB),
                    preferred_element_type=jnp.float32,
                )

        for block in range(blocks):
            image_ref[:, block * TB : (block + 1) * TB] = sum_ref[block]


def make_image(plan, arrived, staged, busiest, share):
    groups, cells, _ = staged.shape
    block_wires = (arrived.shape[1] - TABLE) // share
    ticks = busiest.shape[1]
    return pl.pallas_call(
        functools.partial(image_kernel, share),
        out_shape=jax.ShapeDtypeStruct((cells, ticks), jnp.float32),
        in_specs=[smem(), vmem(), vmem(), vmem()],
        out_specs=vmem(),
        scratch_shapes=[
            pltpu.VMEM((groups * GROUP + 1, block_wires, TB), jnp.bfloat16),
            pltpu.VMEM((ticks // TB, cells, TB), jnp.float32),
        ],
        cost_estimate=pl.CostEstimate(flops=10**8, bytes_accessed=3 * MIB, transcendentals=0),
        compiler_params=pltpu.CompilerParams(vmem_limit_bytes=16 * MIB),
        name="image",
    )(plan, arrived, staged, busiest)


def more_kernel(owner_total, share, plan_ref, table_ref, arrived_ref, geo_ref, before_ref, image_ref):
    cells, ticks = image_ref.shape
    blocks = ticks // TB
    wire_blocks = geo_ref.shape[0] // owner_total
    image_ref[...] = before_ref[...]

    @pl.when(plan_ref[1, 0] != plan_ref[1, 2])
    def _():
        def add(source, carry):
            for slot in range(share):
                block = table_ref[source, slot]
                at = pl.multiple_of((block % blocks) * TB, TB)
                image_ref[:, pl.ds(at, TB)] += lax.dot_general(
                    geo_ref[source * wire_blocks + block // blocks],
                    arrived_ref[source * share + slot],
                    (((0,), (0,)), ((), ())),
                    preferred_element_type=jnp.float32,
                )
            return carry

        lax.fori_loop(0, owner_total, add, 0)


def add_to_image(plan, table, arrived, geometry, owner_total, share, image):
    return pl.pallas_call(
        functools.partial(more_kernel, owner_total, share),
        out_shape=jax.ShapeDtypeStruct(image.shape, jnp.float32),
        in_specs=[smem(), smem()] + [vmem()] * 3,
        out_specs=vmem(),
        compiler_params=pltpu.CompilerParams(vmem_limit_bytes=16 * MIB),
        name="image_more",
    )(plan, table, arrived, geometry, image)


def further_round(trip, image, signal, geometry, rows, packed, plan, owner_total, share):
    trip, signal, rows, packed, plan = lax.optimization_barrier((trip, signal, rows, packed, plan))
    step = trip + plan[1, 3]
    hot = plan[1, 0]
    me = plan[1, 2]
    block_wires = geometry.shape[1]
    wire_count, tick_count = signal.shape
    blocks = tick_count // TB
    wire_blocks = wire_count // block_wires
    ids = jnp.arange(owner_total, dtype=jnp.int32)

    def ranks(owners):
        member = (owners[..., None] == ids).astype(jnp.int32)
        before = jnp.cumsum(member, axis=-2) - member
        return jnp.sum(before * member, axis=-1) - step * share

    def live(owners, rank):
        return (owners < owner_total) & (owners != hot) & (rank >= 0) & (rank < share)

    owners = packed[0] >> 7
    block = packed[0] & 127
    rank = ranks(owners)
    place = jnp.where(live(owners, rank), owners * share + rank, owner_total * share)
    tiles = signal.reshape(wire_blocks, block_wires, blocks, TB).transpose(0, 2, 1, 3)
    tiles = tiles.reshape(wire_blocks * blocks, block_wires, TB)[block]
    payload = jnp.zeros((owner_total * share, block_wires, TB), jnp.bfloat16)
    payload = payload.at[place].set(tiles, mode="drop")
    arrived = exchange(payload.reshape(owner_total, share, block_wires, TB))

    owners = rows >> 7
    rank = ranks(owners)
    source = jnp.arange(owner_total, dtype=jnp.int32)[:, None]
    line = jnp.where(live(owners, rank) & (owners == me), source, owner_total)
    table = jnp.zeros((owner_total, 128), jnp.int32)
    table = table.at[line, jnp.maximum(rank, 0)].set(rows & 127, mode="drop")
    return add_to_image(
        plan,
        table,
        arrived.reshape(owner_total * share, block_wires, TB),
        geometry,
        owner_total,
        share,
        image,
    )


def tick_halo(raw, mask, width):
    devices = lax.axis_size("tick")
    tick = lax.axis_index("tick")
    last = raw[:, -width:] * mask
    leading = raw[:, :width] * mask
    if devices == 2:
        got = lax.ppermute(jnp.where(tick == 0, last, leading), "tick", [(0, 1), (1, 0)])
        nothing = jnp.zeros_like(got)
        return jnp.where(tick == 0, nothing, got), jnp.where(tick == 0, got, nothing)
    up = [(i, i + 1) for i in range(devices - 1)]
    down = [(i + 1, i) for i in range(devices - 1)]
    return lax.ppermute(last, "tick", up), lax.ppermute(leading, "tick", down)


def wire_halo(raw, mask, left, right):
    devices = lax.axis_size("wire")
    up = [(i, i + 1) for i in range(devices - 1)]
    down = [(i + 1, i) for i in range(devices - 1)]

    def edge(where):
        return jnp.concatenate([left[where], raw[where] * mask[where], right[where]], axis=1)

    top = lax.ppermute(edge(slice(-PAD, None)), "wire", up)
    bottom = lax.ppermute(edge(slice(0, PAD)), "wire", down)
    return top, bottom


def exchange(array):
    return lax.all_to_all(array, ("plane", "wire"), split_axis=0, concat_axis=0, tiled=True)


def shards(raw, chan_mask, kernel, geometry, roi_block, roi_owner):
    wires, ticks = raw.shape
    slot_count = roi_block.shape[0]
    block_wires = geometry.shape[1]
    cells = geometry.shape[2]
    tick_blocks = ticks // TB
    owner_total = lax.axis_size("plane") * lax.axis_size("wire")
    share = -(-(slot_count - CAP) // (owner_total - 1))
    me = lax.axis_index("plane") * lax.axis_size("wire") + lax.axis_index("wire")

    packed = jnp.pad(
        roi_owner * 128 + roi_block, (0, 128 - slot_count), constant_values=owner_total * 128
    )
    packed = jnp.where(jnp.arange(128) == 127, owner_total * 128 + me, packed)[None]

    mask = chan_mask[:, None].astype(jnp.bfloat16)
    left, right = tick_halo(raw, mask, TB)
    top, bottom = wire_halo(raw, mask, left, right)
    bands = make_bands(kernel[0])
    inner = convolve_inner(raw, mask, left, right, bands)
    send_plan = make_send_plan(packed, owner_total, share)
    signal, partial = convolve_edges(
        send_plan, inner, raw, mask, left, right, top, bottom, bands, geometry
    )

    busiest = lax.psum(partial, ("plane", "wire"))
    payload = pack_tiles(send_plan, packed, signal, owner_total, share, block_wires)
    arrived = exchange(payload)

    at = share * block_wires
    rows = arrived[:, at].astype(jnp.int32) * 128 + arrived[:, at + 1].astype(jnp.int32)
    plan = make_receive_plan(
        rows, packed, owner_total, share, wires // block_wires, tick_blocks
    )
    staged = stage_geometry(
        plan, geometry, group_total(owner_total, share, tick_blocks), owner_total * share
    )
    image = make_image(plan, arrived, staged, busiest, share)

    trips = agree(plan[1:2, 1:2])[0, 0]
    image = lax.fori_loop(
        0,
        trips,
        lambda trip, now: further_round(
            trip, now, signal, geometry, rows, packed, plan, owner_total, share
        ),
        image,
    )
    return signal, image


def solution(mesh):
    in_specs = (
        P(("plane", "wire"), "tick"),
        P(("plane", "wire")),
        P("plane", None, None),
        P(),
        P(("plane", "wire", "tick")),
        P(("plane", "wire", "tick")),
    )
    out_specs = (P(("plane", "wire"), "tick"), P(("plane", "wire"), "tick"))
    return jax.shard_map(shards, mesh=mesh, in_specs=in_specs, out_specs=out_specs, check_vma=False)
```

```python
import functools

import jax
import jax.numpy as jnp
from jax import lax
from jax.experimental import pallas as pl
from jax.experimental.pallas import tpu as pltpu
from jax.sharding import PartitionSpec as P

TB = 128
CAP = 25
PAD = 16
TABLE = 8
MIB = 1024 * 1024


def vmem():
    return pl.BlockSpec(memory_space=pltpu.VMEM)


def smem():
    return pl.BlockSpec(memory_space=pltpu.SMEM)


GROUP = 8


def home(position, planes, owner_total):
    return (position % planes) * (owner_total // planes) + position // planes


def lane_numbers():
    return lax.broadcasted_iota(jnp.int32, (1, 128), 1)


def earlier_lanes():
    return (
        lax.broadcasted_iota(jnp.int32, (128, 128), 0)
        < lax.broadcasted_iota(jnp.int32, (128, 128), 1)
    ).astype(jnp.bfloat16)


def count_before(member, before):
    return jnp.dot(
        member.astype(jnp.float32).astype(jnp.bfloat16), before, preferred_element_type=jnp.float32
    )


def most_named(owners, owner_total):
    lanes = lane_numbers()
    counts = jnp.full(owners.shape, -1.0, jnp.float32)
    for owner in range(owner_total):
        named = jnp.sum((owners == owner).astype(jnp.float32), axis=1, keepdims=True)
        counts = jnp.where(lanes == owner, named, counts)
    top = jnp.max(counts, axis=1, keepdims=True)
    chosen = jnp.min(
        jnp.where(counts == top, lanes.astype(jnp.float32), 127.0), axis=1, keepdims=True
    )
    return counts, chosen


def prepare_kernel(
    planes,
    owner_total,
    share,
    tick_total,
    raw_hbm,
    mask_hbm,
    owner_hbm,
    block_hbm,
    mask_out,
    first_ref,
    last_ref,
    own_ref,
    out_ref,
    *rest,
):
    wires, ticks = raw_hbm.shape
    count = 1 if tick_total == 2 else 2
    sides = rest[:count]
    side_refs = rest[count : 2 * count]
    first_buf, last_buf, mask_ref, owner_ref, block_ref, sems = rest[2 * count :]
    tick = lax.axis_index("tick")
    me = lax.axis_index("wire") * planes + lax.axis_index("plane")
    if tick_total == 2:
        starts = [pl.multiple_of((1 - tick) * (ticks - TB), TB)]
    else:
        starts = [0, ticks - TB]
    moves = [(mask_hbm, mask_ref), (owner_hbm, owner_ref), (block_hbm, block_ref)]
    moves += [(raw_hbm.at[:, pl.ds(start, TB)], ref) for start, ref in zip(starts, side_refs)]
    moves += [(raw_hbm.at[pl.ds(0, PAD)], first_buf), (raw_hbm.at[pl.ds(wires - PAD, PAD)], last_buf)]
    copies = [
        pltpu.make_async_copy(source, target, sems.at[index])
        for index, (source, target) in enumerate(moves)
    ]
    for copy in copies:
        copy.start()
    for copy in copies[:3]:
        copy.wait()

    for part in range(wires // 128):
        row = mask_ref[part : part + 1].astype(jnp.float32)
        wide = jnp.transpose(jnp.broadcast_to(row, (128, 128)))
        mask_out[part * 128 : (part + 1) * 128] = wide.astype(jnp.bfloat16)

    lanes = lane_numbers()
    slot_count = owner_ref.shape[1]
    owner = owner_ref[...]
    wire_shards = owner_total // planes
    none = owner_total * 128
    own_ref[...] = jnp.where(lanes == 127, none + me, none)
    own_ref[:, 0:slot_count] = (
        (owner % wire_shards) * planes + owner // wire_shards
    ) * 128 + block_ref[...]
    own = own_ref[...]
    _, hot = most_named(own >> 7, owner_total)
    rows = lax.broadcasted_iota(jnp.int32, (owner_total, 128), 0)
    member = (own >> 7) == rows
    rank = count_before(member, earlier_lanes())
    place = jnp.where(rank < share, rows.astype(jnp.float32) * share + rank, -1.0)
    place = jnp.where(rows.astype(jnp.float32) == hot, -2.0, place)
    place = jnp.sum(jnp.where(member, place + 3.0, 0.0), axis=0, keepdims=True)

    column = jnp.transpose(jnp.broadcast_to(own.astype(jnp.float32), (128, 128)))
    column = column.astype(jnp.int32)
    here = ((column & 127) == lanes) & ((column >> 7) < owner_total)
    spread = jnp.transpose(jnp.broadcast_to(place, (128, 128)))
    placed = jnp.sum(jnp.where(here, spread, 0.0), axis=0, keepdims=True)
    trash = float(owner_total * share)
    facts = jnp.where(lanes == 2, me, 0)
    out_ref[...] = jnp.zeros_like(out_ref)
    out_ref[0:1, :] = jnp.where(placed >= 3.0, placed - 3.0, trash).astype(jnp.int32)
    out_ref[1:2, :] = jnp.where(lanes == 0, hot.astype(jnp.int32), facts)
    out_ref[2:3, :] = (placed == 1.0).astype(jnp.int32)

    for copy in copies[3:]:
        copy.wait()
    for side, ref in zip(sides, side_refs):
        side[...] = ref[...] * mask_out[...]
    for block in range(ticks // TB):
        at = slice(block * TB, (block + 1) * TB)
        first_ref[:, at] = first_buf[:, at] * mask_out[0:PAD]
        last_ref[:, at] = last_buf[:, at] * mask_out[wires - PAD : wires]


def prepare(raw, chan_mask, roi_owner, roi_block, planes, owner_total, share):
    wires, ticks = raw.shape
    tick_total = lax.axis_size("tick")
    sides = 1 if tick_total == 2 else 2
    side = jax.ShapeDtypeStruct((wires, TB), jnp.bfloat16)
    edge = jax.ShapeDtypeStruct((PAD, ticks), jnp.bfloat16)
    row = jax.ShapeDtypeStruct((1, 128), jnp.int32)
    table = jax.ShapeDtypeStruct((8, 128), jnp.int32)
    slot_count = roi_owner.shape[0]
    return pl.pallas_call(
        functools.partial(prepare_kernel, planes, owner_total, share, tick_total),
        out_shape=(side, edge, edge, row, table) + (side,) * sides,
        in_specs=[pl.BlockSpec(memory_space=pltpu.HBM)] * 4,
        out_specs=(vmem(),) * (5 + sides),
        scratch_shapes=[pltpu.VMEM((wires, TB), jnp.bfloat16)] * sides
        + [pltpu.VMEM((PAD, ticks), jnp.bfloat16)] * 2
        + [pltpu.VMEM((wires // 128, 128), jnp.int32)]
        + [pltpu.VMEM((1, slot_count), jnp.int32)] * 2
        + [pltpu.SemaphoreType.DMA((sides + 5,))],
        compiler_params=pltpu.CompilerParams(vmem_limit_bytes=60 * MIB),
        name="prepare",
    )(raw, chan_mask.reshape(wires // 128, 128), roi_owner[None], roi_block[None])


def receive_kernel(owner_total, planes, share, wire_blocks, tick_blocks, rows_ref, own_ref, out_ref):
    lanes = lane_numbers()
    lane_f = lanes.astype(jnp.float32)
    every = rows_ref[...]
    owners = every >> 7
    own = own_ref[...]
    me = jnp.sum(jnp.where(lanes == 127, own & 127, 0).astype(jnp.float32), axis=1, keepdims=True)

    counts, chosen = most_named(owners, owner_total)
    hot = jnp.max(chosen, axis=0, keepdims=True)
    agreed = hot == jnp.min(chosen, axis=0, keepdims=True)
    left = jnp.where(agreed & (lane_f == hot), 0.0, counts)
    fullest = jnp.max(jnp.max(left, axis=1, keepdims=True), axis=0, keepdims=True)
    start = agreed.astype(jnp.float32)
    trips = -start
    for step in range(-(-CAP // share)):
        trips = trips + (fullest > step * share).astype(jnp.float32)
    trips = jnp.maximum(trips, 0.0)
    hot = jnp.where(agreed, hot, -1.0)

    to_me = owners.astype(jnp.float32) == me
    before = earlier_lanes()
    rank = count_before(to_me, before)
    blocks = every & 127
    source = lax.broadcasted_iota(jnp.int32, (owner_total, 128), 0)
    line = home(source, planes, owner_total) * wire_blocks + blocks // tick_blocks
    line = line.astype(jnp.float32)
    tick = (blocks % tick_blocks).astype(jnp.float32)
    lines = jnp.zeros((1, 128), jnp.float32)
    ticks = jnp.full((1, 128), -1.0, jnp.float32)
    for slot in range(share):
        got = to_me & (rank == slot)
        here = lanes == source * share + slot
        for value, where in ((line, 0), (tick + 1.0, 1)):
            one = jnp.sum(jnp.where(got, value, 0.0), axis=1, keepdims=True)
            one = jnp.sum(jnp.where(here, one, 0.0), axis=0, keepdims=True)
            if where == 0:
                lines = lines + one
            else:
                ticks = ticks + one

    block_rows = lax.broadcasted_iota(jnp.int32, (tick_blocks, 128), 0).astype(jnp.float32)
    member = block_rows == ticks
    rank = count_before(member, before)
    total = jnp.sum(member.astype(jnp.float32), axis=1, keepdims=True)
    groups = jnp.zeros_like(total)
    for step in range(0, owner_total * share, GROUP):
        groups = groups + (total > step).astype(jnp.float32)
    lower = (
        lax.broadcasted_iota(jnp.int32, (tick_blocks, tick_blocks), 0)
        > lax.broadcasted_iota(jnp.int32, (tick_blocks, tick_blocks), 1)
    ).astype(jnp.bfloat16)
    base = jnp.dot(
        lower,
        jnp.broadcast_to(groups, (tick_blocks, 128)).astype(jnp.bfloat16),
        preferred_element_type=jnp.float32,
    )
    place = jnp.sum(jnp.where(member, base * GROUP + rank, 0.0), axis=0, keepdims=True)
    trash = float(group_total(owner_total, share, tick_blocks) * GROUP)
    place = jnp.where(ticks < 0.0, trash, place)
    inside = (base <= lane_f) & (lane_f < base + groups)
    group_tick = jnp.sum(jnp.where(inside, block_rows, 0.0), axis=0, keepdims=True)

    facts = jnp.where(lanes == 0, hot, 0.0)
    facts = jnp.where(lanes == 1, trips, facts)
    facts = jnp.where(lanes == 2, me, facts)
    facts = jnp.where(lanes == 3, start, facts)
    out_ref[...] = jnp.zeros_like(out_ref)
    out_ref[0:1, :] = place.astype(jnp.int32)
    out_ref[1:2, :] = facts.astype(jnp.int32)
    out_ref[2:3, :] = lines.astype(jnp.int32)
    out_ref[3:4, :] = group_tick.astype(jnp.int32)


def group_total(owner_total, share, tick_blocks):
    return (owner_total * share - tick_blocks) // GROUP + tick_blocks


def make_receive_plan(rows, packed, owner_total, planes, share, wire_blocks, tick_blocks):
    return pl.pallas_call(
        functools.partial(receive_kernel, owner_total, planes, share, wire_blocks, tick_blocks),
        out_shape=jax.ShapeDtypeStruct((8, 128), jnp.int32),
        in_specs=[vmem(), vmem()],
        out_specs=vmem(),
        compiler_params=pltpu.CompilerParams(vmem_limit_bytes=2 * MIB),
        name="receive_plan",
    )(rows, packed)


def agree(rounds):
    devices = lax.axis_size("tick")
    reach = 1
    while reach < devices:
        ring = [(i, (i + reach) % devices) for i in range(devices)]
        rounds = jnp.maximum(rounds, lax.ppermute(rounds, "tick", ring))
        reach *= 2
    return rounds


def band_kernel(taps_w, taps_ref, band_ref):
    row = lax.broadcasted_iota(jnp.int32, (TB, TB), 0)
    col = lax.broadcasted_iota(jnp.int32, (TB, TB), 1)
    pairs = (taps_w + 1) // 2
    band_ref[0, 0 : 3 * TB, TB : 2 * TB] = jnp.zeros((3 * TB, TB), jnp.bfloat16)
    band_ref[pairs - 1, 3 * TB : 6 * TB, 0:TB] = jnp.zeros((3 * TB, TB), jnp.bfloat16)
    taps = taps_ref[...].astype(jnp.float32)
    for tap in range(taps_w):
        spread = jnp.broadcast_to(taps[tap : tap + 1], (TB, 2 * TB))
        rolled = pltpu.roll(spread, TB, 1, stride=1, stride_axis=0)
        middle = rolled[:, :TB]
        outer = rolled[:, TB:]
        bands = (
            jnp.where(col < row, outer, 0.0).astype(jnp.bfloat16),
            middle.astype(jnp.bfloat16),
            jnp.where(col >= row, outer, 0.0).astype(jnp.bfloat16),
        )
        for first, second in ((0, 0), (1, 1), (1, 0), (0, 1)):
            if (tap - first + second) % 2:
                continue
            pair = (tap - first + second) // 2
            for piece in range(3):
                start = (first * 3 + piece) * TB
                band_ref[pair, start : start + TB, second * TB : (second + 1) * TB] = bands[piece]


def make_bands(taps):
    taps_w = taps.shape[0]
    return pl.pallas_call(
        functools.partial(band_kernel, taps_w),
        out_shape=jax.ShapeDtypeStruct(((taps_w + 1) // 2, 6 * TB, 2 * TB), jnp.bfloat16),
        in_specs=[vmem()],
        out_specs=vmem(),
        cost_estimate=pl.CostEstimate(flops=10**9, bytes_accessed=6 * MIB, transcendentals=0),
        compiler_params=pltpu.CompilerParams(vmem_limit_bytes=16 * MIB),
        name="bands",
    )(taps)


def spread_pair(wide_ref, lhs_view, line, pitch, blocks):
    for side in range(2):
        for piece in range(3):
            at = (side * 3 + piece) * TB
            lhs_view[:, at : at + TB] = wide_ref[
                pl.ds((line + side) * pitch + piece, blocks), :
            ].astype(jnp.bfloat16)


def write_lines(total, out_view, signal_ref, line, pairs, blocks):
    for pair in range(pairs):
        for side in range(2):
            out_view[pl.ds((2 * pair + side) * blocks, blocks), :] = total[
                pair * blocks : (pair + 1) * blocks, side * TB : (side + 1) * TB
            ]
    for block in range(blocks):
        signal_ref[line : line + 2 * pairs, block * TB : (block + 1) * TB] = out_view[
            pl.ds(block, 2 * pairs, stride=blocks), :
        ].astype(jnp.bfloat16)


def inner_kernel(
    chunks,
    raw_ref,
    mask_ref,
    left_ref,
    right_ref,
    band_ref,
    inner_ref,
    wide_ref,
    lhs_ref,
    out_ref,
):
    wires, ticks = raw_ref.shape
    blocks = ticks // TB
    pitch = wide_ref.shape[0] // wires
    reach = band_ref.shape[0]
    span = 2 * PAD
    groups = wires // span

    def fill(group, block):
        lines = slice(group * span, (group + 1) * span)
        if block == 0:
            inner = left_ref[lines]
        elif block == blocks + 1:
            inner = right_ref[lines]
        else:
            inner = raw_ref[lines, (block - 1) * TB : block * TB] * mask_ref[lines]
        wide_ref[pl.ds(group * span * pitch + block, span, stride=pitch), :] = inner.astype(
            jnp.float32
        )

    margin = reach - 1
    begin = PAD // 2
    state = {"group": 0, "pair": begin}

    def prepare(upto):
        todo = []
        while state["pair"] < upto:
            line = 2 * state["pair"] - margin
            while state["group"] < groups and line + 1 >= state["group"] * span:
                group = state["group"]
                for block in range(blocks + 2):
                    todo.append(lambda group=group, block=block: fill(group, block))
                state["group"] += 1
            todo.append(
                lambda line=line, pair=state["pair"]: spread_pair(
                    wide_ref, lhs_ref.at[pair - begin], line, pitch, blocks
                )
            )
            state["pair"] += 1
        return todo

    pair = begin
    for job in prepare(pair + chunks[0] + margin):
        job()
    for index, size in enumerate(chunks):
        todo = prepare(pair + size + chunks[index + 1] + margin) if index + 1 < len(chunks) else []
        each = -(-len(todo) // reach)
        total = jnp.zeros((size * blocks, 2 * TB), jnp.float32)
        for step in range(reach):
            rows = lhs_ref[pair - begin + step : pair - begin + step + size]
            total = total + jnp.dot(
                rows.reshape(size * blocks, 6 * TB), band_ref[step], preferred_element_type=jnp.float32
            )
            for job in todo[step * each : (step + 1) * each]:
                job()
        write_lines(total, out_ref.at[index % 2], inner_ref, 2 * (pair - begin), size, blocks)
        pair += size


def convolve_inner(raw, mask, left, right, bands):
    wires, ticks = raw.shape
    reach = bands.shape[0]
    blocks = ticks // TB
    pitch = -(-(blocks + 2) // 8) * 8
    pairs = (wires - 2 * PAD) // 2
    chunks = []
    while sum(chunks) < pairs:
        chunks.append(min(32 if chunks else 16, pairs - sum(chunks)))
    flops = 2 * blocks * pairs * reach * 6 * TB * 2 * TB
    return pl.pallas_call(
        functools.partial(inner_kernel, tuple(chunks)),
        out_shape=jax.ShapeDtypeStruct((wires - 2 * PAD, ticks), jnp.bfloat16),
        in_specs=[vmem()] * 5,
        out_specs=vmem(),
        scratch_shapes=[
            pltpu.VMEM((wires * pitch, TB), jnp.float32),
            pltpu.VMEM((pairs + reach - 1, blocks, 6 * TB), jnp.bfloat16),
            pltpu.VMEM((2, 2 * max(chunks) * blocks, TB), jnp.float32),
        ],
        cost_estimate=pl.CostEstimate(flops=flops, bytes_accessed=6 * MIB, transcendentals=0),
        compiler_params=pltpu.CompilerParams(vmem_limit_bytes=28 * MIB),
        name="inner",
    )(raw, mask, left, right, bands)


def edge_kernel(
    planes,
    plan_ref,
    own_ref,
    inner_ref,
    raw_ref,
    mask_ref,
    left_ref,
    right_ref,
    top_ref,
    bottom_ref,
    band_ref,
    geo_ref,
    signal_ref,
    partial_ref,
    wide_ref,
    lhs_ref,
    out_ref,
):
    wires, ticks = signal_ref.shape
    blocks = ticks // TB
    reach = band_ref.shape[0]
    block_wires = geo_ref.shape[1]
    wire_blocks = wires // block_wires
    near = 2 * PAD
    lines = PAD + near
    pitch = wide_ref.shape[1] // lines
    pairs = PAD // 2
    margin = reach - 1

    signal_ref[PAD : wires - PAD] = inner_ref[...]

    for end in range(2):
        halo_ref = (top_ref, bottom_ref)[end]
        mine = (slice(0, near), slice(wires - near, wires))[end]
        halo_at = (0, near)[end]
        mine_at = (PAD, 0)[end]
        for block in range(blocks + 2):
            columns = slice(block * TB, (block + 1) * TB)
            if block == 0:
                inner = left_ref[mine].astype(jnp.float32)
            elif block == blocks + 1:
                inner = right_ref[mine].astype(jnp.float32)
            else:
                inner = raw_ref[mine, (block - 1) * TB : block * TB] * mask_ref[mine]
                inner = inner.astype(jnp.float32)
            wide_ref[end, pl.ds(halo_at * pitch + block, PAD, stride=pitch), :] = halo_ref[
                :, columns
            ].astype(jnp.float32)
            wide_ref[end, pl.ds(mine_at * pitch + block, near, stride=pitch), :] = inner
        first = (PAD, near - PAD)[end] - margin
        for pair in range(pairs + margin):
            spread_pair(
                wide_ref.at[end], lhs_ref.at[end, pair], first + 2 * pair, pitch, blocks
            )

    total = jnp.zeros((2 * pairs * blocks, 2 * TB), jnp.float32)
    for step in range(reach):
        rows = jnp.concatenate(
            [
                lhs_ref[end, step : step + pairs].reshape(pairs * blocks, 6 * TB)
                for end in range(2)
            ],
            axis=0,
        )
        total = total + jnp.dot(rows, band_ref[step], preferred_element_type=jnp.float32)
    for end in range(2):
        write_lines(
            total[end * pairs * blocks : (end + 1) * pairs * blocks],
            out_ref.at[end],
            signal_ref,
            (0, wires - PAD)[end],
            pairs,
            blocks,
        )

    cells = geo_ref.shape[2]
    own = own_ref[...]
    line = lax.broadcasted_iota(jnp.int32, (TABLE, 128), 0)
    table = jnp.where(line == 0, own >> 7, jnp.where(line == 1, own & 127, 0))
    table = table.astype(jnp.float32).astype(jnp.bfloat16)
    for block in range(blocks):
        partial_ref[block, cells : cells + TABLE] = table

    source = home(plan_ref[1, 2], planes, geo_ref.shape[0] // wire_blocks)
    rows = geo_ref[pl.ds(source * wire_blocks, wire_blocks)].reshape(wires, -1)
    for block in range(0, blocks, 2):
        chosen = []
        for side in range(2):
            at = slice((block + side) * TB, (block + side + 1) * TB)
            column = []
            for line in range(wire_blocks):
                tile = signal_ref[line * block_wires : (line + 1) * block_wires, at]
                asked = plan_ref[2, line * blocks + block + side] == 1
                column.append(jnp.where(asked, tile, jnp.zeros_like(tile)))
            chosen.append(jnp.concatenate(column, axis=0))
        sums = lax.dot_general(
            rows,
            jnp.concatenate(chosen, axis=1),
            (((0,), (0,)), ((), ())),
            preferred_element_type=jnp.float32,
        ).astype(jnp.bfloat16)
        partial_ref[block, 0:cells] = sums[:, :TB]
        partial_ref[block + 1, 0:cells] = sums[:, TB:]


def convolve_edges(
    planes, plan, own, inner, raw, mask, left, right, top, bottom, bands, geometry
):
    wires, ticks = raw.shape
    reach = bands.shape[0]
    cells = geometry.shape[2]
    blocks = ticks // TB
    pitch = -(-(blocks + 2) // 8) * 8
    flops = 2 * blocks * PAD * reach * 6 * TB * 2 * TB
    return pl.pallas_call(
        functools.partial(edge_kernel, planes),
        out_shape=(
            jax.ShapeDtypeStruct((wires, ticks), jnp.bfloat16),
            jax.ShapeDtypeStruct((blocks, cells + TABLE, TB), jnp.bfloat16),
        ),
        in_specs=[smem()] + [vmem()] * 10,
        out_specs=(vmem(), vmem()),
        scratch_shapes=[
            pltpu.VMEM((2, 3 * PAD * pitch, TB), jnp.float32),
            pltpu.VMEM((2, PAD // 2 + reach - 1, blocks, 6 * TB), jnp.bfloat16),
            pltpu.VMEM((2, PAD * blocks, TB), jnp.float32),
        ],
        cost_estimate=pl.CostEstimate(flops=flops, bytes_accessed=6 * MIB, transcendentals=0),
        compiler_params=pltpu.CompilerParams(vmem_limit_bytes=24 * MIB),
        name="edges",
    )(plan, own, inner, raw, mask, left, right, top, bottom, bands, geometry)


def pack_kernel(slots, plan_ref, signal_ref, payload_ref, tiles_ref):
    block_wires = payload_ref.shape[1]
    wires, ticks = signal_ref.shape
    blocks = ticks // TB
    tiles_ref[...] = jnp.zeros_like(tiles_ref)
    for line in range(wires // block_wires):
        for block in range(blocks):
            place = plan_ref[0, line * blocks + block]
            tiles_ref[place] = signal_ref[
                line * block_wires : (line + 1) * block_wires, block * TB : (block + 1) * TB
            ]
    payload_ref[...] = tiles_ref[0:slots]


def pack_tiles(plan, signal, slots, block_wires):
    return pl.pallas_call(
        functools.partial(pack_kernel, slots),
        out_shape=jax.ShapeDtypeStruct((slots, block_wires, TB), jnp.bfloat16),
        in_specs=[smem(), vmem()],
        out_specs=vmem(),
        scratch_shapes=[pltpu.VMEM((slots + 1, block_wires, TB), jnp.bfloat16)],
        cost_estimate=pl.CostEstimate(flops=10**8, bytes_accessed=3 * MIB, transcendentals=0),
        compiler_params=pltpu.CompilerParams(vmem_limit_bytes=8 * MIB),
        name="pack",
    )(plan, signal)


def stage_kernel(slots, plan_ref, geo_ref, out_ref, rows_ref):
    groups = out_ref.shape[0]
    rows_ref[...] = jnp.zeros_like(rows_ref)
    for slot in range(slots):
        rows_ref[plan_ref[0, slot]] = geo_ref[plan_ref[2, slot]]
    for group in range(groups):
        rows = rows_ref[group * GROUP : (group + 1) * GROUP]
        out_ref[group] = jnp.transpose(rows.reshape(-1, rows.shape[-1]))


def stage_geometry(plan, geometry, groups, slots):
    _, block_wires, cells = geometry.shape
    return pl.pallas_call(
        functools.partial(stage_kernel, slots),
        out_shape=jax.ShapeDtypeStruct((groups, cells, GROUP * block_wires), jnp.bfloat16),
        in_specs=[smem(), vmem()],
        out_specs=vmem(),
        scratch_shapes=[pltpu.VMEM((groups * GROUP + 1, block_wires, cells), jnp.bfloat16)],
        cost_estimate=pl.CostEstimate(flops=10**8, bytes_accessed=3 * MIB, transcendentals=0),
        compiler_params=pltpu.CompilerParams(vmem_limit_bytes=12 * MIB),
        name="stage",
    )(plan, geometry)


def image_kernel(owner_total, share, plan_ref, arrived_ref, staged_ref, image_ref, tiles_ref, sum_ref):
    cells, ticks = image_ref.shape
    blocks = ticks // TB
    block_wires = arrived_ref.shape[1]
    groups = staged_ref.shape[0]
    is_hot = plan_ref[1, 0] == plan_ref[1, 2]
    counts = plan_ref[1, 3] == 1

    @pl.when(is_hot)
    def _():
        for source in range(owner_total):
            sums = arrived_ref[source * share : source * share + cells // block_wires]
            image_ref[:, source * TB : (source + 1) * TB] = sums.reshape(cells, TB).astype(
                jnp.float32
            )

    @pl.when(jnp.logical_not(is_hot))
    def _():
        sum_ref[...] = jnp.zeros_like(sum_ref)
        tiles_ref[...] = jnp.zeros_like(tiles_ref)

        @pl.when(counts)
        def _():
            for slot in range(owner_total * share):
                tiles_ref[plan_ref[0, slot]] = arrived_ref[slot]
            for group in range(groups):
                tiles = tiles_ref[group * GROUP : (group + 1) * GROUP]
                sum_ref[plan_ref[3, group]] += jnp.dot(
                    staged_ref[group],
                    tiles.reshape(GROUP * block_wires, TB),
                    preferred_element_type=jnp.float32,
                )

        for block in range(blocks):
            image_ref[:, block * TB : (block + 1) * TB] = sum_ref[block]


def make_image(plan, arrived, staged, owner_total, share, ticks):
    groups, cells, _ = staged.shape
    block_wires = arrived.shape[1]
    return pl.pallas_call(
        functools.partial(image_kernel, owner_total, share),
        out_shape=jax.ShapeDtypeStruct((cells, ticks), jnp.float32),
        in_specs=[smem(), vmem(), vmem()],
        out_specs=vmem(),
        scratch_shapes=[
            pltpu.VMEM((groups * GROUP + 1, block_wires, TB), jnp.bfloat16),
            pltpu.VMEM((ticks // TB, cells, TB), jnp.float32),
        ],
        cost_estimate=pl.CostEstimate(flops=10**8, bytes_accessed=3 * MIB, transcendentals=0),
        compiler_params=pltpu.CompilerParams(vmem_limit_bytes=16 * MIB),
        name="image",
    )(plan, arrived, staged)


def more_kernel(owner_total, planes, share, plan_ref, table_ref, arrived_ref, geo_ref, before_ref, image_ref):
    cells, ticks = image_ref.shape
    blocks = ticks // TB
    wire_blocks = geo_ref.shape[0] // owner_total
    image_ref[...] = before_ref[...]

    @pl.when(plan_ref[1, 0] != plan_ref[1, 2])
    def _():
        def add(source, carry):
            for slot in range(share):
                block = table_ref[source, slot]
                at = pl.multiple_of((block % blocks) * TB, TB)
                image_ref[:, pl.ds(at, TB)] += lax.dot_general(
                    geo_ref[home(source, planes, owner_total) * wire_blocks + block // blocks],
                    arrived_ref[source * share + slot],
                    (((0,), (0,)), ((), ())),
                    preferred_element_type=jnp.float32,
                )
            return carry

        lax.fori_loop(0, owner_total, add, 0)


def add_to_image(plan, table, arrived, geometry, owner_total, planes, share, image):
    return pl.pallas_call(
        functools.partial(more_kernel, owner_total, planes, share),
        out_shape=jax.ShapeDtypeStruct(image.shape, jnp.float32),
        in_specs=[smem(), smem()] + [vmem()] * 3,
        out_specs=vmem(),
        compiler_params=pltpu.CompilerParams(vmem_limit_bytes=16 * MIB),
        name="image_more",
    )(plan, table, arrived, geometry, image)


def further_round(
    trip, image, signal, geometry, rows, packed, plan, owner_total, planes, share
):
    trip, signal, rows, packed, plan = lax.optimization_barrier((trip, signal, rows, packed, plan))
    step = trip + plan[1, 3]
    hot = plan[1, 0]
    me = plan[1, 2]
    block_wires = geometry.shape[1]
    wire_count, tick_count = signal.shape
    blocks = tick_count // TB
    wire_blocks = wire_count // block_wires
    ids = jnp.arange(owner_total, dtype=jnp.int32)

    def ranks(owners):
        member = (owners[..., None] == ids).astype(jnp.int32)
        before = jnp.cumsum(member, axis=-2) - member
        return jnp.sum(before * member, axis=-1) - step * share

    def live(owners, rank):
        return (owners < owner_total) & (owners != hot) & (rank >= 0) & (rank < share)

    owners = packed[0] >> 7
    block = packed[0] & 127
    rank = ranks(owners)
    place = jnp.where(live(owners, rank), owners * share + rank, owner_total * share)
    tiles = signal.reshape(wire_blocks, block_wires, blocks, TB).transpose(0, 2, 1, 3)
    tiles = tiles.reshape(wire_blocks * blocks, block_wires, TB)[block]
    payload = jnp.zeros((owner_total * share, block_wires, TB), jnp.bfloat16)
    payload = payload.at[place].set(tiles, mode="drop")
    arrived = exchange(payload.reshape(owner_total, share, block_wires, TB))

    owners = rows >> 7
    rank = ranks(owners)
    source = jnp.arange(owner_total, dtype=jnp.int32)[:, None]
    line = jnp.where(live(owners, rank) & (owners == me), source, owner_total)
    table = jnp.zeros((owner_total, 128), jnp.int32)
    table = table.at[line, jnp.maximum(rank, 0)].set(rows & 127, mode="drop")
    return add_to_image(
        plan,
        table,
        arrived.reshape(owner_total * share, block_wires, TB),
        geometry,
        owner_total,
        planes,
        share,
        image,
    )


def tick_halo(sides):
    devices = lax.axis_size("tick")
    if devices == 2:
        tick = lax.axis_index("tick")
        got = lax.ppermute(sides[0], "tick", [(0, 1), (1, 0)])
        nothing = jnp.zeros_like(got)
        return jnp.where(tick == 0, nothing, got), jnp.where(tick == 0, got, nothing)
    up = [(i, i + 1) for i in range(devices - 1)]
    down = [(i + 1, i) for i in range(devices - 1)]
    return lax.ppermute(sides[1], "tick", up), lax.ppermute(sides[0], "tick", down)


def wire_halo(first, last, left, right):
    devices = lax.axis_size("wire")
    up = [(i, i + 1) for i in range(devices - 1)]
    down = [(i + 1, i) for i in range(devices - 1)]
    last = jnp.concatenate([left[-PAD:], last, right[-PAD:]], axis=1)
    first = jnp.concatenate([left[:PAD], first, right[:PAD]], axis=1)
    return lax.ppermute(last, "wire", up), lax.ppermute(first, "wire", down)


def exchange(array):
    return lax.all_to_all(array, ("wire", "plane"), split_axis=0, concat_axis=0, tiled=True)


def shards(raw, chan_mask, kernel, geometry, roi_block, roi_owner):
    wires, ticks = raw.shape
    slot_count = roi_block.shape[0]
    block_wires = geometry.shape[1]
    cells = geometry.shape[2]
    tick_blocks = ticks // TB
    planes = lax.axis_size("plane")
    wire_shards = lax.axis_size("wire")
    owner_total = planes * wire_shards
    share = -(-(slot_count - CAP) // (owner_total - 1))

    mask, first, last, packed, send_plan, *sides = prepare(
        raw, chan_mask, roi_owner, roi_block, planes, owner_total, share
    )
    left, right = tick_halo(sides)
    top, bottom = wire_halo(first, last, left, right)
    bands = make_bands(kernel[0])
    inner = convolve_inner(raw, mask, left, right, bands)
    signal, partial = convolve_edges(
        planes, send_plan, packed, inner, raw, mask, left, right, top, bottom, bands, geometry
    )

    pieces = exchange(partial)
    payload = pack_tiles(send_plan, signal, owner_total * share, block_wires)

    rows = pieces[:, cells].astype(jnp.int32) * 128 + pieces[:, cells + 1].astype(jnp.int32)
    plan = make_receive_plan(
        rows, packed, owner_total, planes, share, wires // block_wires, tick_blocks
    )
    staged = stage_geometry(
        plan, geometry, group_total(owner_total, share, tick_blocks), owner_total * share
    )

    sums = jnp.sum(pieces[:, :cells].astype(jnp.float32), axis=0).astype(jnp.bfloat16)
    payload = lax.dynamic_update_slice(
        payload.reshape(owner_total, share, block_wires, TB),
        sums.reshape(1, cells // block_wires, block_wires, TB),
        (send_plan[1, 0], 0, 0, 0),
    )
    arrived = exchange(payload).reshape(owner_total * share, block_wires, TB)
    image = make_image(plan, arrived, staged, owner_total, share, ticks)

    trips = agree(plan[1:2, 1:2])[0, 0]
    image = lax.fori_loop(
        0,
        trips,
        lambda trip, now: further_round(
            trip, now, signal, geometry, rows, packed, plan, owner_total, planes, share
        ),
        image,
    )
    return signal, image


def solution(mesh):
    in_specs = (
        P(("plane", "wire"), "tick"),
        P(("plane", "wire")),
        P("plane", None, None),
        P(),
        P(("plane", "wire", "tick")),
        P(("plane", "wire", "tick")),
    )
    out_specs = (P(("plane", "wire"), "tick"), P(("plane", "wire"), "tick"))
    return jax.shard_map(shards, mesh=mesh, in_specs=in_specs, out_specs=out_specs, check_vma=False)
```

```python
import functools

import jax
import jax.numpy as jnp
from jax import lax
from jax.experimental import pallas as pl
from jax.experimental.pallas import tpu as pltpu
from jax.sharding import PartitionSpec as P

TB = 128
CAP = 25
PAD = 16
TABLE = 8
MIB = 1024 * 1024


def vmem():
    return pl.BlockSpec(memory_space=pltpu.VMEM)


def smem():
    return pl.BlockSpec(memory_space=pltpu.SMEM)


GROUP = 8


def home(position, planes, owner_total):
    return (position % planes) * (owner_total // planes) + position // planes


def lane_numbers():
    return lax.broadcasted_iota(jnp.int32, (1, 128), 1)


def earlier_lanes():
    return (
        lax.broadcasted_iota(jnp.int32, (128, 128), 0)
        < lax.broadcasted_iota(jnp.int32, (128, 128), 1)
    ).astype(jnp.bfloat16)


def count_before(member, before):
    return jnp.dot(
        member.astype(jnp.float32).astype(jnp.bfloat16), before, preferred_element_type=jnp.float32
    )


def most_named(owners, owner_total):
    lanes = lane_numbers()
    counts = jnp.full(owners.shape, -1.0, jnp.float32)
    for owner in range(owner_total):
        named = jnp.sum((owners == owner).astype(jnp.float32), axis=1, keepdims=True)
        counts = jnp.where(lanes == owner, named, counts)
    top = jnp.max(counts, axis=1, keepdims=True)
    chosen = jnp.min(
        jnp.where(counts == top, lanes.astype(jnp.float32), 127.0), axis=1, keepdims=True
    )
    return counts, chosen


def prepare_kernel(
    planes,
    owner_total,
    share,
    tick_total,
    raw_hbm,
    mask_hbm,
    owner_hbm,
    block_hbm,
    mask_out,
    first_ref,
    last_ref,
    own_ref,
    out_ref,
    *rest,
):
    wires, ticks = raw_hbm.shape
    count = 1 if tick_total == 2 else 2
    sides = rest[:count]
    side_refs = rest[count : 2 * count]
    first_buf, last_buf, mask_ref, owner_ref, block_ref, sems = rest[2 * count :]
    tick = lax.axis_index("tick")
    me = lax.axis_index("wire") * planes + lax.axis_index("plane")
    if tick_total == 2:
        starts = [pl.multiple_of((1 - tick) * (ticks - TB), TB)]
    else:
        starts = [0, ticks - TB]
    moves = [(mask_hbm, mask_ref), (owner_hbm, owner_ref), (block_hbm, block_ref)]
    moves += [(raw_hbm.at[:, pl.ds(start, TB)], ref) for start, ref in zip(starts, side_refs)]
    moves += [(raw_hbm.at[pl.ds(0, PAD)], first_buf), (raw_hbm.at[pl.ds(wires - PAD, PAD)], last_buf)]
    copies = [
        pltpu.make_async_copy(source, target, sems.at[index])
        for index, (source, target) in enumerate(moves)
    ]
    for copy in copies:
        copy.start()
    for copy in copies[:3]:
        copy.wait()

    for part in range(wires // 128):
        row = mask_ref[part : part + 1].astype(jnp.float32)
        wide = jnp.transpose(jnp.broadcast_to(row, (128, 128)))
        mask_out[part * 128 : (part + 1) * 128] = wide.astype(jnp.bfloat16)

    lanes = lane_numbers()
    slot_count = owner_ref.shape[1]
    owner = owner_ref[...]
    wire_shards = owner_total // planes
    none = owner_total * 128
    own_ref[...] = jnp.where(lanes == 127, none + me, none)
    own_ref[:, 0:slot_count] = (
        (owner % wire_shards) * planes + owner // wire_shards
    ) * 128 + block_ref[...]
    own = own_ref[...]
    _, hot = most_named(own >> 7, owner_total)
    rows = lax.broadcasted_iota(jnp.int32, (owner_total, 128), 0)
    member = (own >> 7) == rows
    rank = count_before(member, earlier_lanes())
    place = jnp.where(rank < share, rows.astype(jnp.float32) * share + rank, -1.0)
    place = jnp.where(rows.astype(jnp.float32) == hot, -2.0, place)
    place = jnp.sum(jnp.where(member, place + 3.0, 0.0), axis=0, keepdims=True)

    column = jnp.transpose(jnp.broadcast_to(own.astype(jnp.float32), (128, 128)))
    column = column.astype(jnp.int32)
    here = ((column & 127) == lanes) & ((column >> 7) < owner_total)
    spread = jnp.transpose(jnp.broadcast_to(place, (128, 128)))
    placed = jnp.sum(jnp.where(here, spread, 0.0), axis=0, keepdims=True)
    trash = float(owner_total * share)
    facts = jnp.where(lanes == 2, me, 0)
    out_ref[...] = jnp.zeros_like(out_ref)
    out_ref[0:1, :] = jnp.where(placed >= 3.0, placed - 3.0, trash).astype(jnp.int32)
    out_ref[1:2, :] = jnp.where(lanes == 0, hot.astype(jnp.int32), facts)
    out_ref[2:3, :] = (placed == 1.0).astype(jnp.int32)

    for copy in copies[3:]:
        copy.wait()
    for side, ref in zip(sides, side_refs):
        side[...] = ref[...] * mask_out[...]
    for block in range(ticks // TB):
        at = slice(block * TB, (block + 1) * TB)
        first_ref[:, at] = first_buf[:, at] * mask_out[0:PAD]
        last_ref[:, at] = last_buf[:, at] * mask_out[wires - PAD : wires]


def prepare(raw, chan_mask, roi_owner, roi_block, planes, owner_total, share):
    wires, ticks = raw.shape
    tick_total = lax.axis_size("tick")
    sides = 1 if tick_total == 2 else 2
    side = jax.ShapeDtypeStruct((wires, TB), jnp.bfloat16)
    edge = jax.ShapeDtypeStruct((PAD, ticks), jnp.bfloat16)
    row = jax.ShapeDtypeStruct((1, 128), jnp.int32)
    table = jax.ShapeDtypeStruct((8, 128), jnp.int32)
    slot_count = roi_owner.shape[0]
    return pl.pallas_call(
        functools.partial(prepare_kernel, planes, owner_total, share, tick_total),
        out_shape=(side, edge, edge, row, table) + (side,) * sides,
        in_specs=[pl.BlockSpec(memory_space=pltpu.HBM)] * 4,
        out_specs=(vmem(),) * (5 + sides),
        scratch_shapes=[pltpu.VMEM((wires, TB), jnp.bfloat16)] * sides
        + [pltpu.VMEM((PAD, ticks), jnp.bfloat16)] * 2
        + [pltpu.VMEM((wires // 128, 128), jnp.int32)]
        + [pltpu.VMEM((1, slot_count), jnp.int32)] * 2
        + [pltpu.SemaphoreType.DMA((sides + 5,))],
        compiler_params=pltpu.CompilerParams(vmem_limit_bytes=60 * MIB),
        name="prepare",
    )(raw, chan_mask.reshape(wires // 128, 128), roi_owner[None], roi_block[None])


def receive_kernel(owner_total, planes, share, wire_blocks, tick_blocks, rows_ref, own_ref, out_ref):
    lanes = lane_numbers()
    lane_f = lanes.astype(jnp.float32)
    every = rows_ref[...]
    owners = every >> 7
    own = own_ref[...]
    me = jnp.sum(jnp.where(lanes == 127, own & 127, 0).astype(jnp.float32), axis=1, keepdims=True)

    counts, chosen = most_named(owners, owner_total)
    hot = jnp.max(chosen, axis=0, keepdims=True)
    agreed = hot == jnp.min(chosen, axis=0, keepdims=True)
    left = jnp.where(agreed & (lane_f == hot), 0.0, counts)
    fullest = jnp.max(jnp.max(left, axis=1, keepdims=True), axis=0, keepdims=True)
    start = agreed.astype(jnp.float32)
    trips = -start
    for step in range(-(-CAP // share)):
        trips = trips + (fullest > step * share).astype(jnp.float32)
    trips = jnp.maximum(trips, 0.0)
    hot = jnp.where(agreed, hot, -1.0)

    to_me = owners.astype(jnp.float32) == me
    before = earlier_lanes()
    rank = count_before(to_me, before)
    blocks = every & 127
    source = lax.broadcasted_iota(jnp.int32, (owner_total, 128), 0)
    line = home(source, planes, owner_total) * wire_blocks + blocks // tick_blocks
    line = line.astype(jnp.float32)
    tick = (blocks % tick_blocks).astype(jnp.float32)
    lines = jnp.zeros((1, 128), jnp.float32)
    ticks = jnp.full((1, 128), -1.0, jnp.float32)
    for slot in range(share):
        got = to_me & (rank == slot)
        here = lanes == source * share + slot
        for value, where in ((line, 0), (tick + 1.0, 1)):
            one = jnp.sum(jnp.where(got, value, 0.0), axis=1, keepdims=True)
            one = jnp.sum(jnp.where(here, one, 0.0), axis=0, keepdims=True)
            if where == 0:
                lines = lines + one
            else:
                ticks = ticks + one

    block_rows = lax.broadcasted_iota(jnp.int32, (tick_blocks, 128), 0).astype(jnp.float32)
    member = block_rows == ticks
    rank = count_before(member, before)
    total = jnp.sum(member.astype(jnp.float32), axis=1, keepdims=True)
    groups = jnp.zeros_like(total)
    for step in range(0, owner_total * share, GROUP):
        groups = groups + (total > step).astype(jnp.float32)
    lower = (
        lax.broadcasted_iota(jnp.int32, (tick_blocks, tick_blocks), 0)
        > lax.broadcasted_iota(jnp.int32, (tick_blocks, tick_blocks), 1)
    ).astype(jnp.bfloat16)
    base = jnp.dot(
        lower,
        jnp.broadcast_to(groups, (tick_blocks, 128)).astype(jnp.bfloat16),
        preferred_element_type=jnp.float32,
    )
    place = jnp.sum(jnp.where(member, base * GROUP + rank, 0.0), axis=0, keepdims=True)
    trash = float(group_total(owner_total, share, tick_blocks) * GROUP)
    place = jnp.where(ticks < 0.0, trash, place)
    inside = (base <= lane_f) & (lane_f < base + groups)
    group_tick = jnp.sum(jnp.where(inside, block_rows, 0.0), axis=0, keepdims=True)

    facts = jnp.where(lanes == 0, hot, 0.0)
    facts = jnp.where(lanes == 1, trips, facts)
    facts = jnp.where(lanes == 2, me, facts)
    facts = jnp.where(lanes == 3, start, facts)
    out_ref[...] = jnp.zeros_like(out_ref)
    out_ref[0:1, :] = place.astype(jnp.int32)
    out_ref[1:2, :] = facts.astype(jnp.int32)
    out_ref[2:3, :] = lines.astype(jnp.int32)
    out_ref[3:4, :] = group_tick.astype(jnp.int32)


def group_total(owner_total, share, tick_blocks):
    return (owner_total * share - tick_blocks) // GROUP + tick_blocks


def make_receive_plan(rows, packed, owner_total, planes, share, wire_blocks, tick_blocks):
    return pl.pallas_call(
        functools.partial(receive_kernel, owner_total, planes, share, wire_blocks, tick_blocks),
        out_shape=jax.ShapeDtypeStruct((8, 128), jnp.int32),
        in_specs=[vmem(), vmem()],
        out_specs=vmem(),
        compiler_params=pltpu.CompilerParams(vmem_limit_bytes=2 * MIB),
        name="receive_plan",
    )(rows, packed)


def agree(rounds):
    devices = lax.axis_size("tick")
    reach = 1
    while reach < devices:
        ring = [(i, (i + reach) % devices) for i in range(devices)]
        rounds = jnp.maximum(rounds, lax.ppermute(rounds, "tick", ring))
        reach *= 2
    return rounds


def band_kernel(taps_w, taps_ref, band_ref):
    row = lax.broadcasted_iota(jnp.int32, (TB, TB), 0)
    col = lax.broadcasted_iota(jnp.int32, (TB, TB), 1)
    pairs = (taps_w + 1) // 2
    band_ref[0, 0 : 3 * TB, TB : 2 * TB] = jnp.zeros((3 * TB, TB), jnp.bfloat16)
    band_ref[pairs - 1, 3 * TB : 6 * TB, 0:TB] = jnp.zeros((3 * TB, TB), jnp.bfloat16)
    taps = taps_ref[...].astype(jnp.float32)
    for tap in range(taps_w):
        spread = jnp.broadcast_to(taps[tap : tap + 1], (TB, 2 * TB))
        rolled = pltpu.roll(spread, TB, 1, stride=1, stride_axis=0)
        middle = rolled[:, :TB]
        outer = rolled[:, TB:]
        bands = (
            jnp.where(col < row, outer, 0.0).astype(jnp.bfloat16),
            middle.astype(jnp.bfloat16),
            jnp.where(col >= row, outer, 0.0).astype(jnp.bfloat16),
        )
        for first, second in ((0, 0), (1, 1), (1, 0), (0, 1)):
            if (tap - first + second) % 2:
                continue
            pair = (tap - first + second) // 2
            for piece in range(3):
                start = (first * 3 + piece) * TB
                band_ref[pair, start : start + TB, second * TB : (second + 1) * TB] = bands[piece]


def make_bands(taps):
    taps_w = taps.shape[0]
    return pl.pallas_call(
        functools.partial(band_kernel, taps_w),
        out_shape=jax.ShapeDtypeStruct(((taps_w + 1) // 2, 6 * TB, 2 * TB), jnp.bfloat16),
        in_specs=[vmem()],
        out_specs=vmem(),
        cost_estimate=pl.CostEstimate(flops=10**9, bytes_accessed=6 * MIB, transcendentals=0),
        compiler_params=pltpu.CompilerParams(vmem_limit_bytes=16 * MIB),
        name="bands",
    )(taps)


def spread_pair(wide_ref, lhs_view, line, pitch, blocks):
    for side in range(2):
        for piece in range(3):
            at = (side * 3 + piece) * TB
            lhs_view[:, at : at + TB] = wide_ref[
                pl.ds((line + side) * pitch + piece, blocks), :
            ].astype(jnp.bfloat16)


def write_lines(total, out_view, signal_ref, line, pairs, blocks):
    for pair in range(pairs):
        for side in range(2):
            out_view[pl.ds((2 * pair + side) * blocks, blocks), :] = total[
                pair * blocks : (pair + 1) * blocks, side * TB : (side + 1) * TB
            ]
    for block in range(blocks):
        signal_ref[line : line + 2 * pairs, block * TB : (block + 1) * TB] = out_view[
            pl.ds(block, 2 * pairs, stride=blocks), :
        ].astype(jnp.bfloat16)


def inner_kernel(
    chunks,
    raw_ref,
    mask_ref,
    left_ref,
    right_ref,
    band_ref,
    inner_ref,
    wide_ref,
    lhs_ref,
    out_ref,
):
    wires, ticks = raw_ref.shape
    blocks = ticks // TB
    pitch = wide_ref.shape[0] // wires
    reach = band_ref.shape[0]
    span = 2 * PAD
    groups = wires // span

    def fill(group, block):
        lines = slice(group * span, (group + 1) * span)
        if block == 0:
            inner = left_ref[lines]
        elif block == blocks + 1:
            inner = right_ref[lines]
        else:
            inner = raw_ref[lines, (block - 1) * TB : block * TB] * mask_ref[lines]
        wide_ref[pl.ds(group * span * pitch + block, span, stride=pitch), :] = inner.astype(
            jnp.float32
        )

    margin = reach - 1
    begin = PAD // 2
    state = {"group": 0, "pair": begin}

    def prepare(upto):
        todo = []
        while state["pair"] < upto:
            line = 2 * state["pair"] - margin
            while state["group"] < groups and line + 1 >= state["group"] * span:
                group = state["group"]
                for block in range(blocks + 2):
                    todo.append(lambda group=group, block=block: fill(group, block))
                state["group"] += 1
            todo.append(
                lambda line=line, pair=state["pair"]: spread_pair(
                    wide_ref, lhs_ref.at[pair - begin], line, pitch, blocks
                )
            )
            state["pair"] += 1
        return todo

    pair = begin
    for job in prepare(pair + chunks[0] + margin):
        job()
    for index, size in enumerate(chunks):
        todo = prepare(pair + size + chunks[index + 1] + margin) if index + 1 < len(chunks) else []
        each = -(-len(todo) // reach)
        total = jnp.zeros((size * blocks, 2 * TB), jnp.float32)
        for step in range(reach):
            rows = lhs_ref[pair - begin + step : pair - begin + step + size]
            total = total + jnp.dot(
                rows.reshape(size * blocks, 6 * TB), band_ref[step], preferred_element_type=jnp.float32
            )
            for job in todo[step * each : (step + 1) * each]:
                job()
        write_lines(total, out_ref.at[index % 2], inner_ref, 2 * (pair - begin), size, blocks)
        pair += size


def convolve_inner(raw, mask, left, right, bands):
    wires, ticks = raw.shape
    reach = bands.shape[0]
    blocks = ticks // TB
    pitch = -(-(blocks + 2) // 8) * 8
    pairs = (wires - 2 * PAD) // 2
    chunks = []
    while sum(chunks) < pairs:
        chunks.append(min(32 if chunks else 16, pairs - sum(chunks)))
    flops = 2 * blocks * pairs * reach * 6 * TB * 2 * TB
    return pl.pallas_call(
        functools.partial(inner_kernel, tuple(chunks)),
        out_shape=jax.ShapeDtypeStruct((wires - 2 * PAD, ticks), jnp.bfloat16),
        in_specs=[vmem()] * 5,
        out_specs=vmem(),
        scratch_shapes=[
            pltpu.VMEM((wires * pitch, TB), jnp.float32),
            pltpu.VMEM((pairs + reach - 1, blocks, 6 * TB), jnp.bfloat16),
            pltpu.VMEM((2, 2 * max(chunks) * blocks, TB), jnp.float32),
        ],
        cost_estimate=pl.CostEstimate(flops=flops, bytes_accessed=6 * MIB, transcendentals=0),
        compiler_params=pltpu.CompilerParams(vmem_limit_bytes=28 * MIB),
        name="inner",
    )(raw, mask, left, right, bands)


def edge_kernel(
    planes,
    plan_ref,
    own_ref,
    inner_ref,
    raw_ref,
    mask_ref,
    left_ref,
    right_ref,
    top_ref,
    bottom_ref,
    band_ref,
    geo_ref,
    signal_ref,
    partial_ref,
    wide_ref,
    lhs_ref,
    out_ref,
    turned_ref,
):
    wires, ticks = signal_ref.shape
    blocks = ticks // TB
    reach = band_ref.shape[0]
    block_wires = geo_ref.shape[1]
    wire_blocks = wires // block_wires
    near = 2 * PAD
    lines = PAD + near
    pitch = wide_ref.shape[1] // lines
    pairs = PAD // 2
    margin = reach - 1

    signal_ref[PAD : wires - PAD] = inner_ref[...]
    source = home(plan_ref[1, 2], planes, geo_ref.shape[0] // wire_blocks)
    rows = geo_ref[pl.ds(source * wire_blocks, wire_blocks)].reshape(wires, -1)
    turned_ref[...] = jnp.transpose(rows)

    for end in range(2):
        halo_ref = (top_ref, bottom_ref)[end]
        mine = (slice(0, near), slice(wires - near, wires))[end]
        halo_at = (0, near)[end]
        mine_at = (PAD, 0)[end]
        for block in range(blocks + 2):
            columns = slice(block * TB, (block + 1) * TB)
            if block == 0:
                inner = left_ref[mine].astype(jnp.float32)
            elif block == blocks + 1:
                inner = right_ref[mine].astype(jnp.float32)
            else:
                inner = raw_ref[mine, (block - 1) * TB : block * TB] * mask_ref[mine]
                inner = inner.astype(jnp.float32)
            wide_ref[end, pl.ds(halo_at * pitch + block, PAD, stride=pitch), :] = halo_ref[
                :, columns
            ].astype(jnp.float32)
            wide_ref[end, pl.ds(mine_at * pitch + block, near, stride=pitch), :] = inner
        first = (PAD, near - PAD)[end] - margin
        for pair in range(pairs + margin):
            spread_pair(
                wide_ref.at[end], lhs_ref.at[end, pair], first + 2 * pair, pitch, blocks
            )

    total = jnp.zeros((2 * pairs * blocks, 2 * TB), jnp.float32)
    for step in range(reach):
        rows = jnp.concatenate(
            [
                lhs_ref[end, step : step + pairs].reshape(pairs * blocks, 6 * TB)
                for end in range(2)
            ],
            axis=0,
        )
        total = total + jnp.dot(rows, band_ref[step], preferred_element_type=jnp.float32)
    for end in range(2):
        write_lines(
            total[end * pairs * blocks : (end + 1) * pairs * blocks],
            out_ref.at[end],
            signal_ref,
            (0, wires - PAD)[end],
            pairs,
            blocks,
        )

    cells = geo_ref.shape[2]
    shards = partial_ref.shape[1] // cells
    own = own_ref[...]
    line = lax.broadcasted_iota(jnp.int32, (TABLE, 128), 0)
    table = jnp.where(line == 0, own >> 7, jnp.where(line == 1, own & 127, 0))
    table = table.astype(jnp.float32).astype(jnp.bfloat16)
    for plane in range(planes):
        partial_ref[plane, shards * cells : shards * cells + TABLE] = table

    for block in range(0, blocks, 2):
        chosen = []
        for side in range(2):
            at = slice((block + side) * TB, (block + side + 1) * TB)
            column = []
            for line in range(wire_blocks):
                tile = signal_ref[line * block_wires : (line + 1) * block_wires, at]
                asked = plan_ref[2, line * blocks + block + side] == 1
                column.append(jnp.where(asked, tile, jnp.zeros_like(tile)))
            chosen.append(jnp.concatenate(column, axis=0))
        sums = jnp.dot(
            turned_ref[...], jnp.concatenate(chosen, axis=1), preferred_element_type=jnp.float32
        ).astype(jnp.bfloat16)
        for side in range(2):
            shard, plane = divmod(block + side, planes)
            partial_ref[plane, shard * cells : (shard + 1) * cells] = sums[
                :, side * TB : (side + 1) * TB
            ]


def convolve_edges(
    planes, plan, own, inner, raw, mask, left, right, top, bottom, bands, geometry
):
    wires, ticks = raw.shape
    reach = bands.shape[0]
    cells = geometry.shape[2]
    blocks = ticks // TB
    pitch = -(-(blocks + 2) // 8) * 8
    flops = 2 * blocks * PAD * reach * 6 * TB * 2 * TB
    return pl.pallas_call(
        functools.partial(edge_kernel, planes),
        out_shape=(
            jax.ShapeDtypeStruct((wires, ticks), jnp.bfloat16),
            jax.ShapeDtypeStruct((planes, blocks // planes * cells + TABLE, TB), jnp.bfloat16),
        ),
        in_specs=[smem()] + [vmem()] * 10,
        out_specs=(vmem(), vmem()),
        scratch_shapes=[
            pltpu.VMEM((2, 3 * PAD * pitch, TB), jnp.float32),
            pltpu.VMEM((2, PAD // 2 + reach - 1, blocks, 6 * TB), jnp.bfloat16),
            pltpu.VMEM((2, PAD * blocks, TB), jnp.float32),
            pltpu.VMEM((cells, wires), jnp.bfloat16),
        ],
        cost_estimate=pl.CostEstimate(flops=flops, bytes_accessed=6 * MIB, transcendentals=0),
        compiler_params=pltpu.CompilerParams(vmem_limit_bytes=24 * MIB),
        name="edges",
    )(plan, own, inner, raw, mask, left, right, top, bottom, bands, geometry)


def fold_kernel(pieces_ref, out_ref):
    planes, height, _ = pieces_ref.shape
    shards, lines, _ = out_ref.shape
    cells = lines - TABLE
    line = lax.broadcasted_iota(jnp.int32, (TABLE, 128), 0)
    table = jnp.zeros((TABLE, 128), jnp.float32)
    for plane in range(planes):
        tags = pieces_ref[plane, height - TABLE : height].astype(jnp.float32)
        table = jnp.where(line == 2 * plane, tags[0:1], table)
        table = jnp.where(line == 2 * plane + 1, tags[1:2], table)
    for shard in range(shards):
        total = pieces_ref[0, shard * cells : (shard + 1) * cells].astype(jnp.float32)
        for plane in range(1, planes):
            total = total + pieces_ref[plane, shard * cells : (shard + 1) * cells].astype(
                jnp.float32
            )
        out_ref[shard, 0:cells] = total.astype(jnp.bfloat16)
        out_ref[shard, cells:lines] = table.astype(jnp.bfloat16)


def fold(pieces, shards):
    cells = (pieces.shape[1] - TABLE) // shards
    return pl.pallas_call(
        fold_kernel,
        out_shape=jax.ShapeDtypeStruct((shards, cells + TABLE, TB), jnp.bfloat16),
        in_specs=[vmem()],
        out_specs=vmem(),
        compiler_params=pltpu.CompilerParams(vmem_limit_bytes=4 * MIB),
        name="fold",
    )(pieces)


def pack_kernel(slots, plan_ref, signal_ref, payload_ref, tiles_ref):
    block_wires = payload_ref.shape[1]
    wires, ticks = signal_ref.shape
    blocks = ticks // TB
    tiles_ref[...] = jnp.zeros_like(tiles_ref)
    for line in range(wires // block_wires):
        for block in range(blocks):
            place = plan_ref[0, line * blocks + block]
            tiles_ref[place] = signal_ref[
                line * block_wires : (line + 1) * block_wires, block * TB : (block + 1) * TB
            ]
    payload_ref[...] = tiles_ref[0:slots]


def pack_tiles(plan, signal, slots, block_wires):
    return pl.pallas_call(
        functools.partial(pack_kernel, slots),
        out_shape=jax.ShapeDtypeStruct((slots, block_wires, TB), jnp.bfloat16),
        in_specs=[smem(), vmem()],
        out_specs=vmem(),
        scratch_shapes=[pltpu.VMEM((slots + 1, block_wires, TB), jnp.bfloat16)],
        cost_estimate=pl.CostEstimate(flops=10**8, bytes_accessed=3 * MIB, transcendentals=0),
        compiler_params=pltpu.CompilerParams(vmem_limit_bytes=8 * MIB),
        name="pack",
    )(plan, signal)


def stage_kernel(slots, plan_ref, geo_ref, out_ref, rows_ref):
    groups = out_ref.shape[0]
    rows_ref[...] = jnp.zeros_like(rows_ref)
    for slot in range(slots):
        rows_ref[plan_ref[0, slot]] = geo_ref[plan_ref[2, slot]]
    for group in range(groups):
        rows = rows_ref[group * GROUP : (group + 1) * GROUP]
        out_ref[group] = jnp.transpose(rows.reshape(-1, rows.shape[-1]))


def stage_geometry(plan, geometry, groups, slots):
    _, block_wires, cells = geometry.shape
    return pl.pallas_call(
        functools.partial(stage_kernel, slots),
        out_shape=jax.ShapeDtypeStruct((groups, cells, GROUP * block_wires), jnp.bfloat16),
        in_specs=[smem(), vmem()],
        out_specs=vmem(),
        scratch_shapes=[pltpu.VMEM((groups * GROUP + 1, block_wires, cells), jnp.bfloat16)],
        cost_estimate=pl.CostEstimate(flops=10**8, bytes_accessed=3 * MIB, transcendentals=0),
        compiler_params=pltpu.CompilerParams(vmem_limit_bytes=12 * MIB),
        name="stage",
    )(plan, geometry)


def image_kernel(owner_total, share, plan_ref, arrived_ref, staged_ref, image_ref, tiles_ref, sum_ref):
    cells, ticks = image_ref.shape
    blocks = ticks // TB
    block_wires = arrived_ref.shape[1]
    groups = staged_ref.shape[0]
    is_hot = plan_ref[1, 0] == plan_ref[1, 2]
    counts = plan_ref[1, 3] == 1

    @pl.when(is_hot)
    def _():
        for source in range(owner_total):
            sums = arrived_ref[source * share : source * share + cells // block_wires]
            image_ref[:, source * TB : (source + 1) * TB] = sums.reshape(cells, TB).astype(
                jnp.float32
            )

    @pl.when(jnp.logical_not(is_hot))
    def _():
        sum_ref[...] = jnp.zeros_like(sum_ref)
        tiles_ref[...] = jnp.zeros_like(tiles_ref)

        @pl.when(counts)
        def _():
            for slot in range(owner_total * share):
                tiles_ref[plan_ref[0, slot]] = arrived_ref[slot]
            for group in range(groups):
                tiles = tiles_ref[group * GROUP : (group + 1) * GROUP]
                sum_ref[plan_ref[3, group]] += jnp.dot(
                    staged_ref[group],
                    tiles.reshape(GROUP * block_wires, TB),
                    preferred_element_type=jnp.float32,
                )

        for block in range(blocks):
            image_ref[:, block * TB : (block + 1) * TB] = sum_ref[block]


def make_image(plan, arrived, staged, owner_total, share, ticks):
    groups, cells, _ = staged.shape
    block_wires = arrived.shape[1]
    return pl.pallas_call(
        functools.partial(image_kernel, owner_total, share),
        out_shape=jax.ShapeDtypeStruct((cells, ticks), jnp.float32),
        in_specs=[smem(), vmem(), vmem()],
        out_specs=vmem(),
        scratch_shapes=[
            pltpu.VMEM((groups * GROUP + 1, block_wires, TB), jnp.bfloat16),
            pltpu.VMEM((ticks // TB, cells, TB), jnp.float32),
        ],
        cost_estimate=pl.CostEstimate(flops=10**8, bytes_accessed=3 * MIB, transcendentals=0),
        compiler_params=pltpu.CompilerParams(vmem_limit_bytes=16 * MIB),
        name="image",
    )(plan, arrived, staged)


def more_kernel(owner_total, planes, share, plan_ref, table_ref, arrived_ref, geo_ref, before_ref, image_ref):
    cells, ticks = image_ref.shape
    blocks = ticks // TB
    wire_blocks = geo_ref.shape[0] // owner_total
    image_ref[...] = before_ref[...]

    @pl.when(plan_ref[1, 0] != plan_ref[1, 2])
    def _():
        def add(source, carry):
            for slot in range(share):
                block = table_ref[source, slot]
                at = pl.multiple_of((block % blocks) * TB, TB)
                image_ref[:, pl.ds(at, TB)] += lax.dot_general(
                    geo_ref[home(source, planes, owner_total) * wire_blocks + block // blocks],
                    arrived_ref[source * share + slot],
                    (((0,), (0,)), ((), ())),
                    preferred_element_type=jnp.float32,
                )
            return carry

        lax.fori_loop(0, owner_total, add, 0)


def add_to_image(plan, table, arrived, geometry, owner_total, planes, share, image):
    return pl.pallas_call(
        functools.partial(more_kernel, owner_total, planes, share),
        out_shape=jax.ShapeDtypeStruct(image.shape, jnp.float32),
        in_specs=[smem(), smem()] + [vmem()] * 3,
        out_specs=vmem(),
        compiler_params=pltpu.CompilerParams(vmem_limit_bytes=16 * MIB),
        name="image_more",
    )(plan, table, arrived, geometry, image)


def further_round(
    trip, image, signal, geometry, rows, packed, plan, owner_total, planes, share
):
    trip, signal, rows, packed, plan = lax.optimization_barrier((trip, signal, rows, packed, plan))
    step = trip + plan[1, 3]
    hot = plan[1, 0]
    me = plan[1, 2]
    block_wires = geometry.shape[1]
    wire_count, tick_count = signal.shape
    blocks = tick_count // TB
    wire_blocks = wire_count // block_wires
    ids = jnp.arange(owner_total, dtype=jnp.int32)

    def ranks(owners):
        member = (owners[..., None] == ids).astype(jnp.int32)
        before = jnp.cumsum(member, axis=-2) - member
        return jnp.sum(before * member, axis=-1) - step * share

    def live(owners, rank):
        return (owners < owner_total) & (owners != hot) & (rank >= 0) & (rank < share)

    owners = packed[0] >> 7
    block = packed[0] & 127
    rank = ranks(owners)
    place = jnp.where(live(owners, rank), owners * share + rank, owner_total * share)
    tiles = signal.reshape(wire_blocks, block_wires, blocks, TB).transpose(0, 2, 1, 3)
    tiles = tiles.reshape(wire_blocks * blocks, block_wires, TB)[block]
    payload = jnp.zeros((owner_total * share, block_wires, TB), jnp.bfloat16)
    payload = payload.at[place].set(tiles, mode="drop")
    arrived = exchange(payload.reshape(owner_total, share, block_wires, TB))

    owners = rows >> 7
    rank = ranks(owners)
    source = jnp.arange(owner_total, dtype=jnp.int32)[:, None]
    line = jnp.where(live(owners, rank) & (owners == me), source, owner_total)
    table = jnp.zeros((owner_total, 128), jnp.int32)
    table = table.at[line, jnp.maximum(rank, 0)].set(rows & 127, mode="drop")
    return add_to_image(
        plan,
        table,
        arrived.reshape(owner_total * share, block_wires, TB),
        geometry,
        owner_total,
        planes,
        share,
        image,
    )


def tick_halo(sides):
    devices = lax.axis_size("tick")
    if devices == 2:
        tick = lax.axis_index("tick")
        got = lax.ppermute(sides[0], "tick", [(0, 1), (1, 0)])
        nothing = jnp.zeros_like(got)
        return jnp.where(tick == 0, nothing, got), jnp.where(tick == 0, got, nothing)
    up = [(i, i + 1) for i in range(devices - 1)]
    down = [(i + 1, i) for i in range(devices - 1)]
    return lax.ppermute(sides[1], "tick", up), lax.ppermute(sides[0], "tick", down)


def wire_halo(first, last, left, right):
    devices = lax.axis_size("wire")
    up = [(i, i + 1) for i in range(devices - 1)]
    down = [(i + 1, i) for i in range(devices - 1)]
    last = jnp.concatenate([left[-PAD:], last, right[-PAD:]], axis=1)
    first = jnp.concatenate([left[:PAD], first, right[:PAD]], axis=1)
    return lax.ppermute(last, "wire", up), lax.ppermute(first, "wire", down)


def exchange(array, axes=("wire", "plane")):
    return lax.all_to_all(array, axes, split_axis=0, concat_axis=0, tiled=True)


def shards(raw, chan_mask, kernel, geometry, roi_block, roi_owner):
    wires, ticks = raw.shape
    slot_count = roi_block.shape[0]
    block_wires = geometry.shape[1]
    cells = geometry.shape[2]
    tick_blocks = ticks // TB
    planes = lax.axis_size("plane")
    wire_shards = lax.axis_size("wire")
    owner_total = planes * wire_shards
    share = -(-(slot_count - CAP) // (owner_total - 1))

    mask, first, last, packed, send_plan, *sides = prepare(
        raw, chan_mask, roi_owner, roi_block, planes, owner_total, share
    )
    left, right = tick_halo(sides)
    top, bottom = wire_halo(first, last, left, right)
    bands = make_bands(kernel[0])
    inner = convolve_inner(raw, mask, left, right, bands)
    signal, partial = convolve_edges(
        planes, send_plan, packed, inner, raw, mask, left, right, top, bottom, bands, geometry
    )

    pieces = exchange(partial, "plane")
    payload = pack_tiles(send_plan, signal, owner_total * share, block_wires)
    pieces = exchange(fold(pieces, wire_shards), "wire")

    tables = pieces[:, cells : cells + 2 * planes].astype(jnp.int32)
    tables = tables.reshape(owner_total, 2, 128)
    rows = tables[:, 0] * 128 + tables[:, 1]
    plan = make_receive_plan(
        rows, packed, owner_total, planes, share, wires // block_wires, tick_blocks
    )
    staged = stage_geometry(
        plan, geometry, group_total(owner_total, share, tick_blocks), owner_total * share
    )

    sums = jnp.sum(pieces[:, :cells].astype(jnp.float32), axis=0).astype(jnp.bfloat16)
    payload = lax.dynamic_update_slice(
        payload.reshape(owner_total, share, block_wires, TB),
        sums.reshape(1, cells // block_wires, block_wires, TB),
        (send_plan[1, 0], 0, 0, 0),
    )
    arrived = exchange(payload).reshape(owner_total * share, block_wires, TB)
    image = make_image(plan, arrived, staged, owner_total, share, ticks)

    trips = agree(plan[1:2, 1:2])[0, 0]
    image = lax.fori_loop(
        0,
        trips,
        lambda trip, now: further_round(
            trip, now, signal, geometry, rows, packed, plan, owner_total, planes, share
        ),
        image,
    )
    return signal, image


def solution(mesh):
    in_specs = (
        P(("plane", "wire"), "tick"),
        P(("plane", "wire")),
        P("plane", None, None),
        P(),
        P(("plane", "wire", "tick")),
        P(("plane", "wire", "tick")),
    )
    out_specs = (P(("plane", "wire"), "tick"), P(("plane", "wire"), "tick"))
    return jax.shard_map(shards, mesh=mesh, in_specs=in_specs, out_specs=out_specs, check_vma=False)
```

```python
import functools

import jax
import jax.numpy as jnp
from jax import lax
from jax.experimental import pallas as pl
from jax.experimental.pallas import tpu as pltpu
from jax.sharding import PartitionSpec as P

TB = 128
CAP = 25
PAD = 16
TABLE = 8
MIB = 1024 * 1024


def vmem():
    return pl.BlockSpec(memory_space=pltpu.VMEM)


def smem():
    return pl.BlockSpec(memory_space=pltpu.SMEM)


GROUP = 8


def home(position, planes, owner_total):
    return (position % planes) * (owner_total // planes) + position // planes


def lane_numbers():
    return lax.broadcasted_iota(jnp.int32, (1, 128), 1)


def earlier_lanes():
    return (
        lax.broadcasted_iota(jnp.int32, (128, 128), 0)
        < lax.broadcasted_iota(jnp.int32, (128, 128), 1)
    ).astype(jnp.bfloat16)


def count_before(member, before):
    return jnp.dot(
        member.astype(jnp.float32).astype(jnp.bfloat16), before, preferred_element_type=jnp.float32
    )


def most_named(owners, owner_total):
    lanes = lane_numbers()
    counts = jnp.full(owners.shape, -1.0, jnp.float32)
    for owner in range(owner_total):
        named = jnp.sum((owners == owner).astype(jnp.float32), axis=1, keepdims=True)
        counts = jnp.where(lanes == owner, named, counts)
    top = jnp.max(counts, axis=1, keepdims=True)
    chosen = jnp.min(
        jnp.where(counts == top, lanes.astype(jnp.float32), 127.0), axis=1, keepdims=True
    )
    return counts, chosen


def prepare_kernel(
    planes,
    owner_total,
    share,
    tick_total,
    raw_hbm,
    mask_hbm,
    owner_hbm,
    block_hbm,
    mask_out,
    first_ref,
    last_ref,
    own_ref,
    out_ref,
    *rest,
):
    wires, ticks = raw_hbm.shape
    count = 1 if tick_total == 2 else 2
    sides = rest[:count]
    side_refs = rest[count : 2 * count]
    first_buf, last_buf, mask_ref, owner_ref, block_ref, sems = rest[2 * count :]
    tick = lax.axis_index("tick")
    me = lax.axis_index("wire") * planes + lax.axis_index("plane")
    if tick_total == 2:
        starts = [pl.multiple_of((1 - tick) * (ticks - TB), TB)]
    else:
        starts = [0, ticks - TB]
    moves = [(mask_hbm, mask_ref), (owner_hbm, owner_ref), (block_hbm, block_ref)]
    moves += [(raw_hbm.at[:, pl.ds(start, TB)], ref) for start, ref in zip(starts, side_refs)]
    moves += [(raw_hbm.at[pl.ds(0, PAD)], first_buf), (raw_hbm.at[pl.ds(wires - PAD, PAD)], last_buf)]
    copies = [
        pltpu.make_async_copy(source, target, sems.at[index])
        for index, (source, target) in enumerate(moves)
    ]
    for copy in copies:
        copy.start()
    for copy in copies[:3]:
        copy.wait()

    for part in range(wires // 128):
        row = mask_ref[part : part + 1].astype(jnp.float32)
        wide = jnp.transpose(jnp.broadcast_to(row, (128, 128)))
        mask_out[part * 128 : (part + 1) * 128] = wide.astype(jnp.bfloat16)

    lanes = lane_numbers()
    slot_count = owner_ref.shape[1]
    owner = owner_ref[...]
    wire_shards = owner_total // planes
    none = owner_total * 128
    own_ref[...] = jnp.where(lanes == 127, none + me, none)
    own_ref[:, 0:slot_count] = (
        (owner % wire_shards) * planes + owner // wire_shards
    ) * 128 + block_ref[...]
    own = own_ref[...]
    _, hot = most_named(own >> 7, owner_total)
    rows = lax.broadcasted_iota(jnp.int32, (owner_total, 128), 0)
    member = (own >> 7) == rows
    rank = count_before(member, earlier_lanes())
    place = jnp.where(rank < share, rows.astype(jnp.float32) * share + rank, -1.0)
    place = jnp.where(rows.astype(jnp.float32) == hot, -2.0, place)
    place = jnp.sum(jnp.where(member, place + 3.0, 0.0), axis=0, keepdims=True)

    column = jnp.transpose(jnp.broadcast_to(own.astype(jnp.float32), (128, 128)))
    column = column.astype(jnp.int32)
    here = ((column & 127) == lanes) & ((column >> 7) < owner_total)
    spread = jnp.transpose(jnp.broadcast_to(place, (128, 128)))
    placed = jnp.sum(jnp.where(here, spread, 0.0), axis=0, keepdims=True)
    trash = float(owner_total * share)
    facts = jnp.where(lanes == 2, me, 0)
    out_ref[...] = jnp.zeros_like(out_ref)
    out_ref[0:1, :] = jnp.where(placed >= 3.0, placed - 3.0, trash).astype(jnp.int32)
    out_ref[1:2, :] = jnp.where(lanes == 0, hot.astype(jnp.int32), facts)
    out_ref[2:3, :] = (placed == 1.0).astype(jnp.int32)

    for copy in copies[3:]:
        copy.wait()
    for side, ref in zip(sides, side_refs):
        side[...] = ref[...] * mask_out[...]
    for block in range(ticks // TB):
        at = slice(block * TB, (block + 1) * TB)
        first_ref[:, at] = first_buf[:, at] * mask_out[0:PAD]
        last_ref[:, at] = last_buf[:, at] * mask_out[wires - PAD : wires]


def prepare(raw, chan_mask, roi_owner, roi_block, planes, owner_total, share):
    wires, ticks = raw.shape
    tick_total = lax.axis_size("tick")
    sides = 1 if tick_total == 2 else 2
    side = jax.ShapeDtypeStruct((wires, TB), jnp.bfloat16)
    edge = jax.ShapeDtypeStruct((PAD, ticks), jnp.bfloat16)
    row = jax.ShapeDtypeStruct((1, 128), jnp.int32)
    table = jax.ShapeDtypeStruct((8, 128), jnp.int32)
    slot_count = roi_owner.shape[0]
    return pl.pallas_call(
        functools.partial(prepare_kernel, planes, owner_total, share, tick_total),
        out_shape=(side, edge, edge, row, table) + (side,) * sides,
        in_specs=[pl.BlockSpec(memory_space=pltpu.HBM)] * 4,
        out_specs=(vmem(),) * (5 + sides),
        scratch_shapes=[pltpu.VMEM((wires, TB), jnp.bfloat16)] * sides
        + [pltpu.VMEM((PAD, ticks), jnp.bfloat16)] * 2
        + [pltpu.VMEM((wires // 128, 128), jnp.int32)]
        + [pltpu.VMEM((1, slot_count), jnp.int32)] * 2
        + [pltpu.SemaphoreType.DMA((sides + 5,))],
        compiler_params=pltpu.CompilerParams(vmem_limit_bytes=60 * MIB),
        name="prepare",
    )(raw, chan_mask.reshape(wires // 128, 128), roi_owner[None], roi_block[None])


def receive_kernel(owner_total, planes, share, wire_blocks, tick_blocks, rows_ref, own_ref, out_ref):
    lanes = lane_numbers()
    lane_f = lanes.astype(jnp.float32)
    every = rows_ref[...]
    owners = every >> 7
    own = own_ref[...]
    me = jnp.sum(jnp.where(lanes == 127, own & 127, 0).astype(jnp.float32), axis=1, keepdims=True)

    counts, chosen = most_named(owners, owner_total)
    hot = jnp.max(chosen, axis=0, keepdims=True)
    agreed = hot == jnp.min(chosen, axis=0, keepdims=True)
    left = jnp.where(agreed & (lane_f == hot), 0.0, counts)
    fullest = jnp.max(jnp.max(left, axis=1, keepdims=True), axis=0, keepdims=True)
    start = agreed.astype(jnp.float32)
    trips = -start
    for step in range(-(-CAP // share)):
        trips = trips + (fullest > step * share).astype(jnp.float32)
    trips = jnp.maximum(trips, 0.0)
    hot = jnp.where(agreed, hot, -1.0)

    to_me = owners.astype(jnp.float32) == me
    before = earlier_lanes()
    rank = count_before(to_me, before)
    blocks = every & 127
    source = lax.broadcasted_iota(jnp.int32, (owner_total, 128), 0)
    line = home(source, planes, owner_total) * wire_blocks + blocks // tick_blocks
    line = line.astype(jnp.float32)
    tick = (blocks % tick_blocks).astype(jnp.float32)
    lines = jnp.zeros((1, 128), jnp.float32)
    ticks = jnp.full((1, 128), -1.0, jnp.float32)
    for slot in range(share):
        got = to_me & (rank == slot)
        here = lanes == source * share + slot
        for value, where in ((line, 0), (tick + 1.0, 1)):
            one = jnp.sum(jnp.where(got, value, 0.0), axis=1, keepdims=True)
            one = jnp.sum(jnp.where(here, one, 0.0), axis=0, keepdims=True)
            if where == 0:
                lines = lines + one
            else:
                ticks = ticks + one

    block_rows = lax.broadcasted_iota(jnp.int32, (tick_blocks, 128), 0).astype(jnp.float32)
    member = block_rows == ticks
    rank = count_before(member, before)
    total = jnp.sum(member.astype(jnp.float32), axis=1, keepdims=True)
    groups = jnp.zeros_like(total)
    for step in range(0, owner_total * share, GROUP):
        groups = groups + (total > step).astype(jnp.float32)
    lower = (
        lax.broadcasted_iota(jnp.int32, (tick_blocks, tick_blocks), 0)
        > lax.broadcasted_iota(jnp.int32, (tick_blocks, tick_blocks), 1)
    ).astype(jnp.bfloat16)
    base = jnp.dot(
        lower,
        jnp.broadcast_to(groups, (tick_blocks, 128)).astype(jnp.bfloat16),
        preferred_element_type=jnp.float32,
    )
    place = jnp.sum(jnp.where(member, base * GROUP + rank, 0.0), axis=0, keepdims=True)
    trash = float(group_total(owner_total, share, tick_blocks) * GROUP)
    place = jnp.where(ticks < 0.0, trash, place)
    inside = (base <= lane_f) & (lane_f < base + groups)
    group_tick = jnp.sum(jnp.where(inside, block_rows, 0.0), axis=0, keepdims=True)

    facts = jnp.where(lanes == 0, hot, 0.0)
    facts = jnp.where(lanes == 1, trips, facts)
    facts = jnp.where(lanes == 2, me, facts)
    facts = jnp.where(lanes == 3, start, facts)
    out_ref[...] = jnp.zeros_like(out_ref)
    out_ref[0:1, :] = place.astype(jnp.int32)
    out_ref[1:2, :] = facts.astype(jnp.int32)
    out_ref[2:3, :] = lines.astype(jnp.int32)
    out_ref[3:4, :] = group_tick.astype(jnp.int32)


def group_total(owner_total, share, tick_blocks):
    return (owner_total * share - tick_blocks) // GROUP + tick_blocks


def make_receive_plan(rows, packed, owner_total, planes, share, wire_blocks, tick_blocks):
    return pl.pallas_call(
        functools.partial(receive_kernel, owner_total, planes, share, wire_blocks, tick_blocks),
        out_shape=jax.ShapeDtypeStruct((8, 128), jnp.int32),
        in_specs=[vmem(), vmem()],
        out_specs=vmem(),
        compiler_params=pltpu.CompilerParams(vmem_limit_bytes=2 * MIB),
        name="receive_plan",
    )(rows, packed)


def agree(rounds):
    devices = lax.axis_size("tick")
    reach = 1
    while reach < devices:
        ring = [(i, (i + reach) % devices) for i in range(devices)]
        rounds = jnp.maximum(rounds, lax.ppermute(rounds, "tick", ring))
        reach *= 2
    return rounds


def band_kernel(taps_w, taps_ref, band_ref):
    row = lax.broadcasted_iota(jnp.int32, (TB, TB), 0)
    col = lax.broadcasted_iota(jnp.int32, (TB, TB), 1)
    pairs = (taps_w + 1) // 2
    band_ref[0, 0 : 3 * TB, TB : 2 * TB] = jnp.zeros((3 * TB, TB), jnp.bfloat16)
    band_ref[pairs - 1, 3 * TB : 6 * TB, 0:TB] = jnp.zeros((3 * TB, TB), jnp.bfloat16)
    taps = taps_ref[...].astype(jnp.float32)
    for tap in range(taps_w):
        spread = jnp.broadcast_to(taps[tap : tap + 1], (TB, 2 * TB))
        rolled = pltpu.roll(spread, TB, 1, stride=1, stride_axis=0)
        middle = rolled[:, :TB]
        outer = rolled[:, TB:]
        bands = (
            jnp.where(col < row, outer, 0.0).astype(jnp.bfloat16),
            middle.astype(jnp.bfloat16),
            jnp.where(col >= row, outer, 0.0).astype(jnp.bfloat16),
        )
        for first, second in ((0, 0), (1, 1), (1, 0), (0, 1)):
            if (tap - first + second) % 2:
                continue
            pair = (tap - first + second) // 2
            for piece in range(3):
                start = (first * 3 + piece) * TB
                band_ref[pair, start : start + TB, second * TB : (second + 1) * TB] = bands[piece]


def make_bands(taps):
    taps_w = taps.shape[0]
    return pl.pallas_call(
        functools.partial(band_kernel, taps_w),
        out_shape=jax.ShapeDtypeStruct(((taps_w + 1) // 2, 6 * TB, 2 * TB), jnp.bfloat16),
        in_specs=[vmem()],
        out_specs=vmem(),
        cost_estimate=pl.CostEstimate(flops=10**9, bytes_accessed=6 * MIB, transcendentals=0),
        compiler_params=pltpu.CompilerParams(vmem_limit_bytes=16 * MIB),
        name="bands",
    )(taps)


def spread_pair(wide_ref, lhs_view, line, pitch, blocks):
    for side in range(2):
        for piece in range(3):
            at = (side * 3 + piece) * TB
            lhs_view[:, at : at + TB] = wide_ref[
                pl.ds((line + side) * pitch + piece, blocks), :
            ].astype(jnp.bfloat16)


def write_lines(total, out_view, signal_ref, line, pairs, blocks):
    for pair in range(pairs):
        for side in range(2):
            out_view[pl.ds((2 * pair + side) * blocks, blocks), :] = total[
                pair * blocks : (pair + 1) * blocks, side * TB : (side + 1) * TB
            ]
    for block in range(blocks):
        signal_ref[line : line + 2 * pairs, block * TB : (block + 1) * TB] = out_view[
            pl.ds(block, 2 * pairs, stride=blocks), :
        ].astype(jnp.bfloat16)


def inner_kernel(
    chunks,
    raw_ref,
    mask_ref,
    left_ref,
    right_ref,
    band_ref,
    inner_ref,
    wide_ref,
    lhs_ref,
    out_ref,
):
    wires, ticks = raw_ref.shape
    blocks = ticks // TB
    pitch = wide_ref.shape[0] // wires
    reach = band_ref.shape[0]
    span = 2 * PAD
    groups = wires // span

    def fill(group, block):
        lines = slice(group * span, (group + 1) * span)
        if block == 0:
            inner = left_ref[lines]
        elif block == blocks + 1:
            inner = right_ref[lines]
        else:
            inner = raw_ref[lines, (block - 1) * TB : block * TB] * mask_ref[lines]
        wide_ref[pl.ds(group * span * pitch + block, span, stride=pitch), :] = inner.astype(
            jnp.float32
        )

    margin = reach - 1
    begin = PAD // 2
    state = {"group": 0, "pair": begin}

    def prepare(upto):
        todo = []
        while state["pair"] < upto:
            line = 2 * state["pair"] - margin
            while state["group"] < groups and line + 1 >= state["group"] * span:
                group = state["group"]
                for block in range(blocks + 2):
                    todo.append(lambda group=group, block=block: fill(group, block))
                state["group"] += 1
            todo.append(
                lambda line=line, pair=state["pair"]: spread_pair(
                    wide_ref, lhs_ref.at[pair - begin], line, pitch, blocks
                )
            )
            state["pair"] += 1
        return todo

    pair = begin
    for job in prepare(pair + chunks[0] + margin):
        job()
    for index, size in enumerate(chunks):
        todo = prepare(pair + size + chunks[index + 1] + margin) if index + 1 < len(chunks) else []
        each = -(-len(todo) // reach)
        total = jnp.zeros((size * blocks, 2 * TB), jnp.float32)
        for step in range(reach):
            rows = lhs_ref[pair - begin + step : pair - begin + step + size]
            total = total + jnp.dot(
                rows.reshape(size * blocks, 6 * TB), band_ref[step], preferred_element_type=jnp.float32
            )
            for job in todo[step * each : (step + 1) * each]:
                job()
        write_lines(total, out_ref.at[index % 2], inner_ref, 2 * (pair - begin), size, blocks)
        pair += size


def convolve_inner(raw, mask, left, right, bands):
    wires, ticks = raw.shape
    reach = bands.shape[0]
    blocks = ticks // TB
    pitch = -(-(blocks + 2) // 8) * 8
    pairs = (wires - 2 * PAD) // 2
    chunks = []
    while sum(chunks) < pairs:
        chunks.append(min(32 if chunks else 16, pairs - sum(chunks)))
    flops = 2 * blocks * pairs * reach * 6 * TB * 2 * TB
    return pl.pallas_call(
        functools.partial(inner_kernel, tuple(chunks)),
        out_shape=jax.ShapeDtypeStruct((wires - 2 * PAD, ticks), jnp.bfloat16),
        in_specs=[vmem()] * 5,
        out_specs=vmem(),
        scratch_shapes=[
            pltpu.VMEM((wires * pitch, TB), jnp.float32),
            pltpu.VMEM((pairs + reach - 1, blocks, 6 * TB), jnp.bfloat16),
            pltpu.VMEM((2, 2 * max(chunks) * blocks, TB), jnp.float32),
        ],
        cost_estimate=pl.CostEstimate(flops=flops, bytes_accessed=6 * MIB, transcendentals=0),
        compiler_params=pltpu.CompilerParams(vmem_limit_bytes=28 * MIB),
        name="inner",
    )(raw, mask, left, right, bands)


def edge_kernel(
    planes,
    plan_ref,
    own_ref,
    inner_ref,
    raw_ref,
    mask_ref,
    left_ref,
    right_ref,
    top_ref,
    bottom_ref,
    band_ref,
    geo_ref,
    signal_ref,
    partial_ref,
    wide_ref,
    lhs_ref,
    out_ref,
    turned_ref,
):
    wires, ticks = signal_ref.shape
    blocks = ticks // TB
    reach = band_ref.shape[0]
    block_wires = geo_ref.shape[1]
    wire_blocks = wires // block_wires
    near = 2 * PAD
    lines = PAD + near
    pitch = wide_ref.shape[1] // lines
    pairs = PAD // 2
    margin = reach - 1

    signal_ref[PAD : wires - PAD] = inner_ref[...]
    source = home(plan_ref[1, 2], planes, geo_ref.shape[0] // wire_blocks)
    rows = geo_ref[pl.ds(source * wire_blocks, wire_blocks)].reshape(wires, -1)
    turned_ref[...] = jnp.transpose(rows)

    for end in range(2):
        halo_ref = (top_ref, bottom_ref)[end]
        mine = (slice(0, near), slice(wires - near, wires))[end]
        halo_at = (0, near)[end]
        mine_at = (PAD, 0)[end]
        for block in range(blocks + 2):
            columns = slice(block * TB, (block + 1) * TB)
            if block == 0:
                inner = left_ref[mine].astype(jnp.float32)
            elif block == blocks + 1:
                inner = right_ref[mine].astype(jnp.float32)
            else:
                inner = raw_ref[mine, (block - 1) * TB : block * TB] * mask_ref[mine]
                inner = inner.astype(jnp.float32)
            wide_ref[end, pl.ds(halo_at * pitch + block, PAD, stride=pitch), :] = halo_ref[
                :, columns
            ].astype(jnp.float32)
            wide_ref[end, pl.ds(mine_at * pitch + block, near, stride=pitch), :] = inner
        first = (PAD, near - PAD)[end] - margin
        for pair in range(pairs + margin):
            spread_pair(
                wide_ref.at[end], lhs_ref.at[end, pair], first + 2 * pair, pitch, blocks
            )

    total = jnp.zeros((2 * pairs * blocks, 2 * TB), jnp.float32)
    for step in range(reach):
        rows = jnp.concatenate(
            [
                lhs_ref[end, step : step + pairs].reshape(pairs * blocks, 6 * TB)
                for end in range(2)
            ],
            axis=0,
        )
        total = total + jnp.dot(rows, band_ref[step], preferred_element_type=jnp.float32)
    for end in range(2):
        write_lines(
            total[end * pairs * blocks : (end + 1) * pairs * blocks],
            out_ref.at[end],
            signal_ref,
            (0, wires - PAD)[end],
            pairs,
            blocks,
        )

    cells = geo_ref.shape[2]
    shards = partial_ref.shape[1] // cells
    own = own_ref[...]
    line = lax.broadcasted_iota(jnp.int32, (TABLE, 128), 0)
    table = jnp.where(line == 0, own >> 7, jnp.where(line == 1, own & 127, 0))
    table = table.astype(jnp.float32).astype(jnp.bfloat16)
    for plane in range(planes):
        partial_ref[plane, shards * cells : shards * cells + TABLE] = table

    for block in range(0, blocks, 2):
        chosen = []
        for side in range(2):
            at = slice((block + side) * TB, (block + side + 1) * TB)
            column = []
            for line in range(wire_blocks):
                tile = signal_ref[line * block_wires : (line + 1) * block_wires, at]
                asked = plan_ref[2, line * blocks + block + side] == 1
                column.append(jnp.where(asked, tile, jnp.zeros_like(tile)))
            chosen.append(jnp.concatenate(column, axis=0))
        sums = jnp.dot(
            turned_ref[...], jnp.concatenate(chosen, axis=1), preferred_element_type=jnp.float32
        ).astype(jnp.bfloat16)
        for side in range(2):
            shard, plane = divmod(block + side, planes)
            partial_ref[plane, shard * cells : (shard + 1) * cells] = sums[
                :, side * TB : (side + 1) * TB
            ]


def convolve_edges(
    planes, plan, own, inner, raw, mask, left, right, top, bottom, bands, geometry
):
    wires, ticks = raw.shape
    reach = bands.shape[0]
    cells = geometry.shape[2]
    blocks = ticks // TB
    pitch = -(-(blocks + 2) // 8) * 8
    flops = 2 * blocks * PAD * reach * 6 * TB * 2 * TB
    return pl.pallas_call(
        functools.partial(edge_kernel, planes),
        out_shape=(
            jax.ShapeDtypeStruct((wires, ticks), jnp.bfloat16),
            jax.ShapeDtypeStruct((planes, blocks // planes * cells + TABLE, TB), jnp.bfloat16),
        ),
        in_specs=[smem()] + [vmem()] * 10,
        out_specs=(vmem(), vmem()),
        scratch_shapes=[
            pltpu.VMEM((2, 3 * PAD * pitch, TB), jnp.float32),
            pltpu.VMEM((2, PAD // 2 + reach - 1, blocks, 6 * TB), jnp.bfloat16),
            pltpu.VMEM((2, PAD * blocks, TB), jnp.float32),
            pltpu.VMEM((cells, wires), jnp.bfloat16),
        ],
        cost_estimate=pl.CostEstimate(flops=flops, bytes_accessed=6 * MIB, transcendentals=0),
        compiler_params=pltpu.CompilerParams(vmem_limit_bytes=24 * MIB),
        name="edges",
    )(plan, own, inner, raw, mask, left, right, top, bottom, bands, geometry)


def fold_kernel(pieces_ref, out_ref):
    planes, height, _ = pieces_ref.shape
    shards, lines, _ = out_ref.shape
    cells = lines - TABLE
    line = lax.broadcasted_iota(jnp.int32, (TABLE, 128), 0)
    table = jnp.zeros((TABLE, 128), jnp.float32)
    for plane in range(planes):
        tags = pieces_ref[plane, height - TABLE : height].astype(jnp.float32)
        table = jnp.where(line == 2 * plane, tags[0:1], table)
        table = jnp.where(line == 2 * plane + 1, tags[1:2], table)
    for shard in range(shards):
        total = pieces_ref[0, shard * cells : (shard + 1) * cells].astype(jnp.float32)
        for plane in range(1, planes):
            total = total + pieces_ref[plane, shard * cells : (shard + 1) * cells].astype(
                jnp.float32
            )
        out_ref[shard, 0:cells] = total.astype(jnp.bfloat16)
        out_ref[shard, cells:lines] = table.astype(jnp.bfloat16)


def fold(pieces, shards):
    cells = (pieces.shape[1] - TABLE) // shards
    return pl.pallas_call(
        fold_kernel,
        out_shape=jax.ShapeDtypeStruct((shards, cells + TABLE, TB), jnp.bfloat16),
        in_specs=[vmem()],
        out_specs=vmem(),
        compiler_params=pltpu.CompilerParams(vmem_limit_bytes=4 * MIB),
        name="fold",
    )(pieces)


def place_kernel(share, plan_ref, pieces_ref, payload_in, payload_ref, sums_ref, sem):
    shards, lines, _ = pieces_ref.shape
    cells = lines - TABLE
    total = pieces_ref[0, 0:cells].astype(jnp.float32)
    for shard in range(1, shards):
        total = total + pieces_ref[shard, 0:cells].astype(jnp.float32)
    sums_ref[...] = total.astype(jnp.bfloat16).reshape(sums_ref.shape)
    hot = plan_ref[1, 0]
    copy = pltpu.make_async_copy(
        sums_ref, payload_ref.at[pl.ds(hot * share, sums_ref.shape[0])], sem
    )
    copy.start()
    copy.wait()


def place_sums(plan, pieces, payload, share):
    cells = pieces.shape[1] - TABLE
    block_wires = payload.shape[1]
    return pl.pallas_call(
        functools.partial(place_kernel, share),
        out_shape=jax.ShapeDtypeStruct(payload.shape, payload.dtype),
        in_specs=[smem(), vmem(), pl.BlockSpec(memory_space=pl.ANY)],
        out_specs=pl.BlockSpec(memory_space=pl.ANY),
        scratch_shapes=[
            pltpu.VMEM((cells // block_wires, block_wires, TB), jnp.bfloat16),
            pltpu.SemaphoreType.DMA,
        ],
        input_output_aliases={2: 0},
        compiler_params=pltpu.CompilerParams(vmem_limit_bytes=4 * MIB),
        name="place",
    )(plan, pieces, payload)


def pack_kernel(slots, plan_ref, signal_ref, payload_ref, tiles_ref):
    block_wires = payload_ref.shape[1]
    wires, ticks = signal_ref.shape
    blocks = ticks // TB
    tiles_ref[...] = jnp.zeros_like(tiles_ref)
    for line in range(wires // block_wires):
        for block in range(blocks):
            place = plan_ref[0, line * blocks + block]
            tiles_ref[place] = signal_ref[
                line * block_wires : (line + 1) * block_wires, block * TB : (block + 1) * TB
            ]
    payload_ref[...] = tiles_ref[0:slots]


def pack_tiles(plan, signal, slots, block_wires):
    return pl.pallas_call(
        functools.partial(pack_kernel, slots),
        out_shape=jax.ShapeDtypeStruct((slots, block_wires, TB), jnp.bfloat16),
        in_specs=[smem(), vmem()],
        out_specs=vmem(),
        scratch_shapes=[pltpu.VMEM((slots + 1, block_wires, TB), jnp.bfloat16)],
        cost_estimate=pl.CostEstimate(flops=10**8, bytes_accessed=3 * MIB, transcendentals=0),
        compiler_params=pltpu.CompilerParams(vmem_limit_bytes=8 * MIB),
        name="pack",
    )(plan, signal)


def stage_kernel(slots, plan_ref, geo_ref, out_ref, rows_ref):
    groups = out_ref.shape[0]
    rows_ref[...] = jnp.zeros_like(rows_ref)
    for slot in range(slots):
        rows_ref[plan_ref[0, slot]] = geo_ref[plan_ref[2, slot]]
    for group in range(groups):
        rows = rows_ref[group * GROUP : (group + 1) * GROUP]
        out_ref[group] = jnp.transpose(rows.reshape(-1, rows.shape[-1]))


def stage_geometry(plan, geometry, groups, slots):
    _, block_wires, cells = geometry.shape
    return pl.pallas_call(
        functools.partial(stage_kernel, slots),
        out_shape=jax.ShapeDtypeStruct((groups, cells, GROUP * block_wires), jnp.bfloat16),
        in_specs=[smem(), vmem()],
        out_specs=vmem(),
        scratch_shapes=[pltpu.VMEM((groups * GROUP + 1, block_wires, cells), jnp.bfloat16)],
        cost_estimate=pl.CostEstimate(flops=10**8, bytes_accessed=3 * MIB, transcendentals=0),
        compiler_params=pltpu.CompilerParams(vmem_limit_bytes=12 * MIB),
        name="stage",
    )(plan, geometry)


def image_kernel(owner_total, share, plan_ref, arrived_ref, staged_ref, image_ref, tiles_ref):
    cells, ticks = image_ref.shape
    block_wires = arrived_ref.shape[1]
    groups = staged_ref.shape[0]
    is_hot = plan_ref[1, 0] == plan_ref[1, 2]
    counts = plan_ref[1, 3] == 1

    @pl.when(is_hot)
    def _():
        for source in range(owner_total):
            sums = arrived_ref[source * share : source * share + cells // block_wires]
            image_ref[:, source * TB : (source + 1) * TB] = sums.reshape(cells, TB).astype(
                jnp.float32
            )

    @pl.when(jnp.logical_not(is_hot))
    def _():
        image_ref[...] = jnp.zeros_like(image_ref)
        tiles_ref[...] = jnp.zeros_like(tiles_ref)

        @pl.when(counts)
        def _():
            for slot in range(owner_total * share):
                tiles_ref[plan_ref[0, slot]] = arrived_ref[slot]
            for group in range(groups):
                tiles = tiles_ref[group * GROUP : (group + 1) * GROUP]
                at = pl.ds(pl.multiple_of(plan_ref[3, group] * TB, TB), TB)
                image_ref[:, at] += jnp.dot(
                    staged_ref[group],
                    tiles.reshape(GROUP * block_wires, TB),
                    preferred_element_type=jnp.float32,
                )


def make_image(plan, arrived, staged, owner_total, share, ticks):
    groups, cells, _ = staged.shape
    block_wires = arrived.shape[1]
    return pl.pallas_call(
        functools.partial(image_kernel, owner_total, share),
        out_shape=jax.ShapeDtypeStruct((cells, ticks), jnp.float32),
        in_specs=[smem(), vmem(), vmem()],
        out_specs=vmem(),
        scratch_shapes=[
            pltpu.VMEM((groups * GROUP + 1, block_wires, TB), jnp.bfloat16),
        ],
        cost_estimate=pl.CostEstimate(flops=10**8, bytes_accessed=3 * MIB, transcendentals=0),
        compiler_params=pltpu.CompilerParams(vmem_limit_bytes=16 * MIB),
        name="image",
    )(plan, arrived, staged)


def more_kernel(owner_total, planes, share, plan_ref, table_ref, arrived_ref, geo_ref, before_ref, image_ref):
    cells, ticks = image_ref.shape
    blocks = ticks // TB
    wire_blocks = geo_ref.shape[0] // owner_total
    image_ref[...] = before_ref[...]

    @pl.when(plan_ref[1, 0] != plan_ref[1, 2])
    def _():
        def add(source, carry):
            for slot in range(share):
                block = table_ref[source, slot]
                at = pl.multiple_of((block % blocks) * TB, TB)
                image_ref[:, pl.ds(at, TB)] += lax.dot_general(
                    geo_ref[home(source, planes, owner_total) * wire_blocks + block // blocks],
                    arrived_ref[source * share + slot],
                    (((0,), (0,)), ((), ())),
                    preferred_element_type=jnp.float32,
                )
            return carry

        lax.fori_loop(0, owner_total, add, 0)


def add_to_image(plan, table, arrived, geometry, owner_total, planes, share, image):
    return pl.pallas_call(
        functools.partial(more_kernel, owner_total, planes, share),
        out_shape=jax.ShapeDtypeStruct(image.shape, jnp.float32),
        in_specs=[smem(), smem()] + [vmem()] * 3,
        out_specs=vmem(),
        compiler_params=pltpu.CompilerParams(vmem_limit_bytes=16 * MIB),
        name="image_more",
    )(plan, table, arrived, geometry, image)


def further_round(
    trip, image, signal, geometry, rows, packed, plan, owner_total, planes, share
):
    trip, signal, rows, packed, plan = lax.optimization_barrier((trip, signal, rows, packed, plan))
    step = trip + plan[1, 3]
    hot = plan[1, 0]
    me = plan[1, 2]
    block_wires = geometry.shape[1]
    wire_count, tick_count = signal.shape
    blocks = tick_count // TB
    wire_blocks = wire_count // block_wires
    ids = jnp.arange(owner_total, dtype=jnp.int32)

    def ranks(owners):
        member = (owners[..., None] == ids).astype(jnp.int32)
        before = jnp.cumsum(member, axis=-2) - member
        return jnp.sum(before * member, axis=-1) - step * share

    def live(owners, rank):
        return (owners < owner_total) & (owners != hot) & (rank >= 0) & (rank < share)

    owners = packed[0] >> 7
    block = packed[0] & 127
    rank = ranks(owners)
    place = jnp.where(live(owners, rank), owners * share + rank, owner_total * share)
    tiles = signal.reshape(wire_blocks, block_wires, blocks, TB).transpose(0, 2, 1, 3)
    tiles = tiles.reshape(wire_blocks * blocks, block_wires, TB)[block]
    payload = jnp.zeros((owner_total * share, block_wires, TB), jnp.bfloat16)
    payload = payload.at[place].set(tiles, mode="drop")
    arrived = exchange(payload.reshape(owner_total, share, block_wires, TB))

    owners = rows >> 7
    rank = ranks(owners)
    source = jnp.arange(owner_total, dtype=jnp.int32)[:, None]
    line = jnp.where(live(owners, rank) & (owners == me), source, owner_total)
    table = jnp.zeros((owner_total, 128), jnp.int32)
    table = table.at[line, jnp.maximum(rank, 0)].set(rows & 127, mode="drop")
    return add_to_image(
        plan,
        table,
        arrived.reshape(owner_total * share, block_wires, TB),
        geometry,
        owner_total,
        planes,
        share,
        image,
    )


def tick_halo(sides):
    devices = lax.axis_size("tick")
    if devices == 2:
        tick = lax.axis_index("tick")
        got = lax.ppermute(sides[0], "tick", [(0, 1), (1, 0)])
        nothing = jnp.zeros_like(got)
        return jnp.where(tick == 0, nothing, got), jnp.where(tick == 0, got, nothing)
    up = [(i, i + 1) for i in range(devices - 1)]
    down = [(i + 1, i) for i in range(devices - 1)]
    return lax.ppermute(sides[1], "tick", up), lax.ppermute(sides[0], "tick", down)


def wire_halo(first, last, left, right):
    devices = lax.axis_size("wire")
    up = [(i, i + 1) for i in range(devices - 1)]
    down = [(i + 1, i) for i in range(devices - 1)]
    last = jnp.concatenate([left[-PAD:], last, right[-PAD:]], axis=1)
    first = jnp.concatenate([left[:PAD], first, right[:PAD]], axis=1)
    return lax.ppermute(last, "wire", up), lax.ppermute(first, "wire", down)


def exchange(array, axes=("wire", "plane")):
    return lax.all_to_all(array, axes, split_axis=0, concat_axis=0, tiled=True)


def shards(raw, chan_mask, kernel, geometry, roi_block, roi_owner):
    wires, ticks = raw.shape
    slot_count = roi_block.shape[0]
    block_wires = geometry.shape[1]
    cells = geometry.shape[2]
    tick_blocks = ticks // TB
    planes = lax.axis_size("plane")
    wire_shards = lax.axis_size("wire")
    owner_total = planes * wire_shards
    share = -(-(slot_count - CAP) // (owner_total - 1))

    mask, first, last, packed, send_plan, *sides = prepare(
        raw, chan_mask, roi_owner, roi_block, planes, owner_total, share
    )
    left, right = tick_halo(sides)
    top, bottom = wire_halo(first, last, left, right)
    bands = make_bands(kernel[0])
    inner = convolve_inner(raw, mask, left, right, bands)
    signal, partial = convolve_edges(
        planes, send_plan, packed, inner, raw, mask, left, right, top, bottom, bands, geometry
    )

    pieces = exchange(partial, "plane")
    payload = pack_tiles(send_plan, signal, owner_total * share, block_wires)
    pieces, payload = lax.optimization_barrier((pieces, payload))
    pieces = exchange(fold(pieces, wire_shards), "wire")

    tables = pieces[:, cells : cells + 2 * planes].astype(jnp.int32)
    tables = tables.reshape(owner_total, 2, 128)
    rows = tables[:, 0] * 128 + tables[:, 1]
    plan = make_receive_plan(
        rows, packed, owner_total, planes, share, wires // block_wires, tick_blocks
    )
    staged = stage_geometry(
        plan, geometry, group_total(owner_total, share, tick_blocks), owner_total * share
    )

    payload = place_sums(send_plan, pieces, payload, share)
    payload = payload.reshape(owner_total, share, block_wires, TB)
    arrived = exchange(payload).reshape(owner_total * share, block_wires, TB)
    image = make_image(plan, arrived, staged, owner_total, share, ticks)

    trips = agree(plan[1:2, 1:2])[0, 0]
    image = lax.fori_loop(
        0,
        trips,
        lambda trip, now: further_round(
            trip, now, signal, geometry, rows, packed, plan, owner_total, planes, share
        ),
        image,
    )
    return signal, image


def solution(mesh):
    in_specs = (
        P(("plane", "wire"), "tick"),
        P(("plane", "wire")),
        P("plane", None, None),
        P(),
        P(("plane", "wire", "tick")),
        P(("plane", "wire", "tick")),
    )
    out_specs = (P(("plane", "wire"), "tick"), P(("plane", "wire"), "tick"))
    return jax.shard_map(shards, mesh=mesh, in_specs=in_specs, out_specs=out_specs, check_vma=False)
```

```python
import functools

import jax
import jax.numpy as jnp
from jax import lax
from jax.experimental import pallas as pl
from jax.experimental.pallas import tpu as pltpu
from jax.sharding import PartitionSpec as P

TB = 128
CAP = 25
PAD = 16
TABLE = 8
MIB = 1024 * 1024


def vmem():
    return pl.BlockSpec(memory_space=pltpu.VMEM)


def smem():
    return pl.BlockSpec(memory_space=pltpu.SMEM)


GROUP = 8


def home(position, planes, owner_total):
    return (position % planes) * (owner_total // planes) + position // planes


def lane_numbers():
    return lax.broadcasted_iota(jnp.int32, (1, 128), 1)


def earlier_lanes():
    return (
        lax.broadcasted_iota(jnp.int32, (128, 128), 0)
        < lax.broadcasted_iota(jnp.int32, (128, 128), 1)
    ).astype(jnp.bfloat16)


def count_before(member, before):
    return jnp.dot(
        member.astype(jnp.float32).astype(jnp.bfloat16), before, preferred_element_type=jnp.float32
    )


def most_named(owners, owner_total):
    lanes = lane_numbers()
    counts = jnp.full(owners.shape, -1.0, jnp.float32)
    for owner in range(owner_total):
        named = jnp.sum((owners == owner).astype(jnp.float32), axis=1, keepdims=True)
        counts = jnp.where(lanes == owner, named, counts)
    top = jnp.max(counts, axis=1, keepdims=True)
    chosen = jnp.min(
        jnp.where(counts == top, lanes.astype(jnp.float32), 127.0), axis=1, keepdims=True
    )
    return counts, chosen


def prepare_kernel(
    planes,
    owner_total,
    share,
    tick_total,
    raw_hbm,
    mask_hbm,
    owner_hbm,
    block_hbm,
    mask_out,
    first_ref,
    last_ref,
    own_ref,
    out_ref,
    *rest,
):
    wires, ticks = raw_hbm.shape
    count = 1 if tick_total == 2 else 2
    sides = rest[:count]
    side_refs = rest[count : 2 * count]
    first_buf, last_buf, mask_ref, owner_ref, block_ref, sems = rest[2 * count :]
    tick = lax.axis_index("tick")
    me = lax.axis_index("wire") * planes + lax.axis_index("plane")
    if tick_total == 2:
        starts = [pl.multiple_of((1 - tick) * (ticks - TB), TB)]
    else:
        starts = [0, ticks - TB]
    moves = [(mask_hbm, mask_ref), (owner_hbm, owner_ref), (block_hbm, block_ref)]
    moves += [(raw_hbm.at[:, pl.ds(start, TB)], ref) for start, ref in zip(starts, side_refs)]
    moves += [(raw_hbm.at[pl.ds(0, PAD)], first_buf), (raw_hbm.at[pl.ds(wires - PAD, PAD)], last_buf)]
    copies = [
        pltpu.make_async_copy(source, target, sems.at[index])
        for index, (source, target) in enumerate(moves)
    ]
    for copy in copies:
        copy.start()
    for copy in copies[:3]:
        copy.wait()

    for part in range(wires // 128):
        row = mask_ref[part : part + 1].astype(jnp.float32)
        wide = jnp.transpose(jnp.broadcast_to(row, (128, 128)))
        mask_out[part * 128 : (part + 1) * 128] = wide.astype(jnp.bfloat16)

    lanes = lane_numbers()
    slot_count = owner_ref.shape[1]
    owner = owner_ref[...]
    wire_shards = owner_total // planes
    none = owner_total * 128
    own_ref[...] = jnp.where(lanes == 127, none + me, none)
    own_ref[:, 0:slot_count] = (
        (owner % wire_shards) * planes + owner // wire_shards
    ) * 128 + block_ref[...]
    own = own_ref[...]
    _, hot = most_named(own >> 7, owner_total)
    rows = lax.broadcasted_iota(jnp.int32, (owner_total, 128), 0)
    member = (own >> 7) == rows
    rank = count_before(member, earlier_lanes())
    place = jnp.where(rank < share, rows.astype(jnp.float32) * share + rank, -1.0)
    place = jnp.where(rows.astype(jnp.float32) == hot, -2.0, place)
    place = jnp.sum(jnp.where(member, place + 3.0, 0.0), axis=0, keepdims=True)

    column = jnp.transpose(jnp.broadcast_to(own.astype(jnp.float32), (128, 128)))
    column = column.astype(jnp.int32)
    here = ((column & 127) == lanes) & ((column >> 7) < owner_total)
    spread = jnp.transpose(jnp.broadcast_to(place, (128, 128)))
    placed = jnp.sum(jnp.where(here, spread, 0.0), axis=0, keepdims=True)
    trash = float(owner_total * share)
    facts = jnp.where(lanes == 2, me, 0)
    out_ref[...] = jnp.zeros_like(out_ref)
    out_ref[0:1, :] = jnp.where(placed >= 3.0, placed - 3.0, trash).astype(jnp.int32)
    out_ref[1:2, :] = jnp.where(lanes == 0, hot.astype(jnp.int32), facts)
    out_ref[2:3, :] = (placed == 1.0).astype(jnp.int32)

    for copy in copies[3:]:
        copy.wait()
    for side, ref in zip(sides, side_refs):
        side[...] = ref[...] * mask_out[...]
    for block in range(ticks // TB):
        at = slice(block * TB, (block + 1) * TB)
        first_ref[:, at] = first_buf[:, at] * mask_out[0:PAD]
        last_ref[:, at] = last_buf[:, at] * mask_out[wires - PAD : wires]


def prepare(raw, chan_mask, roi_owner, roi_block, planes, owner_total, share):
    wires, ticks = raw.shape
    tick_total = lax.axis_size("tick")
    sides = 1 if tick_total == 2 else 2
    side = jax.ShapeDtypeStruct((wires, TB), jnp.bfloat16)
    edge = jax.ShapeDtypeStruct((PAD, ticks), jnp.bfloat16)
    row = jax.ShapeDtypeStruct((1, 128), jnp.int32)
    table = jax.ShapeDtypeStruct((8, 128), jnp.int32)
    slot_count = roi_owner.shape[0]
    return pl.pallas_call(
        functools.partial(prepare_kernel, planes, owner_total, share, tick_total),
        out_shape=(side, edge, edge, row, table) + (side,) * sides,
        in_specs=[pl.BlockSpec(memory_space=pltpu.HBM)] * 4,
        out_specs=(vmem(),) * (5 + sides),
        scratch_shapes=[pltpu.VMEM((wires, TB), jnp.bfloat16)] * sides
        + [pltpu.VMEM((PAD, ticks), jnp.bfloat16)] * 2
        + [pltpu.VMEM((wires // 128, 128), jnp.int32)]
        + [pltpu.VMEM((1, slot_count), jnp.int32)] * 2
        + [pltpu.SemaphoreType.DMA((sides + 5,))],
        compiler_params=pltpu.CompilerParams(vmem_limit_bytes=60 * MIB),
        name="prepare",
    )(raw, chan_mask.reshape(wires // 128, 128), roi_owner[None], roi_block[None])


def receive_kernel(owner_total, planes, share, wire_blocks, tick_blocks, rows_ref, own_ref, out_ref):
    lanes = lane_numbers()
    lane_f = lanes.astype(jnp.float32)
    every = rows_ref[...]
    owners = every >> 7
    own = own_ref[...]
    me = jnp.sum(jnp.where(lanes == 127, own & 127, 0).astype(jnp.float32), axis=1, keepdims=True)

    counts, chosen = most_named(owners, owner_total)
    hot = jnp.max(chosen, axis=0, keepdims=True)
    agreed = hot == jnp.min(chosen, axis=0, keepdims=True)
    left = jnp.where(agreed & (lane_f == hot), 0.0, counts)
    fullest = jnp.max(jnp.max(left, axis=1, keepdims=True), axis=0, keepdims=True)
    start = agreed.astype(jnp.float32)
    trips = -start
    for step in range(-(-CAP // share)):
        trips = trips + (fullest > step * share).astype(jnp.float32)
    trips = jnp.maximum(trips, 0.0)
    hot = jnp.where(agreed, hot, -1.0)

    to_me = owners.astype(jnp.float32) == me
    before = earlier_lanes()
    rank = count_before(to_me, before)
    blocks = every & 127
    source = lax.broadcasted_iota(jnp.int32, (owner_total, 128), 0)
    line = home(source, planes, owner_total) * wire_blocks + blocks // tick_blocks
    line = line.astype(jnp.float32)
    tick = (blocks % tick_blocks).astype(jnp.float32)
    lines = jnp.zeros((1, 128), jnp.float32)
    ticks = jnp.full((1, 128), -1.0, jnp.float32)
    for slot in range(share):
        got = to_me & (rank == slot)
        here = lanes == source * share + slot
        for value, where in ((line, 0), (tick + 1.0, 1)):
            one = jnp.sum(jnp.where(got, value, 0.0), axis=1, keepdims=True)
            one = jnp.sum(jnp.where(here, one, 0.0), axis=0, keepdims=True)
            if where == 0:
                lines = lines + one
            else:
                ticks = ticks + one

    block_rows = lax.broadcasted_iota(jnp.int32, (tick_blocks, 128), 0).astype(jnp.float32)
    member = block_rows == ticks
    rank = count_before(member, before)
    total = jnp.sum(member.astype(jnp.float32), axis=1, keepdims=True)
    groups = jnp.zeros_like(total)
    for step in range(0, owner_total * share, GROUP):
        groups = groups + (total > step).astype(jnp.float32)
    lower = (
        lax.broadcasted_iota(jnp.int32, (tick_blocks, tick_blocks), 0)
        > lax.broadcasted_iota(jnp.int32, (tick_blocks, tick_blocks), 1)
    ).astype(jnp.bfloat16)
    base = jnp.dot(
        lower,
        jnp.broadcast_to(groups, (tick_blocks, 128)).astype(jnp.bfloat16),
        preferred_element_type=jnp.float32,
    )
    place = jnp.sum(jnp.where(member, base * GROUP + rank, 0.0), axis=0, keepdims=True)
    trash = float(group_total(owner_total, share, tick_blocks) * GROUP)
    place = jnp.where(ticks < 0.0, trash, place)
    inside = (base <= lane_f) & (lane_f < base + groups)
    group_tick = jnp.sum(jnp.where(inside, block_rows, 0.0), axis=0, keepdims=True)

    facts = jnp.where(lanes == 0, hot, 0.0)
    facts = jnp.where(lanes == 1, trips, facts)
    facts = jnp.where(lanes == 2, me, facts)
    facts = jnp.where(lanes == 3, start, facts)
    out_ref[...] = jnp.zeros_like(out_ref)
    out_ref[0:1, :] = place.astype(jnp.int32)
    out_ref[1:2, :] = facts.astype(jnp.int32)
    out_ref[2:3, :] = lines.astype(jnp.int32)
    out_ref[3:4, :] = group_tick.astype(jnp.int32)


def group_total(owner_total, share, tick_blocks):
    return (owner_total * share - tick_blocks) // GROUP + tick_blocks


def make_receive_plan(rows, packed, owner_total, planes, share, wire_blocks, tick_blocks):
    return pl.pallas_call(
        functools.partial(receive_kernel, owner_total, planes, share, wire_blocks, tick_blocks),
        out_shape=jax.ShapeDtypeStruct((8, 128), jnp.int32),
        in_specs=[vmem(), vmem()],
        out_specs=vmem(),
        compiler_params=pltpu.CompilerParams(vmem_limit_bytes=2 * MIB),
        name="receive_plan",
    )(rows, packed)


def agree(rounds):
    devices = lax.axis_size("tick")
    reach = 1
    while reach < devices:
        ring = [(i, (i + reach) % devices) for i in range(devices)]
        rounds = jnp.maximum(rounds, lax.ppermute(rounds, "tick", ring))
        reach *= 2
    return rounds


def clear_bands(band_ref):
    pairs = band_ref.shape[0]
    band_ref[0, 0 : 3 * TB, TB : 2 * TB] = jnp.zeros((3 * TB, TB), jnp.bfloat16)
    band_ref[pairs - 1, 3 * TB : 6 * TB, 0:TB] = jnp.zeros((3 * TB, TB), jnp.bfloat16)


def build_bands(tap, taps_ref, band_ref):
    row = lax.broadcasted_iota(jnp.int32, (TB, TB), 0)
    col = lax.broadcasted_iota(jnp.int32, (TB, TB), 1)
    line = taps_ref[tap : tap + 1].astype(jnp.float32)
    rolled = pltpu.roll(jnp.broadcast_to(line, (TB, 2 * TB)), TB, 1, stride=1, stride_axis=0)
    middle = rolled[:, :TB]
    outer = rolled[:, TB:]
    bands = (
        jnp.where(col < row, outer, 0.0).astype(jnp.bfloat16),
        middle.astype(jnp.bfloat16),
        jnp.where(col >= row, outer, 0.0).astype(jnp.bfloat16),
    )
    for first, second in ((0, 0), (1, 1), (1, 0), (0, 1)):
        if (tap - first + second) % 2:
            continue
        pair = (tap - first + second) // 2
        for piece in range(3):
            start = (first * 3 + piece) * TB
            band_ref[pair, start : start + TB, second * TB : (second + 1) * TB] = bands[piece]


def spread_pair(wide_ref, lhs_view, line, pitch, blocks):
    for side in range(2):
        for piece in range(3):
            at = (side * 3 + piece) * TB
            lhs_view[:, at : at + TB] = wide_ref[
                pl.ds((line + side) * pitch + piece, blocks), :
            ].astype(jnp.bfloat16)


def write_lines(total, out_view, signal_ref, line, pairs, blocks):
    for pair in range(pairs):
        for side in range(2):
            out_view[pl.ds((2 * pair + side) * blocks, blocks), :] = total[
                pair * blocks : (pair + 1) * blocks, side * TB : (side + 1) * TB
            ]
    for block in range(blocks):
        signal_ref[line : line + 2 * pairs, block * TB : (block + 1) * TB] = out_view[
            pl.ds(block, 2 * pairs, stride=blocks), :
        ].astype(jnp.bfloat16)


def inner_kernel(
    chunks,
    raw_ref,
    mask_ref,
    left_ref,
    right_ref,
    taps_ref,
    inner_ref,
    band_ref,
    wide_ref,
    lhs_ref,
    out_ref,
):
    wires, ticks = raw_ref.shape
    blocks = ticks // TB
    pitch = wide_ref.shape[0] // wires
    reach = band_ref.shape[0]
    span = 2 * PAD
    groups = wires // span

    def fill(group, block):
        lines = slice(group * span, (group + 1) * span)
        if block == 0:
            inner = left_ref[lines]
        elif block == blocks + 1:
            inner = right_ref[lines]
        else:
            inner = raw_ref[lines, (block - 1) * TB : block * TB] * mask_ref[lines]
        wide_ref[pl.ds(group * span * pitch + block, span, stride=pitch), :] = inner.astype(
            jnp.float32
        )

    margin = reach - 1
    begin = PAD // 2
    state = {"group": 0, "pair": begin}

    def prepare(upto):
        todo = []
        while state["pair"] < upto:
            line = 2 * state["pair"] - margin
            while state["group"] < groups and line + 1 >= state["group"] * span:
                group = state["group"]
                for block in range(blocks + 2):
                    todo.append(lambda group=group, block=block: fill(group, block))
                state["group"] += 1
            todo.append(
                lambda line=line, pair=state["pair"]: spread_pair(
                    wide_ref, lhs_ref.at[pair - begin], line, pitch, blocks
                )
            )
            state["pair"] += 1
        return todo

    pair = begin
    taps_done = 0
    clear_bands(band_ref)
    for job in prepare(pair + chunks[0] + margin):
        job()
    for index, size in enumerate(chunks):
        todo = prepare(pair + size + chunks[index + 1] + margin) if index + 1 < len(chunks) else []
        each = -(-len(todo) // reach)
        total = jnp.zeros((size * blocks, 2 * TB), jnp.float32)
        for step in range(reach):
            while taps_done < min(2 * step + 2, taps_ref.shape[0]):
                build_bands(taps_done, taps_ref, band_ref)
                taps_done += 1
            rows = lhs_ref[pair - begin + step : pair - begin + step + size]
            total = total + jnp.dot(
                rows.reshape(size * blocks, 6 * TB), band_ref[step], preferred_element_type=jnp.float32
            )
            for job in todo[step * each : (step + 1) * each]:
                job()
        write_lines(total, out_ref.at[index % 2], inner_ref, 2 * (pair - begin), size, blocks)
        pair += size


def convolve_inner(raw, mask, left, right, taps):
    wires, ticks = raw.shape
    reach = (taps.shape[0] + 1) // 2
    blocks = ticks // TB
    pitch = -(-(blocks + 2) // 8) * 8
    pairs = (wires - 2 * PAD) // 2
    chunks = []
    while sum(chunks) < pairs:
        chunks.append(min(32 if chunks else 16, pairs - sum(chunks)))
    flops = 2 * blocks * pairs * reach * 6 * TB * 2 * TB
    return pl.pallas_call(
        functools.partial(inner_kernel, tuple(chunks)),
        out_shape=(
            jax.ShapeDtypeStruct((wires - 2 * PAD, ticks), jnp.bfloat16),
            jax.ShapeDtypeStruct((reach, 6 * TB, 2 * TB), jnp.bfloat16),
        ),
        in_specs=[vmem()] * 5,
        out_specs=(vmem(), vmem()),
        scratch_shapes=[
            pltpu.VMEM((wires * pitch, TB), jnp.float32),
            pltpu.VMEM((pairs + reach - 1, blocks, 6 * TB), jnp.bfloat16),
            pltpu.VMEM((2, 2 * max(chunks) * blocks, TB), jnp.float32),
        ],
        cost_estimate=pl.CostEstimate(flops=flops, bytes_accessed=6 * MIB, transcendentals=0),
        compiler_params=pltpu.CompilerParams(vmem_limit_bytes=28 * MIB),
        name="inner",
    )(raw, mask, left, right, taps)


def edge_kernel(
    planes,
    plan_ref,
    own_ref,
    inner_ref,
    raw_ref,
    mask_ref,
    left_ref,
    right_ref,
    halo_ref,
    band_ref,
    geo_ref,
    signal_ref,
    partial_ref,
    wide_ref,
    lhs_ref,
    out_ref,
    turned_ref,
):
    wires, ticks = signal_ref.shape
    blocks = ticks // TB
    reach = band_ref.shape[0]
    block_wires = geo_ref.shape[1]
    wire_blocks = wires // block_wires
    near = 2 * PAD
    lines = PAD + near
    pitch = wide_ref.shape[1] // lines
    pairs = PAD // 2
    margin = reach - 1

    signal_ref[PAD : wires - PAD] = inner_ref[...]
    source = home(plan_ref[1, 2], planes, geo_ref.shape[0] // wire_blocks)
    rows = geo_ref[pl.ds(source * wire_blocks, wire_blocks)].reshape(wires, -1)
    turned_ref[...] = jnp.transpose(rows)

    for end in range(2):
        shard = lax.axis_index("wire")
        other = (shard - 1, shard + 1)[end]
        there = (other >= 0) & (other < halo_ref.shape[0])
        halo = halo_ref.at[jnp.where(there, other, shard)]
        mine = (slice(0, near), slice(wires - near, wires))[end]
        halo_at = (0, near)[end]
        mine_at = (PAD, 0)[end]
        for block in range(blocks + 2):
            columns = slice(block * TB, (block + 1) * TB)
            if block == 0:
                inner = left_ref[mine].astype(jnp.float32)
            elif block == blocks + 1:
                inner = right_ref[mine].astype(jnp.float32)
            else:
                inner = raw_ref[mine, (block - 1) * TB : block * TB] * mask_ref[mine]
                inner = inner.astype(jnp.float32)
            outer = halo[:, columns].astype(jnp.float32)
            wide_ref[end, pl.ds(halo_at * pitch + block, PAD, stride=pitch), :] = jnp.where(
                there, outer, jnp.zeros_like(outer)
            )
            wide_ref[end, pl.ds(mine_at * pitch + block, near, stride=pitch), :] = inner
        first = (PAD, near - PAD)[end] - margin
        for pair in range(pairs + margin):
            spread_pair(
                wide_ref.at[end], lhs_ref.at[end, pair], first + 2 * pair, pitch, blocks
            )

    total = jnp.zeros((2 * pairs * blocks, 2 * TB), jnp.float32)
    for step in range(reach):
        rows = jnp.concatenate(
            [
                lhs_ref[end, step : step + pairs].reshape(pairs * blocks, 6 * TB)
                for end in range(2)
            ],
            axis=0,
        )
        total = total + jnp.dot(rows, band_ref[step], preferred_element_type=jnp.float32)
    for end in range(2):
        write_lines(
            total[end * pairs * blocks : (end + 1) * pairs * blocks],
            out_ref.at[end],
            signal_ref,
            (0, wires - PAD)[end],
            pairs,
            blocks,
        )

    cells = geo_ref.shape[2]
    shards = partial_ref.shape[1] // cells
    own = own_ref[...]
    line = lax.broadcasted_iota(jnp.int32, (TABLE, 128), 0)
    table = jnp.where(line == 0, own >> 7, jnp.where(line == 1, own & 127, 0))
    table = table.astype(jnp.float32).astype(jnp.bfloat16)
    for plane in range(planes):
        partial_ref[plane, shards * cells : shards * cells + TABLE] = table

    for block in range(0, blocks, 2):
        chosen = []
        for side in range(2):
            at = slice((block + side) * TB, (block + side + 1) * TB)
            column = []
            for line in range(wire_blocks):
                tile = signal_ref[line * block_wires : (line + 1) * block_wires, at]
                asked = plan_ref[2, line * blocks + block + side] == 1
                column.append(jnp.where(asked, tile, jnp.zeros_like(tile)))
            chosen.append(jnp.concatenate(column, axis=0))
        sums = jnp.dot(
            turned_ref[...], jnp.concatenate(chosen, axis=1), preferred_element_type=jnp.float32
        ).astype(jnp.bfloat16)
        for side in range(2):
            shard, plane = divmod(block + side, planes)
            partial_ref[plane, shard * cells : (shard + 1) * cells] = sums[
                :, side * TB : (side + 1) * TB
            ]


def convolve_edges(
    planes, plan, own, inner, raw, mask, left, right, halos, bands, geometry
):
    wires, ticks = raw.shape
    reach = bands.shape[0]
    cells = geometry.shape[2]
    blocks = ticks // TB
    pitch = -(-(blocks + 2) // 8) * 8
    flops = 2 * blocks * PAD * reach * 6 * TB * 2 * TB
    return pl.pallas_call(
        functools.partial(edge_kernel, planes),
        out_shape=(
            jax.ShapeDtypeStruct((wires, ticks), jnp.bfloat16),
            jax.ShapeDtypeStruct((planes, blocks // planes * cells + TABLE, TB), jnp.bfloat16),
        ),
        in_specs=[smem()] + [vmem()] * 9,
        out_specs=(vmem(), vmem()),
        scratch_shapes=[
            pltpu.VMEM((2, 3 * PAD * pitch, TB), jnp.float32),
            pltpu.VMEM((2, PAD // 2 + reach - 1, blocks, 6 * TB), jnp.bfloat16),
            pltpu.VMEM((2, PAD * blocks, TB), jnp.float32),
            pltpu.VMEM((cells, wires), jnp.bfloat16),
        ],
        cost_estimate=pl.CostEstimate(flops=flops, bytes_accessed=6 * MIB, transcendentals=0),
        compiler_params=pltpu.CompilerParams(vmem_limit_bytes=24 * MIB),
        name="edges",
    )(plan, own, inner, raw, mask, left, right, halos, bands, geometry)


def fold_kernel(pieces_ref, out_ref):
    planes, height, _ = pieces_ref.shape
    shards, lines, _ = out_ref.shape
    cells = lines - TABLE
    line = lax.broadcasted_iota(jnp.int32, (TABLE, 128), 0)
    table = jnp.zeros((TABLE, 128), jnp.float32)
    for plane in range(planes):
        tags = pieces_ref[plane, height - TABLE : height].astype(jnp.float32)
        table = jnp.where(line == 2 * plane, tags[0:1], table)
        table = jnp.where(line == 2 * plane + 1, tags[1:2], table)
    for shard in range(shards):
        total = pieces_ref[0, shard * cells : (shard + 1) * cells].astype(jnp.float32)
        for plane in range(1, planes):
            total = total + pieces_ref[plane, shard * cells : (shard + 1) * cells].astype(
                jnp.float32
            )
        out_ref[shard, 0:cells] = total.astype(jnp.bfloat16)
        out_ref[shard, cells:lines] = table.astype(jnp.bfloat16)


def fold(pieces, shards):
    cells = (pieces.shape[1] - TABLE) // shards
    return pl.pallas_call(
        fold_kernel,
        out_shape=jax.ShapeDtypeStruct((shards, cells + TABLE, TB), jnp.bfloat16),
        in_specs=[vmem()],
        out_specs=vmem(),
        compiler_params=pltpu.CompilerParams(vmem_limit_bytes=4 * MIB),
        name="fold",
    )(pieces)


def pack_kernel(slots, plan_ref, signal_ref, payload_ref, tiles_ref):
    block_wires = payload_ref.shape[1]
    wires, ticks = signal_ref.shape
    blocks = ticks // TB
    tiles_ref[...] = jnp.zeros_like(tiles_ref)
    for line in range(wires // block_wires):
        for block in range(blocks):
            place = plan_ref[0, line * blocks + block]
            tiles_ref[place] = signal_ref[
                line * block_wires : (line + 1) * block_wires, block * TB : (block + 1) * TB
            ]
    payload_ref[...] = tiles_ref[0:slots]


def pack_tiles(plan, signal, slots, block_wires):
    return pl.pallas_call(
        functools.partial(pack_kernel, slots),
        out_shape=jax.ShapeDtypeStruct((slots, block_wires, TB), jnp.bfloat16),
        in_specs=[smem(), vmem()],
        out_specs=vmem(),
        scratch_shapes=[pltpu.VMEM((slots + 1, block_wires, TB), jnp.bfloat16)],
        cost_estimate=pl.CostEstimate(flops=10**8, bytes_accessed=3 * MIB, transcendentals=0),
        compiler_params=pltpu.CompilerParams(vmem_limit_bytes=8 * MIB),
        name="pack",
    )(plan, signal)


def stage_kernel(slots, plan_ref, geo_ref, out_ref, rows_ref):
    groups = out_ref.shape[0]
    rows_ref[...] = jnp.zeros_like(rows_ref)
    for slot in range(slots):
        rows_ref[plan_ref[0, slot]] = geo_ref[plan_ref[2, slot]]
    for group in range(groups):
        rows = rows_ref[group * GROUP : (group + 1) * GROUP]
        out_ref[group] = jnp.transpose(rows.reshape(-1, rows.shape[-1]))


def stage_geometry(plan, geometry, groups, slots):
    _, block_wires, cells = geometry.shape
    return pl.pallas_call(
        functools.partial(stage_kernel, slots),
        out_shape=jax.ShapeDtypeStruct((groups, cells, GROUP * block_wires), jnp.bfloat16),
        in_specs=[smem(), vmem()],
        out_specs=vmem(),
        scratch_shapes=[pltpu.VMEM((groups * GROUP + 1, block_wires, cells), jnp.bfloat16)],
        cost_estimate=pl.CostEstimate(flops=10**8, bytes_accessed=3 * MIB, transcendentals=0),
        compiler_params=pltpu.CompilerParams(vmem_limit_bytes=12 * MIB),
        name="stage",
    )(plan, geometry)


def image_kernel(owner_total, share, plan_ref, arrived_ref, staged_ref, image_ref, tiles_ref):
    cells, ticks = image_ref.shape
    block_wires = arrived_ref.shape[1]
    groups = staged_ref.shape[0]
    is_hot = plan_ref[1, 0] == plan_ref[1, 2]
    counts = plan_ref[1, 3] == 1

    @pl.when(is_hot)
    def _():
        for source in range(owner_total):
            sums = arrived_ref[source * share : source * share + cells // block_wires]
            image_ref[:, source * TB : (source + 1) * TB] = sums.reshape(cells, TB).astype(
                jnp.float32
            )

    @pl.when(jnp.logical_not(is_hot))
    def _():
        image_ref[...] = jnp.zeros_like(image_ref)
        tiles_ref[...] = jnp.zeros_like(tiles_ref)

        @pl.when(counts)
        def _():
            for slot in range(owner_total * share):
                tiles_ref[plan_ref[0, slot]] = arrived_ref[slot]
            for group in range(groups):
                tiles = tiles_ref[group * GROUP : (group + 1) * GROUP]
                at = pl.ds(pl.multiple_of(plan_ref[3, group] * TB, TB), TB)
                image_ref[:, at] += jnp.dot(
                    staged_ref[group],
                    tiles.reshape(GROUP * block_wires, TB),
                    preferred_element_type=jnp.float32,
                )


def make_image(plan, arrived, staged, owner_total, share, ticks):
    groups, cells, _ = staged.shape
    block_wires = arrived.shape[1]
    return pl.pallas_call(
        functools.partial(image_kernel, owner_total, share),
        out_shape=jax.ShapeDtypeStruct((cells, ticks), jnp.float32),
        in_specs=[smem(), vmem(), vmem()],
        out_specs=vmem(),
        scratch_shapes=[
            pltpu.VMEM((groups * GROUP + 1, block_wires, TB), jnp.bfloat16),
        ],
        cost_estimate=pl.CostEstimate(flops=10**8, bytes_accessed=3 * MIB, transcendentals=0),
        compiler_params=pltpu.CompilerParams(vmem_limit_bytes=16 * MIB),
        name="image",
    )(plan, arrived, staged)


def more_kernel(owner_total, planes, share, plan_ref, table_ref, arrived_ref, geo_ref, before_ref, image_ref):
    cells, ticks = image_ref.shape
    blocks = ticks // TB
    wire_blocks = geo_ref.shape[0] // owner_total
    image_ref[...] = before_ref[...]

    @pl.when(plan_ref[1, 0] != plan_ref[1, 2])
    def _():
        def add(source, carry):
            for slot in range(share):
                block = table_ref[source, slot]
                at = pl.multiple_of((block % blocks) * TB, TB)
                image_ref[:, pl.ds(at, TB)] += lax.dot_general(
                    geo_ref[home(source, planes, owner_total) * wire_blocks + block // blocks],
                    arrived_ref[source * share + slot],
                    (((0,), (0,)), ((), ())),
                    preferred_element_type=jnp.float32,
                )
            return carry

        lax.fori_loop(0, owner_total, add, 0)


def add_to_image(plan, table, arrived, geometry, owner_total, planes, share, image):
    return pl.pallas_call(
        functools.partial(more_kernel, owner_total, planes, share),
        out_shape=jax.ShapeDtypeStruct(image.shape, jnp.float32),
        in_specs=[smem(), smem()] + [vmem()] * 3,
        out_specs=vmem(),
        compiler_params=pltpu.CompilerParams(vmem_limit_bytes=16 * MIB),
        name="image_more",
    )(plan, table, arrived, geometry, image)


def further_round(
    trip, image, signal, geometry, rows, packed, plan, owner_total, planes, share
):
    trip, signal, rows, packed, plan = lax.optimization_barrier((trip, signal, rows, packed, plan))
    step = trip + plan[1, 3]
    hot = plan[1, 0]
    me = plan[1, 2]
    block_wires = geometry.shape[1]
    wire_count, tick_count = signal.shape
    blocks = tick_count // TB
    wire_blocks = wire_count // block_wires
    ids = jnp.arange(owner_total, dtype=jnp.int32)

    def ranks(owners):
        member = (owners[..., None] == ids).astype(jnp.int32)
        before = jnp.cumsum(member, axis=-2) - member
        return jnp.sum(before * member, axis=-1) - step * share

    def live(owners, rank):
        return (owners < owner_total) & (owners != hot) & (rank >= 0) & (rank < share)

    owners = packed[0] >> 7
    block = packed[0] & 127
    rank = ranks(owners)
    place = jnp.where(live(owners, rank), owners * share + rank, owner_total * share)
    tiles = signal.reshape(wire_blocks, block_wires, blocks, TB).transpose(0, 2, 1, 3)
    tiles = tiles.reshape(wire_blocks * blocks, block_wires, TB)[block]
    payload = jnp.zeros((owner_total * share, block_wires, TB), jnp.bfloat16)
    payload = payload.at[place].set(tiles, mode="drop")
    arrived = exchange(payload.reshape(owner_total, share, block_wires, TB))

    owners = rows >> 7
    rank = ranks(owners)
    source = jnp.arange(owner_total, dtype=jnp.int32)[:, None]
    line = jnp.where(live(owners, rank) & (owners == me), source, owner_total)
    table = jnp.zeros((owner_total, 128), jnp.int32)
    table = table.at[line, jnp.maximum(rank, 0)].set(rows & 127, mode="drop")
    return add_to_image(
        plan,
        table,
        arrived.reshape(owner_total * share, block_wires, TB),
        geometry,
        owner_total,
        planes,
        share,
        image,
    )


def tick_halo(sides):
    devices = lax.axis_size("tick")
    if devices == 2:
        tick = lax.axis_index("tick")
        got = lax.ppermute(sides[0], "tick", [(0, 1), (1, 0)])
        nothing = jnp.zeros_like(got)
        return jnp.where(tick == 0, nothing, got), jnp.where(tick == 0, got, nothing)
    up = [(i, i + 1) for i in range(devices - 1)]
    down = [(i + 1, i) for i in range(devices - 1)]
    return lax.ppermute(sides[1], "tick", up), lax.ppermute(sides[0], "tick", down)


def wire_halo(first, last, left, right):
    devices = lax.axis_size("wire")
    mine = lax.axis_index("wire")
    last = jnp.concatenate([left[-PAD:], last, right[-PAD:]], axis=1)
    first = jnp.concatenate([left[:PAD], first, right[:PAD]], axis=1)
    target = jnp.arange(devices)[:, None, None]
    rows = jnp.where(target == mine - 1, first[None], jnp.zeros_like(first)[None])
    return exchange(jnp.where(target == mine + 1, last[None], rows), "wire")


def exchange(array, axes=("wire", "plane")):
    return lax.all_to_all(array, axes, split_axis=0, concat_axis=0, tiled=True)


def shards(raw, chan_mask, kernel, geometry, roi_block, roi_owner):
    wires, ticks = raw.shape
    slot_count = roi_block.shape[0]
    block_wires = geometry.shape[1]
    cells = geometry.shape[2]
    tick_blocks = ticks // TB
    planes = lax.axis_size("plane")
    wire_shards = lax.axis_size("wire")
    owner_total = planes * wire_shards
    share = -(-(slot_count - CAP) // (owner_total - 1))

    mask, first, last, packed, send_plan, *sides = prepare(
        raw, chan_mask, roi_owner, roi_block, planes, owner_total, share
    )
    left, right = tick_halo(sides)
    halos = wire_halo(first, last, left, right)
    inner, bands = convolve_inner(raw, mask, left, right, kernel[0])
    signal, partial = convolve_edges(
        planes, send_plan, packed, inner, raw, mask, left, right, halos, bands, geometry
    )

    pieces = exchange(partial, "plane")
    payload = pack_tiles(send_plan, signal, owner_total * share, block_wires)
    pieces, payload = lax.optimization_barrier((pieces, payload))
    pieces = exchange(fold(pieces, wire_shards), "wire")

    tables = pieces[:, cells : cells + 2 * planes].astype(jnp.int32)
    tables = tables.reshape(owner_total, 2, 128)
    rows = tables[:, 0] * 128 + tables[:, 1]
    plan = make_receive_plan(
        rows, packed, owner_total, planes, share, wires // block_wires, tick_blocks
    )
    staged = stage_geometry(
        plan, geometry, group_total(owner_total, share, tick_blocks), owner_total * share
    )

    sums = jnp.sum(pieces[:, :cells].astype(jnp.float32), axis=0).astype(jnp.bfloat16)
    payload = lax.dynamic_update_slice(
        payload.reshape(owner_total, share, block_wires, TB),
        sums.reshape(1, cells // block_wires, block_wires, TB),
        (send_plan[1, 0], 0, 0, 0),
    )
    arrived = exchange(payload).reshape(owner_total * share, block_wires, TB)
    image = make_image(plan, arrived, staged, owner_total, share, ticks)

    trips = agree(plan[1:2, 1:2])[0, 0]
    image = lax.fori_loop(
        0,
        trips,
        lambda trip, now: further_round(
            trip, now, signal, geometry, rows, packed, plan, owner_total, planes, share
        ),
        image,
    )
    return signal, image


def solution(mesh):
    in_specs = (
        P(("plane", "wire"), "tick"),
        P(("plane", "wire")),
        P("plane", None, None),
        P(),
        P(("plane", "wire", "tick")),
        P(("plane", "wire", "tick")),
    )
    out_specs = (P(("plane", "wire"), "tick"), P(("plane", "wire"), "tick"))
    return jax.shard_map(shards, mesh=mesh, in_specs=in_specs, out_specs=out_specs, check_vma=False)
```

```python
import functools

import jax
import jax.numpy as jnp
from jax import lax
from jax.experimental import pallas as pl
from jax.experimental.pallas import tpu as pltpu
from jax.sharding import PartitionSpec as P

TB = 128
CAP = 25
PAD = 16
TABLE = 8
STEPS = 4
MIB = 1024 * 1024


def vmem():
    return pl.BlockSpec(memory_space=pltpu.VMEM)


def smem():
    return pl.BlockSpec(memory_space=pltpu.SMEM)


GROUP = 8


def home(position, planes, owner_total):
    return (position % planes) * (owner_total // planes) + position // planes


def lane_numbers():
    return lax.broadcasted_iota(jnp.int32, (1, 128), 1)


def earlier_lanes():
    return (
        lax.broadcasted_iota(jnp.int32, (128, 128), 0)
        < lax.broadcasted_iota(jnp.int32, (128, 128), 1)
    ).astype(jnp.bfloat16)


def count_before(member, before):
    return jnp.dot(
        member.astype(jnp.float32).astype(jnp.bfloat16), before, preferred_element_type=jnp.float32
    )


def most_named(owners, owner_total):
    lanes = lane_numbers()
    counts = jnp.full(owners.shape, -1.0, jnp.float32)
    for owner in range(owner_total):
        named = jnp.sum((owners == owner).astype(jnp.float32), axis=1, keepdims=True)
        counts = jnp.where(lanes == owner, named, counts)
    top = jnp.max(counts, axis=1, keepdims=True)
    chosen = jnp.min(
        jnp.where(counts == top, lanes.astype(jnp.float32), 127.0), axis=1, keepdims=True
    )
    return counts, chosen


def prepare_kernel(
    planes,
    owner_total,
    share,
    tick_total,
    raw_hbm,
    mask_hbm,
    owner_hbm,
    block_hbm,
    mask_out,
    first_ref,
    last_ref,
    own_ref,
    out_ref,
    *rest,
):
    wires, ticks = raw_hbm.shape
    count = 1 if tick_total == 2 else 2
    sides = rest[:count]
    side_refs = rest[count : 2 * count]
    first_buf, last_buf, mask_ref, owner_ref, block_ref, sems = rest[2 * count :]
    tick = lax.axis_index("tick")
    me = lax.axis_index("wire") * planes + lax.axis_index("plane")
    if tick_total == 2:
        starts = [pl.multiple_of((1 - tick) * (ticks - TB), TB)]
    else:
        starts = [0, ticks - TB]
    moves = [(mask_hbm, mask_ref), (owner_hbm, owner_ref), (block_hbm, block_ref)]
    moves += [(raw_hbm.at[:, pl.ds(start, TB)], ref) for start, ref in zip(starts, side_refs)]
    moves += [(raw_hbm.at[pl.ds(0, PAD)], first_buf), (raw_hbm.at[pl.ds(wires - PAD, PAD)], last_buf)]
    copies = [
        pltpu.make_async_copy(source, target, sems.at[index])
        for index, (source, target) in enumerate(moves)
    ]
    for copy in copies:
        copy.start()
    for copy in copies[:3]:
        copy.wait()

    for part in range(wires // 128):
        row = mask_ref[part : part + 1].astype(jnp.float32)
        wide = jnp.transpose(jnp.broadcast_to(row, (128, 128)))
        mask_out[part * 128 : (part + 1) * 128] = wide.astype(jnp.bfloat16)

    lanes = lane_numbers()
    slot_count = owner_ref.shape[1]
    owner = owner_ref[...]
    wire_shards = owner_total // planes
    none = owner_total * 128
    own_ref[...] = jnp.where(lanes == 127, none + me, none)
    own_ref[:, 0:slot_count] = (
        (owner % wire_shards) * planes + owner // wire_shards
    ) * 128 + block_ref[...]
    own = own_ref[...]
    _, hot = most_named(own >> 7, owner_total)
    rows = lax.broadcasted_iota(jnp.int32, (owner_total, 128), 0)
    member = (own >> 7) == rows
    rank = count_before(member, earlier_lanes())
    place = jnp.where(rank < share, rows.astype(jnp.float32) * share + rank, -1.0)
    place = jnp.where(rows.astype(jnp.float32) == hot, -2.0, place)
    place = jnp.sum(jnp.where(member, place + 3.0, 0.0), axis=0, keepdims=True)

    column = jnp.transpose(jnp.broadcast_to(own.astype(jnp.float32), (128, 128)))
    column = column.astype(jnp.int32)
    here = ((column & 127) == lanes) & ((column >> 7) < owner_total)
    spread = jnp.transpose(jnp.broadcast_to(place, (128, 128)))
    placed = jnp.sum(jnp.where(here, spread, 0.0), axis=0, keepdims=True)
    trash = float(owner_total * share)
    facts = jnp.where(lanes == 2, me, 0)
    out_ref[...] = jnp.zeros_like(out_ref)
    out_ref[0:1, :] = jnp.where(placed >= 3.0, placed - 3.0, trash).astype(jnp.int32)
    out_ref[1:2, :] = jnp.where(lanes == 0, hot.astype(jnp.int32), facts)
    out_ref[2:3, :] = (placed == 1.0).astype(jnp.int32)

    for copy in copies[3:]:
        copy.wait()
    for side, ref in zip(sides, side_refs):
        side[...] = ref[...] * mask_out[...]
    for block in range(ticks // TB):
        at = slice(block * TB, (block + 1) * TB)
        first_ref[:, at] = first_buf[:, at] * mask_out[0:PAD]
        last_ref[:, at] = last_buf[:, at] * mask_out[wires - PAD : wires]


def prepare(raw, chan_mask, roi_owner, roi_block, planes, owner_total, share):
    wires, ticks = raw.shape
    tick_total = lax.axis_size("tick")
    sides = 1 if tick_total == 2 else 2
    side = jax.ShapeDtypeStruct((wires, TB), jnp.bfloat16)
    edge = jax.ShapeDtypeStruct((PAD, ticks), jnp.bfloat16)
    row = jax.ShapeDtypeStruct((1, 128), jnp.int32)
    table = jax.ShapeDtypeStruct((8, 128), jnp.int32)
    slot_count = roi_owner.shape[0]
    return pl.pallas_call(
        functools.partial(prepare_kernel, planes, owner_total, share, tick_total),
        out_shape=(side, edge, edge, row, table) + (side,) * sides,
        in_specs=[pl.BlockSpec(memory_space=pltpu.HBM)] * 4,
        out_specs=(vmem(),) * (5 + sides),
        scratch_shapes=[pltpu.VMEM((wires, TB), jnp.bfloat16)] * sides
        + [pltpu.VMEM((PAD, ticks), jnp.bfloat16)] * 2
        + [pltpu.VMEM((wires // 128, 128), jnp.int32)]
        + [pltpu.VMEM((1, slot_count), jnp.int32)] * 2
        + [pltpu.SemaphoreType.DMA((sides + 5,))],
        compiler_params=pltpu.CompilerParams(vmem_limit_bytes=60 * MIB),
        name="prepare",
    )(raw, chan_mask.reshape(wires // 128, 128), roi_owner[None], roi_block[None])


def receive_kernel(owner_total, planes, share, wire_blocks, tick_blocks, rows_ref, own_ref, out_ref):
    lanes = lane_numbers()
    lane_f = lanes.astype(jnp.float32)
    every = rows_ref[...]
    owners = every >> 7
    own = own_ref[...]
    me = jnp.sum(jnp.where(lanes == 127, own & 127, 0).astype(jnp.float32), axis=1, keepdims=True)

    counts, chosen = most_named(owners, owner_total)
    hot = jnp.max(chosen, axis=0, keepdims=True)
    agreed = hot == jnp.min(chosen, axis=0, keepdims=True)
    left = jnp.where(agreed & (lane_f == hot), 0.0, counts)
    fullest = jnp.max(jnp.max(left, axis=1, keepdims=True), axis=0, keepdims=True)
    start = agreed.astype(jnp.float32)
    trips = -start
    for step in range(-(-CAP // share)):
        trips = trips + (fullest > step * share).astype(jnp.float32)
    trips = jnp.maximum(trips, 0.0)
    hot = jnp.where(agreed, hot, -1.0)

    to_me = owners.astype(jnp.float32) == me
    before = earlier_lanes()
    rank = count_before(to_me, before)
    blocks = every & 127
    source = lax.broadcasted_iota(jnp.int32, (owner_total, 128), 0)
    line = home(source, planes, owner_total) * wire_blocks + blocks // tick_blocks
    line = line.astype(jnp.float32)
    tick = (blocks % tick_blocks).astype(jnp.float32)
    lines = jnp.zeros((1, 128), jnp.float32)
    ticks = jnp.full((1, 128), -1.0, jnp.float32)
    for slot in range(share):
        got = to_me & (rank == slot)
        here = lanes == source * share + slot
        for value, where in ((line, 0), (tick + 1.0, 1)):
            one = jnp.sum(jnp.where(got, value, 0.0), axis=1, keepdims=True)
            one = jnp.sum(jnp.where(here, one, 0.0), axis=0, keepdims=True)
            if where == 0:
                lines = lines + one
            else:
                ticks = ticks + one

    block_rows = lax.broadcasted_iota(jnp.int32, (tick_blocks, 128), 0).astype(jnp.float32)
    member = block_rows == ticks
    rank = count_before(member, before)
    total = jnp.sum(member.astype(jnp.float32), axis=1, keepdims=True)
    groups = jnp.zeros_like(total)
    for step in range(0, owner_total * share, GROUP):
        groups = groups + (total > step).astype(jnp.float32)
    lower = (
        lax.broadcasted_iota(jnp.int32, (tick_blocks, tick_blocks), 0)
        > lax.broadcasted_iota(jnp.int32, (tick_blocks, tick_blocks), 1)
    ).astype(jnp.bfloat16)
    base = jnp.dot(
        lower,
        jnp.broadcast_to(groups, (tick_blocks, 128)).astype(jnp.bfloat16),
        preferred_element_type=jnp.float32,
    )
    place = jnp.sum(jnp.where(member, base * GROUP + rank, 0.0), axis=0, keepdims=True)
    trash = float(group_total(owner_total, share, tick_blocks) * GROUP)
    place = jnp.where(ticks < 0.0, trash, place)
    inside = (base <= lane_f) & (lane_f < base + groups)
    group_tick = jnp.sum(jnp.where(inside, block_rows, 0.0), axis=0, keepdims=True)

    facts = jnp.where(lanes == 0, hot, 0.0)
    facts = jnp.where(lanes == 1, trips, facts)
    facts = jnp.where(lanes == 2, me, facts)
    facts = jnp.where(lanes == 3, start, facts)
    out_ref[...] = jnp.zeros_like(out_ref)
    out_ref[0:1, :] = place.astype(jnp.int32)
    out_ref[1:2, :] = facts.astype(jnp.int32)
    out_ref[2:3, :] = lines.astype(jnp.int32)
    out_ref[3:4, :] = group_tick.astype(jnp.int32)


def group_total(owner_total, share, tick_blocks):
    return (owner_total * share - tick_blocks) // GROUP + tick_blocks


def make_receive_plan(rows, packed, owner_total, planes, share, wire_blocks, tick_blocks):
    return pl.pallas_call(
        functools.partial(receive_kernel, owner_total, planes, share, wire_blocks, tick_blocks),
        out_shape=jax.ShapeDtypeStruct((8, 128), jnp.int32),
        in_specs=[vmem(), vmem()],
        out_specs=vmem(),
        compiler_params=pltpu.CompilerParams(vmem_limit_bytes=2 * MIB),
        name="receive_plan",
    )(rows, packed)


def agree(rounds):
    devices = lax.axis_size("tick")
    reach = 1
    while reach < devices:
        ring = [(i, (i + reach) % devices) for i in range(devices)]
        rounds = jnp.maximum(rounds, lax.ppermute(rounds, "tick", ring))
        reach *= 2
    return rounds


def band_kernel(taps_w, taps_ref, band_ref):
    row = lax.broadcasted_iota(jnp.int32, (TB, TB), 0)
    col = lax.broadcasted_iota(jnp.int32, (TB, TB), 1)
    pairs = (taps_w + 1) // 2
    band_ref[0, 0 : 3 * TB, TB : 2 * TB] = jnp.zeros((3 * TB, TB), jnp.bfloat16)
    band_ref[pairs - 1, 3 * TB : 6 * TB, 0:TB] = jnp.zeros((3 * TB, TB), jnp.bfloat16)
    taps = taps_ref[...].astype(jnp.float32)
    for tap in range(taps_w):
        spread = jnp.broadcast_to(taps[tap : tap + 1], (TB, 2 * TB))
        rolled = pltpu.roll(spread, TB, 1, stride=1, stride_axis=0)
        middle = rolled[:, :TB]
        outer = rolled[:, TB:]
        bands = (
            jnp.where(col < row, outer, 0.0).astype(jnp.bfloat16),
            middle.astype(jnp.bfloat16),
            jnp.where(col >= row, outer, 0.0).astype(jnp.bfloat16),
        )
        for first, second in ((0, 0), (1, 1), (1, 0), (0, 1)):
            if (tap - first + second) % 2:
                continue
            pair = (tap - first + second) // 2
            for piece in range(3):
                start = (first * 3 + piece) * TB
                band_ref[pair, start : start + TB, second * TB : (second + 1) * TB] = bands[piece]


def make_bands(taps):
    taps_w = taps.shape[0]
    return pl.pallas_call(
        functools.partial(band_kernel, taps_w),
        out_shape=jax.ShapeDtypeStruct(((taps_w + 1) // 2, 6 * TB, 2 * TB), jnp.bfloat16),
        in_specs=[vmem()],
        out_specs=vmem(),
        cost_estimate=pl.CostEstimate(flops=10**9, bytes_accessed=6 * MIB, transcendentals=0),
        compiler_params=pltpu.CompilerParams(vmem_limit_bytes=16 * MIB),
        name="bands",
    )(taps)


def spread_pair(wide_ref, lhs_view, line, pitch, blocks):
    for side in range(2):
        for piece in range(3):
            at = (side * 3 + piece) * TB
            lhs_view[:, at : at + TB] = wide_ref[
                pl.ds((line + side) * pitch + piece, blocks), :
            ].astype(jnp.bfloat16)


def write_lines(total, out_view, signal_ref, line, pairs, blocks):
    for pair in range(pairs):
        for side in range(2):
            out_view[pl.ds((2 * pair + side) * blocks, blocks), :] = total[
                pair * blocks : (pair + 1) * blocks, side * TB : (side + 1) * TB
            ]
    for block in range(blocks):
        signal_ref[line : line + 2 * pairs, block * TB : (block + 1) * TB] = out_view[
            pl.ds(block, 2 * pairs, stride=blocks), :
        ].astype(jnp.bfloat16)


def inner_kernel(
    chunks,
    raw_ref,
    mask_ref,
    left_ref,
    right_ref,
    band_ref,
    inner_ref,
    wide_ref,
    lhs_ref,
    out_ref,
):
    wires, ticks = raw_ref.shape
    blocks = ticks // TB
    pitch = wide_ref.shape[0] // wires
    reach = band_ref.shape[0]
    span = 2 * PAD
    groups = wires // span

    def fill(group, block):
        lines = slice(group * span, (group + 1) * span)
        if block == 0:
            inner = left_ref[lines]
        elif block == blocks + 1:
            inner = right_ref[lines]
        else:
            inner = raw_ref[lines, (block - 1) * TB : block * TB] * mask_ref[lines]
        wide_ref[pl.ds(group * span * pitch + block, span, stride=pitch), :] = inner.astype(
            jnp.float32
        )

    margin = reach - 1
    begin = PAD // 2
    state = {"group": 0, "pair": begin}

    def prepare(upto):
        todo = []
        while state["pair"] < upto:
            line = 2 * state["pair"] - margin
            while state["group"] < groups and line + 1 >= state["group"] * span:
                group = state["group"]
                for block in range(blocks + 2):
                    todo.append(lambda group=group, block=block: fill(group, block))
                state["group"] += 1
            todo.append(
                lambda line=line, pair=state["pair"]: spread_pair(
                    wide_ref, lhs_ref.at[pair - begin], line, pitch, blocks
                )
            )
            state["pair"] += 1
        return todo

    pair = begin
    for job in prepare(pair + chunks[0] + margin):
        job()
    for index, size in enumerate(chunks):
        todo = prepare(pair + size + chunks[index + 1] + margin) if index + 1 < len(chunks) else []
        each = -(-len(todo) // reach)
        total = jnp.zeros((size * blocks, 2 * TB), jnp.float32)
        for step in range(0, reach, STEPS):
            steps = range(step, min(step + STEPS, reach))
            rows = [
                lhs_ref[pair - begin + one : pair - begin + one + size].reshape(
                    size * blocks, 6 * TB
                )
                for one in steps
            ]
            bands = band_ref[steps[0] : steps[-1] + 1].reshape(len(steps) * 6 * TB, 2 * TB)
            total = total + jnp.dot(
                jnp.concatenate(rows, axis=1), bands, preferred_element_type=jnp.float32
            )
            for job in todo[step * each : (steps[-1] + 1) * each]:
                job()
        write_lines(total, out_ref.at[index % 2], inner_ref, 2 * (pair - begin), size, blocks)
        pair += size


def convolve_inner(raw, mask, left, right, bands):
    wires, ticks = raw.shape
    reach = bands.shape[0]
    blocks = ticks // TB
    pitch = -(-(blocks + 2) // 8) * 8
    pairs = (wires - 2 * PAD) // 2
    chunks = []
    while sum(chunks) < pairs:
        chunks.append(min(32 if chunks else 16, pairs - sum(chunks)))
    flops = 2 * blocks * pairs * reach * 6 * TB * 2 * TB
    return pl.pallas_call(
        functools.partial(inner_kernel, tuple(chunks)),
        out_shape=jax.ShapeDtypeStruct((wires - 2 * PAD, ticks), jnp.bfloat16),
        in_specs=[vmem()] * 5,
        out_specs=vmem(),
        scratch_shapes=[
            pltpu.VMEM((wires * pitch, TB), jnp.float32),
            pltpu.VMEM((pairs + reach - 1, blocks, 6 * TB), jnp.bfloat16),
            pltpu.VMEM((2, 2 * max(chunks) * blocks, TB), jnp.float32),
        ],
        cost_estimate=pl.CostEstimate(flops=flops, bytes_accessed=6 * MIB, transcendentals=0),
        compiler_params=pltpu.CompilerParams(vmem_limit_bytes=28 * MIB),
        name="inner",
    )(raw, mask, left, right, bands)


def edge_kernel(
    planes,
    plan_ref,
    own_ref,
    inner_ref,
    raw_ref,
    mask_ref,
    left_ref,
    right_ref,
    top_ref,
    bottom_ref,
    band_ref,
    geo_ref,
    signal_ref,
    partial_ref,
    wide_ref,
    lhs_ref,
    out_ref,
    turned_ref,
):
    wires, ticks = signal_ref.shape
    blocks = ticks // TB
    reach = band_ref.shape[0]
    block_wires = geo_ref.shape[1]
    wire_blocks = wires // block_wires
    near = 2 * PAD
    lines = PAD + near
    pitch = wide_ref.shape[1] // lines
    pairs = PAD // 2
    margin = reach - 1

    signal_ref[PAD : wires - PAD] = inner_ref[...]
    source = home(plan_ref[1, 2], planes, geo_ref.shape[0] // wire_blocks)
    rows = geo_ref[pl.ds(source * wire_blocks, wire_blocks)].reshape(wires, -1)
    turned_ref[...] = jnp.transpose(rows)

    for end in range(2):
        halo_ref = (top_ref, bottom_ref)[end]
        mine = (slice(0, near), slice(wires - near, wires))[end]
        halo_at = (0, near)[end]
        mine_at = (PAD, 0)[end]
        for block in range(blocks + 2):
            columns = slice(block * TB, (block + 1) * TB)
            if block == 0:
                inner = left_ref[mine].astype(jnp.float32)
            elif block == blocks + 1:
                inner = right_ref[mine].astype(jnp.float32)
            else:
                inner = raw_ref[mine, (block - 1) * TB : block * TB] * mask_ref[mine]
                inner = inner.astype(jnp.float32)
            wide_ref[end, pl.ds(halo_at * pitch + block, PAD, stride=pitch), :] = halo_ref[
                :, columns
            ].astype(jnp.float32)
            wide_ref[end, pl.ds(mine_at * pitch + block, near, stride=pitch), :] = inner
        first = (PAD, near - PAD)[end] - margin
        for pair in range(pairs + margin):
            spread_pair(
                wide_ref.at[end], lhs_ref.at[end, pair], first + 2 * pair, pitch, blocks
            )

    total = jnp.zeros((2 * pairs * blocks, 2 * TB), jnp.float32)
    for step in range(0, reach, STEPS):
        steps = range(step, min(step + STEPS, reach))
        rows = jnp.concatenate(
            [
                jnp.concatenate(
                    [
                        lhs_ref[end, one : one + pairs].reshape(pairs * blocks, 6 * TB)
                        for one in steps
                    ],
                    axis=1,
                )
                for end in range(2)
            ],
            axis=0,
        )
        bands = band_ref[steps[0] : steps[-1] + 1].reshape(len(steps) * 6 * TB, 2 * TB)
        total = total + jnp.dot(rows, bands, preferred_element_type=jnp.float32)
    for end in range(2):
        write_lines(
            total[end * pairs * blocks : (end + 1) * pairs * blocks],
            out_ref.at[end],
            signal_ref,
            (0, wires - PAD)[end],
            pairs,
            blocks,
        )

    cells = geo_ref.shape[2]
    shards = partial_ref.shape[1] // cells
    own = own_ref[...]
    line = lax.broadcasted_iota(jnp.int32, (TABLE, 128), 0)
    table = jnp.where(line == 0, own >> 7, jnp.where(line == 1, own & 127, 0))
    table = table.astype(jnp.float32).astype(jnp.bfloat16)
    for plane in range(planes):
        partial_ref[plane, shards * cells : shards * cells + TABLE] = table

    for block in range(0, blocks, 2):
        chosen = []
        for side in range(2):
            at = slice((block + side) * TB, (block + side + 1) * TB)
            column = []
            for line in range(wire_blocks):
                tile = signal_ref[line * block_wires : (line + 1) * block_wires, at]
                asked = plan_ref[2, line * blocks + block + side] == 1
                column.append(jnp.where(asked, tile, jnp.zeros_like(tile)))
            chosen.append(jnp.concatenate(column, axis=0))
        sums = jnp.dot(
            turned_ref[...], jnp.concatenate(chosen, axis=1), preferred_element_type=jnp.float32
        ).astype(jnp.bfloat16)
        for side in range(2):
            shard, plane = divmod(block + side, planes)
            partial_ref[plane, shard * cells : (shard + 1) * cells] = sums[
                :, side * TB : (side + 1) * TB
            ]


def convolve_edges(
    planes, plan, own, inner, raw, mask, left, right, top, bottom, bands, geometry
):
    wires, ticks = raw.shape
    reach = bands.shape[0]
    cells = geometry.shape[2]
    blocks = ticks // TB
    pitch = -(-(blocks + 2) // 8) * 8
    flops = 2 * blocks * PAD * reach * 6 * TB * 2 * TB
    return pl.pallas_call(
        functools.partial(edge_kernel, planes),
        out_shape=(
            jax.ShapeDtypeStruct((wires, ticks), jnp.bfloat16),
            jax.ShapeDtypeStruct((planes, blocks // planes * cells + TABLE, TB), jnp.bfloat16),
        ),
        in_specs=[smem()] + [vmem()] * 10,
        out_specs=(vmem(), vmem()),
        scratch_shapes=[
            pltpu.VMEM((2, 3 * PAD * pitch, TB), jnp.float32),
            pltpu.VMEM((2, PAD // 2 + reach - 1, blocks, 6 * TB), jnp.bfloat16),
            pltpu.VMEM((2, PAD * blocks, TB), jnp.float32),
            pltpu.VMEM((cells, wires), jnp.bfloat16),
        ],
        cost_estimate=pl.CostEstimate(flops=flops, bytes_accessed=6 * MIB, transcendentals=0),
        compiler_params=pltpu.CompilerParams(vmem_limit_bytes=24 * MIB),
        name="edges",
    )(plan, own, inner, raw, mask, left, right, top, bottom, bands, geometry)


def fold_kernel(pieces_ref, out_ref):
    planes, height, _ = pieces_ref.shape
    shards, lines, _ = out_ref.shape
    cells = lines - TABLE
    line = lax.broadcasted_iota(jnp.int32, (TABLE, 128), 0)
    table = jnp.zeros((TABLE, 128), jnp.float32)
    for plane in range(planes):
        tags = pieces_ref[plane, height - TABLE : height].astype(jnp.float32)
        table = jnp.where(line == 2 * plane, tags[0:1], table)
        table = jnp.where(line == 2 * plane + 1, tags[1:2], table)
    for shard in range(shards):
        total = pieces_ref[0, shard * cells : (shard + 1) * cells].astype(jnp.float32)
        for plane in range(1, planes):
            total = total + pieces_ref[plane, shard * cells : (shard + 1) * cells].astype(
                jnp.float32
            )
        out_ref[shard, 0:cells] = total.astype(jnp.bfloat16)
        out_ref[shard, cells:lines] = table.astype(jnp.bfloat16)


def fold(pieces, shards):
    cells = (pieces.shape[1] - TABLE) // shards
    return pl.pallas_call(
        fold_kernel,
        out_shape=jax.ShapeDtypeStruct((shards, cells + TABLE, TB), jnp.bfloat16),
        in_specs=[vmem()],
        out_specs=vmem(),
        compiler_params=pltpu.CompilerParams(vmem_limit_bytes=4 * MIB),
        name="fold",
    )(pieces)


def pack_kernel(slots, plan_ref, signal_ref, payload_ref, tiles_ref):
    block_wires = payload_ref.shape[1]
    wires, ticks = signal_ref.shape
    blocks = ticks // TB
    tiles_ref[...] = jnp.zeros_like(tiles_ref)
    for line in range(wires // block_wires):
        for block in range(blocks):
            place = plan_ref[0, line * blocks + block]
            tiles_ref[place] = signal_ref[
                line * block_wires : (line + 1) * block_wires, block * TB : (block + 1) * TB
            ]
    payload_ref[...] = tiles_ref[0:slots]


def pack_tiles(plan, signal, slots, block_wires):
    return pl.pallas_call(
        functools.partial(pack_kernel, slots),
        out_shape=jax.ShapeDtypeStruct((slots, block_wires, TB), jnp.bfloat16),
        in_specs=[smem(), vmem()],
        out_specs=vmem(),
        scratch_shapes=[pltpu.VMEM((slots + 1, block_wires, TB), jnp.bfloat16)],
        cost_estimate=pl.CostEstimate(flops=10**8, bytes_accessed=3 * MIB, transcendentals=0),
        compiler_params=pltpu.CompilerParams(vmem_limit_bytes=8 * MIB),
        name="pack",
    )(plan, signal)


def stage_kernel(slots, plan_ref, geo_ref, out_ref, rows_ref):
    groups = out_ref.shape[0]
    rows_ref[...] = jnp.zeros_like(rows_ref)
    for slot in range(slots):
        rows_ref[plan_ref[0, slot]] = geo_ref[plan_ref[2, slot]]
    for group in range(groups):
        rows = rows_ref[group * GROUP : (group + 1) * GROUP]
        out_ref[group] = jnp.transpose(rows.reshape(-1, rows.shape[-1]))


def stage_geometry(plan, geometry, groups, slots):
    _, block_wires, cells = geometry.shape
    return pl.pallas_call(
        functools.partial(stage_kernel, slots),
        out_shape=jax.ShapeDtypeStruct((groups, cells, GROUP * block_wires), jnp.bfloat16),
        in_specs=[smem(), vmem()],
        out_specs=vmem(),
        scratch_shapes=[pltpu.VMEM((groups * GROUP + 1, block_wires, cells), jnp.bfloat16)],
        cost_estimate=pl.CostEstimate(flops=10**8, bytes_accessed=3 * MIB, transcendentals=0),
        compiler_params=pltpu.CompilerParams(vmem_limit_bytes=12 * MIB),
        name="stage",
    )(plan, geometry)


def image_kernel(owner_total, share, plan_ref, arrived_ref, staged_ref, image_ref, tiles_ref):
    cells, ticks = image_ref.shape
    block_wires = arrived_ref.shape[1]
    groups = staged_ref.shape[0]
    is_hot = plan_ref[1, 0] == plan_ref[1, 2]
    counts = plan_ref[1, 3] == 1

    @pl.when(is_hot)
    def _():
        for source in range(owner_total):
            sums = arrived_ref[source * share : source * share + cells // block_wires]
            image_ref[:, source * TB : (source + 1) * TB] = sums.reshape(cells, TB).astype(
                jnp.float32
            )

    @pl.when(jnp.logical_not(is_hot))
    def _():
        image_ref[...] = jnp.zeros_like(image_ref)
        tiles_ref[...] = jnp.zeros_like(tiles_ref)

        @pl.when(counts)
        def _():
            for slot in range(owner_total * share):
                tiles_ref[plan_ref[0, slot]] = arrived_ref[slot]
            for group in range(groups):
                tiles = tiles_ref[group * GROUP : (group + 1) * GROUP]
                at = pl.ds(pl.multiple_of(plan_ref[3, group] * TB, TB), TB)
                image_ref[:, at] += jnp.dot(
                    staged_ref[group],
                    tiles.reshape(GROUP * block_wires, TB),
                    preferred_element_type=jnp.float32,
                )


def make_image(plan, arrived, staged, owner_total, share, ticks):
    groups, cells, _ = staged.shape
    block_wires = arrived.shape[1]
    return pl.pallas_call(
        functools.partial(image_kernel, owner_total, share),
        out_shape=jax.ShapeDtypeStruct((cells, ticks), jnp.float32),
        in_specs=[smem(), vmem(), vmem()],
        out_specs=vmem(),
        scratch_shapes=[
            pltpu.VMEM((groups * GROUP + 1, block_wires, TB), jnp.bfloat16),
        ],
        cost_estimate=pl.CostEstimate(flops=10**8, bytes_accessed=3 * MIB, transcendentals=0),
        compiler_params=pltpu.CompilerParams(vmem_limit_bytes=16 * MIB),
        name="image",
    )(plan, arrived, staged)


def more_kernel(owner_total, planes, share, plan_ref, table_ref, arrived_ref, geo_ref, before_ref, image_ref):
    cells, ticks = image_ref.shape
    blocks = ticks // TB
    wire_blocks = geo_ref.shape[0] // owner_total
    image_ref[...] = before_ref[...]

    @pl.when(plan_ref[1, 0] != plan_ref[1, 2])
    def _():
        def add(source, carry):
            for slot in range(share):
                block = table_ref[source, slot]
                at = pl.multiple_of((block % blocks) * TB, TB)
                image_ref[:, pl.ds(at, TB)] += lax.dot_general(
                    geo_ref[home(source, planes, owner_total) * wire_blocks + block // blocks],
                    arrived_ref[source * share + slot],
                    (((0,), (0,)), ((), ())),
                    preferred_element_type=jnp.float32,
                )
            return carry

        lax.fori_loop(0, owner_total, add, 0)


def add_to_image(plan, table, arrived, geometry, owner_total, planes, share, image):
    return pl.pallas_call(
        functools.partial(more_kernel, owner_total, planes, share),
        out_shape=jax.ShapeDtypeStruct(image.shape, jnp.float32),
        in_specs=[smem(), smem()] + [vmem()] * 3,
        out_specs=vmem(),
        compiler_params=pltpu.CompilerParams(vmem_limit_bytes=16 * MIB),
        name="image_more",
    )(plan, table, arrived, geometry, image)


def further_round(
    trip, image, signal, geometry, rows, packed, plan, owner_total, planes, share
):
    trip, signal, rows, packed, plan = lax.optimization_barrier((trip, signal, rows, packed, plan))
    step = trip + plan[1, 3]
    hot = plan[1, 0]
    me = plan[1, 2]
    block_wires = geometry.shape[1]
    wire_count, tick_count = signal.shape
    blocks = tick_count // TB
    wire_blocks = wire_count // block_wires
    ids = jnp.arange(owner_total, dtype=jnp.int32)

    def ranks(owners):
        member = (owners[..., None] == ids).astype(jnp.int32)
        before = jnp.cumsum(member, axis=-2) - member
        return jnp.sum(before * member, axis=-1) - step * share

    def live(owners, rank):
        return (owners < owner_total) & (owners != hot) & (rank >= 0) & (rank < share)

    owners = packed[0] >> 7
    block = packed[0] & 127
    rank = ranks(owners)
    place = jnp.where(live(owners, rank), owners * share + rank, owner_total * share)
    tiles = signal.reshape(wire_blocks, block_wires, blocks, TB).transpose(0, 2, 1, 3)
    tiles = tiles.reshape(wire_blocks * blocks, block_wires, TB)[block]
    payload = jnp.zeros((owner_total * share, block_wires, TB), jnp.bfloat16)
    payload = payload.at[place].set(tiles, mode="drop")
    arrived = exchange(payload.reshape(owner_total, share, block_wires, TB))

    owners = rows >> 7
    rank = ranks(owners)
    source = jnp.arange(owner_total, dtype=jnp.int32)[:, None]
    line = jnp.where(live(owners, rank) & (owners == me), source, owner_total)
    table = jnp.zeros((owner_total, 128), jnp.int32)
    table = table.at[line, jnp.maximum(rank, 0)].set(rows & 127, mode="drop")
    return add_to_image(
        plan,
        table,
        arrived.reshape(owner_total * share, block_wires, TB),
        geometry,
        owner_total,
        planes,
        share,
        image,
    )


def tick_halo(sides):
    devices = lax.axis_size("tick")
    if devices == 2:
        tick = lax.axis_index("tick")
        got = lax.ppermute(sides[0], "tick", [(0, 1), (1, 0)])
        nothing = jnp.zeros_like(got)
        return jnp.where(tick == 0, nothing, got), jnp.where(tick == 0, got, nothing)
    up = [(i, i + 1) for i in range(devices - 1)]
    down = [(i + 1, i) for i in range(devices - 1)]
    return lax.ppermute(sides[1], "tick", up), lax.ppermute(sides[0], "tick", down)


def wire_halo(first, last, left, right):
    devices = lax.axis_size("wire")
    odd = lax.axis_index("wire") % 2 == 1
    last = jnp.concatenate([left[-PAD:], last, right[-PAD:]], axis=1)
    first = jnp.concatenate([left[:PAD], first, right[:PAD]], axis=1)
    got = []
    for begin, rows in ((0, jnp.where(odd, first, last)), (1, jnp.where(odd, last, first))):
        pairs = [(i, i + 1) for i in range(begin, devices - 1, 2)]
        got.append(lax.ppermute(rows, "wire", pairs + [(j, i) for i, j in pairs]))
    return jnp.where(odd, got[0], got[1]), jnp.where(odd, got[1], got[0])


def exchange(array, axes=("wire", "plane")):
    return lax.all_to_all(array, axes, split_axis=0, concat_axis=0, tiled=True)


def shards(raw, chan_mask, kernel, geometry, roi_block, roi_owner):
    wires, ticks = raw.shape
    slot_count = roi_block.shape[0]
    block_wires = geometry.shape[1]
    cells = geometry.shape[2]
    tick_blocks = ticks // TB
    planes = lax.axis_size("plane")
    wire_shards = lax.axis_size("wire")
    owner_total = planes * wire_shards
    share = -(-(slot_count - CAP) // (owner_total - 1))

    mask, first, last, packed, send_plan, *sides = prepare(
        raw, chan_mask, roi_owner, roi_block, planes, owner_total, share
    )
    left, right = tick_halo(sides)
    top, bottom = wire_halo(first, last, left, right)
    bands = make_bands(kernel[0])
    inner = convolve_inner(raw, mask, left, right, bands)
    signal, partial = convolve_edges(
        planes, send_plan, packed, inner, raw, mask, left, right, top, bottom, bands, geometry
    )

    pieces = exchange(partial, "plane")
    payload = pack_tiles(send_plan, signal, owner_total * share, block_wires)
    pieces, payload = lax.optimization_barrier((pieces, payload))
    pieces = exchange(fold(pieces, wire_shards), "wire")

    tables = pieces[:, cells : cells + 2 * planes].astype(jnp.int32)
    tables = tables.reshape(owner_total, 2, 128)
    rows = tables[:, 0] * 128 + tables[:, 1]
    plan = make_receive_plan(
        rows, packed, owner_total, planes, share, wires // block_wires, tick_blocks
    )
    staged = stage_geometry(
        plan, geometry, group_total(owner_total, share, tick_blocks), owner_total * share
    )

    sums = jnp.sum(pieces[:, :cells].astype(jnp.float32), axis=0).astype(jnp.bfloat16)
    payload = lax.dynamic_update_slice(
        payload.reshape(owner_total, share, block_wires, TB),
        sums.reshape(1, cells // block_wires, block_wires, TB),
        (send_plan[1, 0], 0, 0, 0),
    )
    arrived = exchange(payload).reshape(owner_total * share, block_wires, TB)
    image = make_image(plan, arrived, staged, owner_total, share, ticks)

    trips = agree(plan[1:2, 1:2])[0, 0]
    image = lax.fori_loop(
        0,
        trips,
        lambda trip, now: further_round(
            trip, now, signal, geometry, rows, packed, plan, owner_total, planes, share
        ),
        image,
    )
    return signal, image


def solution(mesh):
    in_specs = (
        P(("plane", "wire"), "tick"),
        P(("plane", "wire")),
        P("plane", None, None),
        P(),
        P(("plane", "wire", "tick")),
        P(("plane", "wire", "tick")),
    )
    out_specs = (P(("plane", "wire"), "tick"), P(("plane", "wire"), "tick"))
    return jax.shard_map(shards, mesh=mesh, in_specs=in_specs, out_specs=out_specs, check_vma=False)
```

```python
import functools

import jax
import jax.numpy as jnp
from jax import lax
from jax.experimental import pallas as pl
from jax.experimental.pallas import tpu as pltpu
from jax.sharding import PartitionSpec as P

TB = 128
CAP = 25
PAD = 16
TABLE = 8
STEPS = 4
MIB = 1024 * 1024


def vmem():
    return pl.BlockSpec(memory_space=pltpu.VMEM)


def smem():
    return pl.BlockSpec(memory_space=pltpu.SMEM)


GROUP = 8


def home(position, planes, owner_total):
    return (position % planes) * (owner_total // planes) + position // planes


def lane_numbers():
    return lax.broadcasted_iota(jnp.int32, (1, 128), 1)


def earlier_lanes():
    return (
        lax.broadcasted_iota(jnp.int32, (128, 128), 0)
        < lax.broadcasted_iota(jnp.int32, (128, 128), 1)
    ).astype(jnp.bfloat16)


def count_before(member, before):
    return jnp.dot(
        member.astype(jnp.float32).astype(jnp.bfloat16), before, preferred_element_type=jnp.float32
    )


def most_named(owners, owner_total):
    lanes = lane_numbers()
    counts = jnp.full(owners.shape, -1.0, jnp.float32)
    for owner in range(owner_total):
        named = jnp.sum((owners == owner).astype(jnp.float32), axis=1, keepdims=True)
        counts = jnp.where(lanes == owner, named, counts)
    top = jnp.max(counts, axis=1, keepdims=True)
    chosen = jnp.min(
        jnp.where(counts == top, lanes.astype(jnp.float32), 127.0), axis=1, keepdims=True
    )
    return counts, chosen


def prepare_kernel(
    planes,
    owner_total,
    share,
    tick_total,
    raw_hbm,
    mask_hbm,
    owner_hbm,
    block_hbm,
    mask_out,
    first_ref,
    last_ref,
    own_ref,
    out_ref,
    *rest,
):
    wires, ticks = raw_hbm.shape
    count = 1 if tick_total == 2 else 2
    sides = rest[:count]
    side_refs = rest[count : 2 * count]
    first_buf, last_buf, mask_ref, owner_ref, block_ref, sems = rest[2 * count :]
    tick = lax.axis_index("tick")
    me = lax.axis_index("wire") * planes + lax.axis_index("plane")
    if tick_total == 2:
        starts = [pl.multiple_of((1 - tick) * (ticks - TB), TB)]
    else:
        starts = [0, ticks - TB]
    moves = [(mask_hbm, mask_ref), (owner_hbm, owner_ref), (block_hbm, block_ref)]
    moves += [(raw_hbm.at[:, pl.ds(start, TB)], ref) for start, ref in zip(starts, side_refs)]
    moves += [(raw_hbm.at[pl.ds(0, PAD)], first_buf), (raw_hbm.at[pl.ds(wires - PAD, PAD)], last_buf)]
    copies = [
        pltpu.make_async_copy(source, target, sems.at[index])
        for index, (source, target) in enumerate(moves)
    ]
    for copy in copies:
        copy.start()
    for copy in copies[:3]:
        copy.wait()

    for part in range(wires // 128):
        row = mask_ref[part : part + 1].astype(jnp.float32)
        wide = jnp.transpose(jnp.broadcast_to(row, (128, 128)))
        mask_out[part * 128 : (part + 1) * 128] = wide.astype(jnp.bfloat16)

    lanes = lane_numbers()
    slot_count = owner_ref.shape[1]
    owner = owner_ref[...]
    wire_shards = owner_total // planes
    none = owner_total * 128
    own_ref[...] = jnp.where(lanes == 127, none + me, none)
    own_ref[:, 0:slot_count] = (
        (owner % wire_shards) * planes + owner // wire_shards
    ) * 128 + block_ref[...]
    own = own_ref[...]
    _, hot = most_named(own >> 7, owner_total)
    rows = lax.broadcasted_iota(jnp.int32, (owner_total, 128), 0)
    member = (own >> 7) == rows
    rank = count_before(member, earlier_lanes())
    place = jnp.where(rank < share, rows.astype(jnp.float32) * share + rank, -1.0)
    place = jnp.where(rows.astype(jnp.float32) == hot, -2.0, place)
    place = jnp.sum(jnp.where(member, place + 3.0, 0.0), axis=0, keepdims=True)

    column = jnp.transpose(jnp.broadcast_to(own.astype(jnp.float32), (128, 128)))
    column = column.astype(jnp.int32)
    here = ((column & 127) == lanes) & ((column >> 7) < owner_total)
    spread = jnp.transpose(jnp.broadcast_to(place, (128, 128)))
    placed = jnp.sum(jnp.where(here, spread, 0.0), axis=0, keepdims=True)
    trash = float(owner_total * share)
    facts = jnp.where(lanes == 2, me, 0)
    out_ref[...] = jnp.zeros_like(out_ref)
    out_ref[0:1, :] = jnp.where(placed >= 3.0, placed - 3.0, trash).astype(jnp.int32)
    out_ref[1:2, :] = jnp.where(lanes == 0, hot.astype(jnp.int32), facts)
    out_ref[2:3, :] = (placed == 1.0).astype(jnp.int32)

    for copy in copies[3:]:
        copy.wait()
    for side, ref in zip(sides, side_refs):
        side[...] = ref[...] * mask_out[...]
    for block in range(ticks // TB):
        at = slice(block * TB, (block + 1) * TB)
        first_ref[:, at] = first_buf[:, at] * mask_out[0:PAD]
        last_ref[:, at] = last_buf[:, at] * mask_out[wires - PAD : wires]


def prepare(raw, chan_mask, roi_owner, roi_block, planes, owner_total, share):
    wires, ticks = raw.shape
    tick_total = lax.axis_size("tick")
    sides = 1 if tick_total == 2 else 2
    side = jax.ShapeDtypeStruct((wires, TB), jnp.bfloat16)
    edge = jax.ShapeDtypeStruct((PAD, ticks), jnp.bfloat16)
    row = jax.ShapeDtypeStruct((1, 128), jnp.int32)
    table = jax.ShapeDtypeStruct((8, 128), jnp.int32)
    slot_count = roi_owner.shape[0]
    return pl.pallas_call(
        functools.partial(prepare_kernel, planes, owner_total, share, tick_total),
        out_shape=(side, edge, edge, row, table) + (side,) * sides,
        in_specs=[pl.BlockSpec(memory_space=pltpu.HBM)] * 4,
        out_specs=(vmem(),) * (5 + sides),
        scratch_shapes=[pltpu.VMEM((wires, TB), jnp.bfloat16)] * sides
        + [pltpu.VMEM((PAD, ticks), jnp.bfloat16)] * 2
        + [pltpu.VMEM((wires // 128, 128), jnp.int32)]
        + [pltpu.VMEM((1, slot_count), jnp.int32)] * 2
        + [pltpu.SemaphoreType.DMA((sides + 5,))],
        compiler_params=pltpu.CompilerParams(vmem_limit_bytes=60 * MIB),
        name="prepare",
    )(raw, chan_mask.reshape(wires // 128, 128), roi_owner[None], roi_block[None])


def receive_kernel(owner_total, planes, share, wire_blocks, tick_blocks, own_ref, *refs):
    pieces = refs[:-2]
    out_ref, rows_ref = refs[-2:]
    lanes = lane_numbers()
    lane_f = lanes.astype(jnp.float32)
    place = lax.broadcasted_iota(jnp.int32, (owner_total, 128), 0)
    shard = lax.axis_index("wire")
    every = jnp.zeros((owner_total, 128), jnp.float32)
    for step, ref in enumerate(pieces):
        tags = ref[ref.shape[0] - TABLE :].astype(jnp.float32)
        at = lax.bitwise_xor(shard, step) * planes
        for plane in range(planes):
            row = tags[2 * plane : 2 * plane + 1] * 128.0 + tags[2 * plane + 1 : 2 * plane + 2]
            every = jnp.where(place == at + plane, row, every)
    every = every.astype(jnp.int32)
    rows_ref[...] = every
    owners = every >> 7
    own = own_ref[...]
    me = jnp.sum(jnp.where(lanes == 127, own & 127, 0).astype(jnp.float32), axis=1, keepdims=True)

    counts, chosen = most_named(owners, owner_total)
    hot = jnp.max(chosen, axis=0, keepdims=True)
    agreed = hot == jnp.min(chosen, axis=0, keepdims=True)
    left = jnp.where(agreed & (lane_f == hot), 0.0, counts)
    fullest = jnp.max(jnp.max(left, axis=1, keepdims=True), axis=0, keepdims=True)
    start = agreed.astype(jnp.float32)
    trips = -start
    for step in range(-(-CAP // share)):
        trips = trips + (fullest > step * share).astype(jnp.float32)
    trips = jnp.maximum(trips, 0.0)
    hot = jnp.where(agreed, hot, -1.0)

    to_me = owners.astype(jnp.float32) == me
    before = earlier_lanes()
    rank = count_before(to_me, before)
    blocks = every & 127
    source = lax.broadcasted_iota(jnp.int32, (owner_total, 128), 0)
    line = home(source, planes, owner_total) * wire_blocks + blocks // tick_blocks
    line = line.astype(jnp.float32)
    tick = (blocks % tick_blocks).astype(jnp.float32)
    lines = jnp.zeros((1, 128), jnp.float32)
    ticks = jnp.full((1, 128), -1.0, jnp.float32)
    for slot in range(share):
        got = to_me & (rank == slot)
        here = lanes == source * share + slot
        for value, where in ((line, 0), (tick + 1.0, 1)):
            one = jnp.sum(jnp.where(got, value, 0.0), axis=1, keepdims=True)
            one = jnp.sum(jnp.where(here, one, 0.0), axis=0, keepdims=True)
            if where == 0:
                lines = lines + one
            else:
                ticks = ticks + one

    block_rows = lax.broadcasted_iota(jnp.int32, (tick_blocks, 128), 0).astype(jnp.float32)
    member = block_rows == ticks
    rank = count_before(member, before)
    total = jnp.sum(member.astype(jnp.float32), axis=1, keepdims=True)
    groups = jnp.zeros_like(total)
    for step in range(0, owner_total * share, GROUP):
        groups = groups + (total > step).astype(jnp.float32)
    lower = (
        lax.broadcasted_iota(jnp.int32, (tick_blocks, tick_blocks), 0)
        > lax.broadcasted_iota(jnp.int32, (tick_blocks, tick_blocks), 1)
    ).astype(jnp.bfloat16)
    base = jnp.dot(
        lower,
        jnp.broadcast_to(groups, (tick_blocks, 128)).astype(jnp.bfloat16),
        preferred_element_type=jnp.float32,
    )
    place = jnp.sum(jnp.where(member, base * GROUP + rank, 0.0), axis=0, keepdims=True)
    trash = float(group_total(owner_total, share, tick_blocks) * GROUP)
    place = jnp.where(ticks < 0.0, trash, place)
    inside = (base <= lane_f) & (lane_f < base + groups)
    group_tick = jnp.sum(jnp.where(inside, block_rows, 0.0), axis=0, keepdims=True)

    facts = jnp.where(lanes == 0, hot, 0.0)
    facts = jnp.where(lanes == 1, trips, facts)
    facts = jnp.where(lanes == 2, me, facts)
    facts = jnp.where(lanes == 3, start, facts)
    out_ref[...] = jnp.zeros_like(out_ref)
    out_ref[0:1, :] = place.astype(jnp.int32)
    out_ref[1:2, :] = facts.astype(jnp.int32)
    out_ref[2:3, :] = lines.astype(jnp.int32)
    out_ref[3:4, :] = group_tick.astype(jnp.int32)


def group_total(owner_total, share, tick_blocks):
    return (owner_total * share - tick_blocks) // GROUP + tick_blocks


def make_receive_plan(pieces, packed, owner_total, planes, share, wire_blocks, tick_blocks):
    return pl.pallas_call(
        functools.partial(receive_kernel, owner_total, planes, share, wire_blocks, tick_blocks),
        out_shape=(
            jax.ShapeDtypeStruct((8, 128), jnp.int32),
            jax.ShapeDtypeStruct((owner_total, 128), jnp.int32),
        ),
        in_specs=[vmem()] * (1 + len(pieces)),
        out_specs=(vmem(), vmem()),
        compiler_params=pltpu.CompilerParams(vmem_limit_bytes=2 * MIB),
        name="receive_plan",
    )(packed, *pieces)


def agree(rounds):
    devices = lax.axis_size("tick")
    reach = 1
    while reach < devices:
        ring = [(i, (i + reach) % devices) for i in range(devices)]
        rounds = jnp.maximum(rounds, lax.ppermute(rounds, "tick", ring))
        reach *= 2
    return rounds


def band_kernel(taps_w, taps_ref, band_ref):
    row = lax.broadcasted_iota(jnp.int32, (TB, TB), 0)
    col = lax.broadcasted_iota(jnp.int32, (TB, TB), 1)
    pairs = (taps_w + 1) // 2
    band_ref[0, 0 : 3 * TB, TB : 2 * TB] = jnp.zeros((3 * TB, TB), jnp.bfloat16)
    band_ref[pairs - 1, 3 * TB : 6 * TB, 0:TB] = jnp.zeros((3 * TB, TB), jnp.bfloat16)
    taps = taps_ref[...].astype(jnp.float32)
    for tap in range(taps_w):
        spread = jnp.broadcast_to(taps[tap : tap + 1], (TB, 2 * TB))
        rolled = pltpu.roll(spread, TB, 1, stride=1, stride_axis=0)
        middle = rolled[:, :TB]
        outer = rolled[:, TB:]
        bands = (
            jnp.where(col < row, outer, 0.0).astype(jnp.bfloat16),
            middle.astype(jnp.bfloat16),
            jnp.where(col >= row, outer, 0.0).astype(jnp.bfloat16),
        )
        for first, second in ((0, 0), (1, 1), (1, 0), (0, 1)):
            if (tap - first + second) % 2:
                continue
            pair = (tap - first + second) // 2
            for piece in range(3):
                start = (first * 3 + piece) * TB
                band_ref[pair, start : start + TB, second * TB : (second + 1) * TB] = bands[piece]


def make_bands(taps):
    taps_w = taps.shape[0]
    return pl.pallas_call(
        functools.partial(band_kernel, taps_w),
        out_shape=jax.ShapeDtypeStruct(((taps_w + 1) // 2, 6 * TB, 2 * TB), jnp.bfloat16),
        in_specs=[vmem()],
        out_specs=vmem(),
        cost_estimate=pl.CostEstimate(flops=10**9, bytes_accessed=6 * MIB, transcendentals=0),
        compiler_params=pltpu.CompilerParams(vmem_limit_bytes=16 * MIB),
        name="bands",
    )(taps)


def spread_pair(wide_ref, lhs_view, line, pitch, blocks):
    for side in range(2):
        for piece in range(3):
            at = (side * 3 + piece) * TB
            lhs_view[:, at : at + TB] = wide_ref[
                pl.ds((line + side) * pitch + piece, blocks), :
            ].astype(jnp.bfloat16)


def write_lines(total, out_view, signal_ref, line, pairs, blocks):
    for pair in range(pairs):
        for side in range(2):
            out_view[pl.ds((2 * pair + side) * blocks, blocks), :] = total[
                pair * blocks : (pair + 1) * blocks, side * TB : (side + 1) * TB
            ]
    for block in range(blocks):
        signal_ref[line : line + 2 * pairs, block * TB : (block + 1) * TB] = out_view[
            pl.ds(block, 2 * pairs, stride=blocks), :
        ].astype(jnp.bfloat16)


def inner_kernel(
    chunks,
    raw_ref,
    mask_ref,
    left_ref,
    right_ref,
    band_ref,
    inner_ref,
    wide_ref,
    lhs_ref,
    out_ref,
):
    wires, ticks = raw_ref.shape
    blocks = ticks // TB
    pitch = wide_ref.shape[0] // wires
    reach = band_ref.shape[0]
    span = 2 * PAD
    groups = wires // span

    def fill(group, block):
        lines = slice(group * span, (group + 1) * span)
        if block == 0:
            inner = left_ref[lines]
        elif block == blocks + 1:
            inner = right_ref[lines]
        else:
            inner = raw_ref[lines, (block - 1) * TB : block * TB] * mask_ref[lines]
        wide_ref[pl.ds(group * span * pitch + block, span, stride=pitch), :] = inner.astype(
            jnp.float32
        )

    margin = reach - 1
    begin = PAD // 2
    state = {"group": 0, "pair": begin}

    def prepare(upto):
        todo = []
        while state["pair"] < upto:
            line = 2 * state["pair"] - margin
            while state["group"] < groups and line + 1 >= state["group"] * span:
                group = state["group"]
                for block in range(blocks + 2):
                    todo.append(lambda group=group, block=block: fill(group, block))
                state["group"] += 1
            todo.append(
                lambda line=line, pair=state["pair"]: spread_pair(
                    wide_ref, lhs_ref.at[pair - begin], line, pitch, blocks
                )
            )
            state["pair"] += 1
        return todo

    pair = begin
    for job in prepare(pair + chunks[0] + margin):
        job()
    for index, size in enumerate(chunks):
        todo = prepare(pair + size + chunks[index + 1] + margin) if index + 1 < len(chunks) else []
        each = -(-len(todo) // reach)
        total = jnp.zeros((size * blocks, 2 * TB), jnp.float32)
        for step in range(0, reach, STEPS):
            steps = range(step, min(step + STEPS, reach))
            rows = [
                lhs_ref[pair - begin + one : pair - begin + one + size].reshape(
                    size * blocks, 6 * TB
                )
                for one in steps
            ]
            bands = band_ref[steps[0] : steps[-1] + 1].reshape(len(steps) * 6 * TB, 2 * TB)
            total = total + jnp.dot(
                jnp.concatenate(rows, axis=1), bands, preferred_element_type=jnp.float32
            )
            for job in todo[step * each : (steps[-1] + 1) * each]:
                job()
        write_lines(total, out_ref.at[index % 2], inner_ref, 2 * (pair - begin), size, blocks)
        pair += size


def convolve_inner(raw, mask, left, right, bands):
    wires, ticks = raw.shape
    reach = bands.shape[0]
    blocks = ticks // TB
    pitch = -(-(blocks + 2) // 8) * 8
    pairs = (wires - 2 * PAD) // 2
    chunks = []
    while sum(chunks) < pairs:
        chunks.append(min(32 if chunks else 16, pairs - sum(chunks)))
    flops = 2 * blocks * pairs * reach * 6 * TB * 2 * TB
    return pl.pallas_call(
        functools.partial(inner_kernel, tuple(chunks)),
        out_shape=jax.ShapeDtypeStruct((wires - 2 * PAD, ticks), jnp.bfloat16),
        in_specs=[vmem()] * 5,
        out_specs=vmem(),
        scratch_shapes=[
            pltpu.VMEM((wires * pitch, TB), jnp.float32),
            pltpu.VMEM((pairs + reach - 1, blocks, 6 * TB), jnp.bfloat16),
            pltpu.VMEM((2, 2 * max(chunks) * blocks, TB), jnp.float32),
        ],
        cost_estimate=pl.CostEstimate(flops=flops, bytes_accessed=6 * MIB, transcendentals=0),
        compiler_params=pltpu.CompilerParams(vmem_limit_bytes=28 * MIB),
        name="inner",
    )(raw, mask, left, right, bands)


def edge_kernel(
    planes,
    plan_ref,
    own_ref,
    inner_ref,
    raw_ref,
    mask_ref,
    left_ref,
    right_ref,
    top_ref,
    bottom_ref,
    band_ref,
    geo_ref,
    signal_ref,
    *refs,
):
    part_refs = refs[:planes]
    partial_ref, wide_ref, lhs_ref, out_ref, turned_ref = refs[planes:]
    wires, ticks = signal_ref.shape
    blocks = ticks // TB
    reach = band_ref.shape[0]
    block_wires = geo_ref.shape[1]
    wire_blocks = wires // block_wires
    near = 2 * PAD
    lines = PAD + near
    pitch = wide_ref.shape[1] // lines
    pairs = PAD // 2
    margin = reach - 1

    signal_ref[PAD : wires - PAD] = inner_ref[...]
    source = home(plan_ref[1, 2], planes, geo_ref.shape[0] // wire_blocks)
    rows = geo_ref[pl.ds(source * wire_blocks, wire_blocks)].reshape(wires, -1)
    turned_ref[...] = jnp.transpose(rows)

    for end in range(2):
        halo_ref = (top_ref, bottom_ref)[end]
        mine = (slice(0, near), slice(wires - near, wires))[end]
        halo_at = (0, near)[end]
        mine_at = (PAD, 0)[end]
        for block in range(blocks + 2):
            columns = slice(block * TB, (block + 1) * TB)
            if block == 0:
                inner = left_ref[mine].astype(jnp.float32)
            elif block == blocks + 1:
                inner = right_ref[mine].astype(jnp.float32)
            else:
                inner = raw_ref[mine, (block - 1) * TB : block * TB] * mask_ref[mine]
                inner = inner.astype(jnp.float32)
            wide_ref[end, pl.ds(halo_at * pitch + block, PAD, stride=pitch), :] = halo_ref[
                :, columns
            ].astype(jnp.float32)
            wide_ref[end, pl.ds(mine_at * pitch + block, near, stride=pitch), :] = inner
        first = (PAD, near - PAD)[end] - margin
        for pair in range(pairs + margin):
            spread_pair(
                wide_ref.at[end], lhs_ref.at[end, pair], first + 2 * pair, pitch, blocks
            )

    total = jnp.zeros((2 * pairs * blocks, 2 * TB), jnp.float32)
    for step in range(0, reach, STEPS):
        steps = range(step, min(step + STEPS, reach))
        rows = jnp.concatenate(
            [
                jnp.concatenate(
                    [
                        lhs_ref[end, one : one + pairs].reshape(pairs * blocks, 6 * TB)
                        for one in steps
                    ],
                    axis=1,
                )
                for end in range(2)
            ],
            axis=0,
        )
        bands = band_ref[steps[0] : steps[-1] + 1].reshape(len(steps) * 6 * TB, 2 * TB)
        total = total + jnp.dot(rows, bands, preferred_element_type=jnp.float32)
    for end in range(2):
        write_lines(
            total[end * pairs * blocks : (end + 1) * pairs * blocks],
            out_ref.at[end],
            signal_ref,
            (0, wires - PAD)[end],
            pairs,
            blocks,
        )

    cells = geo_ref.shape[2]
    shards = partial_ref.shape[1] // cells
    own = own_ref[...]
    line = lax.broadcasted_iota(jnp.int32, (TABLE, 128), 0)
    table = jnp.where(line == 0, own >> 7, jnp.where(line == 1, own & 127, 0))
    table = table.astype(jnp.float32).astype(jnp.bfloat16)
    for plane in range(planes):
        partial_ref[plane, shards * cells : shards * cells + TABLE] = table

    for block in range(0, blocks, 2):
        chosen = []
        for side in range(2):
            at = slice((block + side) * TB, (block + side + 1) * TB)
            column = []
            for line in range(wire_blocks):
                tile = signal_ref[line * block_wires : (line + 1) * block_wires, at]
                asked = plan_ref[2, line * blocks + block + side] == 1
                column.append(jnp.where(asked, tile, jnp.zeros_like(tile)))
            chosen.append(jnp.concatenate(column, axis=0))
        sums = jnp.dot(
            turned_ref[...], jnp.concatenate(chosen, axis=1), preferred_element_type=jnp.float32
        ).astype(jnp.bfloat16)
        for side in range(2):
            shard, plane = divmod(block + side, planes)
            partial_ref[plane, shard * cells : (shard + 1) * cells] = sums[
                :, side * TB : (side + 1) * TB
            ]
    mine = lax.axis_index("plane")
    for step, ref in enumerate(part_refs):
        ref[...] = partial_ref[lax.bitwise_xor(mine, step)]


def convolve_edges(
    planes, plan, own, inner, raw, mask, left, right, top, bottom, bands, geometry
):
    wires, ticks = raw.shape
    reach = bands.shape[0]
    cells = geometry.shape[2]
    blocks = ticks // TB
    pitch = -(-(blocks + 2) // 8) * 8
    height = blocks // planes * cells + TABLE
    flops = 2 * blocks * PAD * reach * 6 * TB * 2 * TB
    return pl.pallas_call(
        functools.partial(edge_kernel, planes),
        out_shape=(
            jax.ShapeDtypeStruct((wires, ticks), jnp.bfloat16),
        )
        + (jax.ShapeDtypeStruct((height, TB), jnp.bfloat16),) * planes,
        in_specs=[smem()] + [vmem()] * 10,
        out_specs=(vmem(),) * (1 + planes),
        scratch_shapes=[
            pltpu.VMEM((planes, height, TB), jnp.bfloat16),
            pltpu.VMEM((2, 3 * PAD * pitch, TB), jnp.float32),
            pltpu.VMEM((2, PAD // 2 + reach - 1, blocks, 6 * TB), jnp.bfloat16),
            pltpu.VMEM((2, PAD * blocks, TB), jnp.float32),
            pltpu.VMEM((cells, wires), jnp.bfloat16),
        ],
        cost_estimate=pl.CostEstimate(flops=flops, bytes_accessed=6 * MIB, transcendentals=0),
        compiler_params=pltpu.CompilerParams(vmem_limit_bytes=24 * MIB),
        name="edges",
    )(plan, own, inner, raw, mask, left, right, top, bottom, bands, geometry)


def fold_kernel(planes, *refs):
    pieces = refs[:planes]
    outs = refs[planes:-1]
    sums_ref = refs[-1]
    shards, lines, _ = sums_ref.shape
    cells = lines - TABLE
    mine = lax.axis_index("plane")
    line = lax.broadcasted_iota(jnp.int32, (TABLE, 128), 0)
    table = jnp.zeros((TABLE, 128), jnp.float32)
    for step, ref in enumerate(pieces):
        tags = ref[shards * cells :].astype(jnp.float32)
        plane = lax.bitwise_xor(mine, step)
        table = jnp.where(line == 2 * plane, tags[0:1], table)
        table = jnp.where(line == 2 * plane + 1, tags[1:2], table)
    for shard in range(shards):
        total = jnp.zeros((cells, TB), jnp.float32)
        for ref in pieces:
            total = total + ref[shard * cells : (shard + 1) * cells].astype(jnp.float32)
        sums_ref[shard, 0:cells] = total.astype(jnp.bfloat16)
        sums_ref[shard, cells:lines] = table.astype(jnp.bfloat16)
    mine = lax.axis_index("wire")
    for step, ref in enumerate(outs):
        ref[...] = sums_ref[lax.bitwise_xor(mine, step)]


def fold(pieces, shards):
    cells = (pieces[0].shape[0] - TABLE) // shards
    out = jax.ShapeDtypeStruct((cells + TABLE, TB), jnp.bfloat16)
    return pl.pallas_call(
        functools.partial(fold_kernel, len(pieces)),
        out_shape=(out,) * shards,
        in_specs=[vmem()] * len(pieces),
        out_specs=(vmem(),) * shards,
        scratch_shapes=[pltpu.VMEM((shards, cells + TABLE, TB), jnp.bfloat16)],
        compiler_params=pltpu.CompilerParams(vmem_limit_bytes=4 * MIB),
        name="fold",
    )(*pieces)


def swap_all(parts, axis):
    got = [parts[0]]
    for step in range(1, len(parts)):
        pairs = [(i, i ^ step) for i in range(len(parts))]
        got.append(lax.ppermute(parts[step], axis, pairs))
    return got


def pack_kernel(slots, plan_ref, signal_ref, payload_ref, tiles_ref):
    block_wires = payload_ref.shape[1]
    wires, ticks = signal_ref.shape
    blocks = ticks // TB
    tiles_ref[...] = jnp.zeros_like(tiles_ref)
    for line in range(wires // block_wires):
        for block in range(blocks):
            place = plan_ref[0, line * blocks + block]
            tiles_ref[place] = signal_ref[
                line * block_wires : (line + 1) * block_wires, block * TB : (block + 1) * TB
            ]
    payload_ref[...] = tiles_ref[0:slots]


def pack_tiles(plan, signal, slots, block_wires):
    return pl.pallas_call(
        functools.partial(pack_kernel, slots),
        out_shape=jax.ShapeDtypeStruct((slots, block_wires, TB), jnp.bfloat16),
        in_specs=[smem(), vmem()],
        out_specs=vmem(),
        scratch_shapes=[pltpu.VMEM((slots + 1, block_wires, TB), jnp.bfloat16)],
        cost_estimate=pl.CostEstimate(flops=10**8, bytes_accessed=3 * MIB, transcendentals=0),
        compiler_params=pltpu.CompilerParams(vmem_limit_bytes=8 * MIB),
        name="pack",
    )(plan, signal)


def stage_kernel(slots, plan_ref, geo_ref, out_ref, rows_ref):
    groups = out_ref.shape[0]
    rows_ref[...] = jnp.zeros_like(rows_ref)
    for slot in range(slots):
        rows_ref[plan_ref[0, slot]] = geo_ref[plan_ref[2, slot]]
    for group in range(groups):
        rows = rows_ref[group * GROUP : (group + 1) * GROUP]
        out_ref[group] = jnp.transpose(rows.reshape(-1, rows.shape[-1]))


def stage_geometry(plan, geometry, groups, slots):
    _, block_wires, cells = geometry.shape
    return pl.pallas_call(
        functools.partial(stage_kernel, slots),
        out_shape=jax.ShapeDtypeStruct((groups, cells, GROUP * block_wires), jnp.bfloat16),
        in_specs=[smem(), vmem()],
        out_specs=vmem(),
        scratch_shapes=[pltpu.VMEM((groups * GROUP + 1, block_wires, cells), jnp.bfloat16)],
        cost_estimate=pl.CostEstimate(flops=10**8, bytes_accessed=3 * MIB, transcendentals=0),
        compiler_params=pltpu.CompilerParams(vmem_limit_bytes=12 * MIB),
        name="stage",
    )(plan, geometry)


def image_kernel(owner_total, share, plan_ref, arrived_ref, staged_ref, image_ref, tiles_ref):
    cells, ticks = image_ref.shape
    block_wires = arrived_ref.shape[1]
    groups = staged_ref.shape[0]
    is_hot = plan_ref[1, 0] == plan_ref[1, 2]
    counts = plan_ref[1, 3] == 1

    @pl.when(is_hot)
    def _():
        for source in range(owner_total):
            sums = arrived_ref[source * share : source * share + cells // block_wires]
            image_ref[:, source * TB : (source + 1) * TB] = sums.reshape(cells, TB).astype(
                jnp.float32
            )

    @pl.when(jnp.logical_not(is_hot))
    def _():
        image_ref[...] = jnp.zeros_like(image_ref)
        tiles_ref[...] = jnp.zeros_like(tiles_ref)

        @pl.when(counts)
        def _():
            for slot in range(owner_total * share):
                tiles_ref[plan_ref[0, slot]] = arrived_ref[slot]
            for group in range(groups):
                tiles = tiles_ref[group * GROUP : (group + 1) * GROUP]
                at = pl.ds(pl.multiple_of(plan_ref[3, group] * TB, TB), TB)
                image_ref[:, at] += jnp.dot(
                    staged_ref[group],
                    tiles.reshape(GROUP * block_wires, TB),
                    preferred_element_type=jnp.float32,
                )


def make_image(plan, arrived, staged, owner_total, share, ticks):
    groups, cells, _ = staged.shape
    block_wires = arrived.shape[1]
    return pl.pallas_call(
        functools.partial(image_kernel, owner_total, share),
        out_shape=jax.ShapeDtypeStruct((cells, ticks), jnp.float32),
        in_specs=[smem(), vmem(), vmem()],
        out_specs=vmem(),
        scratch_shapes=[
            pltpu.VMEM((groups * GROUP + 1, block_wires, TB), jnp.bfloat16),
        ],
        cost_estimate=pl.CostEstimate(flops=10**8, bytes_accessed=3 * MIB, transcendentals=0),
        compiler_params=pltpu.CompilerParams(vmem_limit_bytes=16 * MIB),
        name="image",
    )(plan, arrived, staged)


def more_kernel(owner_total, planes, share, plan_ref, table_ref, arrived_ref, geo_ref, before_ref, image_ref):
    cells, ticks = image_ref.shape
    blocks = ticks // TB
    wire_blocks = geo_ref.shape[0] // owner_total
    image_ref[...] = before_ref[...]

    @pl.when(plan_ref[1, 0] != plan_ref[1, 2])
    def _():
        def add(source, carry):
            for slot in range(share):
                block = table_ref[source, slot]
                at = pl.multiple_of((block % blocks) * TB, TB)
                image_ref[:, pl.ds(at, TB)] += lax.dot_general(
                    geo_ref[home(source, planes, owner_total) * wire_blocks + block // blocks],
                    arrived_ref[source * share + slot],
                    (((0,), (0,)), ((), ())),
                    preferred_element_type=jnp.float32,
                )
            return carry

        lax.fori_loop(0, owner_total, add, 0)


def add_to_image(plan, table, arrived, geometry, owner_total, planes, share, image):
    return pl.pallas_call(
        functools.partial(more_kernel, owner_total, planes, share),
        out_shape=jax.ShapeDtypeStruct(image.shape, jnp.float32),
        in_specs=[smem(), smem()] + [vmem()] * 3,
        out_specs=vmem(),
        compiler_params=pltpu.CompilerParams(vmem_limit_bytes=16 * MIB),
        name="image_more",
    )(plan, table, arrived, geometry, image)


def further_round(
    trip, image, signal, geometry, rows, packed, plan, owner_total, planes, share
):
    trip, signal, rows, packed, plan = lax.optimization_barrier((trip, signal, rows, packed, plan))
    step = trip + plan[1, 3]
    hot = plan[1, 0]
    me = plan[1, 2]
    block_wires = geometry.shape[1]
    wire_count, tick_count = signal.shape
    blocks = tick_count // TB
    wire_blocks = wire_count // block_wires
    ids = jnp.arange(owner_total, dtype=jnp.int32)

    def ranks(owners):
        member = (owners[..., None] == ids).astype(jnp.int32)
        before = jnp.cumsum(member, axis=-2) - member
        return jnp.sum(before * member, axis=-1) - step * share

    def live(owners, rank):
        return (owners < owner_total) & (owners != hot) & (rank >= 0) & (rank < share)

    owners = packed[0] >> 7
    block = packed[0] & 127
    rank = ranks(owners)
    place = jnp.where(live(owners, rank), owners * share + rank, owner_total * share)
    tiles = signal.reshape(wire_blocks, block_wires, blocks, TB).transpose(0, 2, 1, 3)
    tiles = tiles.reshape(wire_blocks * blocks, block_wires, TB)[block]
    payload = jnp.zeros((owner_total * share, block_wires, TB), jnp.bfloat16)
    payload = payload.at[place].set(tiles, mode="drop")
    arrived = exchange(payload.reshape(owner_total, share, block_wires, TB))

    owners = rows >> 7
    rank = ranks(owners)
    source = jnp.arange(owner_total, dtype=jnp.int32)[:, None]
    line = jnp.where(live(owners, rank) & (owners == me), source, owner_total)
    table = jnp.zeros((owner_total, 128), jnp.int32)
    table = table.at[line, jnp.maximum(rank, 0)].set(rows & 127, mode="drop")
    return add_to_image(
        plan,
        table,
        arrived.reshape(owner_total * share, block_wires, TB),
        geometry,
        owner_total,
        planes,
        share,
        image,
    )


def tick_halo(sides):
    devices = lax.axis_size("tick")
    if devices == 2:
        tick = lax.axis_index("tick")
        got = lax.ppermute(sides[0], "tick", [(0, 1), (1, 0)])
        nothing = jnp.zeros_like(got)
        return jnp.where(tick == 0, nothing, got), jnp.where(tick == 0, got, nothing)
    up = [(i, i + 1) for i in range(devices - 1)]
    down = [(i + 1, i) for i in range(devices - 1)]
    return lax.ppermute(sides[1], "tick", up), lax.ppermute(sides[0], "tick", down)


def wire_halo(first, last, left, right):
    devices = lax.axis_size("wire")
    odd = lax.axis_index("wire") % 2 == 1
    last = jnp.concatenate([left[-PAD:], last, right[-PAD:]], axis=1)
    first = jnp.concatenate([left[:PAD], first, right[:PAD]], axis=1)
    got = []
    for begin, rows in ((0, jnp.where(odd, first, last)), (1, jnp.where(odd, last, first))):
        pairs = [(i, i + 1) for i in range(begin, devices - 1, 2)]
        got.append(lax.ppermute(rows, "wire", pairs + [(j, i) for i, j in pairs]))
    return jnp.where(odd, got[0], got[1]), jnp.where(odd, got[1], got[0])


def exchange(array, axes=("wire", "plane")):
    return lax.all_to_all(array, axes, split_axis=0, concat_axis=0, tiled=True)


def shards(raw, chan_mask, kernel, geometry, roi_block, roi_owner):
    wires, ticks = raw.shape
    slot_count = roi_block.shape[0]
    block_wires = geometry.shape[1]
    cells = geometry.shape[2]
    tick_blocks = ticks // TB
    planes = lax.axis_size("plane")
    wire_shards = lax.axis_size("wire")
    owner_total = planes * wire_shards
    share = -(-(slot_count - CAP) // (owner_total - 1))

    mask, first, last, packed, send_plan, *sides = prepare(
        raw, chan_mask, roi_owner, roi_block, planes, owner_total, share
    )
    left, right = tick_halo(sides)
    top, bottom = wire_halo(first, last, left, right)
    bands = make_bands(kernel[0])
    inner = convolve_inner(raw, mask, left, right, bands)
    signal, *parts = convolve_edges(
        planes, send_plan, packed, inner, raw, mask, left, right, top, bottom, bands, geometry
    )

    pieces = swap_all(parts, "plane")
    payload = pack_tiles(send_plan, signal, owner_total * share, block_wires)
    pieces, payload = lax.optimization_barrier((pieces, payload))
    pieces = swap_all(fold(pieces, wire_shards), "wire")

    plan, rows = make_receive_plan(
        pieces, packed, owner_total, planes, share, wires // block_wires, tick_blocks
    )
    staged = stage_geometry(
        plan, geometry, group_total(owner_total, share, tick_blocks), owner_total * share
    )

    sums = sum(piece[:cells].astype(jnp.float32) for piece in pieces).astype(jnp.bfloat16)
    payload = lax.dynamic_update_slice(
        payload.reshape(owner_total, share, block_wires, TB),
        sums.reshape(1, cells // block_wires, block_wires, TB),
        (send_plan[1, 0], 0, 0, 0),
    )
    arrived = exchange(payload).reshape(owner_total * share, block_wires, TB)
    image = make_image(plan, arrived, staged, owner_total, share, ticks)

    trips = agree(plan[1:2, 1:2])[0, 0]
    image = lax.fori_loop(
        0,
        trips,
        lambda trip, now: further_round(
            trip, now, signal, geometry, rows, packed, plan, owner_total, planes, share
        ),
        image,
    )
    return signal, image


def solution(mesh):
    in_specs = (
        P(("plane", "wire"), "tick"),
        P(("plane", "wire")),
        P("plane", None, None),
        P(),
        P(("plane", "wire", "tick")),
        P(("plane", "wire", "tick")),
    )
    out_specs = (P(("plane", "wire"), "tick"), P(("plane", "wire"), "tick"))
    return jax.shard_map(shards, mesh=mesh, in_specs=in_specs, out_specs=out_specs, check_vma=False)
```

```python
import functools

import jax
import jax.numpy as jnp
from jax import lax
from jax.experimental import pallas as pl
from jax.experimental.pallas import tpu as pltpu
from jax.sharding import PartitionSpec as P

TB = 128
CAP = 25
PAD = 16
TABLE = 8
STEPS = 4
MIB = 1024 * 1024


def vmem():
    return pl.BlockSpec(memory_space=pltpu.VMEM)


def smem():
    return pl.BlockSpec(memory_space=pltpu.SMEM)


GROUP = 8


def home(position, planes, owner_total):
    return (position % planes) * (owner_total // planes) + position // planes


def lane_numbers():
    return lax.broadcasted_iota(jnp.int32, (1, 128), 1)


def earlier_lanes():
    return (
        lax.broadcasted_iota(jnp.int32, (128, 128), 0)
        < lax.broadcasted_iota(jnp.int32, (128, 128), 1)
    ).astype(jnp.bfloat16)


def count_before(member, before):
    return jnp.dot(
        member.astype(jnp.float32).astype(jnp.bfloat16), before, preferred_element_type=jnp.float32
    )


def most_named(owners, owner_total):
    lanes = lane_numbers()
    counts = jnp.full(owners.shape, -1.0, jnp.float32)
    for owner in range(owner_total):
        named = jnp.sum((owners == owner).astype(jnp.float32), axis=1, keepdims=True)
        counts = jnp.where(lanes == owner, named, counts)
    top = jnp.max(counts, axis=1, keepdims=True)
    chosen = jnp.min(
        jnp.where(counts == top, lanes.astype(jnp.float32), 127.0), axis=1, keepdims=True
    )
    return counts, chosen


def prepare_kernel(
    planes,
    owner_total,
    share,
    tick_total,
    raw_hbm,
    mask_hbm,
    owner_hbm,
    block_hbm,
    mask_out,
    first_ref,
    last_ref,
    own_ref,
    out_ref,
    *rest,
):
    wires, ticks = raw_hbm.shape
    count = 1 if tick_total == 2 else 2
    sides = rest[:count]
    side_refs = rest[count : 2 * count]
    first_buf, last_buf, mask_ref, owner_ref, block_ref, sems = rest[2 * count :]
    tick = lax.axis_index("tick")
    me = lax.axis_index("wire") * planes + lax.axis_index("plane")
    if tick_total == 2:
        starts = [pl.multiple_of((1 - tick) * (ticks - TB), TB)]
    else:
        starts = [0, ticks - TB]
    moves = [(mask_hbm, mask_ref), (owner_hbm, owner_ref), (block_hbm, block_ref)]
    moves += [(raw_hbm.at[:, pl.ds(start, TB)], ref) for start, ref in zip(starts, side_refs)]
    moves += [(raw_hbm.at[pl.ds(0, PAD)], first_buf), (raw_hbm.at[pl.ds(wires - PAD, PAD)], last_buf)]
    copies = [
        pltpu.make_async_copy(source, target, sems.at[index])
        for index, (source, target) in enumerate(moves)
    ]
    for copy in copies:
        copy.start()
    for copy in copies[:3]:
        copy.wait()

    for part in range(wires // 128):
        row = mask_ref[part : part + 1].astype(jnp.float32)
        wide = jnp.transpose(jnp.broadcast_to(row, (128, 128)))
        mask_out[part * 128 : (part + 1) * 128] = wide.astype(jnp.bfloat16)

    lanes = lane_numbers()
    slot_count = owner_ref.shape[1]
    owner = owner_ref[...]
    wire_shards = owner_total // planes
    none = owner_total * 128
    own_ref[...] = jnp.where(lanes == 127, none + me, none)
    own_ref[:, 0:slot_count] = (
        (owner % wire_shards) * planes + owner // wire_shards
    ) * 128 + block_ref[...]
    own = own_ref[...]
    _, hot = most_named(own >> 7, owner_total)
    rows = lax.broadcasted_iota(jnp.int32, (owner_total, 128), 0)
    member = (own >> 7) == rows
    rank = count_before(member, earlier_lanes())
    step = lax.bitwise_xor(rows, jnp.full_like(rows, me)).astype(jnp.float32)
    place = jnp.where(rank < share, step * share + rank, -1.0)
    place = jnp.where(rows.astype(jnp.float32) == hot, -2.0, place)
    place = jnp.sum(jnp.where(member, place + 3.0, 0.0), axis=0, keepdims=True)

    column = jnp.transpose(jnp.broadcast_to(own.astype(jnp.float32), (128, 128)))
    column = column.astype(jnp.int32)
    here = ((column & 127) == lanes) & ((column >> 7) < owner_total)
    spread = jnp.transpose(jnp.broadcast_to(place, (128, 128)))
    placed = jnp.sum(jnp.where(here, spread, 0.0), axis=0, keepdims=True)
    trash = float(owner_total * share)
    facts = jnp.where(lanes == 2, me, 0)
    out_ref[...] = jnp.zeros_like(out_ref)
    out_ref[0:1, :] = jnp.where(placed >= 3.0, placed - 3.0, trash).astype(jnp.int32)
    out_ref[1:2, :] = jnp.where(lanes == 0, hot.astype(jnp.int32), facts)
    out_ref[2:3, :] = (placed == 1.0).astype(jnp.int32)

    for copy in copies[3:]:
        copy.wait()
    for side, ref in zip(sides, side_refs):
        side[...] = ref[...] * mask_out[...]
    for block in range(ticks // TB):
        at = slice(block * TB, (block + 1) * TB)
        first_ref[:, at] = first_buf[:, at] * mask_out[0:PAD]
        last_ref[:, at] = last_buf[:, at] * mask_out[wires - PAD : wires]


def prepare(raw, chan_mask, roi_owner, roi_block, planes, owner_total, share):
    wires, ticks = raw.shape
    tick_total = lax.axis_size("tick")
    sides = 1 if tick_total == 2 else 2
    side = jax.ShapeDtypeStruct((wires, TB), jnp.bfloat16)
    edge = jax.ShapeDtypeStruct((PAD, ticks), jnp.bfloat16)
    row = jax.ShapeDtypeStruct((1, 128), jnp.int32)
    table = jax.ShapeDtypeStruct((8, 128), jnp.int32)
    slot_count = roi_owner.shape[0]
    return pl.pallas_call(
        functools.partial(prepare_kernel, planes, owner_total, share, tick_total),
        out_shape=(side, edge, edge, row, table) + (side,) * sides,
        in_specs=[pl.BlockSpec(memory_space=pltpu.HBM)] * 4,
        out_specs=(vmem(),) * (5 + sides),
        scratch_shapes=[pltpu.VMEM((wires, TB), jnp.bfloat16)] * sides
        + [pltpu.VMEM((PAD, ticks), jnp.bfloat16)] * 2
        + [pltpu.VMEM((wires // 128, 128), jnp.int32)]
        + [pltpu.VMEM((1, slot_count), jnp.int32)] * 2
        + [pltpu.SemaphoreType.DMA((sides + 5,))],
        compiler_params=pltpu.CompilerParams(vmem_limit_bytes=60 * MIB),
        name="prepare",
    )(raw, chan_mask.reshape(wires // 128, 128), roi_owner[None], roi_block[None])


def receive_kernel(owner_total, planes, share, wire_blocks, tick_blocks, own_ref, *refs):
    pieces = refs[:-2]
    out_ref, rows_ref = refs[-2:]
    lanes = lane_numbers()
    lane_f = lanes.astype(jnp.float32)
    place = lax.broadcasted_iota(jnp.int32, (owner_total, 128), 0)
    shard = lax.axis_index("wire")
    every = jnp.zeros((owner_total, 128), jnp.float32)
    for step, ref in enumerate(pieces):
        tags = ref[ref.shape[0] - TABLE :].astype(jnp.float32)
        at = lax.bitwise_xor(shard, step) * planes
        for plane in range(planes):
            row = tags[2 * plane : 2 * plane + 1] * 128.0 + tags[2 * plane + 1 : 2 * plane + 2]
            every = jnp.where(place == at + plane, row, every)
    every = every.astype(jnp.int32)
    rows_ref[...] = every
    owners = every >> 7
    own = own_ref[...]
    me = jnp.sum(jnp.where(lanes == 127, own & 127, 0).astype(jnp.float32), axis=1, keepdims=True)

    counts, chosen = most_named(owners, owner_total)
    hot = jnp.max(chosen, axis=0, keepdims=True)
    agreed = hot == jnp.min(chosen, axis=0, keepdims=True)
    left = jnp.where(agreed & (lane_f == hot), 0.0, counts)
    fullest = jnp.max(jnp.max(left, axis=1, keepdims=True), axis=0, keepdims=True)
    start = agreed.astype(jnp.float32)
    trips = -start
    for step in range(-(-CAP // share)):
        trips = trips + (fullest > step * share).astype(jnp.float32)
    trips = jnp.maximum(trips, 0.0)
    hot = jnp.where(agreed, hot, -1.0)

    to_me = owners.astype(jnp.float32) == me
    before = earlier_lanes()
    rank = count_before(to_me, before)
    blocks = every & 127
    source = lax.broadcasted_iota(jnp.int32, (owner_total, 128), 0)
    line = home(source, planes, owner_total) * wire_blocks + blocks // tick_blocks
    line = line.astype(jnp.float32)
    tick = (blocks % tick_blocks).astype(jnp.float32)
    lines = jnp.zeros((1, 128), jnp.float32)
    ticks = jnp.full((1, 128), -1.0, jnp.float32)
    for slot in range(share):
        got = to_me & (rank == slot)
        here = lanes == source * share + slot
        for value, where in ((line, 0), (tick + 1.0, 1)):
            one = jnp.sum(jnp.where(got, value, 0.0), axis=1, keepdims=True)
            one = jnp.sum(jnp.where(here, one, 0.0), axis=0, keepdims=True)
            if where == 0:
                lines = lines + one
            else:
                ticks = ticks + one

    block_rows = lax.broadcasted_iota(jnp.int32, (tick_blocks, 128), 0).astype(jnp.float32)
    member = block_rows == ticks
    rank = count_before(member, before)
    total = jnp.sum(member.astype(jnp.float32), axis=1, keepdims=True)
    groups = jnp.zeros_like(total)
    for step in range(0, owner_total * share, GROUP):
        groups = groups + (total > step).astype(jnp.float32)
    lower = (
        lax.broadcasted_iota(jnp.int32, (tick_blocks, tick_blocks), 0)
        > lax.broadcasted_iota(jnp.int32, (tick_blocks, tick_blocks), 1)
    ).astype(jnp.bfloat16)
    base = jnp.dot(
        lower,
        jnp.broadcast_to(groups, (tick_blocks, 128)).astype(jnp.bfloat16),
        preferred_element_type=jnp.float32,
    )
    place = jnp.sum(jnp.where(member, base * GROUP + rank, 0.0), axis=0, keepdims=True)
    trash = float(group_total(owner_total, share, tick_blocks) * GROUP)
    place = jnp.where(ticks < 0.0, trash, place)
    inside = (base <= lane_f) & (lane_f < base + groups)
    group_tick = jnp.sum(jnp.where(inside, block_rows, 0.0), axis=0, keepdims=True)

    facts = jnp.where(lanes == 0, hot, 0.0)
    facts = jnp.where(lanes == 1, trips, facts)
    facts = jnp.where(lanes == 2, me, facts)
    facts = jnp.where(lanes == 3, start, facts)
    out_ref[...] = jnp.zeros_like(out_ref)
    out_ref[0:1, :] = place.astype(jnp.int32)
    out_ref[1:2, :] = facts.astype(jnp.int32)
    out_ref[2:3, :] = lines.astype(jnp.int32)
    out_ref[3:4, :] = group_tick.astype(jnp.int32)


def group_total(owner_total, share, tick_blocks):
    return (owner_total * share - tick_blocks) // GROUP + tick_blocks


def make_receive_plan(pieces, packed, owner_total, planes, share, wire_blocks, tick_blocks):
    return pl.pallas_call(
        functools.partial(receive_kernel, owner_total, planes, share, wire_blocks, tick_blocks),
        out_shape=(
            jax.ShapeDtypeStruct((8, 128), jnp.int32),
            jax.ShapeDtypeStruct((owner_total, 128), jnp.int32),
        ),
        in_specs=[vmem()] * (1 + len(pieces)),
        out_specs=(vmem(), vmem()),
        compiler_params=pltpu.CompilerParams(vmem_limit_bytes=2 * MIB),
        name="receive_plan",
    )(packed, *pieces)


def agree(rounds):
    devices = lax.axis_size("tick")
    reach = 1
    while reach < devices:
        ring = [(i, (i + reach) % devices) for i in range(devices)]
        rounds = jnp.maximum(rounds, lax.ppermute(rounds, "tick", ring))
        reach *= 2
    return rounds


def band_kernel(taps_w, taps_ref, band_ref):
    row = lax.broadcasted_iota(jnp.int32, (TB, TB), 0)
    col = lax.broadcasted_iota(jnp.int32, (TB, TB), 1)
    pairs = (taps_w + 1) // 2
    band_ref[0, 0 : 3 * TB, TB : 2 * TB] = jnp.zeros((3 * TB, TB), jnp.bfloat16)
    band_ref[pairs - 1, 3 * TB : 6 * TB, 0:TB] = jnp.zeros((3 * TB, TB), jnp.bfloat16)
    taps = taps_ref[...].astype(jnp.float32)
    for tap in range(taps_w):
        spread = jnp.broadcast_to(taps[tap : tap + 1], (TB, 2 * TB))
        rolled = pltpu.roll(spread, TB, 1, stride=1, stride_axis=0)
        middle = rolled[:, :TB]
        outer = rolled[:, TB:]
        bands = (
            jnp.where(col < row, outer, 0.0).astype(jnp.bfloat16),
            middle.astype(jnp.bfloat16),
            jnp.where(col >= row, outer, 0.0).astype(jnp.bfloat16),
        )
        for first, second in ((0, 0), (1, 1), (1, 0), (0, 1)):
            if (tap - first + second) % 2:
                continue
            pair = (tap - first + second) // 2
            for piece in range(3):
                start = (first * 3 + piece) * TB
                band_ref[pair, start : start + TB, second * TB : (second + 1) * TB] = bands[piece]


def make_bands(taps):
    taps_w = taps.shape[0]
    return pl.pallas_call(
        functools.partial(band_kernel, taps_w),
        out_shape=jax.ShapeDtypeStruct(((taps_w + 1) // 2, 6 * TB, 2 * TB), jnp.bfloat16),
        in_specs=[vmem()],
        out_specs=vmem(),
        cost_estimate=pl.CostEstimate(flops=10**9, bytes_accessed=6 * MIB, transcendentals=0),
        compiler_params=pltpu.CompilerParams(vmem_limit_bytes=16 * MIB),
        name="bands",
    )(taps)


def spread_pair(wide_ref, lhs_view, line, pitch, blocks):
    for side in range(2):
        for piece in range(3):
            at = (side * 3 + piece) * TB
            lhs_view[:, at : at + TB] = wide_ref[
                pl.ds((line + side) * pitch + piece, blocks), :
            ].astype(jnp.bfloat16)


def write_lines(total, out_view, signal_ref, line, pairs, blocks):
    for pair in range(pairs):
        for side in range(2):
            out_view[pl.ds((2 * pair + side) * blocks, blocks), :] = total[
                pair * blocks : (pair + 1) * blocks, side * TB : (side + 1) * TB
            ]
    for block in range(blocks):
        signal_ref[line : line + 2 * pairs, block * TB : (block + 1) * TB] = out_view[
            pl.ds(block, 2 * pairs, stride=blocks), :
        ].astype(jnp.bfloat16)


def inner_kernel(
    chunks,
    raw_ref,
    mask_ref,
    left_ref,
    right_ref,
    band_ref,
    inner_ref,
    wide_ref,
    lhs_ref,
    out_ref,
):
    wires, ticks = raw_ref.shape
    blocks = ticks // TB
    pitch = wide_ref.shape[0] // wires
    reach = band_ref.shape[0]
    span = 2 * PAD
    groups = wires // span

    def fill(group, block):
        lines = slice(group * span, (group + 1) * span)
        if block == 0:
            inner = left_ref[lines]
        elif block == blocks + 1:
            inner = right_ref[lines]
        else:
            inner = raw_ref[lines, (block - 1) * TB : block * TB] * mask_ref[lines]
        wide_ref[pl.ds(group * span * pitch + block, span, stride=pitch), :] = inner.astype(
            jnp.float32
        )

    margin = reach - 1
    begin = PAD // 2
    state = {"group": 0, "pair": begin}

    def prepare(upto):
        todo = []
        while state["pair"] < upto:
            line = 2 * state["pair"] - margin
            while state["group"] < groups and line + 1 >= state["group"] * span:
                group = state["group"]
                for block in range(blocks + 2):
                    todo.append(lambda group=group, block=block: fill(group, block))
                state["group"] += 1
            todo.append(
                lambda line=line, pair=state["pair"]: spread_pair(
                    wide_ref, lhs_ref.at[pair - begin], line, pitch, blocks
                )
            )
            state["pair"] += 1
        return todo

    pair = begin
    for job in prepare(pair + chunks[0] + margin):
        job()
    for index, size in enumerate(chunks):
        todo = prepare(pair + size + chunks[index + 1] + margin) if index + 1 < len(chunks) else []
        each = -(-len(todo) // reach)
        total = jnp.zeros((size * blocks, 2 * TB), jnp.float32)
        for step in range(0, reach, STEPS):
            steps = range(step, min(step + STEPS, reach))
            rows = [
                lhs_ref[pair - begin + one : pair - begin + one + size].reshape(
                    size * blocks, 6 * TB
                )
                for one in steps
            ]
            bands = band_ref[steps[0] : steps[-1] + 1].reshape(len(steps) * 6 * TB, 2 * TB)
            total = total + jnp.dot(
                jnp.concatenate(rows, axis=1), bands, preferred_element_type=jnp.float32
            )
            for job in todo[step * each : (steps[-1] + 1) * each]:
                job()
        write_lines(total, out_ref.at[index % 2], inner_ref, 2 * (pair - begin), size, blocks)
        pair += size


def convolve_inner(raw, mask, left, right, bands):
    wires, ticks = raw.shape
    reach = bands.shape[0]
    blocks = ticks // TB
    pitch = -(-(blocks + 2) // 8) * 8
    pairs = (wires - 2 * PAD) // 2
    chunks = []
    while sum(chunks) < pairs:
        chunks.append(min(32 if chunks else 16, pairs - sum(chunks)))
    flops = 2 * blocks * pairs * reach * 6 * TB * 2 * TB
    return pl.pallas_call(
        functools.partial(inner_kernel, tuple(chunks)),
        out_shape=jax.ShapeDtypeStruct((wires - 2 * PAD, ticks), jnp.bfloat16),
        in_specs=[vmem()] * 5,
        out_specs=vmem(),
        scratch_shapes=[
            pltpu.VMEM((wires * pitch, TB), jnp.float32),
            pltpu.VMEM((pairs + reach - 1, blocks, 6 * TB), jnp.bfloat16),
            pltpu.VMEM((2, 2 * max(chunks) * blocks, TB), jnp.float32),
        ],
        cost_estimate=pl.CostEstimate(flops=flops, bytes_accessed=6 * MIB, transcendentals=0),
        compiler_params=pltpu.CompilerParams(vmem_limit_bytes=28 * MIB),
        name="inner",
    )(raw, mask, left, right, bands)


def edge_kernel(
    planes,
    plan_ref,
    own_ref,
    inner_ref,
    raw_ref,
    mask_ref,
    left_ref,
    right_ref,
    top_ref,
    bottom_ref,
    band_ref,
    geo_ref,
    signal_ref,
    *refs,
):
    part_refs = refs[:planes]
    partial_ref, wide_ref, lhs_ref, out_ref, turned_ref = refs[planes:]
    wires, ticks = signal_ref.shape
    blocks = ticks // TB
    reach = band_ref.shape[0]
    block_wires = geo_ref.shape[1]
    wire_blocks = wires // block_wires
    near = 2 * PAD
    lines = PAD + near
    pitch = wide_ref.shape[1] // lines
    pairs = PAD // 2
    margin = reach - 1

    signal_ref[PAD : wires - PAD] = inner_ref[...]
    source = home(plan_ref[1, 2], planes, geo_ref.shape[0] // wire_blocks)
    rows = geo_ref[pl.ds(source * wire_blocks, wire_blocks)].reshape(wires, -1)
    turned_ref[...] = jnp.transpose(rows)

    for end in range(2):
        halo_ref = (top_ref, bottom_ref)[end]
        mine = (slice(0, near), slice(wires - near, wires))[end]
        halo_at = (0, near)[end]
        mine_at = (PAD, 0)[end]
        for block in range(blocks + 2):
            columns = slice(block * TB, (block + 1) * TB)
            if block == 0:
                inner = left_ref[mine].astype(jnp.float32)
            elif block == blocks + 1:
                inner = right_ref[mine].astype(jnp.float32)
            else:
                inner = raw_ref[mine, (block - 1) * TB : block * TB] * mask_ref[mine]
                inner = inner.astype(jnp.float32)
            wide_ref[end, pl.ds(halo_at * pitch + block, PAD, stride=pitch), :] = halo_ref[
                :, columns
            ].astype(jnp.float32)
            wide_ref[end, pl.ds(mine_at * pitch + block, near, stride=pitch), :] = inner
        first = (PAD, near - PAD)[end] - margin
        for pair in range(pairs + margin):
            spread_pair(
                wide_ref.at[end], lhs_ref.at[end, pair], first + 2 * pair, pitch, blocks
            )

    total = jnp.zeros((2 * pairs * blocks, 2 * TB), jnp.float32)
    for step in range(0, reach, STEPS):
        steps = range(step, min(step + STEPS, reach))
        rows = jnp.concatenate(
            [
                jnp.concatenate(
                    [
                        lhs_ref[end, one : one + pairs].reshape(pairs * blocks, 6 * TB)
                        for one in steps
                    ],
                    axis=1,
                )
                for end in range(2)
            ],
            axis=0,
        )
        bands = band_ref[steps[0] : steps[-1] + 1].reshape(len(steps) * 6 * TB, 2 * TB)
        total = total + jnp.dot(rows, bands, preferred_element_type=jnp.float32)
    for end in range(2):
        write_lines(
            total[end * pairs * blocks : (end + 1) * pairs * blocks],
            out_ref.at[end],
            signal_ref,
            (0, wires - PAD)[end],
            pairs,
            blocks,
        )

    cells = geo_ref.shape[2]
    shards = partial_ref.shape[1] // cells
    own = own_ref[...]
    line = lax.broadcasted_iota(jnp.int32, (TABLE, 128), 0)
    table = jnp.where(line == 0, own >> 7, jnp.where(line == 1, own & 127, 0))
    table = table.astype(jnp.float32).astype(jnp.bfloat16)
    for plane in range(planes):
        partial_ref[plane, shards * cells : shards * cells + TABLE] = table

    for block in range(0, blocks, 2):
        chosen = []
        for side in range(2):
            at = slice((block + side) * TB, (block + side + 1) * TB)
            column = []
            for line in range(wire_blocks):
                tile = signal_ref[line * block_wires : (line + 1) * block_wires, at]
                asked = plan_ref[2, line * blocks + block + side] == 1
                column.append(jnp.where(asked, tile, jnp.zeros_like(tile)))
            chosen.append(jnp.concatenate(column, axis=0))
        sums = jnp.dot(
            turned_ref[...], jnp.concatenate(chosen, axis=1), preferred_element_type=jnp.float32
        ).astype(jnp.bfloat16)
        for side in range(2):
            shard, plane = divmod(block + side, planes)
            partial_ref[plane, shard * cells : (shard + 1) * cells] = sums[
                :, side * TB : (side + 1) * TB
            ]
    mine = lax.axis_index("plane")
    for step, ref in enumerate(part_refs):
        ref[...] = partial_ref[lax.bitwise_xor(mine, step)]


def convolve_edges(
    planes, plan, own, inner, raw, mask, left, right, top, bottom, bands, geometry
):
    wires, ticks = raw.shape
    reach = bands.shape[0]
    cells = geometry.shape[2]
    blocks = ticks // TB
    pitch = -(-(blocks + 2) // 8) * 8
    height = blocks // planes * cells + TABLE
    flops = 2 * blocks * PAD * reach * 6 * TB * 2 * TB
    return pl.pallas_call(
        functools.partial(edge_kernel, planes),
        out_shape=(
            jax.ShapeDtypeStruct((wires, ticks), jnp.bfloat16),
        )
        + (jax.ShapeDtypeStruct((height, TB), jnp.bfloat16),) * planes,
        in_specs=[smem()] + [vmem()] * 10,
        out_specs=(vmem(),) * (1 + planes),
        scratch_shapes=[
            pltpu.VMEM((planes, height, TB), jnp.bfloat16),
            pltpu.VMEM((2, 3 * PAD * pitch, TB), jnp.float32),
            pltpu.VMEM((2, PAD // 2 + reach - 1, blocks, 6 * TB), jnp.bfloat16),
            pltpu.VMEM((2, PAD * blocks, TB), jnp.float32),
            pltpu.VMEM((cells, wires), jnp.bfloat16),
        ],
        cost_estimate=pl.CostEstimate(flops=flops, bytes_accessed=6 * MIB, transcendentals=0),
        compiler_params=pltpu.CompilerParams(vmem_limit_bytes=24 * MIB),
        name="edges",
    )(plan, own, inner, raw, mask, left, right, top, bottom, bands, geometry)


def fold_kernel(planes, *refs):
    pieces = refs[:planes]
    outs = refs[planes:-1]
    sums_ref = refs[-1]
    shards, lines, _ = sums_ref.shape
    cells = lines - TABLE
    mine = lax.axis_index("plane")
    line = lax.broadcasted_iota(jnp.int32, (TABLE, 128), 0)
    table = jnp.zeros((TABLE, 128), jnp.float32)
    for step, ref in enumerate(pieces):
        tags = ref[shards * cells :].astype(jnp.float32)
        plane = lax.bitwise_xor(mine, step)
        table = jnp.where(line == 2 * plane, tags[0:1], table)
        table = jnp.where(line == 2 * plane + 1, tags[1:2], table)
    for shard in range(shards):
        total = jnp.zeros((cells, TB), jnp.float32)
        for ref in pieces:
            total = total + ref[shard * cells : (shard + 1) * cells].astype(jnp.float32)
        sums_ref[shard, 0:cells] = total.astype(jnp.bfloat16)
        sums_ref[shard, cells:lines] = table.astype(jnp.bfloat16)
    mine = lax.axis_index("wire")
    for step, ref in enumerate(outs):
        ref[...] = sums_ref[lax.bitwise_xor(mine, step)]


def fold(pieces, shards):
    cells = (pieces[0].shape[0] - TABLE) // shards
    out = jax.ShapeDtypeStruct((cells + TABLE, TB), jnp.bfloat16)
    return pl.pallas_call(
        functools.partial(fold_kernel, len(pieces)),
        out_shape=(out,) * shards,
        in_specs=[vmem()] * len(pieces),
        out_specs=(vmem(),) * shards,
        scratch_shapes=[pltpu.VMEM((shards, cells + TABLE, TB), jnp.bfloat16)],
        compiler_params=pltpu.CompilerParams(vmem_limit_bytes=4 * MIB),
        name="fold",
    )(*pieces)


def swap_all(parts, axis):
    got = [parts[0]] * len(parts)
    for step in reversed(range(1, len(parts))):
        other = step
        if axis == ("plane", "wire"):
            planes = lax.axis_size("plane")
            other = step % planes * lax.axis_size("wire") + step // planes
        pairs = [(i, i ^ other) for i in range(len(parts))]
        got[step] = lax.ppermute(parts[step], axis, pairs)
    return got


def pack_kernel(slots, plan_ref, signal_ref, payload_ref, tiles_ref):
    block_wires = payload_ref.shape[1]
    wires, ticks = signal_ref.shape
    blocks = ticks // TB
    tiles_ref[...] = jnp.zeros_like(tiles_ref)
    for line in range(wires // block_wires):
        for block in range(blocks):
            place = plan_ref[0, line * blocks + block]
            tiles_ref[place] = signal_ref[
                line * block_wires : (line + 1) * block_wires, block * TB : (block + 1) * TB
            ]
    payload_ref[...] = tiles_ref[0:slots]


def pack_tiles(plan, signal, slots, block_wires):
    return pl.pallas_call(
        functools.partial(pack_kernel, slots),
        out_shape=jax.ShapeDtypeStruct((slots, block_wires, TB), jnp.bfloat16),
        in_specs=[smem(), vmem()],
        out_specs=vmem(),
        scratch_shapes=[pltpu.VMEM((slots + 1, block_wires, TB), jnp.bfloat16)],
        cost_estimate=pl.CostEstimate(flops=10**8, bytes_accessed=3 * MIB, transcendentals=0),
        compiler_params=pltpu.CompilerParams(vmem_limit_bytes=8 * MIB),
        name="pack",
    )(plan, signal)


def place_kernel(shards, share, plan_ref, tiles_ref, *refs):
    pieces = refs[:shards]
    outs = refs[shards:]
    block_wires = tiles_ref.shape[1]
    cells = pieces[0].shape[0] - TABLE
    total = jnp.zeros((cells, TB), jnp.float32)
    for ref in pieces:
        total = total + ref[0:cells].astype(jnp.float32)
    sums = total.astype(jnp.bfloat16).reshape(cells // block_wires, block_wires, TB)
    hot = lax.bitwise_xor(plan_ref[1, 0], plan_ref[1, 2])
    for step, ref in enumerate(outs):
        ref[...] = tiles_ref[step * share : (step + 1) * share]

        @pl.when(hot == step)
        def _(ref=ref):
            ref[0 : cells // block_wires] = sums


def place_sums(plan, tiles, pieces, owner_total, share):
    out = jax.ShapeDtypeStruct((share,) + tiles.shape[1:], tiles.dtype)
    return pl.pallas_call(
        functools.partial(place_kernel, len(pieces), share),
        out_shape=(out,) * owner_total,
        in_specs=[smem()] + [vmem()] * (1 + len(pieces)),
        out_specs=(vmem(),) * owner_total,
        compiler_params=pltpu.CompilerParams(vmem_limit_bytes=6 * MIB),
        name="place",
    )(plan, tiles, *pieces)


def stage_kernel(slots, plan_ref, geo_ref, out_ref, rows_ref):
    groups = out_ref.shape[0]
    rows_ref[...] = jnp.zeros_like(rows_ref)
    for slot in range(slots):
        rows_ref[plan_ref[0, slot]] = geo_ref[plan_ref[2, slot]]
    for group in range(groups):
        rows = rows_ref[group * GROUP : (group + 1) * GROUP]
        out_ref[group] = jnp.transpose(rows.reshape(-1, rows.shape[-1]))


def stage_geometry(plan, geometry, groups, slots):
    _, block_wires, cells = geometry.shape
    return pl.pallas_call(
        functools.partial(stage_kernel, slots),
        out_shape=jax.ShapeDtypeStruct((groups, cells, GROUP * block_wires), jnp.bfloat16),
        in_specs=[smem(), vmem()],
        out_specs=vmem(),
        scratch_shapes=[pltpu.VMEM((groups * GROUP + 1, block_wires, cells), jnp.bfloat16)],
        cost_estimate=pl.CostEstimate(flops=10**8, bytes_accessed=3 * MIB, transcendentals=0),
        compiler_params=pltpu.CompilerParams(vmem_limit_bytes=12 * MIB),
        name="stage",
    )(plan, geometry)


def image_kernel(owner_total, share, plan_ref, staged_ref, *refs):
    arrived = refs[:owner_total]
    image_ref, tiles_ref = refs[owner_total:]
    cells, ticks = image_ref.shape
    block_wires = arrived[0].shape[1]
    groups = staged_ref.shape[0]
    me = plan_ref[1, 2]
    is_hot = plan_ref[1, 0] == me
    counts = plan_ref[1, 3] == 1

    @pl.when(is_hot)
    def _():
        for step, ref in enumerate(arrived):
            at = pl.multiple_of(lax.bitwise_xor(me, step) * TB, TB)
            sums = ref[0 : cells // block_wires]
            image_ref[:, pl.ds(at, TB)] = sums.reshape(cells, TB).astype(jnp.float32)

    @pl.when(jnp.logical_not(is_hot))
    def _():
        image_ref[...] = jnp.zeros_like(image_ref)
        tiles_ref[...] = jnp.zeros_like(tiles_ref)

        @pl.when(counts)
        def _():
            for step, ref in enumerate(arrived):
                source = lax.bitwise_xor(me, step)
                for slot in range(share):
                    tiles_ref[plan_ref[0, source * share + slot]] = ref[slot]
            for group in range(groups):
                tiles = tiles_ref[group * GROUP : (group + 1) * GROUP]
                at = pl.ds(pl.multiple_of(plan_ref[3, group] * TB, TB), TB)
                image_ref[:, at] += jnp.dot(
                    staged_ref[group],
                    tiles.reshape(GROUP * block_wires, TB),
                    preferred_element_type=jnp.float32,
                )


def make_image(plan, arrived, staged, share, ticks):
    groups, cells, _ = staged.shape
    block_wires = arrived[0].shape[1]
    return pl.pallas_call(
        functools.partial(image_kernel, len(arrived), share),
        out_shape=jax.ShapeDtypeStruct((cells, ticks), jnp.float32),
        in_specs=[smem()] + [vmem()] * (1 + len(arrived)),
        out_specs=vmem(),
        scratch_shapes=[
            pltpu.VMEM((groups * GROUP + 1, block_wires, TB), jnp.bfloat16),
        ],
        cost_estimate=pl.CostEstimate(flops=10**8, bytes_accessed=3 * MIB, transcendentals=0),
        compiler_params=pltpu.CompilerParams(vmem_limit_bytes=16 * MIB),
        name="image",
    )(plan, staged, *arrived)


def more_kernel(owner_total, planes, share, plan_ref, table_ref, arrived_ref, geo_ref, before_ref, image_ref):
    cells, ticks = image_ref.shape
    blocks = ticks // TB
    wire_blocks = geo_ref.shape[0] // owner_total
    image_ref[...] = before_ref[...]

    @pl.when(plan_ref[1, 0] != plan_ref[1, 2])
    def _():
        def add(source, carry):
            for slot in range(share):
                block = table_ref[source, slot]
                at = pl.multiple_of((block % blocks) * TB, TB)
                image_ref[:, pl.ds(at, TB)] += lax.dot_general(
                    geo_ref[home(source, planes, owner_total) * wire_blocks + block // blocks],
                    arrived_ref[source * share + slot],
                    (((0,), (0,)), ((), ())),
                    preferred_element_type=jnp.float32,
                )
            return carry

        lax.fori_loop(0, owner_total, add, 0)


def add_to_image(plan, table, arrived, geometry, owner_total, planes, share, image):
    return pl.pallas_call(
        functools.partial(more_kernel, owner_total, planes, share),
        out_shape=jax.ShapeDtypeStruct(image.shape, jnp.float32),
        in_specs=[smem(), smem()] + [vmem()] * 3,
        out_specs=vmem(),
        compiler_params=pltpu.CompilerParams(vmem_limit_bytes=16 * MIB),
        name="image_more",
    )(plan, table, arrived, geometry, image)


def further_round(
    trip, image, signal, geometry, rows, packed, plan, owner_total, planes, share
):
    trip, signal, rows, packed, plan = lax.optimization_barrier((trip, signal, rows, packed, plan))
    step = trip + plan[1, 3]
    hot = plan[1, 0]
    me = plan[1, 2]
    block_wires = geometry.shape[1]
    wire_count, tick_count = signal.shape
    blocks = tick_count // TB
    wire_blocks = wire_count // block_wires
    ids = jnp.arange(owner_total, dtype=jnp.int32)

    def ranks(owners):
        member = (owners[..., None] == ids).astype(jnp.int32)
        before = jnp.cumsum(member, axis=-2) - member
        return jnp.sum(before * member, axis=-1) - step * share

    def live(owners, rank):
        return (owners < owner_total) & (owners != hot) & (rank >= 0) & (rank < share)

    owners = packed[0] >> 7
    block = packed[0] & 127
    rank = ranks(owners)
    place = jnp.where(live(owners, rank), owners * share + rank, owner_total * share)
    tiles = signal.reshape(wire_blocks, block_wires, blocks, TB).transpose(0, 2, 1, 3)
    tiles = tiles.reshape(wire_blocks * blocks, block_wires, TB)[block]
    payload = jnp.zeros((owner_total * share, block_wires, TB), jnp.bfloat16)
    payload = payload.at[place].set(tiles, mode="drop")
    arrived = exchange(payload.reshape(owner_total, share, block_wires, TB))

    owners = rows >> 7
    rank = ranks(owners)
    source = jnp.arange(owner_total, dtype=jnp.int32)[:, None]
    line = jnp.where(live(owners, rank) & (owners == me), source, owner_total)
    table = jnp.zeros((owner_total, 128), jnp.int32)
    table = table.at[line, jnp.maximum(rank, 0)].set(rows & 127, mode="drop")
    return add_to_image(
        plan,
        table,
        arrived.reshape(owner_total * share, block_wires, TB),
        geometry,
        owner_total,
        planes,
        share,
        image,
    )


def tick_halo(sides):
    devices = lax.axis_size("tick")
    if devices == 2:
        tick = lax.axis_index("tick")
        got = lax.ppermute(sides[0], "tick", [(0, 1), (1, 0)])
        nothing = jnp.zeros_like(got)
        return jnp.where(tick == 0, nothing, got), jnp.where(tick == 0, got, nothing)
    up = [(i, i + 1) for i in range(devices - 1)]
    down = [(i + 1, i) for i in range(devices - 1)]
    return lax.ppermute(sides[1], "tick", up), lax.ppermute(sides[0], "tick", down)


def wire_halo(first, last, left, right):
    devices = lax.axis_size("wire")
    odd = lax.axis_index("wire") % 2 == 1
    last = jnp.concatenate([left[-PAD:], last, right[-PAD:]], axis=1)
    first = jnp.concatenate([left[:PAD], first, right[:PAD]], axis=1)
    got = []
    for begin, rows in ((0, jnp.where(odd, first, last)), (1, jnp.where(odd, last, first))):
        pairs = [(i, i + 1) for i in range(begin, devices - 1, 2)]
        got.append(lax.ppermute(rows, "wire", pairs + [(j, i) for i, j in pairs]))
    return jnp.where(odd, got[0], got[1]), jnp.where(odd, got[1], got[0])


def exchange(array, axes=("wire", "plane")):
    return lax.all_to_all(array, axes, split_axis=0, concat_axis=0, tiled=True)


def shards(raw, chan_mask, kernel, geometry, roi_block, roi_owner):
    wires, ticks = raw.shape
    slot_count = roi_block.shape[0]
    block_wires = geometry.shape[1]
    cells = geometry.shape[2]
    tick_blocks = ticks // TB
    planes = lax.axis_size("plane")
    wire_shards = lax.axis_size("wire")
    owner_total = planes * wire_shards
    share = -(-(slot_count - CAP) // (owner_total - 1))

    mask, first, last, packed, send_plan, *sides = prepare(
        raw, chan_mask, roi_owner, roi_block, planes, owner_total, share
    )
    left, right = tick_halo(sides)
    top, bottom = wire_halo(first, last, left, right)
    bands = make_bands(kernel[0])
    inner = convolve_inner(raw, mask, left, right, bands)
    signal, *parts = convolve_edges(
        planes, send_plan, packed, inner, raw, mask, left, right, top, bottom, bands, geometry
    )

    pieces = swap_all(parts, "plane")
    payload = pack_tiles(send_plan, signal, owner_total * share, block_wires)
    pieces, payload = lax.optimization_barrier((pieces, payload))
    pieces = swap_all(fold(pieces, wire_shards), "wire")

    plan, rows = make_receive_plan(
        pieces, packed, owner_total, planes, share, wires // block_wires, tick_blocks
    )
    staged = stage_geometry(
        plan, geometry, group_total(owner_total, share, tick_blocks), owner_total * share
    )

    payload = place_sums(send_plan, payload, pieces, owner_total, share)
    arrived = swap_all(payload, ("plane", "wire"))
    image = make_image(plan, arrived, staged, share, ticks)

    trips = agree(plan[1:2, 1:2])[0, 0]
    image = lax.fori_loop(
        0,
        trips,
        lambda trip, now: further_round(
            trip, now, signal, geometry, rows, packed, plan, owner_total, planes, share
        ),
        image,
    )
    return signal, image


def solution(mesh):
    in_specs = (
        P(("plane", "wire"), "tick"),
        P(("plane", "wire")),
        P("plane", None, None),
        P(),
        P(("plane", "wire", "tick")),
        P(("plane", "wire", "tick")),
    )
    out_specs = (P(("plane", "wire"), "tick"), P(("plane", "wire"), "tick"))
    return jax.shard_map(shards, mesh=mesh, in_specs=in_specs, out_specs=out_specs, check_vma=False)
```

```python
import functools

import jax
import jax.numpy as jnp
from jax import lax
from jax.experimental import pallas as pl
from jax.experimental.pallas import tpu as pltpu
from jax.sharding import PartitionSpec as P

TB = 128
CAP = 25
PAD = 16
TABLE = 8
STEPS = 4
MIB = 1024 * 1024


def vmem():
    return pl.BlockSpec(memory_space=pltpu.VMEM)


def smem():
    return pl.BlockSpec(memory_space=pltpu.SMEM)


GROUP = 8


def home(position, planes, owner_total):
    return (position % planes) * (owner_total // planes) + position // planes


def lane_numbers():
    return lax.broadcasted_iota(jnp.int32, (1, 128), 1)


def earlier_lanes():
    return (
        lax.broadcasted_iota(jnp.int32, (128, 128), 0)
        < lax.broadcasted_iota(jnp.int32, (128, 128), 1)
    ).astype(jnp.bfloat16)


def count_before(member, before):
    return jnp.dot(
        member.astype(jnp.float32).astype(jnp.bfloat16), before, preferred_element_type=jnp.float32
    )


def most_named(owners, owner_total):
    lanes = lane_numbers()
    counts = jnp.full(owners.shape, -1.0, jnp.float32)
    for owner in range(owner_total):
        named = jnp.sum((owners == owner).astype(jnp.float32), axis=1, keepdims=True)
        counts = jnp.where(lanes == owner, named, counts)
    top = jnp.max(counts, axis=1, keepdims=True)
    chosen = jnp.min(
        jnp.where(counts == top, lanes.astype(jnp.float32), 127.0), axis=1, keepdims=True
    )
    return counts, chosen


def prepare_kernel(
    planes,
    owner_total,
    share,
    tick_total,
    raw_hbm,
    mask_hbm,
    owner_hbm,
    block_hbm,
    mask_out,
    first_ref,
    last_ref,
    own_ref,
    out_ref,
    *rest,
):
    wires, ticks = raw_hbm.shape
    count = 1 if tick_total == 2 else 2
    sides = rest[:count]
    side_refs = rest[count : 2 * count]
    first_buf, last_buf, mask_ref, owner_ref, block_ref, sems = rest[2 * count :]
    tick = lax.axis_index("tick")
    me = lax.axis_index("wire") * planes + lax.axis_index("plane")
    if tick_total == 2:
        starts = [pl.multiple_of((1 - tick) * (ticks - TB), TB)]
    else:
        starts = [0, ticks - TB]
    moves = [(mask_hbm, mask_ref), (owner_hbm, owner_ref), (block_hbm, block_ref)]
    moves += [(raw_hbm.at[:, pl.ds(start, TB)], ref) for start, ref in zip(starts, side_refs)]
    moves += [(raw_hbm.at[pl.ds(0, PAD)], first_buf), (raw_hbm.at[pl.ds(wires - PAD, PAD)], last_buf)]
    copies = [
        pltpu.make_async_copy(source, target, sems.at[index])
        for index, (source, target) in enumerate(moves)
    ]
    for copy in copies:
        copy.start()
    for copy in copies[:3]:
        copy.wait()

    for part in range(wires // 128):
        row = mask_ref[part : part + 1].astype(jnp.float32)
        wide = jnp.transpose(jnp.broadcast_to(row, (128, 128)))
        mask_out[part * 128 : (part + 1) * 128] = wide.astype(jnp.bfloat16)

    lanes = lane_numbers()
    slot_count = owner_ref.shape[1]
    owner = owner_ref[...]
    wire_shards = owner_total // planes
    none = owner_total * 128
    own_ref[...] = jnp.where(lanes == 127, none + me, none)
    own_ref[:, 0:slot_count] = (
        (owner % wire_shards) * planes + owner // wire_shards
    ) * 128 + block_ref[...]
    own = own_ref[...]
    _, hot = most_named(own >> 7, owner_total)
    rows = lax.broadcasted_iota(jnp.int32, (owner_total, 128), 0)
    member = (own >> 7) == rows
    rank = count_before(member, earlier_lanes())
    place = jnp.where(rank < share, rows.astype(jnp.float32) * share + rank, -1.0)
    place = jnp.where(rows.astype(jnp.float32) == hot, -2.0, place)
    place = jnp.sum(jnp.where(member, place + 3.0, 0.0), axis=0, keepdims=True)

    column = jnp.transpose(jnp.broadcast_to(own.astype(jnp.float32), (128, 128)))
    column = column.astype(jnp.int32)
    here = ((column & 127) == lanes) & ((column >> 7) < owner_total)
    spread = jnp.transpose(jnp.broadcast_to(place, (128, 128)))
    placed = jnp.sum(jnp.where(here, spread, 0.0), axis=0, keepdims=True)
    trash = float(owner_total * share)
    facts = jnp.where(lanes == 2, me, 0)
    out_ref[...] = jnp.zeros_like(out_ref)
    out_ref[0:1, :] = jnp.where(placed >= 3.0, placed - 3.0, trash).astype(jnp.int32)
    out_ref[1:2, :] = jnp.where(lanes == 0, hot.astype(jnp.int32), facts)
    out_ref[2:3, :] = (placed == 1.0).astype(jnp.int32)

    for copy in copies[3:]:
        copy.wait()
    for side, ref in zip(sides, side_refs):
        side[...] = ref[...] * mask_out[...]
    for block in range(ticks // TB):
        at = slice(block * TB, (block + 1) * TB)
        first_ref[:, at] = first_buf[:, at] * mask_out[0:PAD]
        last_ref[:, at] = last_buf[:, at] * mask_out[wires - PAD : wires]


def prepare(raw, chan_mask, roi_owner, roi_block, planes, owner_total, share):
    wires, ticks = raw.shape
    tick_total = lax.axis_size("tick")
    sides = 1 if tick_total == 2 else 2
    side = jax.ShapeDtypeStruct((wires, TB), jnp.bfloat16)
    edge = jax.ShapeDtypeStruct((PAD, ticks), jnp.bfloat16)
    row = jax.ShapeDtypeStruct((1, 128), jnp.int32)
    table = jax.ShapeDtypeStruct((8, 128), jnp.int32)
    slot_count = roi_owner.shape[0]
    return pl.pallas_call(
        functools.partial(prepare_kernel, planes, owner_total, share, tick_total),
        out_shape=(side, edge, edge, row, table) + (side,) * sides,
        in_specs=[pl.BlockSpec(memory_space=pltpu.HBM)] * 4,
        out_specs=(vmem(),) * (5 + sides),
        scratch_shapes=[pltpu.VMEM((wires, TB), jnp.bfloat16)] * sides
        + [pltpu.VMEM((PAD, ticks), jnp.bfloat16)] * 2
        + [pltpu.VMEM((wires // 128, 128), jnp.int32)]
        + [pltpu.VMEM((1, slot_count), jnp.int32)] * 2
        + [pltpu.SemaphoreType.DMA((sides + 5,))],
        compiler_params=pltpu.CompilerParams(vmem_limit_bytes=60 * MIB),
        name="prepare",
    )(raw, chan_mask.reshape(wires // 128, 128), roi_owner[None], roi_block[None])


def receive_kernel(owner_total, planes, share, wire_blocks, tick_blocks, own_ref, *refs):
    pieces = refs[:-2]
    out_ref, rows_ref = refs[-2:]
    lanes = lane_numbers()
    lane_f = lanes.astype(jnp.float32)
    place = lax.broadcasted_iota(jnp.int32, (owner_total, 128), 0)
    shard = lax.axis_index("wire")
    every = jnp.zeros((owner_total, 128), jnp.float32)
    for step, ref in enumerate(pieces):
        tags = ref[ref.shape[0] - TABLE :].astype(jnp.float32)
        at = lax.bitwise_xor(shard, step) * planes
        for plane in range(planes):
            row = tags[2 * plane : 2 * plane + 1] * 128.0 + tags[2 * plane + 1 : 2 * plane + 2]
            every = jnp.where(place == at + plane, row, every)
    every = every.astype(jnp.int32)
    rows_ref[...] = every
    owners = every >> 7
    own = own_ref[...]
    me = jnp.sum(jnp.where(lanes == 127, own & 127, 0).astype(jnp.float32), axis=1, keepdims=True)

    counts, chosen = most_named(owners, owner_total)
    hot = jnp.max(chosen, axis=0, keepdims=True)
    agreed = hot == jnp.min(chosen, axis=0, keepdims=True)
    left = jnp.where(agreed & (lane_f == hot), 0.0, counts)
    fullest = jnp.max(jnp.max(left, axis=1, keepdims=True), axis=0, keepdims=True)
    start = agreed.astype(jnp.float32)
    trips = -start
    for step in range(-(-CAP // share)):
        trips = trips + (fullest > step * share).astype(jnp.float32)
    trips = jnp.maximum(trips, 0.0)
    hot = jnp.where(agreed, hot, -1.0)

    to_me = owners.astype(jnp.float32) == me
    before = earlier_lanes()
    rank = count_before(to_me, before)
    blocks = every & 127
    source = lax.broadcasted_iota(jnp.int32, (owner_total, 128), 0)
    line = home(source, planes, owner_total) * wire_blocks + blocks // tick_blocks
    line = line.astype(jnp.float32)
    tick = (blocks % tick_blocks).astype(jnp.float32)
    lines = jnp.zeros((1, 128), jnp.float32)
    ticks = jnp.full((1, 128), -1.0, jnp.float32)
    for slot in range(share):
        got = to_me & (rank == slot)
        here = lanes == source * share + slot
        for value, where in ((line, 0), (tick + 1.0, 1)):
            one = jnp.sum(jnp.where(got, value, 0.0), axis=1, keepdims=True)
            one = jnp.sum(jnp.where(here, one, 0.0), axis=0, keepdims=True)
            if where == 0:
                lines = lines + one
            else:
                ticks = ticks + one

    block_rows = lax.broadcasted_iota(jnp.int32, (tick_blocks, 128), 0).astype(jnp.float32)
    member = block_rows == ticks
    rank = count_before(member, before)
    total = jnp.sum(member.astype(jnp.float32), axis=1, keepdims=True)
    groups = jnp.zeros_like(total)
    for step in range(0, owner_total * share, GROUP):
        groups = groups + (total > step).astype(jnp.float32)
    lower = (
        lax.broadcasted_iota(jnp.int32, (tick_blocks, tick_blocks), 0)
        > lax.broadcasted_iota(jnp.int32, (tick_blocks, tick_blocks), 1)
    ).astype(jnp.bfloat16)
    base = jnp.dot(
        lower,
        jnp.broadcast_to(groups, (tick_blocks, 128)).astype(jnp.bfloat16),
        preferred_element_type=jnp.float32,
    )
    place = jnp.sum(jnp.where(member, base * GROUP + rank, 0.0), axis=0, keepdims=True)
    trash = float(group_total(owner_total, share, tick_blocks) * GROUP)
    place = jnp.where(ticks < 0.0, trash, place)
    inside = (base <= lane_f) & (lane_f < base + groups)
    group_tick = jnp.sum(jnp.where(inside, block_rows, 0.0), axis=0, keepdims=True)

    facts = jnp.where(lanes == 0, hot, 0.0)
    facts = jnp.where(lanes == 1, trips, facts)
    facts = jnp.where(lanes == 2, me, facts)
    facts = jnp.where(lanes == 3, start, facts)
    out_ref[...] = jnp.zeros_like(out_ref)
    out_ref[0:1, :] = place.astype(jnp.int32)
    out_ref[1:2, :] = facts.astype(jnp.int32)
    out_ref[2:3, :] = lines.astype(jnp.int32)
    out_ref[3:4, :] = group_tick.astype(jnp.int32)


def group_total(owner_total, share, tick_blocks):
    return (owner_total * share - tick_blocks) // GROUP + tick_blocks


def make_receive_plan(pieces, packed, owner_total, planes, share, wire_blocks, tick_blocks):
    return pl.pallas_call(
        functools.partial(receive_kernel, owner_total, planes, share, wire_blocks, tick_blocks),
        out_shape=(
            jax.ShapeDtypeStruct((8, 128), jnp.int32),
            jax.ShapeDtypeStruct((owner_total, 128), jnp.int32),
        ),
        in_specs=[vmem()] * (1 + len(pieces)),
        out_specs=(vmem(), vmem()),
        compiler_params=pltpu.CompilerParams(vmem_limit_bytes=2 * MIB),
        name="receive_plan",
    )(packed, *pieces)


def agree(rounds):
    devices = lax.axis_size("tick")
    reach = 1
    while reach < devices:
        ring = [(i, (i + reach) % devices) for i in range(devices)]
        rounds = jnp.maximum(rounds, lax.ppermute(rounds, "tick", ring))
        reach *= 2
    return rounds


def band_kernel(taps_w, taps_ref, band_ref):
    row = lax.broadcasted_iota(jnp.int32, (TB, TB), 0)
    col = lax.broadcasted_iota(jnp.int32, (TB, TB), 1)
    pairs = (taps_w + 1) // 2
    band_ref[0, 0 : 3 * TB, TB : 2 * TB] = jnp.zeros((3 * TB, TB), jnp.bfloat16)
    band_ref[pairs - 1, 3 * TB : 6 * TB, 0:TB] = jnp.zeros((3 * TB, TB), jnp.bfloat16)
    taps = taps_ref[...].astype(jnp.float32)
    for tap in range(taps_w):
        spread = jnp.broadcast_to(taps[tap : tap + 1], (TB, 2 * TB))
        rolled = pltpu.roll(spread, TB, 1, stride=1, stride_axis=0)
        middle = rolled[:, :TB]
        outer = rolled[:, TB:]
        bands = (
            jnp.where(col < row, outer, 0.0).astype(jnp.bfloat16),
            middle.astype(jnp.bfloat16),
            jnp.where(col >= row, outer, 0.0).astype(jnp.bfloat16),
        )
        for first, second in ((0, 0), (1, 1), (1, 0), (0, 1)):
            if (tap - first + second) % 2:
                continue
            pair = (tap - first + second) // 2
            for piece in range(3):
                start = (first * 3 + piece) * TB
                band_ref[pair, start : start + TB, second * TB : (second + 1) * TB] = bands[piece]


def make_bands(taps):
    taps_w = taps.shape[0]
    return pl.pallas_call(
        functools.partial(band_kernel, taps_w),
        out_shape=jax.ShapeDtypeStruct(((taps_w + 1) // 2, 6 * TB, 2 * TB), jnp.bfloat16),
        in_specs=[vmem()],
        out_specs=vmem(),
        cost_estimate=pl.CostEstimate(flops=10**9, bytes_accessed=6 * MIB, transcendentals=0),
        compiler_params=pltpu.CompilerParams(vmem_limit_bytes=16 * MIB),
        name="bands",
    )(taps)


def spread_pair(wide_ref, lhs_view, line, pitch, blocks):
    for side in range(2):
        for piece in range(3):
            at = (side * 3 + piece) * TB
            lhs_view[:, at : at + TB] = wide_ref[
                pl.ds((line + side) * pitch + piece, blocks), :
            ].astype(jnp.bfloat16)


def write_lines(total, out_view, signal_ref, line, pairs, blocks):
    for pair in range(pairs):
        for side in range(2):
            out_view[pl.ds((2 * pair + side) * blocks, blocks), :] = total[
                pair * blocks : (pair + 1) * blocks, side * TB : (side + 1) * TB
            ]
    for block in range(blocks):
        signal_ref[line : line + 2 * pairs, block * TB : (block + 1) * TB] = out_view[
            pl.ds(block, 2 * pairs, stride=blocks), :
        ].astype(jnp.bfloat16)


def inner_kernel(
    chunks,
    raw_ref,
    mask_ref,
    left_ref,
    right_ref,
    band_ref,
    inner_ref,
    wide_ref,
    lhs_ref,
    out_ref,
):
    wires, ticks = raw_ref.shape
    blocks = ticks // TB
    pitch = wide_ref.shape[0] // wires
    reach = band_ref.shape[0]
    span = 2 * PAD
    groups = wires // span

    def fill(group, block):
        lines = slice(group * span, (group + 1) * span)
        if block == 0:
            inner = left_ref[lines]
        elif block == blocks + 1:
            inner = right_ref[lines]
        else:
            inner = raw_ref[lines, (block - 1) * TB : block * TB] * mask_ref[lines]
        wide_ref[pl.ds(group * span * pitch + block, span, stride=pitch), :] = inner.astype(
            jnp.float32
        )

    margin = reach - 1
    begin = PAD // 2
    state = {"group": 0, "pair": begin}

    def prepare(upto):
        todo = []
        while state["pair"] < upto:
            line = 2 * state["pair"] - margin
            while state["group"] < groups and line + 1 >= state["group"] * span:
                group = state["group"]
                for block in range(blocks + 2):
                    todo.append(lambda group=group, block=block: fill(group, block))
                state["group"] += 1
            todo.append(
                lambda line=line, pair=state["pair"]: spread_pair(
                    wide_ref, lhs_ref.at[pair - begin], line, pitch, blocks
                )
            )
            state["pair"] += 1
        return todo

    pair = begin
    for job in prepare(pair + chunks[0] + margin):
        job()
    for index, size in enumerate(chunks):
        todo = prepare(pair + size + chunks[index + 1] + margin) if index + 1 < len(chunks) else []
        each = -(-len(todo) // reach)
        total = jnp.zeros((size * blocks, 2 * TB), jnp.float32)
        for step in range(0, reach, STEPS):
            steps = range(step, min(step + STEPS, reach))
            rows = [
                lhs_ref[pair - begin + one : pair - begin + one + size].reshape(
                    size * blocks, 6 * TB
                )
                for one in steps
            ]
            bands = band_ref[steps[0] : steps[-1] + 1].reshape(len(steps) * 6 * TB, 2 * TB)
            total = total + jnp.dot(
                jnp.concatenate(rows, axis=1), bands, preferred_element_type=jnp.float32
            )
            for job in todo[step * each : (steps[-1] + 1) * each]:
                job()
        write_lines(total, out_ref.at[index % 2], inner_ref, 2 * (pair - begin), size, blocks)
        pair += size


def convolve_inner(raw, mask, left, right, bands):
    wires, ticks = raw.shape
    reach = bands.shape[0]
    blocks = ticks // TB
    pitch = -(-(blocks + 2) // 8) * 8
    pairs = (wires - 2 * PAD) // 2
    chunks = []
    while sum(chunks) < pairs:
        chunks.append(min(32 if chunks else 24, pairs - sum(chunks)))
    flops = 2 * blocks * pairs * reach * 6 * TB * 2 * TB
    return pl.pallas_call(
        functools.partial(inner_kernel, tuple(chunks)),
        out_shape=jax.ShapeDtypeStruct((wires - 2 * PAD, ticks), jnp.bfloat16),
        in_specs=[vmem()] * 5,
        out_specs=vmem(),
        scratch_shapes=[
            pltpu.VMEM(((wires + 1) * pitch, TB), jnp.float32),
            pltpu.VMEM((pairs + reach - 1, blocks, 6 * TB), jnp.bfloat16),
            pltpu.VMEM((2, (2 * max(chunks) + 1) * blocks, TB), jnp.float32),
        ],
        cost_estimate=pl.CostEstimate(flops=flops, bytes_accessed=6 * MIB, transcendentals=0),
        compiler_params=pltpu.CompilerParams(vmem_limit_bytes=28 * MIB),
        name="inner",
    )(raw, mask, left, right, bands)


def edge_kernel(
    planes,
    plan_ref,
    own_ref,
    inner_ref,
    raw_ref,
    mask_ref,
    left_ref,
    right_ref,
    top_ref,
    bottom_ref,
    band_ref,
    geo_ref,
    signal_ref,
    *refs,
):
    part_refs = refs[:planes]
    partial_ref, wide_ref, lhs_ref, out_ref, turned_ref = refs[planes:]
    wires, ticks = signal_ref.shape
    blocks = ticks // TB
    reach = band_ref.shape[0]
    block_wires = geo_ref.shape[1]
    wire_blocks = wires // block_wires
    near = 2 * PAD
    lines = PAD + near
    pitch = wide_ref.shape[1] // lines
    pairs = PAD // 2
    margin = reach - 1

    signal_ref[PAD : wires - PAD] = inner_ref[...]
    source = home(plan_ref[1, 2], planes, geo_ref.shape[0] // wire_blocks)
    rows = geo_ref[pl.ds(source * wire_blocks, wire_blocks)].reshape(wires, -1)
    turned_ref[...] = jnp.transpose(rows)

    for end in range(2):
        halo_ref = (top_ref, bottom_ref)[end]
        mine = (slice(0, near), slice(wires - near, wires))[end]
        halo_at = (0, near)[end]
        mine_at = (PAD, 0)[end]
        for block in range(blocks + 2):
            columns = slice(block * TB, (block + 1) * TB)
            if block == 0:
                inner = left_ref[mine].astype(jnp.float32)
            elif block == blocks + 1:
                inner = right_ref[mine].astype(jnp.float32)
            else:
                inner = raw_ref[mine, (block - 1) * TB : block * TB] * mask_ref[mine]
                inner = inner.astype(jnp.float32)
            wide_ref[end, pl.ds(halo_at * pitch + block, PAD, stride=pitch), :] = halo_ref[
                :, columns
            ].astype(jnp.float32)
            wide_ref[end, pl.ds(mine_at * pitch + block, near, stride=pitch), :] = inner
        first = (PAD, near - PAD)[end] - margin
        for pair in range(pairs + margin):
            spread_pair(
                wide_ref.at[end], lhs_ref.at[end, pair], first + 2 * pair, pitch, blocks
            )

    total = jnp.zeros((2 * pairs * blocks, 2 * TB), jnp.float32)
    for step in range(0, reach, STEPS):
        steps = range(step, min(step + STEPS, reach))
        rows = jnp.concatenate(
            [
                jnp.concatenate(
                    [
                        lhs_ref[end, one : one + pairs].reshape(pairs * blocks, 6 * TB)
                        for one in steps
                    ],
                    axis=1,
                )
                for end in range(2)
            ],
            axis=0,
        )
        bands = band_ref[steps[0] : steps[-1] + 1].reshape(len(steps) * 6 * TB, 2 * TB)
        total = total + jnp.dot(rows, bands, preferred_element_type=jnp.float32)
    for end in range(2):
        write_lines(
            total[end * pairs * blocks : (end + 1) * pairs * blocks],
            out_ref.at[end],
            signal_ref,
            (0, wires - PAD)[end],
            pairs,
            blocks,
        )

    cells = geo_ref.shape[2]
    shards = partial_ref.shape[1] // cells
    own = own_ref[...]
    line = lax.broadcasted_iota(jnp.int32, (TABLE, 128), 0)
    table = jnp.where(line == 0, own >> 7, jnp.where(line == 1, own & 127, 0))
    table = table.astype(jnp.float32).astype(jnp.bfloat16)
    for plane in range(planes):
        partial_ref[plane, shards * cells : shards * cells + TABLE] = table

    for block in range(0, blocks, 2):
        chosen = []
        for side in range(2):
            at = slice((block + side) * TB, (block + side + 1) * TB)
            column = []
            for line in range(wire_blocks):
                tile = signal_ref[line * block_wires : (line + 1) * block_wires, at]
                asked = plan_ref[2, line * blocks + block + side] == 1
                column.append(jnp.where(asked, tile, jnp.zeros_like(tile)))
            chosen.append(jnp.concatenate(column, axis=0))
        sums = jnp.dot(
            turned_ref[...], jnp.concatenate(chosen, axis=1), preferred_element_type=jnp.float32
        ).astype(jnp.bfloat16)
        for side in range(2):
            shard, plane = divmod(block + side, planes)
            partial_ref[plane, shard * cells : (shard + 1) * cells] = sums[
                :, side * TB : (side + 1) * TB
            ]
    mine = lax.axis_index("plane")
    for step, ref in enumerate(part_refs):
        ref[...] = partial_ref[lax.bitwise_xor(mine, step)]


def convolve_edges(
    planes, plan, own, inner, raw, mask, left, right, top, bottom, bands, geometry
):
    wires, ticks = raw.shape
    reach = bands.shape[0]
    cells = geometry.shape[2]
    blocks = ticks // TB
    pitch = -(-(blocks + 2) // 8) * 8
    height = blocks // planes * cells + TABLE
    flops = 2 * blocks * PAD * reach * 6 * TB * 2 * TB
    return pl.pallas_call(
        functools.partial(edge_kernel, planes),
        out_shape=(
            jax.ShapeDtypeStruct((wires, ticks), jnp.bfloat16),
        )
        + (jax.ShapeDtypeStruct((height, TB), jnp.bfloat16),) * planes,
        in_specs=[smem()] + [vmem()] * 10,
        out_specs=(vmem(),) * (1 + planes),
        scratch_shapes=[
            pltpu.VMEM((planes, height, TB), jnp.bfloat16),
            pltpu.VMEM((2, (3 * PAD + 1) * pitch, TB), jnp.float32),
            pltpu.VMEM((2, PAD // 2 + reach - 1, blocks, 6 * TB), jnp.bfloat16),
            pltpu.VMEM((2, (PAD + 1) * blocks, TB), jnp.float32),
            pltpu.VMEM((cells, wires), jnp.bfloat16),
        ],
        cost_estimate=pl.CostEstimate(flops=flops, bytes_accessed=6 * MIB, transcendentals=0),
        compiler_params=pltpu.CompilerParams(vmem_limit_bytes=24 * MIB),
        name="edges",
    )(plan, own, inner, raw, mask, left, right, top, bottom, bands, geometry)


def fold_kernel(planes, *refs):
    pieces = refs[:planes]
    outs = refs[planes:-1]
    sums_ref = refs[-1]
    shards, lines, _ = sums_ref.shape
    cells = lines - TABLE
    mine = lax.axis_index("plane")
    line = lax.broadcasted_iota(jnp.int32, (TABLE, 128), 0)
    table = jnp.zeros((TABLE, 128), jnp.float32)
    for step, ref in enumerate(pieces):
        tags = ref[shards * cells :].astype(jnp.float32)
        plane = lax.bitwise_xor(mine, step)
        table = jnp.where(line == 2 * plane, tags[0:1], table)
        table = jnp.where(line == 2 * plane + 1, tags[1:2], table)
    for shard in range(shards):
        total = jnp.zeros((cells, TB), jnp.float32)
        for ref in pieces:
            total = total + ref[shard * cells : (shard + 1) * cells].astype(jnp.float32)
        sums_ref[shard, 0:cells] = total.astype(jnp.bfloat16)
        sums_ref[shard, cells:lines] = table.astype(jnp.bfloat16)
    mine = lax.axis_index("wire")
    for step, ref in enumerate(outs):
        ref[...] = sums_ref[lax.bitwise_xor(mine, step)]


def fold(pieces, shards):
    cells = (pieces[0].shape[0] - TABLE) // shards
    out = jax.ShapeDtypeStruct((cells + TABLE, TB), jnp.bfloat16)
    return pl.pallas_call(
        functools.partial(fold_kernel, len(pieces)),
        out_shape=(out,) * shards,
        in_specs=[vmem()] * len(pieces),
        out_specs=(vmem(),) * shards,
        scratch_shapes=[pltpu.VMEM((shards, cells + TABLE, TB), jnp.bfloat16)],
        compiler_params=pltpu.CompilerParams(vmem_limit_bytes=4 * MIB),
        name="fold",
    )(*pieces)


def swap_all(parts, axis):
    got = [parts[0]]
    for step in range(1, len(parts)):
        pairs = [(i, i ^ step) for i in range(len(parts))]
        got.append(lax.ppermute(parts[step], axis, pairs))
    return got


def pack_kernel(slots, plan_ref, signal_ref, payload_ref, tiles_ref):
    block_wires = payload_ref.shape[1]
    wires, ticks = signal_ref.shape
    blocks = ticks // TB
    tiles_ref[...] = jnp.zeros_like(tiles_ref)
    for line in range(wires // block_wires):
        for block in range(blocks):
            place = plan_ref[0, line * blocks + block]
            tiles_ref[place] = signal_ref[
                line * block_wires : (line + 1) * block_wires, block * TB : (block + 1) * TB
            ]
    payload_ref[...] = tiles_ref[0:slots]


def pack_tiles(plan, signal, slots, block_wires):
    return pl.pallas_call(
        functools.partial(pack_kernel, slots),
        out_shape=jax.ShapeDtypeStruct((slots, block_wires, TB), jnp.bfloat16),
        in_specs=[smem(), vmem()],
        out_specs=vmem(),
        scratch_shapes=[pltpu.VMEM((slots + 1, block_wires, TB), jnp.bfloat16)],
        cost_estimate=pl.CostEstimate(flops=10**8, bytes_accessed=3 * MIB, transcendentals=0),
        compiler_params=pltpu.CompilerParams(vmem_limit_bytes=8 * MIB),
        name="pack",
    )(plan, signal)


def stage_kernel(slots, plan_ref, geo_ref, out_ref, rows_ref):
    groups = out_ref.shape[0]
    rows_ref[...] = jnp.zeros_like(rows_ref)
    for slot in range(slots):
        rows_ref[plan_ref[0, slot]] = geo_ref[plan_ref[2, slot]]
    for group in range(groups):
        rows = rows_ref[group * GROUP : (group + 1) * GROUP]
        out_ref[group] = jnp.transpose(rows.reshape(-1, rows.shape[-1]))


def stage_geometry(plan, geometry, groups, slots):
    _, block_wires, cells = geometry.shape
    return pl.pallas_call(
        functools.partial(stage_kernel, slots),
        out_shape=jax.ShapeDtypeStruct((groups, cells, GROUP * block_wires), jnp.bfloat16),
        in_specs=[smem(), vmem()],
        out_specs=vmem(),
        scratch_shapes=[pltpu.VMEM((groups * GROUP + 1, block_wires, cells), jnp.bfloat16)],
        cost_estimate=pl.CostEstimate(flops=10**8, bytes_accessed=3 * MIB, transcendentals=0),
        compiler_params=pltpu.CompilerParams(vmem_limit_bytes=12 * MIB),
        name="stage",
    )(plan, geometry)


def image_kernel(owner_total, share, plan_ref, arrived_ref, staged_ref, image_ref, tiles_ref):
    cells, ticks = image_ref.shape
    block_wires = arrived_ref.shape[1]
    groups = staged_ref.shape[0]
    is_hot = plan_ref[1, 0] == plan_ref[1, 2]
    counts = plan_ref[1, 3] == 1

    @pl.when(is_hot)
    def _():
        for source in range(owner_total):
            sums = arrived_ref[source * share : source * share + cells // block_wires]
            image_ref[:, source * TB : (source + 1) * TB] = sums.reshape(cells, TB).astype(
                jnp.float32
            )

    @pl.when(jnp.logical_not(is_hot))
    def _():
        image_ref[...] = jnp.zeros_like(image_ref)
        tiles_ref[...] = jnp.zeros_like(tiles_ref)

        @pl.when(counts)
        def _():
            for slot in range(owner_total * share):
                tiles_ref[plan_ref[0, slot]] = arrived_ref[slot]
            for group in range(groups):
                tiles = tiles_ref[group * GROUP : (group + 1) * GROUP]
                at = pl.ds(pl.multiple_of(plan_ref[3, group] * TB, TB), TB)
                image_ref[:, at] += jnp.dot(
                    staged_ref[group],
                    tiles.reshape(GROUP * block_wires, TB),
                    preferred_element_type=jnp.float32,
                )


def make_image(plan, arrived, staged, owner_total, share, ticks):
    groups, cells, _ = staged.shape
    block_wires = arrived.shape[1]
    return pl.pallas_call(
        functools.partial(image_kernel, owner_total, share),
        out_shape=jax.ShapeDtypeStruct((cells, ticks), jnp.float32),
        in_specs=[smem(), vmem(), vmem()],
        out_specs=vmem(),
        scratch_shapes=[
            pltpu.VMEM((groups * GROUP + 1, block_wires, TB), jnp.bfloat16),
        ],
        cost_estimate=pl.CostEstimate(flops=10**8, bytes_accessed=3 * MIB, transcendentals=0),
        compiler_params=pltpu.CompilerParams(vmem_limit_bytes=16 * MIB),
        name="image",
    )(plan, arrived, staged)


def more_kernel(owner_total, planes, share, plan_ref, table_ref, arrived_ref, geo_ref, before_ref, image_ref):
    cells, ticks = image_ref.shape
    blocks = ticks // TB
    wire_blocks = geo_ref.shape[0] // owner_total
    image_ref[...] = before_ref[...]

    @pl.when(plan_ref[1, 0] != plan_ref[1, 2])
    def _():
        def add(source, carry):
            for slot in range(share):
                block = table_ref[source, slot]
                at = pl.multiple_of((block % blocks) * TB, TB)
                image_ref[:, pl.ds(at, TB)] += lax.dot_general(
                    geo_ref[home(source, planes, owner_total) * wire_blocks + block // blocks],
                    arrived_ref[source * share + slot],
                    (((0,), (0,)), ((), ())),
                    preferred_element_type=jnp.float32,
                )
            return carry

        lax.fori_loop(0, owner_total, add, 0)


def add_to_image(plan, table, arrived, geometry, owner_total, planes, share, image):
    return pl.pallas_call(
        functools.partial(more_kernel, owner_total, planes, share),
        out_shape=jax.ShapeDtypeStruct(image.shape, jnp.float32),
        in_specs=[smem(), smem()] + [vmem()] * 3,
        out_specs=vmem(),
        compiler_params=pltpu.CompilerParams(vmem_limit_bytes=16 * MIB),
        name="image_more",
    )(plan, table, arrived, geometry, image)


def further_round(
    trip, image, signal, geometry, rows, packed, plan, owner_total, planes, share
):
    trip, signal, rows, packed, plan = lax.optimization_barrier((trip, signal, rows, packed, plan))
    step = trip + plan[1, 3]
    hot = plan[1, 0]
    me = plan[1, 2]
    block_wires = geometry.shape[1]
    wire_count, tick_count = signal.shape
    blocks = tick_count // TB
    wire_blocks = wire_count // block_wires
    ids = jnp.arange(owner_total, dtype=jnp.int32)

    def ranks(owners):
        member = (owners[..., None] == ids).astype(jnp.int32)
        before = jnp.cumsum(member, axis=-2) - member
        return jnp.sum(before * member, axis=-1) - step * share

    def live(owners, rank):
        return (owners < owner_total) & (owners != hot) & (rank >= 0) & (rank < share)

    owners = packed[0] >> 7
    block = packed[0] & 127
    rank = ranks(owners)
    place = jnp.where(live(owners, rank), owners * share + rank, owner_total * share)
    tiles = signal.reshape(wire_blocks, block_wires, blocks, TB).transpose(0, 2, 1, 3)
    tiles = tiles.reshape(wire_blocks * blocks, block_wires, TB)[block]
    payload = jnp.zeros((owner_total * share, block_wires, TB), jnp.bfloat16)
    payload = payload.at[place].set(tiles, mode="drop")
    arrived = exchange(payload.reshape(owner_total, share, block_wires, TB))

    owners = rows >> 7
    rank = ranks(owners)
    source = jnp.arange(owner_total, dtype=jnp.int32)[:, None]
    line = jnp.where(live(owners, rank) & (owners == me), source, owner_total)
    table = jnp.zeros((owner_total, 128), jnp.int32)
    table = table.at[line, jnp.maximum(rank, 0)].set(rows & 127, mode="drop")
    return add_to_image(
        plan,
        table,
        arrived.reshape(owner_total * share, block_wires, TB),
        geometry,
        owner_total,
        planes,
        share,
        image,
    )


def tick_halo(sides):
    devices = lax.axis_size("tick")
    if devices == 2:
        tick = lax.axis_index("tick")
        got = lax.ppermute(sides[0], "tick", [(0, 1), (1, 0)])
        nothing = jnp.zeros_like(got)
        return jnp.where(tick == 0, nothing, got), jnp.where(tick == 0, got, nothing)
    up = [(i, i + 1) for i in range(devices - 1)]
    down = [(i + 1, i) for i in range(devices - 1)]
    return lax.ppermute(sides[1], "tick", up), lax.ppermute(sides[0], "tick", down)


def wire_halo(first, last, left, right):
    devices = lax.axis_size("wire")
    odd = lax.axis_index("wire") % 2 == 1
    last = jnp.concatenate([left[-PAD:], last, right[-PAD:]], axis=1)
    first = jnp.concatenate([left[:PAD], first, right[:PAD]], axis=1)
    got = []
    for begin, rows in ((0, jnp.where(odd, first, last)), (1, jnp.where(odd, last, first))):
        pairs = [(i, i + 1) for i in range(begin, devices - 1, 2)]
        got.append(lax.ppermute(rows, "wire", pairs + [(j, i) for i, j in pairs]))
    return jnp.where(odd, got[0], got[1]), jnp.where(odd, got[1], got[0])


def exchange(array, axes=("wire", "plane")):
    return lax.all_to_all(array, axes, split_axis=0, concat_axis=0, tiled=True)


def shards(raw, chan_mask, kernel, geometry, roi_block, roi_owner):
    wires, ticks = raw.shape
    slot_count = roi_block.shape[0]
    block_wires = geometry.shape[1]
    cells = geometry.shape[2]
    tick_blocks = ticks // TB
    planes = lax.axis_size("plane")
    wire_shards = lax.axis_size("wire")
    owner_total = planes * wire_shards
    share = -(-(slot_count - CAP) // (owner_total - 1))

    mask, first, last, packed, send_plan, *sides = prepare(
        raw, chan_mask, roi_owner, roi_block, planes, owner_total, share
    )
    left, right = tick_halo(sides)
    top, bottom = wire_halo(first, last, left, right)
    bands = make_bands(kernel[0])
    inner = convolve_inner(raw, mask, left, right, bands)
    signal, *parts = convolve_edges(
        planes, send_plan, packed, inner, raw, mask, left, right, top, bottom, bands, geometry
    )

    pieces = swap_all(parts, "plane")
    payload = pack_tiles(send_plan, signal, owner_total * share, block_wires)
    pieces, payload = lax.optimization_barrier((pieces, payload))
    pieces = swap_all(fold(pieces, wire_shards), "wire")

    plan, rows = make_receive_plan(
        pieces, packed, owner_total, planes, share, wires // block_wires, tick_blocks
    )
    staged = stage_geometry(
        plan, geometry, group_total(owner_total, share, tick_blocks), owner_total * share
    )

    sums = sum(piece[:cells].astype(jnp.float32) for piece in pieces).astype(jnp.bfloat16)
    payload = lax.dynamic_update_slice(
        payload.reshape(owner_total, share, block_wires, TB),
        sums.reshape(1, cells // block_wires, block_wires, TB),
        (send_plan[1, 0], 0, 0, 0),
    )
    arrived = exchange(payload).reshape(owner_total * share, block_wires, TB)
    image = make_image(plan, arrived, staged, owner_total, share, ticks)

    trips = agree(plan[1:2, 1:2])[0, 0]
    image = lax.fori_loop(
        0,
        trips,
        lambda trip, now: further_round(
            trip, now, signal, geometry, rows, packed, plan, owner_total, planes, share
        ),
        image,
    )
    return signal, image


def solution(mesh):
    in_specs = (
        P(("plane", "wire"), "tick"),
        P(("plane", "wire")),
        P("plane", None, None),
        P(),
        P(("plane", "wire", "tick")),
        P(("plane", "wire", "tick")),
    )
    out_specs = (P(("plane", "wire"), "tick"), P(("plane", "wire"), "tick"))
    return jax.shard_map(shards, mesh=mesh, in_specs=in_specs, out_specs=out_specs, check_vma=False)
```

```python
import functools

import jax
import jax.numpy as jnp
from jax import lax
from jax.experimental import pallas as pl
from jax.experimental.pallas import tpu as pltpu
from jax.sharding import PartitionSpec as P

TB = 128
CAP = 25
PAD = 16
TABLE = 8
STEPS = 11
MIB = 1024 * 1024


def vmem():
    return pl.BlockSpec(memory_space=pltpu.VMEM)


def smem():
    return pl.BlockSpec(memory_space=pltpu.SMEM)


GROUP = 8


def home(position, planes, owner_total):
    return (position % planes) * (owner_total // planes) + position // planes


def lane_numbers():
    return lax.broadcasted_iota(jnp.int32, (1, 128), 1)


def earlier_lanes():
    return (
        lax.broadcasted_iota(jnp.int32, (128, 128), 0)
        < lax.broadcasted_iota(jnp.int32, (128, 128), 1)
    ).astype(jnp.bfloat16)


def count_before(member, before):
    return jnp.dot(
        member.astype(jnp.float32).astype(jnp.bfloat16), before, preferred_element_type=jnp.float32
    )


def most_named(owners, owner_total):
    lanes = lane_numbers()
    counts = jnp.full(owners.shape, -1.0, jnp.float32)
    for owner in range(owner_total):
        named = jnp.sum((owners == owner).astype(jnp.float32), axis=1, keepdims=True)
        counts = jnp.where(lanes == owner, named, counts)
    top = jnp.max(counts, axis=1, keepdims=True)
    chosen = jnp.min(
        jnp.where(counts == top, lanes.astype(jnp.float32), 127.0), axis=1, keepdims=True
    )
    return counts, chosen


def prepare_kernel(
    planes,
    owner_total,
    share,
    tick_total,
    raw_hbm,
    mask_hbm,
    owner_hbm,
    block_hbm,
    mask_out,
    first_ref,
    last_ref,
    own_ref,
    out_ref,
    *rest,
):
    wires, ticks = raw_hbm.shape
    count = 1 if tick_total == 2 else 2
    sides = rest[:count]
    side_refs = rest[count : 2 * count]
    first_buf, last_buf, mask_ref, owner_ref, block_ref, sems = rest[2 * count :]
    tick = lax.axis_index("tick")
    me = lax.axis_index("wire") * planes + lax.axis_index("plane")
    if tick_total == 2:
        starts = [pl.multiple_of((1 - tick) * (ticks - TB), TB)]
    else:
        starts = [0, ticks - TB]
    moves = [(mask_hbm, mask_ref), (owner_hbm, owner_ref), (block_hbm, block_ref)]
    moves += [(raw_hbm.at[:, pl.ds(start, TB)], ref) for start, ref in zip(starts, side_refs)]
    moves += [(raw_hbm.at[pl.ds(0, PAD)], first_buf), (raw_hbm.at[pl.ds(wires - PAD, PAD)], last_buf)]
    copies = [
        pltpu.make_async_copy(source, target, sems.at[index])
        for index, (source, target) in enumerate(moves)
    ]
    for copy in copies:
        copy.start()
    for copy in copies[:3]:
        copy.wait()

    for part in range(wires // 128):
        row = mask_ref[part : part + 1].astype(jnp.float32)
        wide = jnp.transpose(jnp.broadcast_to(row, (128, 128)))
        mask_out[part * 128 : (part + 1) * 128] = wide.astype(jnp.bfloat16)

    lanes = lane_numbers()
    slot_count = owner_ref.shape[1]
    owner = owner_ref[...]
    wire_shards = owner_total // planes
    none = owner_total * 128
    own_ref[...] = jnp.where(lanes == 127, none + me, none)
    own_ref[:, 0:slot_count] = (
        (owner % wire_shards) * planes + owner // wire_shards
    ) * 128 + block_ref[...]
    own = own_ref[...]
    _, hot = most_named(own >> 7, owner_total)
    rows = lax.broadcasted_iota(jnp.int32, (owner_total, 128), 0)
    member = (own >> 7) == rows
    rank = count_before(member, earlier_lanes())
    place = jnp.where(rank < share, rows.astype(jnp.float32) * share + rank, -1.0)
    place = jnp.where(rows.astype(jnp.float32) == hot, -2.0, place)
    place = jnp.sum(jnp.where(member, place + 3.0, 0.0), axis=0, keepdims=True)

    column = jnp.transpose(jnp.broadcast_to(own.astype(jnp.float32), (128, 128)))
    column = column.astype(jnp.int32)
    here = ((column & 127) == lanes) & ((column >> 7) < owner_total)
    spread = jnp.transpose(jnp.broadcast_to(place, (128, 128)))
    placed = jnp.sum(jnp.where(here, spread, 0.0), axis=0, keepdims=True)
    trash = float(owner_total * share)
    facts = jnp.where(lanes == 2, me, 0)
    out_ref[...] = jnp.zeros_like(out_ref)
    out_ref[0:1, :] = jnp.where(placed >= 3.0, placed - 3.0, trash).astype(jnp.int32)
    out_ref[1:2, :] = jnp.where(lanes == 0, hot.astype(jnp.int32), facts)
    out_ref[2:3, :] = (placed == 1.0).astype(jnp.int32)

    for copy in copies[3:]:
        copy.wait()
    for side, ref in zip(sides, side_refs):
        side[...] = ref[...] * mask_out[...]
    for block in range(ticks // TB):
        at = slice(block * TB, (block + 1) * TB)
        first_ref[:, at] = first_buf[:, at] * mask_out[0:PAD]
        last_ref[:, at] = last_buf[:, at] * mask_out[wires - PAD : wires]


def prepare(raw, chan_mask, roi_owner, roi_block, planes, owner_total, share):
    wires, ticks = raw.shape
    tick_total = lax.axis_size("tick")
    sides = 1 if tick_total == 2 else 2
    side = jax.ShapeDtypeStruct((wires, TB), jnp.bfloat16)
    edge = jax.ShapeDtypeStruct((PAD, ticks), jnp.bfloat16)
    row = jax.ShapeDtypeStruct((1, 128), jnp.int32)
    table = jax.ShapeDtypeStruct((8, 128), jnp.int32)
    slot_count = roi_owner.shape[0]
    return pl.pallas_call(
        functools.partial(prepare_kernel, planes, owner_total, share, tick_total),
        out_shape=(side, edge, edge, row, table) + (side,) * sides,
        in_specs=[pl.BlockSpec(memory_space=pltpu.HBM)] * 4,
        out_specs=(vmem(),) * (5 + sides),
        scratch_shapes=[pltpu.VMEM((wires, TB), jnp.bfloat16)] * sides
        + [pltpu.VMEM((PAD, ticks), jnp.bfloat16)] * 2
        + [pltpu.VMEM((wires // 128, 128), jnp.int32)]
        + [pltpu.VMEM((1, slot_count), jnp.int32)] * 2
        + [pltpu.SemaphoreType.DMA((sides + 5,))],
        compiler_params=pltpu.CompilerParams(vmem_limit_bytes=60 * MIB),
        name="prepare",
    )(raw, chan_mask.reshape(wires // 128, 128), roi_owner[None], roi_block[None])


def receive_kernel(owner_total, planes, share, wire_blocks, tick_blocks, own_ref, *refs):
    pieces = refs[:-2]
    out_ref, rows_ref = refs[-2:]
    lanes = lane_numbers()
    lane_f = lanes.astype(jnp.float32)
    place = lax.broadcasted_iota(jnp.int32, (owner_total, 128), 0)
    shard = lax.axis_index("wire")
    every = jnp.zeros((owner_total, 128), jnp.float32)
    for step, ref in enumerate(pieces):
        tags = ref[ref.shape[0] - TABLE :].astype(jnp.float32)
        at = lax.bitwise_xor(shard, step) * planes
        for plane in range(planes):
            row = tags[2 * plane : 2 * plane + 1] * 128.0 + tags[2 * plane + 1 : 2 * plane + 2]
            every = jnp.where(place == at + plane, row, every)
    every = every.astype(jnp.int32)
    rows_ref[...] = every
    owners = every >> 7
    own = own_ref[...]
    me = jnp.sum(jnp.where(lanes == 127, own & 127, 0).astype(jnp.float32), axis=1, keepdims=True)

    counts, chosen = most_named(owners, owner_total)
    hot = jnp.max(chosen, axis=0, keepdims=True)
    agreed = hot == jnp.min(chosen, axis=0, keepdims=True)
    left = jnp.where(agreed & (lane_f == hot), 0.0, counts)
    fullest = jnp.max(jnp.max(left, axis=1, keepdims=True), axis=0, keepdims=True)
    start = agreed.astype(jnp.float32)
    trips = -start
    for step in range(-(-CAP // share)):
        trips = trips + (fullest > step * share).astype(jnp.float32)
    trips = jnp.maximum(trips, 0.0)
    hot = jnp.where(agreed, hot, -1.0)

    to_me = owners.astype(jnp.float32) == me
    before = earlier_lanes()
    rank = count_before(to_me, before)
    blocks = every & 127
    source = lax.broadcasted_iota(jnp.int32, (owner_total, 128), 0)
    line = home(source, planes, owner_total) * wire_blocks + blocks // tick_blocks
    line = line.astype(jnp.float32)
    tick = (blocks % tick_blocks).astype(jnp.float32)
    lines = jnp.zeros((1, 128), jnp.float32)
    ticks = jnp.full((1, 128), -1.0, jnp.float32)
    for slot in range(share):
        got = to_me & (rank == slot)
        here = lanes == source * share + slot
        for value, where in ((line, 0), (tick + 1.0, 1)):
            one = jnp.sum(jnp.where(got, value, 0.0), axis=1, keepdims=True)
            one = jnp.sum(jnp.where(here, one, 0.0), axis=0, keepdims=True)
            if where == 0:
                lines = lines + one
            else:
                ticks = ticks + one

    block_rows = lax.broadcasted_iota(jnp.int32, (tick_blocks, 128), 0).astype(jnp.float32)
    member = block_rows == ticks
    rank = count_before(member, before)
    total = jnp.sum(member.astype(jnp.float32), axis=1, keepdims=True)
    groups = jnp.zeros_like(total)
    for step in range(0, owner_total * share, GROUP):
        groups = groups + (total > step).astype(jnp.float32)
    lower = (
        lax.broadcasted_iota(jnp.int32, (tick_blocks, tick_blocks), 0)
        > lax.broadcasted_iota(jnp.int32, (tick_blocks, tick_blocks), 1)
    ).astype(jnp.bfloat16)
    base = jnp.dot(
        lower,
        jnp.broadcast_to(groups, (tick_blocks, 128)).astype(jnp.bfloat16),
        preferred_element_type=jnp.float32,
    )
    place = jnp.sum(jnp.where(member, base * GROUP + rank, 0.0), axis=0, keepdims=True)
    trash = float(group_total(owner_total, share, tick_blocks) * GROUP)
    place = jnp.where(ticks < 0.0, trash, place)
    inside = (base <= lane_f) & (lane_f < base + groups)
    group_tick = jnp.sum(jnp.where(inside, block_rows, 0.0), axis=0, keepdims=True)

    facts = jnp.where(lanes == 0, hot, 0.0)
    facts = jnp.where(lanes == 1, trips, facts)
    facts = jnp.where(lanes == 2, me, facts)
    facts = jnp.where(lanes == 3, start, facts)
    out_ref[...] = jnp.zeros_like(out_ref)
    out_ref[0:1, :] = place.astype(jnp.int32)
    out_ref[1:2, :] = facts.astype(jnp.int32)
    out_ref[2:3, :] = lines.astype(jnp.int32)
    out_ref[3:4, :] = group_tick.astype(jnp.int32)


def group_total(owner_total, share, tick_blocks):
    return (owner_total * share - tick_blocks) // GROUP + tick_blocks


def make_receive_plan(pieces, packed, owner_total, planes, share, wire_blocks, tick_blocks):
    return pl.pallas_call(
        functools.partial(receive_kernel, owner_total, planes, share, wire_blocks, tick_blocks),
        out_shape=(
            jax.ShapeDtypeStruct((8, 128), jnp.int32),
            jax.ShapeDtypeStruct((owner_total, 128), jnp.int32),
        ),
        in_specs=[vmem()] * (1 + len(pieces)),
        out_specs=(vmem(), vmem()),
        compiler_params=pltpu.CompilerParams(vmem_limit_bytes=2 * MIB),
        name="receive_plan",
    )(packed, *pieces)


def agree(rounds):
    devices = lax.axis_size("tick")
    reach = 1
    while reach < devices:
        ring = [(i, (i + reach) % devices) for i in range(devices)]
        rounds = jnp.maximum(rounds, lax.ppermute(rounds, "tick", ring))
        reach *= 2
    return rounds


def band_kernel(taps_w, taps_ref, band_ref):
    row = lax.broadcasted_iota(jnp.int32, (TB, TB), 0)
    col = lax.broadcasted_iota(jnp.int32, (TB, TB), 1)
    pairs = (taps_w + 1) // 2
    band_ref[0, 0 : 3 * TB, TB : 2 * TB] = jnp.zeros((3 * TB, TB), jnp.bfloat16)
    band_ref[pairs - 1, 3 * TB : 6 * TB, 0:TB] = jnp.zeros((3 * TB, TB), jnp.bfloat16)
    taps = taps_ref[...].astype(jnp.float32)
    for tap in range(taps_w):
        spread = jnp.broadcast_to(taps[tap : tap + 1], (TB, 2 * TB))
        rolled = pltpu.roll(spread, TB, 1, stride=1, stride_axis=0)
        middle = rolled[:, :TB]
        outer = rolled[:, TB:]
        bands = (
            jnp.where(col < row, outer, 0.0).astype(jnp.bfloat16),
            middle.astype(jnp.bfloat16),
            jnp.where(col >= row, outer, 0.0).astype(jnp.bfloat16),
        )
        for first, second in ((0, 0), (1, 1), (1, 0), (0, 1)):
            if (tap - first + second) % 2:
                continue
            pair = (tap - first + second) // 2
            for piece in range(3):
                start = (first * 3 + piece) * TB
                band_ref[pair, start : start + TB, second * TB : (second + 1) * TB] = bands[piece]


def make_bands(taps):
    taps_w = taps.shape[0]
    return pl.pallas_call(
        functools.partial(band_kernel, taps_w),
        out_shape=jax.ShapeDtypeStruct(((taps_w + 1) // 2, 6 * TB, 2 * TB), jnp.bfloat16),
        in_specs=[vmem()],
        out_specs=vmem(),
        cost_estimate=pl.CostEstimate(flops=10**9, bytes_accessed=6 * MIB, transcendentals=0),
        compiler_params=pltpu.CompilerParams(vmem_limit_bytes=16 * MIB),
        name="bands",
    )(taps)


def spread_pair(wide_ref, lhs_view, line, pitch, blocks):
    for side in range(2):
        for piece in range(3):
            at = (side * 3 + piece) * TB
            lhs_view[:, at : at + TB] = wide_ref[
                pl.ds((line + side) * pitch + piece, blocks), :
            ].astype(jnp.bfloat16)


def write_lines(total, out_view, signal_ref, line, pairs, blocks):
    for pair in range(pairs):
        for side in range(2):
            out_view[pl.ds((2 * pair + side) * blocks, blocks), :] = total[
                pair * blocks : (pair + 1) * blocks, side * TB : (side + 1) * TB
            ]
    for block in range(blocks):
        signal_ref[line : line + 2 * pairs, block * TB : (block + 1) * TB] = out_view[
            pl.ds(block, 2 * pairs, stride=blocks), :
        ].astype(jnp.bfloat16)


def inner_kernel(
    chunks,
    raw_ref,
    mask_ref,
    left_ref,
    right_ref,
    band_ref,
    inner_ref,
    wide_ref,
    lhs_ref,
    out_ref,
):
    wires, ticks = raw_ref.shape
    blocks = ticks // TB
    pitch = wide_ref.shape[0] // wires
    reach = band_ref.shape[0]
    span = 2 * PAD
    groups = wires // span

    def fill(group, block):
        lines = slice(group * span, (group + 1) * span)
        if block == 0:
            inner = left_ref[lines]
        elif block == blocks + 1:
            inner = right_ref[lines]
        else:
            inner = raw_ref[lines, (block - 1) * TB : block * TB] * mask_ref[lines]
        wide_ref[pl.ds(group * span * pitch + block, span, stride=pitch), :] = inner.astype(
            jnp.float32
        )

    margin = reach - 1
    begin = PAD // 2
    state = {"group": 0, "pair": begin}

    def prepare(upto):
        todo = []
        while state["pair"] < upto:
            line = 2 * state["pair"] - margin
            while state["group"] < groups and line + 1 >= state["group"] * span:
                group = state["group"]
                for block in range(blocks + 2):
                    todo.append(lambda group=group, block=block: fill(group, block))
                state["group"] += 1
            todo.append(
                lambda line=line, pair=state["pair"]: spread_pair(
                    wide_ref, lhs_ref.at[pair - begin], line, pitch, blocks
                )
            )
            state["pair"] += 1
        return todo

    pair = begin
    for job in prepare(pair + chunks[0] + margin):
        job()
    for index, size in enumerate(chunks):
        todo = prepare(pair + size + chunks[index + 1] + margin) if index + 1 < len(chunks) else []
        each = -(-len(todo) // reach)
        total = jnp.zeros((size * blocks, 2 * TB), jnp.float32)
        for step in range(0, reach, STEPS):
            steps = range(step, min(step + STEPS, reach))
            rows = [
                lhs_ref[pair - begin + one : pair - begin + one + size].reshape(
                    size * blocks, 6 * TB
                )
                for one in steps
            ]
            bands = band_ref[steps[0] : steps[-1] + 1].reshape(len(steps) * 6 * TB, 2 * TB)
            total = total + jnp.dot(
                jnp.concatenate(rows, axis=1), bands, preferred_element_type=jnp.float32
            )
            for job in todo[step * each : (steps[-1] + 1) * each]:
                job()
        write_lines(total, out_ref.at[index % 2], inner_ref, 2 * (pair - begin), size, blocks)
        pair += size


def convolve_inner(raw, mask, left, right, bands):
    wires, ticks = raw.shape
    reach = bands.shape[0]
    blocks = ticks // TB
    pitch = -(-(blocks + 2) // 8) * 8
    pairs = (wires - 2 * PAD) // 2
    chunks = []
    while sum(chunks) < pairs:
        chunks.append(min(32 if chunks else 24, pairs - sum(chunks)))
    flops = 2 * blocks * pairs * reach * 6 * TB * 2 * TB
    return pl.pallas_call(
        functools.partial(inner_kernel, tuple(chunks)),
        out_shape=jax.ShapeDtypeStruct((wires - 2 * PAD, ticks), jnp.bfloat16),
        in_specs=[vmem()] * 5,
        out_specs=vmem(),
        scratch_shapes=[
            pltpu.VMEM(((wires + 1) * pitch, TB), jnp.float32),
            pltpu.VMEM((pairs + reach - 1, blocks, 6 * TB), jnp.bfloat16),
            pltpu.VMEM((2, (2 * max(chunks) + 1) * blocks, TB), jnp.float32),
        ],
        cost_estimate=pl.CostEstimate(flops=flops, bytes_accessed=6 * MIB, transcendentals=0),
        compiler_params=pltpu.CompilerParams(vmem_limit_bytes=28 * MIB),
        name="inner",
    )(raw, mask, left, right, bands)


def edge_kernel(
    planes,
    plan_ref,
    own_ref,
    inner_ref,
    raw_ref,
    mask_ref,
    left_ref,
    right_ref,
    top_ref,
    bottom_ref,
    band_ref,
    geo_ref,
    signal_ref,
    *refs,
):
    part_refs = refs[:planes]
    partial_ref, wide_ref, lhs_ref, out_ref, turned_ref = refs[planes:]
    wires, ticks = signal_ref.shape
    blocks = ticks // TB
    reach = band_ref.shape[0]
    block_wires = geo_ref.shape[1]
    wire_blocks = wires // block_wires
    near = 2 * PAD
    lines = PAD + near
    pitch = wide_ref.shape[1] // lines
    pairs = PAD // 2
    margin = reach - 1

    signal_ref[PAD : wires - PAD] = inner_ref[...]
    source = home(plan_ref[1, 2], planes, geo_ref.shape[0] // wire_blocks)
    rows = geo_ref[pl.ds(source * wire_blocks, wire_blocks)].reshape(wires, -1)
    turned_ref[...] = jnp.transpose(rows)

    for end in range(2):
        halo_ref = (top_ref, bottom_ref)[end]
        mine = (slice(0, near), slice(wires - near, wires))[end]
        halo_at = (0, near)[end]
        mine_at = (PAD, 0)[end]
        for block in range(blocks + 2):
            columns = slice(block * TB, (block + 1) * TB)
            if block == 0:
                inner = left_ref[mine].astype(jnp.float32)
            elif block == blocks + 1:
                inner = right_ref[mine].astype(jnp.float32)
            else:
                inner = raw_ref[mine, (block - 1) * TB : block * TB] * mask_ref[mine]
                inner = inner.astype(jnp.float32)
            wide_ref[end, pl.ds(halo_at * pitch + block, PAD, stride=pitch), :] = halo_ref[
                :, columns
            ].astype(jnp.float32)
            wide_ref[end, pl.ds(mine_at * pitch + block, near, stride=pitch), :] = inner
        first = (PAD, near - PAD)[end] - margin
        for pair in range(pairs + margin):
            spread_pair(
                wide_ref.at[end], lhs_ref.at[end, pair], first + 2 * pair, pitch, blocks
            )

    total = jnp.zeros((2 * pairs * blocks, 2 * TB), jnp.float32)
    for step in range(0, reach, STEPS):
        steps = range(step, min(step + STEPS, reach))
        rows = jnp.concatenate(
            [
                jnp.concatenate(
                    [
                        lhs_ref[end, one : one + pairs].reshape(pairs * blocks, 6 * TB)
                        for one in steps
                    ],
                    axis=1,
                )
                for end in range(2)
            ],
            axis=0,
        )
        bands = band_ref[steps[0] : steps[-1] + 1].reshape(len(steps) * 6 * TB, 2 * TB)
        total = total + jnp.dot(rows, bands, preferred_element_type=jnp.float32)
    for end in range(2):
        write_lines(
            total[end * pairs * blocks : (end + 1) * pairs * blocks],
            out_ref.at[end],
            signal_ref,
            (0, wires - PAD)[end],
            pairs,
            blocks,
        )

    cells = geo_ref.shape[2]
    shards = partial_ref.shape[1] // cells
    own = own_ref[...]
    line = lax.broadcasted_iota(jnp.int32, (TABLE, 128), 0)
    table = jnp.where(line == 0, own >> 7, jnp.where(line == 1, own & 127, 0))
    table = table.astype(jnp.float32).astype(jnp.bfloat16)
    for plane in range(planes):
        partial_ref[plane, shards * cells : shards * cells + TABLE] = table

    for block in range(0, blocks, 2):
        chosen = []
        for side in range(2):
            at = slice((block + side) * TB, (block + side + 1) * TB)
            column = []
            for line in range(wire_blocks):
                tile = signal_ref[line * block_wires : (line + 1) * block_wires, at]
                asked = plan_ref[2, line * blocks + block + side] == 1
                column.append(jnp.where(asked, tile, jnp.zeros_like(tile)))
            chosen.append(jnp.concatenate(column, axis=0))
        sums = jnp.dot(
            turned_ref[...], jnp.concatenate(chosen, axis=1), preferred_element_type=jnp.float32
        ).astype(jnp.bfloat16)
        for side in range(2):
            shard, plane = divmod(block + side, planes)
            partial_ref[plane, shard * cells : (shard + 1) * cells] = sums[
                :, side * TB : (side + 1) * TB
            ]
    mine = lax.axis_index("plane")
    for step, ref in enumerate(part_refs):
        ref[...] = partial_ref[lax.bitwise_xor(mine, step)]


def convolve_edges(
    planes, plan, own, inner, raw, mask, left, right, top, bottom, bands, geometry
):
    wires, ticks = raw.shape
    reach = bands.shape[0]
    cells = geometry.shape[2]
    blocks = ticks // TB
    pitch = -(-(blocks + 2) // 8) * 8
    height = blocks // planes * cells + TABLE
    flops = 2 * blocks * PAD * reach * 6 * TB * 2 * TB
    return pl.pallas_call(
        functools.partial(edge_kernel, planes),
        out_shape=(
            jax.ShapeDtypeStruct((wires, ticks), jnp.bfloat16),
        )
        + (jax.ShapeDtypeStruct((height, TB), jnp.bfloat16),) * planes,
        in_specs=[smem()] + [vmem()] * 10,
        out_specs=(vmem(),) * (1 + planes),
        scratch_shapes=[
            pltpu.VMEM((planes, height, TB), jnp.bfloat16),
            pltpu.VMEM((2, (3 * PAD + 1) * pitch, TB), jnp.float32),
            pltpu.VMEM((2, PAD // 2 + reach - 1, blocks, 6 * TB), jnp.bfloat16),
            pltpu.VMEM((2, (PAD + 1) * blocks, TB), jnp.float32),
            pltpu.VMEM((cells, wires), jnp.bfloat16),
        ],
        cost_estimate=pl.CostEstimate(flops=flops, bytes_accessed=6 * MIB, transcendentals=0),
        compiler_params=pltpu.CompilerParams(vmem_limit_bytes=24 * MIB),
        name="edges",
    )(plan, own, inner, raw, mask, left, right, top, bottom, bands, geometry)


def fold_kernel(planes, *refs):
    pieces = refs[:planes]
    outs = refs[planes:-1]
    sums_ref = refs[-1]
    shards, lines, _ = sums_ref.shape
    cells = lines - TABLE
    mine = lax.axis_index("plane")
    line = lax.broadcasted_iota(jnp.int32, (TABLE, 128), 0)
    table = jnp.zeros((TABLE, 128), jnp.float32)
    for step, ref in enumerate(pieces):
        tags = ref[shards * cells :].astype(jnp.float32)
        plane = lax.bitwise_xor(mine, step)
        table = jnp.where(line == 2 * plane, tags[0:1], table)
        table = jnp.where(line == 2 * plane + 1, tags[1:2], table)
    for shard in range(shards):
        total = jnp.zeros((cells, TB), jnp.float32)
        for ref in pieces:
            total = total + ref[shard * cells : (shard + 1) * cells].astype(jnp.float32)
        sums_ref[shard, 0:cells] = total.astype(jnp.bfloat16)
        sums_ref[shard, cells:lines] = table.astype(jnp.bfloat16)
    mine = lax.axis_index("wire")
    for step, ref in enumerate(outs):
        ref[...] = sums_ref[lax.bitwise_xor(mine, step)]


def fold(pieces, shards):
    cells = (pieces[0].shape[0] - TABLE) // shards
    out = jax.ShapeDtypeStruct((cells + TABLE, TB), jnp.bfloat16)
    return pl.pallas_call(
        functools.partial(fold_kernel, len(pieces)),
        out_shape=(out,) * shards,
        in_specs=[vmem()] * len(pieces),
        out_specs=(vmem(),) * shards,
        scratch_shapes=[pltpu.VMEM((shards, cells + TABLE, TB), jnp.bfloat16)],
        compiler_params=pltpu.CompilerParams(vmem_limit_bytes=4 * MIB),
        name="fold",
    )(*pieces)


def swap_all(parts, axis):
    got = [parts[0]]
    for step in range(1, len(parts)):
        pairs = [(i, i ^ step) for i in range(len(parts))]
        got.append(lax.ppermute(parts[step], axis, pairs))
    return got


def pack_kernel(slots, plan_ref, signal_ref, payload_ref, tiles_ref):
    block_wires = payload_ref.shape[1]
    wires, ticks = signal_ref.shape
    blocks = ticks // TB
    tiles_ref[...] = jnp.zeros_like(tiles_ref)
    for line in range(wires // block_wires):
        for block in range(blocks):
            place = plan_ref[0, line * blocks + block]
            tiles_ref[place] = signal_ref[
                line * block_wires : (line + 1) * block_wires, block * TB : (block + 1) * TB
            ]
    payload_ref[...] = tiles_ref[0:slots]


def pack_tiles(plan, signal, slots, block_wires):
    return pl.pallas_call(
        functools.partial(pack_kernel, slots),
        out_shape=jax.ShapeDtypeStruct((slots, block_wires, TB), jnp.bfloat16),
        in_specs=[smem(), vmem()],
        out_specs=vmem(),
        scratch_shapes=[pltpu.VMEM((slots + 1, block_wires, TB), jnp.bfloat16)],
        cost_estimate=pl.CostEstimate(flops=10**8, bytes_accessed=3 * MIB, transcendentals=0),
        compiler_params=pltpu.CompilerParams(vmem_limit_bytes=8 * MIB),
        name="pack",
    )(plan, signal)


def stage_kernel(slots, plan_ref, geo_ref, out_ref, rows_ref):
    groups = out_ref.shape[0]
    rows_ref[...] = jnp.zeros_like(rows_ref)
    for slot in range(slots):
        rows_ref[plan_ref[0, slot]] = geo_ref[plan_ref[2, slot]]
    for group in range(groups):
        rows = rows_ref[group * GROUP : (group + 1) * GROUP]
        out_ref[group] = jnp.transpose(rows.reshape(-1, rows.shape[-1]))


def stage_geometry(plan, geometry, groups, slots):
    _, block_wires, cells = geometry.shape
    return pl.pallas_call(
        functools.partial(stage_kernel, slots),
        out_shape=jax.ShapeDtypeStruct((groups, cells, GROUP * block_wires), jnp.bfloat16),
        in_specs=[smem(), vmem()],
        out_specs=vmem(),
        scratch_shapes=[pltpu.VMEM((groups * GROUP + 1, block_wires, cells), jnp.bfloat16)],
        cost_estimate=pl.CostEstimate(flops=10**8, bytes_accessed=3 * MIB, transcendentals=0),
        compiler_params=pltpu.CompilerParams(vmem_limit_bytes=12 * MIB),
        name="stage",
    )(plan, geometry)


def image_kernel(owner_total, share, plan_ref, arrived_ref, staged_ref, image_ref, tiles_ref):
    cells, ticks = image_ref.shape
    block_wires = arrived_ref.shape[1]
    groups = staged_ref.shape[0]
    is_hot = plan_ref[1, 0] == plan_ref[1, 2]
    counts = plan_ref[1, 3] == 1

    @pl.when(is_hot)
    def _():
        for source in range(owner_total):
            sums = arrived_ref[source * share : source * share + cells // block_wires]
            image_ref[:, source * TB : (source + 1) * TB] = sums.reshape(cells, TB).astype(
                jnp.float32
            )

    @pl.when(jnp.logical_not(is_hot))
    def _():
        image_ref[...] = jnp.zeros_like(image_ref)
        tiles_ref[...] = jnp.zeros_like(tiles_ref)

        @pl.when(counts)
        def _():
            for slot in range(owner_total * share):
                tiles_ref[plan_ref[0, slot]] = arrived_ref[slot]
            for group in range(groups):
                tiles = tiles_ref[group * GROUP : (group + 1) * GROUP]
                at = pl.ds(pl.multiple_of(plan_ref[3, group] * TB, TB), TB)
                image_ref[:, at] += jnp.dot(
                    staged_ref[group],
                    tiles.reshape(GROUP * block_wires, TB),
                    preferred_element_type=jnp.float32,
                )


def make_image(plan, arrived, staged, owner_total, share, ticks):
    groups, cells, _ = staged.shape
    block_wires = arrived.shape[1]
    return pl.pallas_call(
        functools.partial(image_kernel, owner_total, share),
        out_shape=jax.ShapeDtypeStruct((cells, ticks), jnp.float32),
        in_specs=[smem(), vmem(), vmem()],
        out_specs=vmem(),
        scratch_shapes=[
            pltpu.VMEM((groups * GROUP + 1, block_wires, TB), jnp.bfloat16),
        ],
        cost_estimate=pl.CostEstimate(flops=10**8, bytes_accessed=3 * MIB, transcendentals=0),
        compiler_params=pltpu.CompilerParams(vmem_limit_bytes=16 * MIB),
        name="image",
    )(plan, arrived, staged)


def more_kernel(owner_total, planes, share, plan_ref, table_ref, arrived_ref, geo_ref, before_ref, image_ref):
    cells, ticks = image_ref.shape
    blocks = ticks // TB
    wire_blocks = geo_ref.shape[0] // owner_total
    image_ref[...] = before_ref[...]

    @pl.when(plan_ref[1, 0] != plan_ref[1, 2])
    def _():
        def add(source, carry):
            for slot in range(share):
                block = table_ref[source, slot]
                at = pl.multiple_of((block % blocks) * TB, TB)
                image_ref[:, pl.ds(at, TB)] += lax.dot_general(
                    geo_ref[home(source, planes, owner_total) * wire_blocks + block // blocks],
                    arrived_ref[source * share + slot],
                    (((0,), (0,)), ((), ())),
                    preferred_element_type=jnp.float32,
                )
            return carry

        lax.fori_loop(0, owner_total, add, 0)


def add_to_image(plan, table, arrived, geometry, owner_total, planes, share, image):
    return pl.pallas_call(
        functools.partial(more_kernel, owner_total, planes, share),
        out_shape=jax.ShapeDtypeStruct(image.shape, jnp.float32),
        in_specs=[smem(), smem()] + [vmem()] * 3,
        out_specs=vmem(),
        compiler_params=pltpu.CompilerParams(vmem_limit_bytes=16 * MIB),
        name="image_more",
    )(plan, table, arrived, geometry, image)


def further_round(
    trip, image, signal, geometry, rows, packed, plan, owner_total, planes, share
):
    trip, signal, rows, packed, plan = lax.optimization_barrier((trip, signal, rows, packed, plan))
    step = trip + plan[1, 3]
    hot = plan[1, 0]
    me = plan[1, 2]
    block_wires = geometry.shape[1]
    wire_count, tick_count = signal.shape
    blocks = tick_count // TB
    wire_blocks = wire_count // block_wires
    ids = jnp.arange(owner_total, dtype=jnp.int32)

    def ranks(owners):
        member = (owners[..., None] == ids).astype(jnp.int32)
        before = jnp.cumsum(member, axis=-2) - member
        return jnp.sum(before * member, axis=-1) - step * share

    def live(owners, rank):
        return (owners < owner_total) & (owners != hot) & (rank >= 0) & (rank < share)

    owners = packed[0] >> 7
    block = packed[0] & 127
    rank = ranks(owners)
    place = jnp.where(live(owners, rank), owners * share + rank, owner_total * share)
    tiles = signal.reshape(wire_blocks, block_wires, blocks, TB).transpose(0, 2, 1, 3)
    tiles = tiles.reshape(wire_blocks * blocks, block_wires, TB)[block]
    payload = jnp.zeros((owner_total * share, block_wires, TB), jnp.bfloat16)
    payload = payload.at[place].set(tiles, mode="drop")
    arrived = exchange(payload.reshape(owner_total, share, block_wires, TB))

    owners = rows >> 7
    rank = ranks(owners)
    source = jnp.arange(owner_total, dtype=jnp.int32)[:, None]
    line = jnp.where(live(owners, rank) & (owners == me), source, owner_total)
    table = jnp.zeros((owner_total, 128), jnp.int32)
    table = table.at[line, jnp.maximum(rank, 0)].set(rows & 127, mode="drop")
    return add_to_image(
        plan,
        table,
        arrived.reshape(owner_total * share, block_wires, TB),
        geometry,
        owner_total,
        planes,
        share,
        image,
    )


def tick_halo(sides):
    devices = lax.axis_size("tick")
    if devices == 2:
        tick = lax.axis_index("tick")
        got = lax.ppermute(sides[0], "tick", [(0, 1), (1, 0)])
        nothing = jnp.zeros_like(got)
        return jnp.where(tick == 0, nothing, got), jnp.where(tick == 0, got, nothing)
    up = [(i, i + 1) for i in range(devices - 1)]
    down = [(i + 1, i) for i in range(devices - 1)]
    return lax.ppermute(sides[1], "tick", up), lax.ppermute(sides[0], "tick", down)


def wire_halo(first, last, left, right):
    devices = lax.axis_size("wire")
    odd = lax.axis_index("wire") % 2 == 1
    last = jnp.concatenate([left[-PAD:], last, right[-PAD:]], axis=1)
    first = jnp.concatenate([left[:PAD], first, right[:PAD]], axis=1)
    got = []
    for begin, rows in ((0, jnp.where(odd, first, last)), (1, jnp.where(odd, last, first))):
        pairs = [(i, i + 1) for i in range(begin, devices - 1, 2)]
        got.append(lax.ppermute(rows, "wire", pairs + [(j, i) for i, j in pairs]))
    return jnp.where(odd, got[0], got[1]), jnp.where(odd, got[1], got[0])


def exchange(array, axes=("wire", "plane")):
    return lax.all_to_all(array, axes, split_axis=0, concat_axis=0, tiled=True)


def shards(raw, chan_mask, kernel, geometry, roi_block, roi_owner):
    wires, ticks = raw.shape
    slot_count = roi_block.shape[0]
    block_wires = geometry.shape[1]
    cells = geometry.shape[2]
    tick_blocks = ticks // TB
    planes = lax.axis_size("plane")
    wire_shards = lax.axis_size("wire")
    owner_total = planes * wire_shards
    share = -(-(slot_count - CAP) // (owner_total - 1))

    mask, first, last, packed, send_plan, *sides = prepare(
        raw, chan_mask, roi_owner, roi_block, planes, owner_total, share
    )
    left, right = tick_halo(sides)
    top, bottom = wire_halo(first, last, left, right)
    bands = make_bands(kernel[0])
    inner = convolve_inner(raw, mask, left, right, bands)
    signal, *parts = convolve_edges(
        planes, send_plan, packed, inner, raw, mask, left, right, top, bottom, bands, geometry
    )

    pieces = swap_all(parts, "plane")
    payload = pack_tiles(send_plan, signal, owner_total * share, block_wires)
    pieces, payload = lax.optimization_barrier((pieces, payload))
    pieces = swap_all(fold(pieces, wire_shards), "wire")

    plan, rows = make_receive_plan(
        pieces, packed, owner_total, planes, share, wires // block_wires, tick_blocks
    )
    staged = stage_geometry(
        plan, geometry, group_total(owner_total, share, tick_blocks), owner_total * share
    )

    sums = sum(piece[:cells].astype(jnp.float32) for piece in pieces).astype(jnp.bfloat16)
    payload = lax.dynamic_update_slice(
        payload.reshape(owner_total, share, block_wires, TB),
        sums.reshape(1, cells // block_wires, block_wires, TB),
        (send_plan[1, 0], 0, 0, 0),
    )
    arrived = exchange(payload).reshape(owner_total * share, block_wires, TB)
    image = make_image(plan, arrived, staged, owner_total, share, ticks)

    trips = agree(plan[1:2, 1:2])[0, 0]
    image = lax.fori_loop(
        0,
        trips,
        lambda trip, now: further_round(
            trip, now, signal, geometry, rows, packed, plan, owner_total, planes, share
        ),
        image,
    )
    return signal, image


def solution(mesh):
    in_specs = (
        P(("plane", "wire"), "tick"),
        P(("plane", "wire")),
        P("plane", None, None),
        P(),
        P(("plane", "wire", "tick")),
        P(("plane", "wire", "tick")),
    )
    out_specs = (P(("plane", "wire"), "tick"), P(("plane", "wire"), "tick"))
    return jax.shard_map(shards, mesh=mesh, in_specs=in_specs, out_specs=out_specs, check_vma=False)
```
